32 devices in a mesh: ctx: 8 (over z, x), fsdp: 4 (over y, core).
Axes of the slice: x: 2, y: 2, z: 4, core: 2. Of those that a mesh axis runs over, the one named last changes fastest.
Arguments:
- tokens: bfloat16 [4, 1024, 2048], P('fsdp', 'ctx'), may hold values from -6 to 6
- doc_lengths: int32 [4, 16], P('fsdp'), may hold values from 1 to 512, 1024 in all within a row
- routes: int32 [4, 1024, 3], P('fsdp', 'ctx'), may hold values from 0 to 5, all different within a row
- slot_order: int32 [4, 1024, 3], P('fsdp', 'ctx'), may hold values from 0 to 383, as said below
- attn_gain: bfloat16 [2048], P('fsdp'), may hold values from 0.5 to 1.5
- w_qkv: bfloat16 [2048, 6144], P('fsdp'), may hold values from -0.125 to 0.125
- q_gain: bfloat16 [2048], P('fsdp'), may hold values from 0.5 to 1.5
- k_gain: bfloat16 [2048], P('fsdp'), may hold values from 0.5 to 1.5
- w_out: bfloat16 [2048, 2048], P('fsdp'), may hold values from -0.375 to 0.375
- ffn_gain: bfloat16 [2048], P('fsdp'), may hold values from 0.5 to 1.5
- w_router: bfloat16 [2048, 6], P('fsdp'), may hold values from -0.09375 to 0.09375
- w_gate: bfloat16 [6, 2048, 1024], P(None, None, 'fsdp'), may hold values from -0.125 to 0.125
- w_up: bfloat16 [6, 2048, 1024], P(None, None, 'fsdp'), may hold values from -0.125 to 0.125
- w_down: bfloat16 [6, 1024, 2048], P(None, 'fsdp'), may hold values from -0.75 to 0.75
- cotangent: bfloat16 [4, 1024, 2048], P('fsdp', 'ctx'), may hold values from -6 to 6
Outputs:
- activations: bfloat16 [4, 1024, 2048], P('fsdp', 'ctx')
- input_grad: float32 [4, 1024, 2048], P('fsdp', 'ctx')
- g_attn_gain: float32 [2048], P('fsdp')
- g_qkv: float32 [2048, 6144], P('fsdp', 'ctx')
- g_q_gain: float32 [2048], P('fsdp')
- g_k_gain: float32 [2048], P('fsdp')
- g_out: float32 [2048, 2048], P('fsdp', 'ctx')
- g_ffn_gain: float32 [2048], P('fsdp')
- g_router: float32 [2048, 6], P('fsdp')
- g_gate: float32 [6, 2048, 1024], P(None, 'ctx', 'fsdp')
- g_up: float32 [6, 2048, 1024], P(None, 'ctx', 'fsdp')
- g_down: float32 [6, 1024, 2048], P(None, 'fsdp', 'ctx')
The draws below stay inside these ranges and needn't reach their ends.
Inputs may be any that keep to these rules, and one draw needn't show every extreme that they name: `slot_order`: within each aligned block of 128 rows of a stream the 384 values are a permutation. `doc_lengths`: the lengths of a stream sum to 1024; the longest is 512. `routes`: each row names 3 different experts.
All inputs are finite; a program needn't handle non-finite values.
Results may differ from the reference program's by a relative error of at most 0.02.
Values may be sent and summed in bfloat16 or wider, within the bound.
A program may use at most 448 MiB of HBM per device.

```python
import math
import jax
import jax.numpy as jnp
import numpy as np
from jax import lax

D = 2048
HEADS = 16
HEAD_DIM = 128
H = 1024
E = 6
TOPK = 3
TOK_DEV = 128
STREAM_LEN = 1024
STREAMS = 4
NDOCS = 16
DOC_MOST = 512
N_CTX = 8


def draw_one_order(subkey):
    return jax.random.permutation(subkey, TOK_DEV * TOPK)


def draw_slot_order(key, part):
    block_total = STREAMS * (STREAM_LEN // TOK_DEV)
    subkeys = jax.random.split(key, block_total)
    orders = jax.vmap(draw_one_order)(subkeys)
    return orders.reshape(STREAMS, STREAM_LEN, TOPK).astype(jnp.int32)


def shard_levels(key, shape, cuts, low, high):
    def one(position, blocks):
        draws = jax.random.uniform(jax.random.fold_in(jax.random.fold_in(key, 6), position), (blocks,), jnp.float32, low / len(cuts), high / len(cuts))
        return jnp.repeat(jnp.exp(draws), shape[position] // blocks).reshape((-1,) + (1,) * (len(shape) - position - 1))

    level = one(*cuts[0])
    for cut in cuts[1:]:
        level = level * one(*cut)
    return level


def picks_of(own_key, rows, count, top, lift):
    order = jax.random.permutation(jax.random.fold_in(own_key, 1), count)
    pull = order
    for power in range(3):
        pull = pull * pull // count
    pull = pull * lift // count
    tickets = jax.random.randint(jax.random.fold_in(own_key, 2), (rows, count), 0, 4096) + pull
    fixed_rows = jax.random.permutation(jax.random.fold_in(own_key, 3), rows)[jnp.arange(count) % rows]
    tickets = jnp.where(jnp.arange(rows)[:, None] == fixed_rows[None, :], 1 << 14, tickets)
    score = tickets * count + jnp.arange(count)
    return lax.top_k(score.astype(jnp.int32), top)[1].astype(jnp.int32)


def profile(count, total, bound, lean):
    loads = [(1 << 20) // math.isqrt(standing ** lean) + 1 for standing in range(2, count + 1)]
    surplus, counts = total - bound - (count - 1), [1] * (count - 1)
    while surplus > 0:
        candidates = [i for i in range(count - 1) if counts[i] < bound]
        whole, remaining = sum([loads[i] for i in candidates]), surplus
        for i in candidates:
            addition = min(bound - counts[i], max(1, remaining * loads[i] // whole), surplus)
            counts[i] = counts[i] + addition
            surplus = surplus - addition
    return np.array([bound] + counts)


def ragged_sizes(key, amount, total, limit, skew):
    if amount == 2:
        one = jax.random.randint(key, (), max(1, total - limit), min(limit, total - 1) + 1)
        return jnp.stack([one, total - one])
    tallies = jnp.asarray(profile(amount, total, limit, skew), jnp.int32)
    pairs = (amount - 1) // 2
    donor, receiver = tallies[1:1 + 2 * pairs:2], tallies[2:2 + 2 * pairs:2]
    slack = jnp.minimum(donor - 1, limit - receiver)
    moved = jax.random.randint(jax.random.fold_in(key, 1), (pairs,), 0, 1 << 20) % (slack + 1)
    tallies = tallies.at[1:1 + 2 * pairs:2].set(donor - moved).at[2:2 + 2 * pairs:2].set(receiver + moved)
    return tallies[jax.random.permutation(jax.random.fold_in(key, 2), amount)]


def bell_draw(key, dims, scale, bound, cuts=(), kind=jnp.bfloat16):
    gain = shard_levels(key, dims, cuts, -0.22, 0.18) if cuts else 1.0
    drawn = jax.random.normal(key, dims, jnp.float32) * scale * gain
    return jnp.minimum(jnp.maximum(drawn, -bound), bound).astype(kind)


def setup_inputs(seed: int = 0) -> dict:
    arg_keys = jax.random.split(jax.random.key(seed), 16)
    tokens = bell_draw(arg_keys[0], (STREAMS, STREAM_LEN, D), 1.0, 6.0, ((0, 4), (1, 8)))
    doc_lengths = jax.vmap(lambda own: ragged_sizes(own, NDOCS, STREAM_LEN, DOC_MOST, 2))(jax.random.split(arg_keys[1], STREAMS)).reshape((STREAMS, NDOCS)).astype(jnp.int32)
    routes = picks_of(arg_keys[2], STREAMS * STREAM_LEN, E, TOPK, 4096).reshape((STREAMS, STREAM_LEN, TOPK))
    slot_order = draw_slot_order(jax.random.fold_in(arg_keys[15], 71), 0)
    attn_gain = jnp.clip(1.0 + 0.1 * jax.random.normal(arg_keys[4], (D,), jnp.float32), 0.5, 1.5).astype(jnp.bfloat16)
    w_qkv = bell_draw(arg_keys[5], (D, 3 * D), D ** -0.5, 0.125, ((0, 4),))
    q_gain = jnp.clip(1.0 + 0.1 * jax.random.normal(arg_keys[6], (D,), jnp.float32), 0.5, 1.5).astype(jnp.bfloat16)
    k_gain = jnp.clip(1.0 + 0.1 * jax.random.normal(arg_keys[7], (D,), jnp.float32), 0.5, 1.5).astype(jnp.bfloat16)
    w_out = bell_draw(arg_keys[8], (D, D), (D // 8) ** -0.5, 0.375, ((0, 4),))
    ffn_gain = jnp.clip(1.0 + 0.1 * jax.random.normal(arg_keys[9], (D,), jnp.float32), 0.5, 1.5).astype(jnp.bfloat16)
    w_router = bell_draw(arg_keys[10], (D, E), (2 * D) ** -0.5, 0.09375, ((0, 4),))
    w_gate = bell_draw(arg_keys[11], (E, D, H), D ** -0.5, 0.125, ((2, 4),))
    w_up = bell_draw(arg_keys[12], (E, D, H), D ** -0.5, 0.125, ((2, 4),))
    w_down = bell_draw(arg_keys[13], (E, H, D), (H // 16) ** -0.5, 0.75, ((1, 4),))
    cotangent = bell_draw(arg_keys[14], (STREAMS, STREAM_LEN, D), 1.0, 6.0, ((0, 4), (1, 8)))
    return {"tokens": tokens, "doc_lengths": doc_lengths, "routes": routes, "slot_order": slot_order, "attn_gain": attn_gain, "w_qkv": w_qkv, "q_gain": q_gain, "k_gain": k_gain, "w_out": w_out, "ffn_gain": ffn_gain, "w_router": w_router, "w_gate": w_gate, "w_up": w_up, "w_down": w_down, "cotangent": cotangent}


EPSILON = 1e-05
ROPE_BASE = 10000.0
HIGHEST = lax.Precision.HIGHEST

@jax.custom_vjp
def low(v):
    return lax.optimization_barrier(v.astype(jnp.bfloat16)).astype(jnp.float32)

@jax.custom_vjp
def low_back(v):
    return v

def low_keep(v):
    return (low(v), None)

def low_pass(kept, grad):
    return (grad,)

def back_keep(v):
    return (v, None)

def back_low(kept, grad):
    return (low(grad),)
low.defvjp(low_keep, low_pass)
low_back.defvjp(back_keep, back_low)

def rms_scale(values, gain_vector):
    return values * lax.rsqrt(lax.optimization_barrier(jnp.mean(values * values, axis=-1, keepdims=True)) + EPSILON) * gain_vector

def rotate(values, inner_pos):
    half_dim = values.shape[-1] // 2
    freq_table = ROPE_BASE ** (-2.0 * jnp.arange(half_dim, dtype=jnp.float32) / values.shape[-1])
    angles = inner_pos.astype(jnp.float32)[:, None] * freq_table[None, :]
    cosine = jnp.cos(angles)[:, None, :]
    sine_part = jnp.sin(angles)[:, None, :]
    first_half = values[..., :half_dim]
    second_half = values[..., half_dim:]
    return jnp.concatenate([first_half * cosine - second_half * sine_part, second_half * cosine + first_half * sine_part], axis=-1)

def dealt_position(flat_index, per_device, device_count):
    device_index = flat_index // per_device
    within = flat_index % per_device
    half_rows = per_device // 2
    return jnp.where(within < half_rows, device_index * half_rows + within, (2 * device_count - 1 - device_index) * half_rows + within - half_rows).astype(jnp.int32)

def document_info(positions, lengths):
    doc_ends = jnp.cumsum(lengths).astype(jnp.int32)
    passed = doc_ends[None, :] <= positions[:, None]
    doc_ids = lax.optimization_barrier(jnp.sum(passed.astype(jnp.int32), axis=1)).astype(jnp.int32)
    inner_pos = (positions - lax.optimization_barrier(jnp.sum(jnp.where(passed, lengths[None, :], 0), axis=1))).astype(jnp.int32)
    return (doc_ids, inner_pos)

def slot_table(route_ids, order_ids, capacity, expert_count):
    pair_count = route_ids.shape[0] * route_ids.shape[1]
    expert_flat = route_ids.reshape(pair_count)
    rank_flat = order_ids.reshape(pair_count)
    earlier = (expert_flat[None, :] == expert_flat[:, None]) & (rank_flat[None, :] < rank_flat[:, None])
    slot_index = lax.optimization_barrier(jnp.sum(earlier.astype(jnp.int32), axis=1)).astype(jnp.int32)
    placed = jnp.where(slot_index < capacity, expert_flat * capacity + slot_index, expert_count * capacity).astype(jnp.int32)
    source = jnp.full((expert_count * capacity + 1,), pair_count, jnp.int32).at[placed].set(jnp.arange(pair_count, dtype=jnp.int32))
    return (placed, source[:expert_count * capacity])

def attend(queries, keys_rot, values_in, positions, doc_ids):
    row_count = queries.shape[0]
    block_rows = math.gcd(row_count, 512)
    block_count = row_count // block_rows
    score_scale = queries.shape[-1] ** (-0.5)

    def one_block(pieces):
        query_block, pos_block, doc_block = pieces
        scores = low_back(jnp.einsum('qhd,khd->hqk', query_block, keys_rot, precision=HIGHEST) * score_scale)
        allowed = (doc_block[:, None] == doc_ids[None, :]) & (positions[None, :] <= pos_block[:, None])
        scores = jnp.where(allowed[None], scores, -jnp.inf)
        prob_low = low(jax.nn.softmax(scores, axis=-1))
        return jnp.einsum('hqk,khd->qhd', prob_low, values_in, precision=HIGHEST)
    outputs = lax.map(jax.checkpoint(one_block), (queries.reshape(block_count, block_rows, queries.shape[1], queries.shape[2]), positions.reshape(block_count, block_rows), doc_ids.reshape(block_count, block_rows)))
    return outputs.reshape(queries.shape)

def expert_layer(normed, route_ids, order_ids, w_router, w_gate, w_up, w_down):
    row_count = normed.shape[0]
    model_width = normed.shape[1]
    expert_count = w_gate.shape[0]
    top_count = route_ids.shape[1]
    capacity = row_count * top_count // expert_count
    logits = low_back(jnp.dot(normed, w_router, precision=HIGHEST))
    router_probs = jax.nn.softmax(logits, axis=-1)
    chosen = (route_ids[:, :, None] == jnp.arange(expert_count, dtype=jnp.int32)[None, None, :]).astype(jnp.float32)
    gate_values = lax.optimization_barrier(jnp.sum(chosen * router_probs[:, None, :], axis=-1))
    placed, source = slot_table(route_ids, order_ids, capacity, expert_count)
    padded = jnp.concatenate([normed, jnp.zeros((1, model_width), jnp.float32)], axis=0)
    expert_in = padded[source // top_count].reshape(expert_count, capacity, model_width)
    gate_pre = low_back(jnp.einsum('ecd,edh->ech', expert_in, w_gate, precision=HIGHEST))
    up_pre = low_back(jnp.einsum('ecd,edh->ech', expert_in, w_up, precision=HIGHEST))
    hidden = low(jax.nn.silu(gate_pre) * up_pre)
    expert_out = low_back(jnp.einsum('ech,ehd->ecd', hidden, w_down, precision=HIGHEST))
    out_padded = jnp.concatenate([expert_out.reshape(expert_count * capacity, model_width), jnp.zeros((1, model_width), jnp.float32)], axis=0)
    per_pair = out_padded[placed].reshape(row_count, top_count, model_width)
    return lax.optimization_barrier(jnp.sum(gate_values[:, :, None] * per_pair, axis=1))

def one_stream(stream_rows, lengths, route_ids, order_ids, weights):
    attn_gain, w_qkv, q_gain, k_gain, w_out, ffn_gain, w_router, w_gate, w_up, w_down = weights
    row_count = stream_rows.shape[0]
    model_width = stream_rows.shape[1]
    positions = dealt_position(jnp.arange(row_count, dtype=jnp.int32), TOK_DEV, N_CTX)
    doc_ids, inner_pos = document_info(positions, lengths)
    normed = low(rms_scale(stream_rows, attn_gain))
    projected = jnp.dot(normed, w_qkv, precision=HIGHEST)
    query_lin = low_back(projected[:, :model_width])
    key_lin = low_back(projected[:, model_width:2 * model_width])
    value_low = low(low_back(projected[:, 2 * model_width:]))
    queries = low(rotate(rms_scale(query_lin, q_gain).reshape(row_count, HEADS, HEAD_DIM), inner_pos))
    keys_rot = low(rotate(rms_scale(key_lin, k_gain).reshape(row_count, HEADS, HEAD_DIM), inner_pos))
    attended = attend(queries, keys_rot, value_low.reshape(row_count, HEADS, HEAD_DIM), positions, doc_ids).reshape(row_count, model_width)
    attended = low(low_back(attended))
    mixed = stream_rows + low_back(jnp.dot(attended, w_out, precision=HIGHEST))
    normed_two = low(rms_scale(mixed, ffn_gain))
    blocks = row_count // TOK_DEV
    expert_sum = jax.vmap(expert_layer, in_axes=(0, 0, 0, None, None, None, None))(normed_two.reshape(blocks, TOK_DEV, model_width), route_ids.reshape(blocks, TOK_DEV, TOPK), order_ids.reshape(blocks, TOK_DEV, TOPK), w_router, w_gate, w_up, w_down)
    return mixed + expert_sum.reshape(row_count, model_width)

def reference(tokens, doc_lengths, routes, slot_order, attn_gain, w_qkv, q_gain, k_gain, w_out, ffn_gain, w_router, w_gate, w_up, w_down, cotangent):
    floats = (tokens, attn_gain, w_qkv, q_gain, k_gain, w_out, ffn_gain, w_router, w_gate, w_up, w_down)
    floats = tuple((item.astype(jnp.float32) for item in floats))

    def forward(token_rows, *weights):

        def per_stream(pieces):
            return one_stream(pieces[0], pieces[1], pieces[2], pieces[3], weights)
        return lax.map(per_stream, (token_rows, doc_lengths, routes, slot_order))
    outputs, pullback = jax.vjp(forward, *floats)
    gradients = pullback(cotangent.astype(jnp.float32))
    return (outputs.astype(jnp.bfloat16), gradients[0], gradients[1], gradients[2], gradients[3], gradients[4], gradients[5], gradients[6], gradients[7], gradients[8], gradients[9], gradients[10])
```

```python
import math

import jax
import jax.numpy as jnp
from jax import lax
from jax.sharding import PartitionSpec as P

HEADS = 16


EPSILON = 1e-05
ROPE_BASE = 10000.0
MASKED = -1e30


def rms_scale(values, gain_vector):
    return (
        values
        * lax.rsqrt(jnp.mean(values * values, axis=-1, keepdims=True) + EPSILON)
        * gain_vector
    )


def rotate(values, inner_pos):
    half_dim = values.shape[-1] // 2
    freq_table = ROPE_BASE ** (-2.0 * jnp.arange(half_dim, dtype=jnp.float32) / values.shape[-1])
    angles = inner_pos.astype(jnp.float32)[:, None] * freq_table[None, :]
    cosine = jnp.cos(angles)[:, None, :]
    sine_part = jnp.sin(angles)[:, None, :]
    first_half = values[..., :half_dim]
    second_half = values[..., half_dim:]
    return jnp.concatenate(
        [
            first_half * cosine - second_half * sine_part,
            second_half * cosine + first_half * sine_part,
        ],
        axis=-1,
    )


def dealt_position(flat_index, per_device, device_count):
    device_index = flat_index // per_device
    within = flat_index % per_device
    half_rows = per_device // 2
    return jnp.where(
        within < half_rows,
        device_index * half_rows + within,
        (2 * device_count - 1 - device_index) * half_rows + within - half_rows,
    )


def document_info(positions, lengths):
    doc_ends = jnp.sum(jnp.where(jnp.arange(lengths.shape[0])[:, None] >= jnp.arange(lengths.shape[0])[None, :], lengths[None, :], 0), axis=1)
    passed = doc_ends[None, :] <= positions[:, None]
    doc_ids = jnp.sum(passed.astype(jnp.int32), axis=1)
    inner_pos = positions - jnp.sum(jnp.where(passed, lengths[None, :], 0), axis=1)
    return (doc_ids, inner_pos)


def slot_table(route_ids, order_ids, capacity, expert_count):
    pair_count = route_ids.shape[0] * route_ids.shape[1]
    expert_flat = route_ids.reshape(pair_count)
    rank_flat = order_ids.reshape(pair_count)
    earlier = (expert_flat[None, :] == expert_flat[:, None]) & (
        rank_flat[None, :] < rank_flat[:, None]
    )
    slot_index = jnp.sum(earlier.astype(jnp.int32), axis=1)
    placed = jnp.where(
        slot_index < capacity, expert_flat * capacity + slot_index, expert_count * capacity
    )
    source = (
        jnp.full((expert_count * capacity + 1,), pair_count, jnp.int32)
        .at[placed]
        .set(jnp.arange(pair_count, dtype=jnp.int32))
    )
    return (placed, source[: expert_count * capacity])


def masked_scores(query_block, key_block, query_pos, query_doc, key_pos, key_doc, score_scale):
    scores = (
        jnp.einsum("qhd,khd->hqk", query_block, key_block, preferred_element_type=jnp.float32)
        * score_scale
    )
    allowed = (query_doc[:, None] == key_doc[None, :]) & (key_pos[None, :] <= query_pos[:, None])
    return jnp.where(allowed[None], scores, MASKED)


def silu_parts(hidden_grad, slot_gate, slot_up):
    sigma = jax.nn.sigmoid(slot_gate)
    gate_grad_low = (hidden_grad * slot_up * sigma * (1.0 + slot_gate * (1.0 - sigma))).astype(
        jnp.bfloat16
    )
    up_grad_low = (hidden_grad * slot_gate * sigma).astype(jnp.bfloat16)
    return (gate_grad_low, up_grad_low)


def on_device(
    tokens,
    doc_lengths,
    routes,
    slot_order,
    attn_gain,
    w_qkv,
    q_gain,
    k_gain,
    w_out,
    ffn_gain,
    w_router,
    w_gate,
    w_up,
    w_down,
    cotangent,
):
    row_count = tokens.shape[1]
    model_width = tokens.shape[2]
    head_count = HEADS
    head_dim = model_width // head_count
    score_scale = head_dim ** (-0.5)
    ctx_count = lax.axis_size("ctx")
    ctx_index = lax.axis_index("ctx")
    total_rows = row_count * ctx_count
    lengths = doc_lengths[0]
    local_pos = dealt_position(
        ctx_index * row_count + jnp.arange(row_count, dtype=jnp.int32), row_count, ctx_count
    )
    local_doc, local_inner = document_info(local_pos, lengths)
    stream_pos = dealt_position(jnp.arange(total_rows, dtype=jnp.int32), row_count, ctx_count)
    stream_doc, stream_inner = document_info(stream_pos, lengths)
    block_rows = math.gcd(total_rows, 512)
    block_count = total_rows // block_rows
    block_ids = jnp.arange(block_count, dtype=jnp.int32)
    gain_one, qkv_weight, gain_query, gain_key, out_weight = (
        lax.all_gather(attn_gain, "fsdp", axis=0, tiled=True),
        lax.all_gather(w_qkv, "fsdp", axis=0, tiled=True),
        lax.all_gather(q_gain, "fsdp", axis=0, tiled=True),
        lax.all_gather(k_gain, "fsdp", axis=0, tiled=True),
        lax.all_gather(w_out, "fsdp", axis=0, tiled=True),
    )
    gain_two, router_weight, gate_weight, up_weight, down_weight = (
        lax.all_gather(ffn_gain, "fsdp", axis=0, tiled=True),
        lax.all_gather(w_router, "fsdp", axis=0, tiled=True),
        lax.all_gather(w_gate, "fsdp", axis=2, tiled=True),
        lax.all_gather(w_up, "fsdp", axis=2, tiled=True),
        lax.all_gather(w_down, "fsdp", axis=1, tiled=True),
    )
    inputs = tokens[0].astype(jnp.float32)
    normed_f, norm_one_pull = jax.vjp(rms_scale, inputs, gain_one.astype(jnp.float32))
    normed_low = normed_f.astype(jnp.bfloat16)
    projected = jnp.dot(normed_low, qkv_weight, preferred_element_type=jnp.float32)
    query_lin = projected[:, :model_width]
    key_lin = projected[:, model_width : 2 * model_width]
    value_low = (
        projected[:, 2 * model_width :]
        .astype(jnp.bfloat16)
        .reshape(row_count, head_count, head_dim)
    )

    def head_shape(values, gain_vector):
        return rotate(
            rms_scale(values, gain_vector).reshape(row_count, head_count, head_dim), local_inner
        )

    query_f, query_pull = jax.vjp(head_shape, query_lin, gain_query.astype(jnp.float32))
    key_f, key_pull = jax.vjp(head_shape, key_lin, gain_key.astype(jnp.float32))
    query_low = query_f.astype(jnp.bfloat16)
    key_low = key_f.astype(jnp.bfloat16)
    keys_all, values_all = (
        lax.all_gather(key_low, "ctx", axis=0, tiled=True),
        lax.all_gather(value_low, "ctx", axis=0, tiled=True),
    )

    def key_slice(block_index):
        first_row = block_index * block_rows
        return (
            lax.dynamic_slice_in_dim(keys_all, first_row, block_rows, 0),
            lax.dynamic_slice_in_dim(values_all, first_row, block_rows, 0),
            lax.dynamic_slice_in_dim(stream_pos, first_row, block_rows, 0),
            lax.dynamic_slice_in_dim(stream_doc, first_row, block_rows, 0),
        )

    def stats_step(carry, block_index):
        running_top, running_total = carry
        key_block, value_block, key_pos, key_doc = key_slice(block_index)
        scores = masked_scores(
            query_low, key_block, local_pos, local_doc, key_pos, key_doc, score_scale
        )
        new_top = jnp.maximum(running_top, jnp.max(scores, axis=-1))
        running_total = running_total * jnp.exp(running_top - new_top) + jnp.sum(
            jnp.exp(scores - new_top[..., None]), axis=-1
        )
        return ((new_top, running_total), None)

    start_stats = (
        jnp.full((head_count, row_count), MASKED, jnp.float32),
        jnp.zeros((head_count, row_count), jnp.float32),
    )
    (score_top, score_total), _ = lax.scan(stats_step, start_stats, block_ids)
    log_total = score_top + jnp.log(score_total)

    def output_step(accum, block_index):
        key_block, value_block, key_pos, key_doc = key_slice(block_index)
        scores = masked_scores(
            query_low, key_block, local_pos, local_doc, key_pos, key_doc, score_scale
        )
        prob_block = jnp.exp(scores - log_total[..., None]).astype(jnp.bfloat16)
        return (
            accum
            + jnp.einsum(
                "hqk,khd->qhd", prob_block, value_block, preferred_element_type=jnp.float32
            ),
            None,
        )

    attended_f, _ = lax.scan(
        output_step, jnp.zeros((row_count, head_count, head_dim), jnp.float32), block_ids
    )
    attended_low = attended_f.reshape(row_count, model_width).astype(jnp.bfloat16)
    mixed = inputs + jnp.dot(attended_low, out_weight, preferred_element_type=jnp.float32)
    normed_two_f, norm_two_pull = jax.vjp(rms_scale, mixed, gain_two.astype(jnp.float32))
    normed_two = normed_two_f.astype(jnp.bfloat16)
    expert_count = gate_weight.shape[0]
    route_ids = routes[0]
    top_count = route_ids.shape[1]
    pair_count = row_count * top_count
    capacity = pair_count // expert_count
    logits = jnp.dot(normed_two, router_weight, preferred_element_type=jnp.float32)
    router_probs = jax.nn.softmax(logits, axis=-1)
    chosen = (
        route_ids[:, :, None] == jnp.arange(expert_count, dtype=jnp.int32)[None, None, :]
    ).astype(jnp.float32)
    gate_values = jnp.sum(chosen * router_probs[:, None, :], axis=-1)
    placed, source = slot_table(route_ids, slot_order[0], capacity, expert_count)
    padded_in = jnp.concatenate([normed_two, jnp.zeros((1, model_width), jnp.bfloat16)], axis=0)
    expert_in = padded_in[source // top_count].reshape(expert_count, capacity, model_width)
    gate_pre = jnp.einsum(
        "ecd,edh->ech", expert_in, gate_weight, preferred_element_type=jnp.float32
    )
    up_pre = jnp.einsum("ecd,edh->ech", expert_in, up_weight, preferred_element_type=jnp.float32)
    hidden_low = (jax.nn.silu(gate_pre) * up_pre).astype(jnp.bfloat16)
    expert_out = jnp.einsum(
        "ech,ehd->ecd", hidden_low, down_weight, preferred_element_type=jnp.float32
    )
    out_padded = jnp.concatenate(
        [
            expert_out.reshape(expert_count * capacity, model_width),
            jnp.zeros((1, model_width), jnp.float32),
        ],
        axis=0,
    )
    per_pair = out_padded[placed].reshape(row_count, top_count, model_width)
    layer_out = mixed + jnp.sum(gate_values[:, :, None] * per_pair, axis=1)
    out_grad = cotangent[0].astype(jnp.float32)
    gate_grad = jnp.sum(out_grad[:, None, :] * per_pair, axis=-1)
    pair_grad = (gate_values[:, :, None] * out_grad[:, None, :]).reshape(pair_count, model_width)
    pair_padded = jnp.concatenate([pair_grad, jnp.zeros((1, model_width), jnp.float32)], axis=0)
    slot_grad = (
        pair_padded[source].reshape(expert_count, capacity, model_width).astype(jnp.bfloat16)
    )

    def expert_step(carry, pieces):
        slot_in, slot_hidden, slot_dy, slot_gate, slot_up, gate_matrix, up_matrix, down_matrix = (
            pieces
        )
        hidden_grad = jnp.einsum(
            "cd,hd->ch", slot_dy, down_matrix, preferred_element_type=jnp.float32
        )
        gate_grad_low, up_grad_low = silu_parts(hidden_grad, slot_gate, slot_up)
        in_grad = jnp.einsum(
            "ch,dh->cd", gate_grad_low, gate_matrix, preferred_element_type=jnp.float32
        ) + jnp.einsum("ch,dh->cd", up_grad_low, up_matrix, preferred_element_type=jnp.float32)
        gate_term = jnp.einsum(
            "cd,ch->dh", slot_in, gate_grad_low, preferred_element_type=jnp.float32
        )
        up_term = jnp.einsum("cd,ch->dh", slot_in, up_grad_low, preferred_element_type=jnp.float32)
        down_term = jnp.einsum(
            "ch,cd->hd", slot_hidden, slot_dy, preferred_element_type=jnp.float32
        )
        gate_shard, up_shard, down_shard = (
            lax.psum_scatter(
                gate_term.astype(jnp.bfloat16), "fsdp", scatter_dimension=1, tiled=True
            ).astype(jnp.float32),
            lax.psum_scatter(
                up_term.astype(jnp.bfloat16), "fsdp", scatter_dimension=1, tiled=True
            ).astype(jnp.float32),
            lax.psum_scatter(
                down_term.astype(jnp.bfloat16), "fsdp", scatter_dimension=0, tiled=True
            ).astype(jnp.float32),
        )
        gate_part, up_part, down_part = (
            lax.psum_scatter(
                gate_shard.astype(jnp.bfloat16), "ctx", scatter_dimension=0, tiled=True
            ).astype(jnp.float32),
            lax.psum_scatter(
                up_shard.astype(jnp.bfloat16), "ctx", scatter_dimension=0, tiled=True
            ).astype(jnp.float32),
            lax.psum_scatter(
                down_shard.astype(jnp.bfloat16), "ctx", scatter_dimension=1, tiled=True
            ).astype(jnp.float32),
        )
        return (carry, (in_grad, gate_part, up_part, down_part))

    _, (expert_in_grad, gate_parts, up_parts, down_parts) = lax.scan(
        expert_step,
        None,
        (expert_in, hidden_low, slot_grad, gate_pre, up_pre, gate_weight, up_weight, down_weight),
    )
    in_padded = jnp.concatenate(
        [
            expert_in_grad.reshape(expert_count * capacity, model_width),
            jnp.zeros((1, model_width), jnp.float32),
        ],
        axis=0,
    )
    normed_two_grad = jnp.sum(in_padded[placed].reshape(row_count, top_count, model_width), axis=1)
    prob_grad_router = jnp.sum(chosen * gate_grad[:, :, None], axis=1)
    logit_grad = (
        router_probs
        * (prob_grad_router - jnp.sum(router_probs * prob_grad_router, axis=-1, keepdims=True))
    ).astype(jnp.bfloat16)
    normed_two_grad = normed_two_grad + jnp.einsum(
        "te,de->td", logit_grad, router_weight, preferred_element_type=jnp.float32
    )
    router_grad = jnp.einsum(
        "td,te->de", normed_two, logit_grad, preferred_element_type=jnp.float32
    )
    mixed_norm_grad, gain_two_grad = norm_two_pull(normed_two_grad)
    mixed_grad = out_grad + mixed_norm_grad
    mixed_low = mixed_grad.astype(jnp.bfloat16)
    out_weight_grad = jnp.einsum(
        "td,te->de", attended_low, mixed_low, preferred_element_type=jnp.float32
    )
    output_grad = (
        jnp.einsum("te,de->td", mixed_low, out_weight, preferred_element_type=jnp.float32)
        .astype(jnp.bfloat16)
        .reshape(row_count, head_count, head_dim)
    )
    row_delta = jnp.sum(output_grad.astype(jnp.float32) * attended_f, axis=-1).T

    def query_grad_step(accum, block_index):
        key_block, value_block, key_pos, key_doc = key_slice(block_index)
        scores = masked_scores(
            query_low, key_block, local_pos, local_doc, key_pos, key_doc, score_scale
        )
        prob_block = jnp.exp(scores - log_total[..., None])
        prob_grad = jnp.einsum(
            "qhd,khd->hqk", output_grad, value_block, preferred_element_type=jnp.float32
        )
        score_grad = (prob_block * (prob_grad - row_delta[..., None])).astype(jnp.bfloat16)
        return (
            accum
            + jnp.einsum("hqk,khd->qhd", score_grad, key_block, preferred_element_type=jnp.float32)
            * score_scale,
            None,
        )

    query_grad, _ = lax.scan(
        query_grad_step, jnp.zeros((row_count, head_count, head_dim), jnp.float32), block_ids
    )
    inner_rows = math.gcd(row_count * lax.axis_size("ctx"), 512)

    def piece_step(carry, piece_index):
        first_row = piece_index * inner_rows
        key_block = lax.dynamic_slice_in_dim(keys_all, first_row, inner_rows, 0)
        value_block = lax.dynamic_slice_in_dim(values_all, first_row, inner_rows, 0)
        key_pos = lax.dynamic_slice_in_dim(stream_pos, first_row, inner_rows, 0)
        key_doc = lax.dynamic_slice_in_dim(stream_doc, first_row, inner_rows, 0)
        scores = masked_scores(
            query_low, key_block, local_pos, local_doc, key_pos, key_doc, score_scale
        )
        prob_block = jnp.exp(scores - log_total[..., None])
        prob_grad = jnp.einsum(
            "qhd,khd->hqk", output_grad, value_block, preferred_element_type=jnp.float32
        )
        score_grad = (prob_block * (prob_grad - row_delta[..., None])).astype(jnp.bfloat16)
        value_part = jnp.einsum(
            "hqk,qhd->khd",
            prob_block.astype(jnp.bfloat16),
            output_grad,
            preferred_element_type=jnp.float32,
        )
        key_part = (
            jnp.einsum("hqk,qhd->khd", score_grad, query_low, preferred_element_type=jnp.float32)
            * score_scale
        )
        return (
            carry,
            jnp.concatenate(
                [
                    key_part.reshape(inner_rows, model_width),
                    value_part.reshape(inner_rows, model_width),
                ],
                axis=1,
            ),
        )

    _, stacked = lax.scan(
        piece_step,
        None,
        jnp.arange(row_count * lax.axis_size("ctx") // inner_rows, dtype=jnp.int32),
    )
    key_value_grad = lax.psum_scatter(
        stacked.reshape(row_count * lax.axis_size("ctx"), 2 * model_width).astype(jnp.bfloat16),
        "ctx",
        scatter_dimension=0,
        tiled=True,
    ).astype(jnp.float32)
    key_grad = key_value_grad[:, :model_width].reshape(row_count, head_count, head_dim)
    value_grad = key_value_grad[:, model_width:]
    query_lin_grad, gain_query_grad = query_pull(query_grad)
    key_lin_grad, gain_key_grad = key_pull(key_grad)
    proj_grad = jnp.concatenate(
        [
            query_lin_grad.astype(jnp.bfloat16),
            key_lin_grad.astype(jnp.bfloat16),
            value_grad.astype(jnp.bfloat16),
        ],
        axis=1,
    )
    qkv_weight_grad = jnp.einsum(
        "td,te->de", normed_low, proj_grad, preferred_element_type=jnp.float32
    )
    normed_grad = jnp.einsum("te,de->td", proj_grad, qkv_weight, preferred_element_type=jnp.float32)
    input_norm_grad, gain_one_grad = norm_one_pull(normed_grad)
    input_grad = mixed_grad + input_norm_grad
    qkv_shard, out_shard = (
        lax.psum_scatter(
            qkv_weight_grad.astype(jnp.bfloat16), "fsdp", scatter_dimension=0, tiled=True
        ).astype(jnp.float32),
        lax.psum_scatter(
            out_weight_grad.astype(jnp.bfloat16), "fsdp", scatter_dimension=0, tiled=True
        ).astype(jnp.float32),
    )
    qkv_part, out_part = (
        lax.psum_scatter(
            qkv_shard.astype(jnp.bfloat16), "ctx", scatter_dimension=1, tiled=True
        ).astype(jnp.float32),
        lax.psum_scatter(
            out_shard.astype(jnp.bfloat16), "ctx", scatter_dimension=1, tiled=True
        ).astype(jnp.float32),
    )
    gain_one_sum, gain_query_sum, gain_key_sum, gain_two_sum, router_sum = lax.psum(
        (gain_one_grad, gain_query_grad, gain_key_grad, gain_two_grad, router_grad), ("ctx", "fsdp")
    )
    shard_rows = model_width // lax.axis_size("fsdp")
    shard_start = lax.axis_index("fsdp") * shard_rows

    def own_rows(full_array):
        return lax.dynamic_slice_in_dim(full_array, shard_start, shard_rows, 0)

    return (
        layer_out.astype(jnp.bfloat16)[None],
        input_grad[None],
        own_rows(gain_one_sum),
        qkv_part,
        own_rows(gain_query_sum),
        own_rows(gain_key_sum),
        out_part,
        own_rows(gain_two_sum),
        own_rows(router_sum),
        gate_parts,
        up_parts,
        down_parts,
    )


def rms_unit(values):
    return lax.rsqrt(jnp.mean(values * values, axis=-1, keepdims=True) + EPSILON)


def rope_tables(inner_pos, head_dim):
    half_dim = head_dim // 2
    freq_table = ROPE_BASE ** (-2.0 * jnp.arange(half_dim, dtype=jnp.float32) / head_dim)
    angles = inner_pos.astype(jnp.float32)[:, None] * freq_table[None, :]
    return (jnp.cos(angles), jnp.sin(angles))


def turn(values, cosine, sine_part):
    half_dim = cosine.shape[-1]
    cosine, sine_part = cosine[:, None, :], sine_part[:, None, :]
    first_half, second_half = values[..., :half_dim], values[..., half_dim:]
    return jnp.concatenate(
        [
            first_half * cosine - second_half * sine_part,
            second_half * cosine + first_half * sine_part,
        ],
        axis=-1,
    )


def slot_of_pairs(route_ids, order_ids):
    pair_count = route_ids.shape[0] * route_ids.shape[1]
    expert_flat = route_ids.reshape(pair_count)
    rank_flat = order_ids.reshape(pair_count)
    earlier = (expert_flat[None, :] == expert_flat[:, None]) & (
        rank_flat[None, :] < rank_flat[:, None]
    )
    return jnp.sum(earlier.astype(jnp.int32), axis=1).reshape(route_ids.shape)


def dot32(spec, left, right):
    return jnp.einsum(spec, left, right, preferred_element_type=jnp.float32)


def on_device_heads(
    tokens,
    doc_lengths,
    routes,
    slot_order,
    attn_gain,
    w_qkv,
    q_gain,
    k_gain,
    w_out,
    ffn_gain,
    w_router,
    w_gate,
    w_up,
    w_down,
    cotangent,
):
    rows, width = tokens.shape[1], tokens.shape[2]
    ctx, fsdp = lax.axis_size("ctx"), lax.axis_size("fsdp")
    me, mine = lax.axis_index("ctx"), lax.axis_index("fsdp")
    head_dim = width // HEADS
    heads = HEADS // ctx
    cols = heads * head_dim
    part = width // fsdp
    total = rows * ctx
    score_scale = head_dim ** (-0.5)
    lengths = doc_lengths[0]
    bf16, f32 = jnp.bfloat16, jnp.float32

    tokens_all = lax.all_gather(tokens[0], "ctx", axis=0, tiled=True)
    small = jnp.concatenate(
        [jnp.stack([attn_gain, q_gain, k_gain, ffn_gain]), w_router.T], axis=0
    )
    small = lax.all_gather(small, "fsdp", axis=1, tiled=True)
    gain_one, gain_query, gain_key, gain_two = (small[i].astype(f32) for i in range(4))
    router_weight = small[4:]
    own_cols = jnp.concatenate(
        [
            lax.dynamic_slice_in_dim(w_qkv, kind * width + me * cols, cols, 1)
            for kind in range(3)
        ],
        axis=1,
    )
    qkv_weight = lax.all_gather(own_cols, "fsdp", axis=0, tiled=True)
    dy_all = lax.all_gather(cotangent[0], "fsdp", axis=0, tiled=True)
    pairs_all = lax.all_gather(jnp.stack([routes[0], slot_order[0]]), "fsdp", axis=0)

    stream_pos = dealt_position(jnp.arange(total, dtype=jnp.int32), rows, ctx)
    stream_doc, stream_inner = document_info(stream_pos, lengths)
    cosine, sine_part = rope_tables(stream_inner, head_dim)
    inputs_all = tokens_all.astype(f32)
    unit_all = inputs_all * rms_unit(inputs_all)
    normed_all = (unit_all * gain_one).astype(bf16)
    projected = dot32("td,de->te", normed_all, qkv_weight)
    query_lin, key_lin = projected[:, :cols], projected[:, cols : 2 * cols]
    value_low = projected[:, 2 * cols :].astype(bf16).reshape(total, heads, head_dim)
    squares = jnp.stack(
        [jnp.sum(query_lin * query_lin, axis=1), jnp.sum(key_lin * key_lin, axis=1)]
    )
    scales = lax.rsqrt(lax.psum(squares, "ctx") / width + EPSILON)
    own_gain_query = lax.dynamic_slice_in_dim(gain_query, me * cols, cols, 0)
    own_gain_key = lax.dynamic_slice_in_dim(gain_key, me * cols, cols, 0)
    query_unit = query_lin * scales[0][:, None]
    key_unit = key_lin * scales[1][:, None]

    def by_head(values):
        return values.reshape(total, heads, head_dim)

    query_low = turn(by_head(query_unit * own_gain_query), cosine, sine_part).astype(bf16)
    key_low = turn(by_head(key_unit * own_gain_key), cosine, sine_part).astype(bf16)
    scores = masked_scores(
        query_low, key_low, stream_pos, stream_doc, stream_pos, stream_doc, score_scale
    )
    weights = jnp.exp(scores - jnp.max(scores, axis=-1, keepdims=True))
    probs = weights / jnp.sum(weights, axis=-1, keepdims=True)
    prob_low = probs.astype(bf16)
    attended = dot32("hqk,khd->qhd", prob_low, value_low)

    def to_rows(values):
        values = lax.all_to_all(values, "ctx", 0, 1, tiled=True)
        return lax.all_to_all(values, "fsdp", 1, 0, tiled=True)

    def to_heads(values):
        values = lax.all_to_all(values, "fsdp", 0, 1, tiled=True)
        return lax.all_to_all(values, "ctx", 1, 0, tiled=True)

    attended_part = to_rows(attended.reshape(total, cols).astype(bf16))
    mixed_part = dot32("td,de->te", attended_part, w_out).astype(bf16)
    inputs = tokens[0].astype(f32)
    mixed = inputs + lax.psum_scatter(
        mixed_part, "fsdp", scatter_dimension=0, tiled=True
    ).astype(f32)
    scale_two = rms_unit(mixed)
    unit_two = mixed * scale_two
    normed_two = (unit_two * gain_two).astype(bf16)
    group = lax.all_gather(normed_two, "fsdp", axis=0, tiled=True)

    experts = w_gate.shape[0]
    top = routes.shape[2]
    capacity = rows * top // experts
    slots = jax.vmap(slot_of_pairs)(pairs_all[:, 0], pairs_all[:, 1])
    expert_ids = jnp.arange(experts, dtype=jnp.int32)
    chosen = pairs_all[:, 0][:, :, :, None] == expert_ids
    slot_by_expert = jnp.sum(jnp.where(chosen, slots[..., None] + 1, 0), axis=2) - 1
    spread = (
        slot_by_expert.transpose(0, 2, 1)[:, :, None, :]
        == jnp.arange(capacity, dtype=jnp.int32)[None, None, :, None]
    )
    disp = spread.astype(bf16).reshape(fsdp, experts * capacity, rows)
    logits = dot32("td,ed->te", group, router_weight)
    router_probs = jax.nn.softmax(logits, axis=-1).reshape(fsdp, rows, experts)
    slot_gate_value = jnp.sum(
        jnp.where(spread, router_probs.transpose(0, 2, 1)[:, :, None, :], 0.0), axis=-1
    )
    slot_gate_value = slot_gate_value.transpose(1, 0, 2).reshape(experts, fsdp * capacity)

    def dispatch(values):
        picked = dot32("bst,btd->bsd", disp, values.reshape(fsdp, rows, width)).astype(bf16)
        picked = picked.reshape(fsdp, experts, capacity, width).transpose(1, 0, 2, 3)
        return picked.reshape(experts, fsdp * capacity, width)

    def combine(values):
        values = values.reshape(experts, fsdp, capacity, width).transpose(1, 0, 2, 3)
        return dot32("bst,bsd->btd", disp, values.reshape(fsdp, experts * capacity, width))

    expert_in = dispatch(group)
    gate_pre = dot32("ecd,edh->ech", expert_in, w_gate)
    up_pre = dot32("ecd,edh->ech", expert_in, w_up)
    hidden = (jax.nn.silu(gate_pre) * up_pre).astype(bf16)
    expert_out = dot32("ech,ehd->ecd", hidden, w_down) * slot_gate_value[..., None]
    moved = lax.psum_scatter(
        combine(expert_out.astype(bf16)).reshape(fsdp * rows, width).astype(bf16),
        "fsdp",
        scatter_dimension=0,
        tiled=True,
    )
    activations = (mixed + moved.astype(f32)).astype(bf16)

    slot_dy = dispatch(dy_all)
    raw_grad = dot32("ecd,ehd->ech", slot_dy, w_down)
    slot_gate_grad = jnp.sum(hidden.astype(f32) * raw_grad, axis=-1)
    hidden_grad = raw_grad * slot_gate_value[..., None]
    gate_low, up_low = silu_parts(hidden_grad, gate_pre, up_pre)
    in_grad = dot32("ech,edh->ecd", gate_low, w_gate) + dot32("ech,edh->ecd", up_low, w_up)
    g_gate = dot32("ecd,ech->edh", expert_in, gate_low).astype(bf16)
    g_up = dot32("ecd,ech->edh", expert_in, up_low).astype(bf16)
    scaled_hidden = (hidden.astype(f32) * slot_gate_value[..., None]).astype(bf16)
    g_down = dot32("ech,ecd->ehd", scaled_hidden, slot_dy).astype(bf16)
    prob_grad = jnp.sum(
        jnp.where(
            spread,
            slot_gate_grad.reshape(experts, fsdp, capacity).transpose(1, 0, 2)[..., None],
            0.0,
        ),
        axis=2,
    ).transpose(0, 2, 1)
    logit_grad = (
        router_probs * (prob_grad - jnp.sum(router_probs * prob_grad, axis=-1, keepdims=True))
    ).reshape(fsdp * rows, experts).astype(bf16)
    group_grad = combine(in_grad.astype(bf16)).reshape(fsdp * rows, width) + dot32(
        "te,ed->td", logit_grad, router_weight
    )
    g_router = dot32("te,td->ed", logit_grad, group)
    normed_two_grad = lax.psum_scatter(
        group_grad.astype(bf16), "fsdp", scatter_dimension=0, tiled=True
    ).astype(f32)
    g_ffn_gain = jnp.sum(normed_two_grad * unit_two, axis=0)
    pulled = normed_two_grad * gain_two
    out_grad = cotangent[0].astype(f32)
    mixed_grad = out_grad + scale_two * (
        pulled - unit_two * jnp.mean(unit_two * pulled, axis=-1, keepdims=True)
    )
    mixed_all = lax.all_gather(mixed_grad.astype(bf16), "fsdp", axis=0, tiled=True)
    output_part = dot32("te,de->td", mixed_all, w_out).astype(bf16)
    g_out = dot32("td,te->de", attended_part, mixed_all).astype(bf16)
    output_grad = by_head(to_heads(output_part))

    row_delta = jnp.sum(output_grad.astype(f32) * attended, axis=-1).T
    prob_grad_attn = dot32("qhd,khd->hqk", output_grad, value_low)
    score_grad = (probs * (prob_grad_attn - row_delta[..., None])).astype(bf16)
    query_grad = dot32("hqk,khd->qhd", score_grad, key_low) * score_scale
    key_grad = dot32("hqk,qhd->khd", score_grad, query_low) * score_scale
    value_grad = dot32("hqk,qhd->khd", prob_low, output_grad)
    query_back = turn(query_grad, cosine, -sine_part).reshape(total, cols)
    key_back = turn(key_grad, cosine, -sine_part).reshape(total, cols)
    own_g_query = jnp.sum(query_back * query_unit, axis=0)
    own_g_key = jnp.sum(key_back * key_unit, axis=0)
    query_back = query_back * own_gain_query
    key_back = key_back * own_gain_key
    inner_sums = lax.psum(
        jnp.stack(
            [jnp.sum(query_back * query_unit, axis=1), jnp.sum(key_back * key_unit, axis=1)]
        ),
        "ctx",
    ) / width
    proj_grad = jnp.concatenate(
        [
            scales[0][:, None] * (query_back - query_unit * inner_sums[0][:, None]),
            scales[1][:, None] * (key_back - key_unit * inner_sums[1][:, None]),
            value_grad.reshape(total, cols),
        ],
        axis=1,
    ).astype(bf16)
    g_qkv = dot32("td,te->de", normed_all, proj_grad).astype(bf16)
    normed_grad_part = dot32("te,de->td", proj_grad, qkv_weight)
    g_attn_gain = jnp.sum(normed_grad_part * unit_all, axis=0)
    normed_grad = lax.psum_scatter(
        normed_grad_part.astype(bf16), "ctx", scatter_dimension=0, tiled=True
    ).astype(f32)
    scale_one = rms_unit(inputs)
    unit_one = inputs * scale_one
    pulled_one = normed_grad * gain_one
    input_grad = mixed_grad + scale_one * (
        pulled_one - unit_one * jnp.mean(unit_one * pulled_one, axis=-1, keepdims=True)
    )

    gate_parts = lax.psum_scatter(g_gate, "ctx", scatter_dimension=1, tiled=True).astype(f32)
    up_parts = lax.psum_scatter(g_up, "ctx", scatter_dimension=1, tiled=True).astype(f32)
    down_parts = lax.psum_scatter(g_down, "ctx", scatter_dimension=2, tiled=True).astype(f32)
    out_part = lax.psum_scatter(g_out, "ctx", scatter_dimension=1, tiled=True).astype(f32)
    qkv_shard = lax.psum_scatter(g_qkv, "fsdp", scatter_dimension=0, tiled=True)
    qkv_full = lax.all_gather(qkv_shard, "ctx", axis=0)
    qkv_full = qkv_full.reshape(ctx, part, 3, cols).transpose(1, 2, 0, 3).reshape(part, 3 * width)
    qkv_part = lax.dynamic_slice_in_dim(
        qkv_full, me * (3 * width // ctx), 3 * width // ctx, 1
    ).astype(f32)

    def placed_cols(values):
        return lax.dynamic_update_slice_in_dim(jnp.zeros((width,), f32), values, me * cols, 0)

    sums = jnp.concatenate(
        [
            jnp.stack([g_attn_gain, placed_cols(own_g_query), placed_cols(own_g_key), g_ffn_gain]),
            g_router,
        ],
        axis=0,
    )
    sums = lax.psum(sums, ("ctx", "fsdp"))
    sums = lax.dynamic_slice_in_dim(sums, mine * part, part, 1)
    return (
        activations[None],
        input_grad[None],
        sums[0],
        qkv_part,
        sums[1],
        sums[2],
        out_part,
        sums[3],
        sums[4:].T,
        gate_parts,
        up_parts,
        down_parts,
    )


def solution(mesh):
    in_specs = (
        P("fsdp", "ctx", None),
        P("fsdp", None),
        P("fsdp", "ctx", None),
        P("fsdp", "ctx", None),
        P("fsdp"),
        P("fsdp", None),
        P("fsdp"),
        P("fsdp"),
        P("fsdp", None),
        P("fsdp"),
        P("fsdp", None),
        P(None, None, "fsdp"),
        P(None, None, "fsdp"),
        P(None, "fsdp", None),
        P("fsdp", "ctx", None),
    )
    out_specs = (
        P("fsdp", "ctx", None),
        P("fsdp", "ctx", None),
        P("fsdp"),
        P("fsdp", "ctx"),
        P("fsdp"),
        P("fsdp"),
        P("fsdp", "ctx"),
        P("fsdp"),
        P("fsdp", None),
        P(None, "ctx", "fsdp"),
        P(None, "ctx", "fsdp"),
        P(None, "fsdp", "ctx"),
    )
    body = on_device_heads if HEADS % mesh.shape["ctx"] == 0 else on_device
    return jax.shard_map(
        body, mesh=mesh, in_specs=in_specs, out_specs=out_specs, check_vma=False
    )
```

```python
import math

import jax
import jax.numpy as jnp
from jax import lax
from jax.experimental import pallas as pl
from jax.experimental.pallas import tpu as pltpu
from jax.sharding import PartitionSpec as P

HEADS = 16
MESH = pl.DeviceIdType.MESH
ANY = pl.BlockSpec(memory_space=pl.ANY)
VMEM = pl.BlockSpec(memory_space=pltpu.VMEM)
DMA = pltpu.SemaphoreType.DMA

EPSILON = 1e-05
ROPE_BASE = 10000.0
MASKED = -1e30


def rms_scale(values, gain_vector):
    return (
        values
        * lax.rsqrt(jnp.mean(values * values, axis=-1, keepdims=True) + EPSILON)
        * gain_vector
    )


def rotate(values, inner_pos):
    half_dim = values.shape[-1] // 2
    freq_table = ROPE_BASE ** (-2.0 * jnp.arange(half_dim, dtype=jnp.float32) / values.shape[-1])
    angles = inner_pos.astype(jnp.float32)[:, None] * freq_table[None, :]
    cosine = jnp.cos(angles)[:, None, :]
    sine_part = jnp.sin(angles)[:, None, :]
    first_half = values[..., :half_dim]
    second_half = values[..., half_dim:]
    return jnp.concatenate(
        [
            first_half * cosine - second_half * sine_part,
            second_half * cosine + first_half * sine_part,
        ],
        axis=-1,
    )


def dealt_position(flat_index, per_device, device_count):
    device_index = flat_index // per_device
    within = flat_index % per_device
    half_rows = per_device // 2
    return jnp.where(
        within < half_rows,
        device_index * half_rows + within,
        (2 * device_count - 1 - device_index) * half_rows + within - half_rows,
    )


def document_info(positions, lengths):
    doc_ends = jnp.sum(jnp.where(jnp.arange(lengths.shape[0])[:, None] >= jnp.arange(lengths.shape[0])[None, :], lengths[None, :], 0), axis=1)
    passed = doc_ends[None, :] <= positions[:, None]
    doc_ids = jnp.sum(passed.astype(jnp.int32), axis=1)
    inner_pos = positions - jnp.sum(jnp.where(passed, lengths[None, :], 0), axis=1)
    return (doc_ids, inner_pos)


def slot_table(route_ids, order_ids, capacity, expert_count):
    pair_count = route_ids.shape[0] * route_ids.shape[1]
    expert_flat = route_ids.reshape(pair_count)
    rank_flat = order_ids.reshape(pair_count)
    earlier = (expert_flat[None, :] == expert_flat[:, None]) & (
        rank_flat[None, :] < rank_flat[:, None]
    )
    slot_index = jnp.sum(earlier.astype(jnp.int32), axis=1)
    placed = jnp.where(
        slot_index < capacity, expert_flat * capacity + slot_index, expert_count * capacity
    )
    source = (
        jnp.full((expert_count * capacity + 1,), pair_count, jnp.int32)
        .at[placed]
        .set(jnp.arange(pair_count, dtype=jnp.int32))
    )
    return (placed, source[: expert_count * capacity])


def masked_scores(query_block, key_block, query_pos, query_doc, key_pos, key_doc, score_scale):
    scores = (
        jnp.einsum("qhd,khd->hqk", query_block, key_block, preferred_element_type=jnp.float32)
        * score_scale
    )
    allowed = (query_doc[:, None] == key_doc[None, :]) & (key_pos[None, :] <= query_pos[:, None])
    return jnp.where(allowed[None], scores, MASKED)


def silu_parts(hidden_grad, slot_gate, slot_up):
    sigma = jax.nn.sigmoid(slot_gate)
    gate_grad_low = (hidden_grad * slot_up * sigma * (1.0 + slot_gate * (1.0 - sigma))).astype(
        jnp.bfloat16
    )
    up_grad_low = (hidden_grad * slot_gate * sigma).astype(jnp.bfloat16)
    return (gate_grad_low, up_grad_low)


def on_device(
    tokens,
    doc_lengths,
    routes,
    slot_order,
    attn_gain,
    w_qkv,
    q_gain,
    k_gain,
    w_out,
    ffn_gain,
    w_router,
    w_gate,
    w_up,
    w_down,
    cotangent,
):
    row_count = tokens.shape[1]
    model_width = tokens.shape[2]
    head_count = HEADS
    head_dim = model_width // head_count
    score_scale = head_dim ** (-0.5)
    ctx_count = lax.axis_size("ctx")
    ctx_index = lax.axis_index("ctx")
    total_rows = row_count * ctx_count
    lengths = doc_lengths[0]
    local_pos = dealt_position(
        ctx_index * row_count + jnp.arange(row_count, dtype=jnp.int32), row_count, ctx_count
    )
    local_doc, local_inner = document_info(local_pos, lengths)
    stream_pos = dealt_position(jnp.arange(total_rows, dtype=jnp.int32), row_count, ctx_count)
    stream_doc, stream_inner = document_info(stream_pos, lengths)
    block_rows = math.gcd(total_rows, 512)
    block_count = total_rows // block_rows
    block_ids = jnp.arange(block_count, dtype=jnp.int32)
    gain_one, qkv_weight, gain_query, gain_key, out_weight = (
        lax.all_gather(attn_gain, "fsdp", axis=0, tiled=True),
        lax.all_gather(w_qkv, "fsdp", axis=0, tiled=True),
        lax.all_gather(q_gain, "fsdp", axis=0, tiled=True),
        lax.all_gather(k_gain, "fsdp", axis=0, tiled=True),
        lax.all_gather(w_out, "fsdp", axis=0, tiled=True),
    )
    gain_two, router_weight, gate_weight, up_weight, down_weight = (
        lax.all_gather(ffn_gain, "fsdp", axis=0, tiled=True),
        lax.all_gather(w_router, "fsdp", axis=0, tiled=True),
        lax.all_gather(w_gate, "fsdp", axis=2, tiled=True),
        lax.all_gather(w_up, "fsdp", axis=2, tiled=True),
        lax.all_gather(w_down, "fsdp", axis=1, tiled=True),
    )
    inputs = tokens[0].astype(jnp.float32)
    normed_f, norm_one_pull = jax.vjp(rms_scale, inputs, gain_one.astype(jnp.float32))
    normed_low = normed_f.astype(jnp.bfloat16)
    projected = jnp.dot(normed_low, qkv_weight, preferred_element_type=jnp.float32)
    query_lin = projected[:, :model_width]
    key_lin = projected[:, model_width : 2 * model_width]
    value_low = (
        projected[:, 2 * model_width :]
        .astype(jnp.bfloat16)
        .reshape(row_count, head_count, head_dim)
    )

    def head_shape(values, gain_vector):
        return rotate(
            rms_scale(values, gain_vector).reshape(row_count, head_count, head_dim), local_inner
        )

    query_f, query_pull = jax.vjp(head_shape, query_lin, gain_query.astype(jnp.float32))
    key_f, key_pull = jax.vjp(head_shape, key_lin, gain_key.astype(jnp.float32))
    query_low = query_f.astype(jnp.bfloat16)
    key_low = key_f.astype(jnp.bfloat16)
    keys_all, values_all = (
        lax.all_gather(key_low, "ctx", axis=0, tiled=True),
        lax.all_gather(value_low, "ctx", axis=0, tiled=True),
    )

    def key_slice(block_index):
        first_row = block_index * block_rows
        return (
            lax.dynamic_slice_in_dim(keys_all, first_row, block_rows, 0),
            lax.dynamic_slice_in_dim(values_all, first_row, block_rows, 0),
            lax.dynamic_slice_in_dim(stream_pos, first_row, block_rows, 0),
            lax.dynamic_slice_in_dim(stream_doc, first_row, block_rows, 0),
        )

    def stats_step(carry, block_index):
        running_top, running_total = carry
        key_block, value_block, key_pos, key_doc = key_slice(block_index)
        scores = masked_scores(
            query_low, key_block, local_pos, local_doc, key_pos, key_doc, score_scale
        )
        new_top = jnp.maximum(running_top, jnp.max(scores, axis=-1))
        running_total = running_total * jnp.exp(running_top - new_top) + jnp.sum(
            jnp.exp(scores - new_top[..., None]), axis=-1
        )
        return ((new_top, running_total), None)

    start_stats = (
        jnp.full((head_count, row_count), MASKED, jnp.float32),
        jnp.zeros((head_count, row_count), jnp.float32),
    )
    (score_top, score_total), _ = lax.scan(stats_step, start_stats, block_ids)
    log_total = score_top + jnp.log(score_total)

    def output_step(accum, block_index):
        key_block, value_block, key_pos, key_doc = key_slice(block_index)
        scores = masked_scores(
            query_low, key_block, local_pos, local_doc, key_pos, key_doc, score_scale
        )
        prob_block = jnp.exp(scores - log_total[..., None]).astype(jnp.bfloat16)
        return (
            accum
            + jnp.einsum(
                "hqk,khd->qhd", prob_block, value_block, preferred_element_type=jnp.float32
            ),
            None,
        )

    attended_f, _ = lax.scan(
        output_step, jnp.zeros((row_count, head_count, head_dim), jnp.float32), block_ids
    )
    attended_low = attended_f.reshape(row_count, model_width).astype(jnp.bfloat16)
    mixed = inputs + jnp.dot(attended_low, out_weight, preferred_element_type=jnp.float32)
    normed_two_f, norm_two_pull = jax.vjp(rms_scale, mixed, gain_two.astype(jnp.float32))
    normed_two = normed_two_f.astype(jnp.bfloat16)
    expert_count = gate_weight.shape[0]
    route_ids = routes[0]
    top_count = route_ids.shape[1]
    pair_count = row_count * top_count
    capacity = pair_count // expert_count
    logits = jnp.dot(normed_two, router_weight, preferred_element_type=jnp.float32)
    router_probs = jax.nn.softmax(logits, axis=-1)
    chosen = (
        route_ids[:, :, None] == jnp.arange(expert_count, dtype=jnp.int32)[None, None, :]
    ).astype(jnp.float32)
    gate_values = jnp.sum(chosen * router_probs[:, None, :], axis=-1)
    placed, source = slot_table(route_ids, slot_order[0], capacity, expert_count)
    padded_in = jnp.concatenate([normed_two, jnp.zeros((1, model_width), jnp.bfloat16)], axis=0)
    expert_in = padded_in[source // top_count].reshape(expert_count, capacity, model_width)
    gate_pre = jnp.einsum(
        "ecd,edh->ech", expert_in, gate_weight, preferred_element_type=jnp.float32
    )
    up_pre = jnp.einsum("ecd,edh->ech", expert_in, up_weight, preferred_element_type=jnp.float32)
    hidden_low = (jax.nn.silu(gate_pre) * up_pre).astype(jnp.bfloat16)
    expert_out = jnp.einsum(
        "ech,ehd->ecd", hidden_low, down_weight, preferred_element_type=jnp.float32
    )
    out_padded = jnp.concatenate(
        [
            expert_out.reshape(expert_count * capacity, model_width),
            jnp.zeros((1, model_width), jnp.float32),
        ],
        axis=0,
    )
    per_pair = out_padded[placed].reshape(row_count, top_count, model_width)
    layer_out = mixed + jnp.sum(gate_values[:, :, None] * per_pair, axis=1)
    out_grad = cotangent[0].astype(jnp.float32)
    gate_grad = jnp.sum(out_grad[:, None, :] * per_pair, axis=-1)
    pair_grad = (gate_values[:, :, None] * out_grad[:, None, :]).reshape(pair_count, model_width)
    pair_padded = jnp.concatenate([pair_grad, jnp.zeros((1, model_width), jnp.float32)], axis=0)
    slot_grad = (
        pair_padded[source].reshape(expert_count, capacity, model_width).astype(jnp.bfloat16)
    )

    def expert_step(carry, pieces):
        slot_in, slot_hidden, slot_dy, slot_gate, slot_up, gate_matrix, up_matrix, down_matrix = (
            pieces
        )
        hidden_grad = jnp.einsum(
            "cd,hd->ch", slot_dy, down_matrix, preferred_element_type=jnp.float32
        )
        gate_grad_low, up_grad_low = silu_parts(hidden_grad, slot_gate, slot_up)
        in_grad = jnp.einsum(
            "ch,dh->cd", gate_grad_low, gate_matrix, preferred_element_type=jnp.float32
        ) + jnp.einsum("ch,dh->cd", up_grad_low, up_matrix, preferred_element_type=jnp.float32)
        gate_term = jnp.einsum(
            "cd,ch->dh", slot_in, gate_grad_low, preferred_element_type=jnp.float32
        )
        up_term = jnp.einsum("cd,ch->dh", slot_in, up_grad_low, preferred_element_type=jnp.float32)
        down_term = jnp.einsum(
            "ch,cd->hd", slot_hidden, slot_dy, preferred_element_type=jnp.float32
        )
        gate_shard, up_shard, down_shard = (
            lax.psum_scatter(
                gate_term.astype(jnp.bfloat16), "fsdp", scatter_dimension=1, tiled=True
            ).astype(jnp.float32),
            lax.psum_scatter(
                up_term.astype(jnp.bfloat16), "fsdp", scatter_dimension=1, tiled=True
            ).astype(jnp.float32),
            lax.psum_scatter(
                down_term.astype(jnp.bfloat16), "fsdp", scatter_dimension=0, tiled=True
            ).astype(jnp.float32),
        )
        gate_part, up_part, down_part = (
            lax.psum_scatter(
                gate_shard.astype(jnp.bfloat16), "ctx", scatter_dimension=0, tiled=True
            ).astype(jnp.float32),
            lax.psum_scatter(
                up_shard.astype(jnp.bfloat16), "ctx", scatter_dimension=0, tiled=True
            ).astype(jnp.float32),
            lax.psum_scatter(
                down_shard.astype(jnp.bfloat16), "ctx", scatter_dimension=1, tiled=True
            ).astype(jnp.float32),
        )
        return (carry, (in_grad, gate_part, up_part, down_part))

    _, (expert_in_grad, gate_parts, up_parts, down_parts) = lax.scan(
        expert_step,
        None,
        (expert_in, hidden_low, slot_grad, gate_pre, up_pre, gate_weight, up_weight, down_weight),
    )
    in_padded = jnp.concatenate(
        [
            expert_in_grad.reshape(expert_count * capacity, model_width),
            jnp.zeros((1, model_width), jnp.float32),
        ],
        axis=0,
    )
    normed_two_grad = jnp.sum(in_padded[placed].reshape(row_count, top_count, model_width), axis=1)
    prob_grad_router = jnp.sum(chosen * gate_grad[:, :, None], axis=1)
    logit_grad = (
        router_probs
        * (prob_grad_router - jnp.sum(router_probs * prob_grad_router, axis=-1, keepdims=True))
    ).astype(jnp.bfloat16)
    normed_two_grad = normed_two_grad + jnp.einsum(
        "te,de->td", logit_grad, router_weight, preferred_element_type=jnp.float32
    )
    router_grad = jnp.einsum(
        "td,te->de", normed_two, logit_grad, preferred_element_type=jnp.float32
    )
    mixed_norm_grad, gain_two_grad = norm_two_pull(normed_two_grad)
    mixed_grad = out_grad + mixed_norm_grad
    mixed_low = mixed_grad.astype(jnp.bfloat16)
    out_weight_grad = jnp.einsum(
        "td,te->de", attended_low, mixed_low, preferred_element_type=jnp.float32
    )
    output_grad = (
        jnp.einsum("te,de->td", mixed_low, out_weight, preferred_element_type=jnp.float32)
        .astype(jnp.bfloat16)
        .reshape(row_count, head_count, head_dim)
    )
    row_delta = jnp.sum(output_grad.astype(jnp.float32) * attended_f, axis=-1).T

    def query_grad_step(accum, block_index):
        key_block, value_block, key_pos, key_doc = key_slice(block_index)
        scores = masked_scores(
            query_low, key_block, local_pos, local_doc, key_pos, key_doc, score_scale
        )
        prob_block = jnp.exp(scores - log_total[..., None])
        prob_grad = jnp.einsum(
            "qhd,khd->hqk", output_grad, value_block, preferred_element_type=jnp.float32
        )
        score_grad = (prob_block * (prob_grad - row_delta[..., None])).astype(jnp.bfloat16)
        return (
            accum
            + jnp.einsum("hqk,khd->qhd", score_grad, key_block, preferred_element_type=jnp.float32)
            * score_scale,
            None,
        )

    query_grad, _ = lax.scan(
        query_grad_step, jnp.zeros((row_count, head_count, head_dim), jnp.float32), block_ids
    )
    inner_rows = math.gcd(row_count * lax.axis_size("ctx"), 512)

    def piece_step(carry, piece_index):
        first_row = piece_index * inner_rows
        key_block = lax.dynamic_slice_in_dim(keys_all, first_row, inner_rows, 0)
        value_block = lax.dynamic_slice_in_dim(values_all, first_row, inner_rows, 0)
        key_pos = lax.dynamic_slice_in_dim(stream_pos, first_row, inner_rows, 0)
        key_doc = lax.dynamic_slice_in_dim(stream_doc, first_row, inner_rows, 0)
        scores = masked_scores(
            query_low, key_block, local_pos, local_doc, key_pos, key_doc, score_scale
        )
        prob_block = jnp.exp(scores - log_total[..., None])
        prob_grad = jnp.einsum(
            "qhd,khd->hqk", output_grad, value_block, preferred_element_type=jnp.float32
        )
        score_grad = (prob_block * (prob_grad - row_delta[..., None])).astype(jnp.bfloat16)
        value_part = jnp.einsum(
            "hqk,qhd->khd",
            prob_block.astype(jnp.bfloat16),
            output_grad,
            preferred_element_type=jnp.float32,
        )
        key_part = (
            jnp.einsum("hqk,qhd->khd", score_grad, query_low, preferred_element_type=jnp.float32)
            * score_scale
        )
        return (
            carry,
            jnp.concatenate(
                [
                    key_part.reshape(inner_rows, model_width),
                    value_part.reshape(inner_rows, model_width),
                ],
                axis=1,
            ),
        )

    _, stacked = lax.scan(
        piece_step,
        None,
        jnp.arange(row_count * lax.axis_size("ctx") // inner_rows, dtype=jnp.int32),
    )
    key_value_grad = lax.psum_scatter(
        stacked.reshape(row_count * lax.axis_size("ctx"), 2 * model_width).astype(jnp.bfloat16),
        "ctx",
        scatter_dimension=0,
        tiled=True,
    ).astype(jnp.float32)
    key_grad = key_value_grad[:, :model_width].reshape(row_count, head_count, head_dim)
    value_grad = key_value_grad[:, model_width:]
    query_lin_grad, gain_query_grad = query_pull(query_grad)
    key_lin_grad, gain_key_grad = key_pull(key_grad)
    proj_grad = jnp.concatenate(
        [
            query_lin_grad.astype(jnp.bfloat16),
            key_lin_grad.astype(jnp.bfloat16),
            value_grad.astype(jnp.bfloat16),
        ],
        axis=1,
    )
    qkv_weight_grad = jnp.einsum(
        "td,te->de", normed_low, proj_grad, preferred_element_type=jnp.float32
    )
    normed_grad = jnp.einsum("te,de->td", proj_grad, qkv_weight, preferred_element_type=jnp.float32)
    input_norm_grad, gain_one_grad = norm_one_pull(normed_grad)
    input_grad = mixed_grad + input_norm_grad
    qkv_shard, out_shard = (
        lax.psum_scatter(
            qkv_weight_grad.astype(jnp.bfloat16), "fsdp", scatter_dimension=0, tiled=True
        ).astype(jnp.float32),
        lax.psum_scatter(
            out_weight_grad.astype(jnp.bfloat16), "fsdp", scatter_dimension=0, tiled=True
        ).astype(jnp.float32),
    )
    qkv_part, out_part = (
        lax.psum_scatter(
            qkv_shard.astype(jnp.bfloat16), "ctx", scatter_dimension=1, tiled=True
        ).astype(jnp.float32),
        lax.psum_scatter(
            out_shard.astype(jnp.bfloat16), "ctx", scatter_dimension=1, tiled=True
        ).astype(jnp.float32),
    )
    gain_one_sum, gain_query_sum, gain_key_sum, gain_two_sum, router_sum = lax.psum(
        (gain_one_grad, gain_query_grad, gain_key_grad, gain_two_grad, router_grad), ("ctx", "fsdp")
    )
    shard_rows = model_width // lax.axis_size("fsdp")
    shard_start = lax.axis_index("fsdp") * shard_rows

    def own_rows(full_array):
        return lax.dynamic_slice_in_dim(full_array, shard_start, shard_rows, 0)

    return (
        layer_out.astype(jnp.bfloat16)[None],
        input_grad[None],
        own_rows(gain_one_sum),
        qkv_part,
        own_rows(gain_query_sum),
        own_rows(gain_key_sum),
        out_part,
        own_rows(gain_two_sum),
        own_rows(router_sum),
        gate_parts,
        up_parts,
        down_parts,
    )


def rms_unit(values):
    return lax.rsqrt(jnp.mean(values * values, axis=-1, keepdims=True) + EPSILON)


def rope_tables(inner_pos, head_dim):
    half_dim = head_dim // 2
    freq_table = ROPE_BASE ** (-2.0 * jnp.arange(half_dim, dtype=jnp.float32) / head_dim)
    angles = inner_pos.astype(jnp.float32)[:, None] * freq_table[None, :]
    return (jnp.cos(angles), jnp.sin(angles))


def turn(values, cosine, sine_part):
    half_dim = cosine.shape[-1]
    cosine, sine_part = cosine[:, None, :], sine_part[:, None, :]
    first_half, second_half = values[..., :half_dim], values[..., half_dim:]
    return jnp.concatenate(
        [
            first_half * cosine - second_half * sine_part,
            second_half * cosine + first_half * sine_part,
        ],
        axis=-1,
    )


def slot_of_pairs(route_ids, order_ids):
    pair_count = route_ids.shape[0] * route_ids.shape[1]
    expert_flat = route_ids.reshape(pair_count)
    rank_flat = order_ids.reshape(pair_count)
    earlier = (expert_flat[None, :] == expert_flat[:, None]) & (
        rank_flat[None, :] < rank_flat[:, None]
    )
    return jnp.sum(earlier.astype(jnp.int32), axis=1).reshape(route_ids.shape)


def dot32(spec, left, right):
    return jnp.einsum(spec, left, right, preferred_element_type=jnp.float32)


def greet(peers):
    barrier = pltpu.get_barrier_semaphore()
    for peer in peers:
        pl.semaphore_signal(barrier, inc=1, device_id=peer, device_id_type=MESH)
    pl.semaphore_wait(barrier, len(peers))


def send(source, target, send_sem, recv_sem, peer):
    copy = pltpu.make_async_remote_copy(
        source, target, send_sem, recv_sem, device_id=peer, device_id_type=MESH
    )
    copy.start()
    return copy


def comm_call(kernel, name, collective_id, out_shape, in_specs, out_specs, scratch_shapes, cost):
    return pl.pallas_call(
        kernel,
        out_shape=out_shape,
        in_specs=in_specs,
        out_specs=out_specs,
        scratch_shapes=scratch_shapes,
        compiler_params=pltpu.CompilerParams(
            collective_id=collective_id, has_side_effects=True, vmem_limit_bytes=48 * 2**20
        ),
        cost_estimate=pl.CostEstimate(flops=0, bytes_accessed=cost, transcendentals=0),
        name=name,
    )


def ctx_sum(values, collective_id):
    ctx = lax.axis_size("ctx")

    def kernel(own_ref, out_ref, held, send_sems, recv_sems):
        me, mine = lax.axis_index("ctx"), lax.axis_index("fsdp")
        peers = [(lax.rem(me + step, ctx), mine) for step in range(1, ctx)]
        greet(peers)
        copies = [
            send(own_ref, held.at[i], send_sems.at[i], recv_sems.at[i], peer)
            for i, peer in enumerate(peers)
        ]
        total = own_ref[...]
        for i, copy in enumerate(copies):
            copy.wait_recv()
            total = total + held[i]
        out_ref[...] = total
        for copy in copies:
            copy.wait_send()

    return comm_call(
        kernel,
        "ctx_sum",
        collective_id,
        jax.ShapeDtypeStruct(values.shape, values.dtype),
        [VMEM],
        VMEM,
        [
            pltpu.VMEM((ctx - 1,) + values.shape, values.dtype),
            DMA((ctx - 1,)),
            DMA((ctx - 1,)),
        ],
        20 * 2**20,
    )(values)


def mesh_sum(values, collective_id):
    ctx, fsdp = lax.axis_size("ctx"), lax.axis_size("fsdp")
    rows, part = values.shape[0], values.shape[1] // fsdp

    def kernel(own_ref, out_ref, parts, sums, held, part_send, part_recv, send_sems, recv_sems):
        me, mine = lax.axis_index("ctx"), lax.axis_index("fsdp")
        near = [lax.rem(mine + step, fsdp) for step in range(1, fsdp)]
        peers = [(lax.rem(me + step, ctx), mine) for step in range(1, ctx)]
        greet([(me, other) for other in near] + peers)

        def columns(index):
            return pl.ds(pl.multiple_of(index * part, part), part)

        copies = [
            send(
                own_ref.at[:, columns(other)],
                parts.at[i],
                part_send.at[i],
                part_recv.at[i],
                (me, other),
            )
            for i, other in enumerate(near)
        ]
        total = own_ref[:, columns(mine)]
        for i, copy in enumerate(copies):
            copy.wait_recv()
            total = total + parts[i]
        sums[...] = total
        wide = [
            send(sums, held.at[i], send_sems.at[i], recv_sems.at[i], peer)
            for i, peer in enumerate(peers)
        ]
        for i, copy in enumerate(wide):
            copy.wait_recv()
            total = total + held[i]
        out_ref[...] = total
        for copy in copies + wide:
            copy.wait_send()

    return comm_call(
        kernel,
        "mesh_sum",
        collective_id,
        jax.ShapeDtypeStruct((rows, part), values.dtype),
        [VMEM],
        VMEM,
        [
            pltpu.VMEM((fsdp - 1, rows, part), values.dtype),
            pltpu.VMEM((rows, part), values.dtype),
            pltpu.VMEM((ctx - 1, rows, part), values.dtype),
            DMA((fsdp - 1,)),
            DMA((fsdp - 1,)),
            DMA((ctx - 1,)),
            DMA((ctx - 1,)),
        ],
        30 * 2**20,
    )(values)


def heads_to_rows(values, collective_id):
    ctx, fsdp = lax.axis_size("ctx"), lax.axis_size("fsdp")
    rows, cols = values.shape[0] // ctx, values.shape[1]
    share = ctx // fsdp

    def kernel(own_ref, out_ref, send_sems, recv_sems):
        me, mine = lax.axis_index("ctx"), lax.axis_index("fsdp")
        keeper, place = me // share, lax.rem(me, share)
        own_keeper = (keeper == mine).astype(jnp.int32)
        barrier = pltpu.get_barrier_semaphore()
        for step in range(share * fsdp):
            source, stream = mine * share + step // fsdp, step % fsdp

            @pl.when(jnp.logical_or(source != me, stream != mine))
            def _():
                pl.semaphore_signal(
                    barrier, inc=1, device_id=(source, stream), device_id_type=MESH
                )

        pl.semaphore_wait(barrier, ctx - own_keeper)

        def block(index):
            return own_ref.at[pl.ds(pl.multiple_of(index * rows, rows), rows), :]

        def landing(stream, position):
            return out_ref.at[
                pl.ds(pl.multiple_of(stream * rows, rows), rows),
                pl.ds(pl.multiple_of(position * cols, cols), cols),
            ]

        slot = place * fsdp + mine

        def copy_to(step):
            other = lax.rem(me + step, ctx)
            return pltpu.make_async_remote_copy(
                block(other),
                landing(mine, place),
                send_sems.at[step],
                recv_sems.at[slot],
                device_id=(other, keeper),
                device_id_type=MESH,
            )

        kept = pltpu.make_async_copy(block(me), landing(mine, place), send_sems.at[0])
        for step in range(1, ctx):
            copy_to(step).start()

        @pl.when(own_keeper == 0)
        def _():
            copy_to(0).start()

        @pl.when(own_keeper == 1)
        def _():
            kept.start()
            kept.wait()

        for step in range(share * fsdp):

            @pl.when(
                jnp.logical_or(mine * share + step // fsdp != me, step % fsdp != mine)
            )
            def _():
                pltpu.make_async_copy(
                    block(0), landing(step % fsdp, step // fsdp), recv_sems.at[step]
                ).wait()

        for step in range(1, ctx):
            copy_to(step).wait_send()

        @pl.when(own_keeper == 0)
        def _():
            copy_to(0).wait_send()

    return comm_call(
        kernel,
        "heads_to_rows",
        collective_id,
        jax.ShapeDtypeStruct((fsdp * rows, share * cols), values.dtype),
        [ANY],
        ANY,
        [DMA((ctx,)), DMA((share * fsdp,))],
        40 * 2**20,
    )(values)


def rows_to_heads(values, collective_id):
    ctx, fsdp = lax.axis_size("ctx"), lax.axis_size("fsdp")
    share = ctx // fsdp
    rows, cols = values.shape[0] // fsdp, values.shape[1] // share

    def kernel(own_ref, out_ref, send_sems, recv_sems):
        me, mine = lax.axis_index("ctx"), lax.axis_index("fsdp")
        keeper, place = me // share, lax.rem(me, share)
        own_keeper = (keeper == mine).astype(jnp.int32)
        barrier = pltpu.get_barrier_semaphore()
        for step in range(ctx):
            source = lax.rem(me + step, ctx)

            @pl.when(jnp.logical_or(source != me, keeper != mine))
            def _():
                pl.semaphore_signal(
                    barrier, inc=1, device_id=(source, keeper), device_id_type=MESH
                )

        pl.semaphore_wait(barrier, share * fsdp - own_keeper)

        def block(stream, position):
            return own_ref.at[
                pl.ds(pl.multiple_of(stream * rows, rows), rows),
                pl.ds(pl.multiple_of(position * cols, cols), cols),
            ]

        def landing(index):
            return out_ref.at[pl.ds(pl.multiple_of(index * rows, rows), rows), :]

        def copy_to(step):
            return pltpu.make_async_remote_copy(
                block(step % fsdp, step // fsdp),
                landing(me),
                send_sems.at[step],
                recv_sems.at[me],
                device_id=(mine * share + step // fsdp, step % fsdp),
                device_id_type=MESH,
            )

        def is_far(step):
            return jnp.logical_or(mine * share + step // fsdp != me, step % fsdp != mine)

        for step in range(share * fsdp):
            pl.when(is_far(step))(copy_to(step).start)

        @pl.when(own_keeper == 1)
        def _():
            kept = pltpu.make_async_copy(block(mine, place), landing(me), recv_sems.at[me])
            kept.start()
            kept.wait()

        for step in range(ctx):
            source = lax.rem(me + step, ctx)

            @pl.when(jnp.logical_or(source != me, keeper != mine))
            def _():
                pltpu.make_async_copy(block(0, 0), landing(source), recv_sems.at[source]).wait()

        for step in range(share * fsdp):
            pl.when(is_far(step))(copy_to(step).wait_send)

    return comm_call(
        kernel,
        "rows_to_heads",
        collective_id,
        jax.ShapeDtypeStruct((ctx * rows, cols), values.dtype),
        [ANY],
        ANY,
        [DMA((share * fsdp,)), DMA((ctx,))],
        40 * 2**20,
    )(values)


def deal_columns(values, collective_id):
    ctx = lax.axis_size("ctx")
    kinds = values.shape[0]

    def kernel(own_ref, out_ref, send_sems, recv_sems):
        me, mine = lax.axis_index("ctx"), lax.axis_index("fsdp")
        greet([(lax.rem(me + step, ctx), mine) for step in range(1, ctx)])

        def copy_to(kind):
            index = kind * ctx + me
            return pltpu.make_async_remote_copy(
                own_ref.at[kind],
                out_ref.at[lax.rem(index, kinds)],
                send_sems.at[kind],
                recv_sems.at[lax.rem(index, kinds)],
                device_id=(index // kinds, mine),
                device_id_type=MESH,
            )

        def keep(kind):
            slot = lax.rem(kind * ctx + me, kinds)
            return pltpu.make_async_copy(own_ref.at[kind], out_ref.at[slot], send_sems.at[kind])

        def is_far(kind):
            return (kind * ctx + me) // kinds != me

        for kind in range(kinds):
            pl.when(is_far(kind))(copy_to(kind).start)
            pl.when(jnp.logical_not(is_far(kind)))(keep(kind).start)
        for kind in range(kinds):
            pl.when(is_far(kind))(copy_to(kind).wait_send)
            pl.when(jnp.logical_not(is_far(kind)))(keep(kind).wait)
        for slot in range(kinds):

            @pl.when(lax.rem(me * kinds + slot, ctx) != me)
            def _():
                pltpu.make_async_copy(
                    own_ref.at[slot], out_ref.at[slot], recv_sems.at[slot]
                ).wait()

    return comm_call(
        kernel,
        "deal_columns",
        collective_id,
        jax.ShapeDtypeStruct(values.shape, values.dtype),
        [ANY],
        ANY,
        [DMA((kinds,)), DMA((kinds,))],
        40 * 2**20,
    )(values)


def swap(values, axis, bit):
    return lax.ppermute(values, axis, [(i, i ^ bit) for i in range(lax.axis_size(axis))])


def halved(values, dim, axis, bit):
    own = (lax.axis_index(axis) // bit) % 2
    given = lax.dynamic_index_in_dim(values, 1 - own, dim, keepdims=False).astype(jnp.bfloat16)
    kept = lax.dynamic_index_in_dim(values, own, dim, keepdims=False)
    return kept.astype(jnp.float32) + swap(given, axis, bit).astype(jnp.float32)


def scatter_sum(values, dim, axis, bits):
    count = len(bits)
    shape = values.shape
    values = values.reshape(
        shape[:dim] + (2,) * count + (shape[dim] // 2**count,) + shape[dim + 1 :]
    )
    for left in range(count - 1, -1, -1):
        values = halved(values, dim + left, axis, bits[count - 1 - left])
    return values


def on_device_heads(
    tokens,
    doc_lengths,
    routes,
    slot_order,
    attn_gain,
    w_qkv,
    q_gain,
    k_gain,
    w_out,
    ffn_gain,
    w_router,
    w_gate,
    w_up,
    w_down,
    cotangent,
):
    rows, width = tokens.shape[1], tokens.shape[2]
    ctx, fsdp = lax.axis_size("ctx"), lax.axis_size("fsdp")
    me = lax.axis_index("ctx")
    head_dim = width // HEADS
    heads = HEADS // ctx
    cols = heads * head_dim
    part = width // fsdp
    total = rows * ctx
    score_scale = head_dim ** (-0.5)
    lengths = doc_lengths[0]
    bf16, f32 = jnp.bfloat16, jnp.float32

    tokens_all = lax.all_gather(tokens[0], "ctx", axis=0, tiled=True)
    small = jnp.concatenate(
        [jnp.stack([attn_gain, q_gain, k_gain, ffn_gain]), w_router.T], axis=0
    )
    small = lax.all_gather(small, "fsdp", axis=1, tiled=True)
    gain_one, gain_query, gain_key, gain_two = (small[i].astype(f32) for i in range(4))
    router_weight = small[4:]
    own_cols = jnp.concatenate(
        [
            lax.dynamic_slice_in_dim(w_qkv, kind * width + me * cols, cols, 1)
            for kind in range(3)
        ],
        axis=1,
    )
    qkv_weight = lax.all_gather(own_cols, "fsdp", axis=0, tiled=True)
    dy_all = lax.all_gather(cotangent[0], "fsdp", axis=0, tiled=True)
    pairs_all = lax.all_gather(jnp.stack([routes[0], slot_order[0]]), "fsdp", axis=0)

    stream_pos = dealt_position(jnp.arange(total, dtype=jnp.int32), rows, ctx)
    stream_doc, stream_inner = document_info(stream_pos, lengths)
    cosine, sine_part = rope_tables(stream_inner, head_dim)
    inputs_all = tokens_all.astype(f32)
    unit_all = inputs_all * rms_unit(inputs_all)
    normed_all = (unit_all * gain_one).astype(bf16)
    projected = dot32("td,de->te", normed_all, qkv_weight)
    query_lin, key_lin = projected[:, :cols], projected[:, cols : 2 * cols]
    value_low = projected[:, 2 * cols :].astype(bf16).reshape(total, heads, head_dim)
    squares = jnp.stack(
        [jnp.sum(query_lin * query_lin, axis=1), jnp.sum(key_lin * key_lin, axis=1)]
    )
    squares = ctx_sum(squares.reshape(-1, 128), 1).reshape(2, total)
    scales = lax.rsqrt(squares / width + EPSILON)
    own_gain_query = lax.dynamic_slice_in_dim(gain_query, me * cols, cols, 0)
    own_gain_key = lax.dynamic_slice_in_dim(gain_key, me * cols, cols, 0)
    query_unit = query_lin * scales[0][:, None]
    key_unit = key_lin * scales[1][:, None]

    def by_head(values):
        return values.reshape(total, heads, head_dim)

    query_low = turn(by_head(query_unit * own_gain_query), cosine, sine_part).astype(bf16)
    key_low = turn(by_head(key_unit * own_gain_key), cosine, sine_part).astype(bf16)
    scores = masked_scores(
        query_low, key_low, stream_pos, stream_doc, stream_pos, stream_doc, score_scale
    )
    weights = jnp.exp(scores - jnp.max(scores, axis=-1, keepdims=True))
    probs = weights / jnp.sum(weights, axis=-1, keepdims=True)
    prob_low = probs.astype(bf16)
    attended = dot32("hqk,khd->qhd", prob_low, value_low)

    attended_part = heads_to_rows(attended.reshape(total, cols).astype(bf16), 2)
    mixed_part = dot32("td,de->te", attended_part, w_out).astype(bf16)
    inputs = tokens[0].astype(f32)
    mixed = inputs + lax.psum_scatter(
        mixed_part, "fsdp", scatter_dimension=0, tiled=True
    ).astype(f32)
    scale_two = rms_unit(mixed)
    unit_two = mixed * scale_two
    normed_two = (unit_two * gain_two).astype(bf16)
    group = lax.all_gather(normed_two, "fsdp", axis=0, tiled=True)

    experts = w_gate.shape[0]
    top = routes.shape[2]
    capacity = rows * top // experts
    expert_ids = jnp.arange(experts, dtype=jnp.int32)

    def spread_of(pairs):
        slots = jax.vmap(slot_of_pairs)(pairs[:, 0], pairs[:, 1])
        chosen = pairs[:, 0][:, :, :, None] == expert_ids
        slot_by_expert = jnp.sum(jnp.where(chosen, slots[..., None] + 1, 0), axis=2) - 1
        return (
            slot_by_expert.transpose(0, 2, 1)[:, :, None, :]
            == jnp.arange(capacity, dtype=jnp.int32)[None, None, :, None]
        )

    spread = spread_of(pairs_all)
    disp = spread.astype(bf16).reshape(fsdp, experts * capacity, rows)
    logits = dot32("td,ed->te", group, router_weight)
    router_probs = jax.nn.softmax(logits, axis=-1).reshape(fsdp, rows, experts)
    slot_gate_value = jnp.sum(
        jnp.where(spread, router_probs.transpose(0, 2, 1)[:, :, None, :], 0.0), axis=-1
    )
    slot_gate_value = slot_gate_value.transpose(1, 0, 2).reshape(experts, fsdp * capacity)

    def dispatch(values):
        picked = dot32("bst,btd->bsd", disp, values.reshape(fsdp, rows, width)).astype(bf16)
        picked = picked.reshape(fsdp, experts, capacity, width).transpose(1, 0, 2, 3)
        return picked.reshape(experts, fsdp * capacity, width)

    def combine(values):
        values = values.reshape(experts, fsdp, capacity, width).transpose(1, 0, 2, 3)
        return dot32("bst,bsd->btd", disp, values.reshape(fsdp, experts * capacity, width))

    expert_in = dispatch(group)
    gate_pre = dot32("ecd,edh->ech", expert_in, w_gate)
    up_pre = dot32("ecd,edh->ech", expert_in, w_up)
    hidden = (jax.nn.silu(gate_pre) * up_pre).astype(bf16)
    expert_out = dot32("ech,ehd->ecd", hidden, w_down) * slot_gate_value[..., None]
    moved = lax.psum_scatter(
        combine(expert_out.astype(bf16)).reshape(fsdp * rows, width).astype(bf16),
        "fsdp",
        scatter_dimension=0,
        tiled=True,
    )
    activations = (mixed + moved.astype(f32)).astype(bf16)

    slot_dy = dispatch(dy_all)
    raw_grad = dot32("ecd,ehd->ech", slot_dy, w_down)
    slot_gate_grad = jnp.sum(hidden.astype(f32) * raw_grad, axis=-1)
    hidden_grad = raw_grad * slot_gate_value[..., None]
    gate_low, up_low = silu_parts(hidden_grad, gate_pre, up_pre)
    in_grad = dot32("ech,edh->ecd", gate_low, w_gate) + dot32("ech,edh->ecd", up_low, w_up)
    scaled_hidden = (hidden.astype(f32) * slot_gate_value[..., None]).astype(bf16)

    def both(values):
        return jnp.concatenate([values, swap(values, "ctx", 1)], axis=1)

    def half(values, which):
        values = values.reshape(-1, ctx // 2, 2, cols)
        return lax.dynamic_index_in_dim(values, which, 2, keepdims=False).reshape(-1, width // 2)

    def half_of_both(values):
        other = swap(half(values, 1 - me % 2), "ctx", 1)
        values = jnp.concatenate([half(values, me % 2), other], axis=0)
        picked = dot32("bst,btd->bsd", disp_both, values.reshape(2 * fsdp, rows, width // 2))
        picked = picked.astype(bf16).reshape(2 * fsdp, experts, capacity, width // 2)
        return picked.transpose(1, 0, 2, 3).reshape(experts, 2 * fsdp * capacity, width // 2)

    disp_both = jnp.concatenate(
        [disp, spread_of(swap(pairs_all, "ctx", 1)).astype(bf16).reshape(disp.shape)], axis=0
    )
    high_bits = [2**i for i in range(1, ctx.bit_length() - 1)]
    half_in, half_dy = half_of_both(group), half_of_both(dy_all)
    down_parts = scatter_sum(
        dot32("ech,ecd->ehd", both(scaled_hidden), half_dy).astype(bf16), 2, "ctx", high_bits
    )
    gate_parts = scatter_sum(
        dot32("ecd,ech->edh", half_in, both(gate_low)).astype(bf16), 1, "ctx", high_bits
    )
    up_parts = scatter_sum(
        dot32("ecd,ech->edh", half_in, both(up_low)).astype(bf16), 1, "ctx", high_bits
    )
    prob_grad = jnp.sum(
        jnp.where(
            spread,
            slot_gate_grad.reshape(experts, fsdp, capacity).transpose(1, 0, 2)[..., None],
            0.0,
        ),
        axis=2,
    ).transpose(0, 2, 1)
    logit_grad = (
        router_probs * (prob_grad - jnp.sum(router_probs * prob_grad, axis=-1, keepdims=True))
    ).reshape(fsdp * rows, experts).astype(bf16)
    group_grad = combine(in_grad.astype(bf16)).reshape(fsdp * rows, width) + dot32(
        "te,ed->td", logit_grad, router_weight
    )
    g_router = dot32("te,td->ed", logit_grad, group)
    normed_two_grad = lax.psum_scatter(
        group_grad.astype(bf16), "fsdp", scatter_dimension=0, tiled=True
    ).astype(f32)
    g_ffn_gain = jnp.sum(normed_two_grad * unit_two, axis=0)
    pulled = normed_two_grad * gain_two
    out_grad = cotangent[0].astype(f32)
    mixed_grad = out_grad + scale_two * (
        pulled - unit_two * jnp.mean(unit_two * pulled, axis=-1, keepdims=True)
    )
    mixed_all = lax.all_gather(mixed_grad.astype(bf16), "fsdp", axis=0, tiled=True)
    output_part = dot32("te,de->td", mixed_all, w_out).astype(bf16)
    g_out = dot32("td,te->de", attended_part, mixed_all).astype(bf16)
    output_grad = by_head(rows_to_heads(output_part, 3))

    row_delta = jnp.sum(output_grad.astype(f32) * attended, axis=-1).T
    prob_grad_attn = dot32("qhd,khd->hqk", output_grad, value_low)
    score_grad = (probs * (prob_grad_attn - row_delta[..., None])).astype(bf16)
    query_grad = dot32("hqk,khd->qhd", score_grad, key_low) * score_scale
    key_grad = dot32("hqk,qhd->khd", score_grad, query_low) * score_scale
    value_grad = dot32("hqk,qhd->khd", prob_low, output_grad)
    query_back = turn(query_grad, cosine, -sine_part).reshape(total, cols)
    key_back = turn(key_grad, cosine, -sine_part).reshape(total, cols)
    own_g_query = jnp.sum(query_back * query_unit, axis=0)
    own_g_key = jnp.sum(key_back * key_unit, axis=0)
    query_back = query_back * own_gain_query
    key_back = key_back * own_gain_key
    inner_sums = jnp.stack(
        [jnp.sum(query_back * query_unit, axis=1), jnp.sum(key_back * key_unit, axis=1)]
    )
    inner_sums = ctx_sum(inner_sums.reshape(-1, 128), 1).reshape(2, total) / width
    proj_grad = jnp.concatenate(
        [
            scales[0][:, None] * (query_back - query_unit * inner_sums[0][:, None]),
            scales[1][:, None] * (key_back - key_unit * inner_sums[1][:, None]),
            value_grad.reshape(total, cols),
        ],
        axis=1,
    ).astype(bf16)
    g_qkv = dot32("td,te->de", normed_all, proj_grad).astype(bf16)
    normed_grad_part = dot32("te,de->td", proj_grad, qkv_weight)
    g_attn_gain = jnp.sum(normed_grad_part * unit_all, axis=0)
    normed_grad = lax.psum_scatter(
        normed_grad_part.astype(bf16), "ctx", scatter_dimension=0, tiled=True
    ).astype(f32)
    scale_one = rms_unit(inputs)
    unit_one = inputs * scale_one
    pulled_one = normed_grad * gain_one
    input_grad = mixed_grad + scale_one * (
        pulled_one - unit_one * jnp.mean(unit_one * pulled_one, axis=-1, keepdims=True)
    )

    out_part = scatter_sum(g_out, 1, "ctx", [1] + high_bits)
    qkv_shard = scatter_sum(g_qkv, 0, "fsdp", [2**i for i in range(fsdp.bit_length() - 1)])
    qkv_shard = qkv_shard.astype(bf16).reshape(part, 3, cols).transpose(1, 0, 2)
    qkv_part = deal_columns(qkv_shard, 4).transpose(1, 0, 2).reshape(part, 3 * cols).astype(f32)

    def placed_cols(values):
        return lax.dynamic_update_slice_in_dim(jnp.zeros((width,), f32), values, me * cols, 0)

    sums = jnp.concatenate(
        [
            jnp.stack([g_attn_gain, placed_cols(own_g_query), placed_cols(own_g_key), g_ffn_gain]),
            g_router,
        ],
        axis=0,
    )
    sums = mesh_sum(jnp.pad(sums, ((0, -sums.shape[0] % 8), (0, 0))), 5)
    return (
        activations[None],
        input_grad[None],
        sums[0],
        qkv_part,
        sums[1],
        sums[2],
        out_part,
        sums[3],
        sums[4 : 4 + experts].T,
        gate_parts,
        up_parts,
        down_parts,
    )


def solution(mesh):
    in_specs = (
        P("fsdp", "ctx", None),
        P("fsdp", None),
        P("fsdp", "ctx", None),
        P("fsdp", "ctx", None),
        P("fsdp"),
        P("fsdp", None),
        P("fsdp"),
        P("fsdp"),
        P("fsdp", None),
        P("fsdp"),
        P("fsdp", None),
        P(None, None, "fsdp"),
        P(None, None, "fsdp"),
        P(None, "fsdp", None),
        P("fsdp", "ctx", None),
    )
    out_specs = (
        P("fsdp", "ctx", None),
        P("fsdp", "ctx", None),
        P("fsdp"),
        P("fsdp", "ctx"),
        P("fsdp"),
        P("fsdp"),
        P("fsdp", "ctx"),
        P("fsdp"),
        P("fsdp", None),
        P(None, "ctx", "fsdp"),
        P(None, "ctx", "fsdp"),
        P(None, "fsdp", "ctx"),
    )
    ctx, fsdp = mesh.shape["ctx"], mesh.shape["fsdp"]
    by_heads = HEADS % ctx == 0 and ctx % fsdp == 0 and ctx & (ctx - 1) == 0 and fsdp == 4
    body = on_device_heads if by_heads else on_device
    return jax.shard_map(
        body, mesh=mesh, in_specs=in_specs, out_specs=out_specs, check_vma=False
    )
```

```python
import math

import jax
import jax.numpy as jnp
from jax import lax
from jax.experimental import pallas as pl
from jax.experimental.pallas import tpu as pltpu
from jax.sharding import PartitionSpec as P

HEADS = 16
MESH = pl.DeviceIdType.MESH
ANY = pl.BlockSpec(memory_space=pl.ANY)
VMEM = pl.BlockSpec(memory_space=pltpu.VMEM)
DMA = pltpu.SemaphoreType.DMA

EPSILON = 1e-05
ROPE_BASE = 10000.0
MASKED = -1e30


def rms_scale(values, gain_vector):
    return (
        values
        * lax.rsqrt(jnp.mean(values * values, axis=-1, keepdims=True) + EPSILON)
        * gain_vector
    )


def rotate(values, inner_pos):
    half_dim = values.shape[-1] // 2
    freq_table = ROPE_BASE ** (-2.0 * jnp.arange(half_dim, dtype=jnp.float32) / values.shape[-1])
    angles = inner_pos.astype(jnp.float32)[:, None] * freq_table[None, :]
    cosine = jnp.cos(angles)[:, None, :]
    sine_part = jnp.sin(angles)[:, None, :]
    first_half = values[..., :half_dim]
    second_half = values[..., half_dim:]
    return jnp.concatenate(
        [
            first_half * cosine - second_half * sine_part,
            second_half * cosine + first_half * sine_part,
        ],
        axis=-1,
    )


def dealt_position(flat_index, per_device, device_count):
    device_index = flat_index // per_device
    within = flat_index % per_device
    half_rows = per_device // 2
    return jnp.where(
        within < half_rows,
        device_index * half_rows + within,
        (2 * device_count - 1 - device_index) * half_rows + within - half_rows,
    )


def document_info(positions, lengths):
    doc_ends = jnp.sum(jnp.where(jnp.arange(lengths.shape[0])[:, None] >= jnp.arange(lengths.shape[0])[None, :], lengths[None, :], 0), axis=1)
    passed = doc_ends[None, :] <= positions[:, None]
    doc_ids = jnp.sum(passed.astype(jnp.int32), axis=1)
    inner_pos = positions - jnp.sum(jnp.where(passed, lengths[None, :], 0), axis=1)
    return (doc_ids, inner_pos)


def slot_table(route_ids, order_ids, capacity, expert_count):
    pair_count = route_ids.shape[0] * route_ids.shape[1]
    expert_flat = route_ids.reshape(pair_count)
    rank_flat = order_ids.reshape(pair_count)
    earlier = (expert_flat[None, :] == expert_flat[:, None]) & (
        rank_flat[None, :] < rank_flat[:, None]
    )
    slot_index = jnp.sum(earlier.astype(jnp.int32), axis=1)
    placed = jnp.where(
        slot_index < capacity, expert_flat * capacity + slot_index, expert_count * capacity
    )
    source = (
        jnp.full((expert_count * capacity + 1,), pair_count, jnp.int32)
        .at[placed]
        .set(jnp.arange(pair_count, dtype=jnp.int32))
    )
    return (placed, source[: expert_count * capacity])


def masked_scores(query_block, key_block, query_pos, query_doc, key_pos, key_doc, score_scale):
    scores = (
        jnp.einsum("qhd,khd->hqk", query_block, key_block, preferred_element_type=jnp.float32)
        * score_scale
    )
    allowed = (query_doc[:, None] == key_doc[None, :]) & (key_pos[None, :] <= query_pos[:, None])
    return jnp.where(allowed[None], scores, MASKED)


def silu_parts(hidden_grad, slot_gate, slot_up):
    sigma = jax.nn.sigmoid(slot_gate)
    gate_grad_low = (hidden_grad * slot_up * sigma * (1.0 + slot_gate * (1.0 - sigma))).astype(
        jnp.bfloat16
    )
    up_grad_low = (hidden_grad * slot_gate * sigma).astype(jnp.bfloat16)
    return (gate_grad_low, up_grad_low)


def on_device(
    tokens,
    doc_lengths,
    routes,
    slot_order,
    attn_gain,
    w_qkv,
    q_gain,
    k_gain,
    w_out,
    ffn_gain,
    w_router,
    w_gate,
    w_up,
    w_down,
    cotangent,
):
    row_count = tokens.shape[1]
    model_width = tokens.shape[2]
    head_count = HEADS
    head_dim = model_width // head_count
    score_scale = head_dim ** (-0.5)
    ctx_count = lax.axis_size("ctx")
    ctx_index = lax.axis_index("ctx")
    total_rows = row_count * ctx_count
    lengths = doc_lengths[0]
    local_pos = dealt_position(
        ctx_index * row_count + jnp.arange(row_count, dtype=jnp.int32), row_count, ctx_count
    )
    local_doc, local_inner = document_info(local_pos, lengths)
    stream_pos = dealt_position(jnp.arange(total_rows, dtype=jnp.int32), row_count, ctx_count)
    stream_doc, stream_inner = document_info(stream_pos, lengths)
    block_rows = math.gcd(total_rows, 512)
    block_count = total_rows // block_rows
    block_ids = jnp.arange(block_count, dtype=jnp.int32)
    gain_one, qkv_weight, gain_query, gain_key, out_weight = (
        lax.all_gather(attn_gain, "fsdp", axis=0, tiled=True),
        lax.all_gather(w_qkv, "fsdp", axis=0, tiled=True),
        lax.all_gather(q_gain, "fsdp", axis=0, tiled=True),
        lax.all_gather(k_gain, "fsdp", axis=0, tiled=True),
        lax.all_gather(w_out, "fsdp", axis=0, tiled=True),
    )
    gain_two, router_weight, gate_weight, up_weight, down_weight = (
        lax.all_gather(ffn_gain, "fsdp", axis=0, tiled=True),
        lax.all_gather(w_router, "fsdp", axis=0, tiled=True),
        lax.all_gather(w_gate, "fsdp", axis=2, tiled=True),
        lax.all_gather(w_up, "fsdp", axis=2, tiled=True),
        lax.all_gather(w_down, "fsdp", axis=1, tiled=True),
    )
    inputs = tokens[0].astype(jnp.float32)
    normed_f, norm_one_pull = jax.vjp(rms_scale, inputs, gain_one.astype(jnp.float32))
    normed_low = normed_f.astype(jnp.bfloat16)
    projected = jnp.dot(normed_low, qkv_weight, preferred_element_type=jnp.float32)
    query_lin = projected[:, :model_width]
    key_lin = projected[:, model_width : 2 * model_width]
    value_low = (
        projected[:, 2 * model_width :]
        .astype(jnp.bfloat16)
        .reshape(row_count, head_count, head_dim)
    )

    def head_shape(values, gain_vector):
        return rotate(
            rms_scale(values, gain_vector).reshape(row_count, head_count, head_dim), local_inner
        )

    query_f, query_pull = jax.vjp(head_shape, query_lin, gain_query.astype(jnp.float32))
    key_f, key_pull = jax.vjp(head_shape, key_lin, gain_key.astype(jnp.float32))
    query_low = query_f.astype(jnp.bfloat16)
    key_low = key_f.astype(jnp.bfloat16)
    keys_all, values_all = (
        lax.all_gather(key_low, "ctx", axis=0, tiled=True),
        lax.all_gather(value_low, "ctx", axis=0, tiled=True),
    )

    def key_slice(block_index):
        first_row = block_index * block_rows
        return (
            lax.dynamic_slice_in_dim(keys_all, first_row, block_rows, 0),
            lax.dynamic_slice_in_dim(values_all, first_row, block_rows, 0),
            lax.dynamic_slice_in_dim(stream_pos, first_row, block_rows, 0),
            lax.dynamic_slice_in_dim(stream_doc, first_row, block_rows, 0),
        )

    def stats_step(carry, block_index):
        running_top, running_total = carry
        key_block, value_block, key_pos, key_doc = key_slice(block_index)
        scores = masked_scores(
            query_low, key_block, local_pos, local_doc, key_pos, key_doc, score_scale
        )
        new_top = jnp.maximum(running_top, jnp.max(scores, axis=-1))
        running_total = running_total * jnp.exp(running_top - new_top) + jnp.sum(
            jnp.exp(scores - new_top[..., None]), axis=-1
        )
        return ((new_top, running_total), None)

    start_stats = (
        jnp.full((head_count, row_count), MASKED, jnp.float32),
        jnp.zeros((head_count, row_count), jnp.float32),
    )
    (score_top, score_total), _ = lax.scan(stats_step, start_stats, block_ids)
    log_total = score_top + jnp.log(score_total)

    def output_step(accum, block_index):
        key_block, value_block, key_pos, key_doc = key_slice(block_index)
        scores = masked_scores(
            query_low, key_block, local_pos, local_doc, key_pos, key_doc, score_scale
        )
        prob_block = jnp.exp(scores - log_total[..., None]).astype(jnp.bfloat16)
        return (
            accum
            + jnp.einsum(
                "hqk,khd->qhd", prob_block, value_block, preferred_element_type=jnp.float32
            ),
            None,
        )

    attended_f, _ = lax.scan(
        output_step, jnp.zeros((row_count, head_count, head_dim), jnp.float32), block_ids
    )
    attended_low = attended_f.reshape(row_count, model_width).astype(jnp.bfloat16)
    mixed = inputs + jnp.dot(attended_low, out_weight, preferred_element_type=jnp.float32)
    normed_two_f, norm_two_pull = jax.vjp(rms_scale, mixed, gain_two.astype(jnp.float32))
    normed_two = normed_two_f.astype(jnp.bfloat16)
    expert_count = gate_weight.shape[0]
    route_ids = routes[0]
    top_count = route_ids.shape[1]
    pair_count = row_count * top_count
    capacity = pair_count // expert_count
    logits = jnp.dot(normed_two, router_weight, preferred_element_type=jnp.float32)
    router_probs = jax.nn.softmax(logits, axis=-1)
    chosen = (
        route_ids[:, :, None] == jnp.arange(expert_count, dtype=jnp.int32)[None, None, :]
    ).astype(jnp.float32)
    gate_values = jnp.sum(chosen * router_probs[:, None, :], axis=-1)
    placed, source = slot_table(route_ids, slot_order[0], capacity, expert_count)
    padded_in = jnp.concatenate([normed_two, jnp.zeros((1, model_width), jnp.bfloat16)], axis=0)
    expert_in = padded_in[source // top_count].reshape(expert_count, capacity, model_width)
    gate_pre = jnp.einsum(
        "ecd,edh->ech", expert_in, gate_weight, preferred_element_type=jnp.float32
    )
    up_pre = jnp.einsum("ecd,edh->ech", expert_in, up_weight, preferred_element_type=jnp.float32)
    hidden_low = (jax.nn.silu(gate_pre) * up_pre).astype(jnp.bfloat16)
    expert_out = jnp.einsum(
        "ech,ehd->ecd", hidden_low, down_weight, preferred_element_type=jnp.float32
    )
    out_padded = jnp.concatenate(
        [
            expert_out.reshape(expert_count * capacity, model_width),
            jnp.zeros((1, model_width), jnp.float32),
        ],
        axis=0,
    )
    per_pair = out_padded[placed].reshape(row_count, top_count, model_width)
    layer_out = mixed + jnp.sum(gate_values[:, :, None] * per_pair, axis=1)
    out_grad = cotangent[0].astype(jnp.float32)
    gate_grad = jnp.sum(out_grad[:, None, :] * per_pair, axis=-1)
    pair_grad = (gate_values[:, :, None] * out_grad[:, None, :]).reshape(pair_count, model_width)
    pair_padded = jnp.concatenate([pair_grad, jnp.zeros((1, model_width), jnp.float32)], axis=0)
    slot_grad = (
        pair_padded[source].reshape(expert_count, capacity, model_width).astype(jnp.bfloat16)
    )

    def expert_step(carry, pieces):
        slot_in, slot_hidden, slot_dy, slot_gate, slot_up, gate_matrix, up_matrix, down_matrix = (
            pieces
        )
        hidden_grad = jnp.einsum(
            "cd,hd->ch", slot_dy, down_matrix, preferred_element_type=jnp.float32
        )
        gate_grad_low, up_grad_low = silu_parts(hidden_grad, slot_gate, slot_up)
        in_grad = jnp.einsum(
            "ch,dh->cd", gate_grad_low, gate_matrix, preferred_element_type=jnp.float32
        ) + jnp.einsum("ch,dh->cd", up_grad_low, up_matrix, preferred_element_type=jnp.float32)
        gate_term = jnp.einsum(
            "cd,ch->dh", slot_in, gate_grad_low, preferred_element_type=jnp.float32
        )
        up_term = jnp.einsum("cd,ch->dh", slot_in, up_grad_low, preferred_element_type=jnp.float32)
        down_term = jnp.einsum(
            "ch,cd->hd", slot_hidden, slot_dy, preferred_element_type=jnp.float32
        )
        gate_shard, up_shard, down_shard = (
            lax.psum_scatter(
                gate_term.astype(jnp.bfloat16), "fsdp", scatter_dimension=1, tiled=True
            ).astype(jnp.float32),
            lax.psum_scatter(
                up_term.astype(jnp.bfloat16), "fsdp", scatter_dimension=1, tiled=True
            ).astype(jnp.float32),
            lax.psum_scatter(
                down_term.astype(jnp.bfloat16), "fsdp", scatter_dimension=0, tiled=True
            ).astype(jnp.float32),
        )
        gate_part, up_part, down_part = (
            lax.psum_scatter(
                gate_shard.astype(jnp.bfloat16), "ctx", scatter_dimension=0, tiled=True
            ).astype(jnp.float32),
            lax.psum_scatter(
                up_shard.astype(jnp.bfloat16), "ctx", scatter_dimension=0, tiled=True
            ).astype(jnp.float32),
            lax.psum_scatter(
                down_shard.astype(jnp.bfloat16), "ctx", scatter_dimension=1, tiled=True
            ).astype(jnp.float32),
        )
        return (carry, (in_grad, gate_part, up_part, down_part))

    _, (expert_in_grad, gate_parts, up_parts, down_parts) = lax.scan(
        expert_step,
        None,
        (expert_in, hidden_low, slot_grad, gate_pre, up_pre, gate_weight, up_weight, down_weight),
    )
    in_padded = jnp.concatenate(
        [
            expert_in_grad.reshape(expert_count * capacity, model_width),
            jnp.zeros((1, model_width), jnp.float32),
        ],
        axis=0,
    )
    normed_two_grad = jnp.sum(in_padded[placed].reshape(row_count, top_count, model_width), axis=1)
    prob_grad_router = jnp.sum(chosen * gate_grad[:, :, None], axis=1)
    logit_grad = (
        router_probs
        * (prob_grad_router - jnp.sum(router_probs * prob_grad_router, axis=-1, keepdims=True))
    ).astype(jnp.bfloat16)
    normed_two_grad = normed_two_grad + jnp.einsum(
        "te,de->td", logit_grad, router_weight, preferred_element_type=jnp.float32
    )
    router_grad = jnp.einsum(
        "td,te->de", normed_two, logit_grad, preferred_element_type=jnp.float32
    )
    mixed_norm_grad, gain_two_grad = norm_two_pull(normed_two_grad)
    mixed_grad = out_grad + mixed_norm_grad
    mixed_low = mixed_grad.astype(jnp.bfloat16)
    out_weight_grad = jnp.einsum(
        "td,te->de", attended_low, mixed_low, preferred_element_type=jnp.float32
    )
    output_grad = (
        jnp.einsum("te,de->td", mixed_low, out_weight, preferred_element_type=jnp.float32)
        .astype(jnp.bfloat16)
        .reshape(row_count, head_count, head_dim)
    )
    row_delta = jnp.sum(output_grad.astype(jnp.float32) * attended_f, axis=-1).T

    def query_grad_step(accum, block_index):
        key_block, value_block, key_pos, key_doc = key_slice(block_index)
        scores = masked_scores(
            query_low, key_block, local_pos, local_doc, key_pos, key_doc, score_scale
        )
        prob_block = jnp.exp(scores - log_total[..., None])
        prob_grad = jnp.einsum(
            "qhd,khd->hqk", output_grad, value_block, preferred_element_type=jnp.float32
        )
        score_grad = (prob_block * (prob_grad - row_delta[..., None])).astype(jnp.bfloat16)
        return (
            accum
            + jnp.einsum("hqk,khd->qhd", score_grad, key_block, preferred_element_type=jnp.float32)
            * score_scale,
            None,
        )

    query_grad, _ = lax.scan(
        query_grad_step, jnp.zeros((row_count, head_count, head_dim), jnp.float32), block_ids
    )
    inner_rows = math.gcd(row_count * lax.axis_size("ctx"), 512)

    def piece_step(carry, piece_index):
        first_row = piece_index * inner_rows
        key_block = lax.dynamic_slice_in_dim(keys_all, first_row, inner_rows, 0)
        value_block = lax.dynamic_slice_in_dim(values_all, first_row, inner_rows, 0)
        key_pos = lax.dynamic_slice_in_dim(stream_pos, first_row, inner_rows, 0)
        key_doc = lax.dynamic_slice_in_dim(stream_doc, first_row, inner_rows, 0)
        scores = masked_scores(
            query_low, key_block, local_pos, local_doc, key_pos, key_doc, score_scale
        )
        prob_block = jnp.exp(scores - log_total[..., None])
        prob_grad = jnp.einsum(
            "qhd,khd->hqk", output_grad, value_block, preferred_element_type=jnp.float32
        )
        score_grad = (prob_block * (prob_grad - row_delta[..., None])).astype(jnp.bfloat16)
        value_part = jnp.einsum(
            "hqk,qhd->khd",
            prob_block.astype(jnp.bfloat16),
            output_grad,
            preferred_element_type=jnp.float32,
        )
        key_part = (
            jnp.einsum("hqk,qhd->khd", score_grad, query_low, preferred_element_type=jnp.float32)
            * score_scale
        )
        return (
            carry,
            jnp.concatenate(
                [
                    key_part.reshape(inner_rows, model_width),
                    value_part.reshape(inner_rows, model_width),
                ],
                axis=1,
            ),
        )

    _, stacked = lax.scan(
        piece_step,
        None,
        jnp.arange(row_count * lax.axis_size("ctx") // inner_rows, dtype=jnp.int32),
    )
    key_value_grad = lax.psum_scatter(
        stacked.reshape(row_count * lax.axis_size("ctx"), 2 * model_width).astype(jnp.bfloat16),
        "ctx",
        scatter_dimension=0,
        tiled=True,
    ).astype(jnp.float32)
    key_grad = key_value_grad[:, :model_width].reshape(row_count, head_count, head_dim)
    value_grad = key_value_grad[:, model_width:]
    query_lin_grad, gain_query_grad = query_pull(query_grad)
    key_lin_grad, gain_key_grad = key_pull(key_grad)
    proj_grad = jnp.concatenate(
        [
            query_lin_grad.astype(jnp.bfloat16),
            key_lin_grad.astype(jnp.bfloat16),
            value_grad.astype(jnp.bfloat16),
        ],
        axis=1,
    )
    qkv_weight_grad = jnp.einsum(
        "td,te->de", normed_low, proj_grad, preferred_element_type=jnp.float32
    )
    normed_grad = jnp.einsum("te,de->td", proj_grad, qkv_weight, preferred_element_type=jnp.float32)
    input_norm_grad, gain_one_grad = norm_one_pull(normed_grad)
    input_grad = mixed_grad + input_norm_grad
    qkv_shard, out_shard = (
        lax.psum_scatter(
            qkv_weight_grad.astype(jnp.bfloat16), "fsdp", scatter_dimension=0, tiled=True
        ).astype(jnp.float32),
        lax.psum_scatter(
            out_weight_grad.astype(jnp.bfloat16), "fsdp", scatter_dimension=0, tiled=True
        ).astype(jnp.float32),
    )
    qkv_part, out_part = (
        lax.psum_scatter(
            qkv_shard.astype(jnp.bfloat16), "ctx", scatter_dimension=1, tiled=True
        ).astype(jnp.float32),
        lax.psum_scatter(
            out_shard.astype(jnp.bfloat16), "ctx", scatter_dimension=1, tiled=True
        ).astype(jnp.float32),
    )
    gain_one_sum, gain_query_sum, gain_key_sum, gain_two_sum, router_sum = lax.psum(
        (gain_one_grad, gain_query_grad, gain_key_grad, gain_two_grad, router_grad), ("ctx", "fsdp")
    )
    shard_rows = model_width // lax.axis_size("fsdp")
    shard_start = lax.axis_index("fsdp") * shard_rows

    def own_rows(full_array):
        return lax.dynamic_slice_in_dim(full_array, shard_start, shard_rows, 0)

    return (
        layer_out.astype(jnp.bfloat16)[None],
        input_grad[None],
        own_rows(gain_one_sum),
        qkv_part,
        own_rows(gain_query_sum),
        own_rows(gain_key_sum),
        out_part,
        own_rows(gain_two_sum),
        own_rows(router_sum),
        gate_parts,
        up_parts,
        down_parts,
    )


def rms_unit(values):
    return lax.rsqrt(jnp.mean(values * values, axis=-1, keepdims=True) + EPSILON)


def rope_tables(inner_pos, head_dim):
    half_dim = head_dim // 2
    freq_table = ROPE_BASE ** (-2.0 * jnp.arange(half_dim, dtype=jnp.float32) / head_dim)
    angles = inner_pos.astype(jnp.float32)[:, None] * freq_table[None, :]
    return (jnp.cos(angles), jnp.sin(angles))


def slot_of_pairs(route_ids, order_ids):
    pair_count = route_ids.shape[0] * route_ids.shape[1]
    expert_flat = route_ids.reshape(pair_count)
    rank_flat = order_ids.reshape(pair_count)
    earlier = (expert_flat[None, :] == expert_flat[:, None]) & (
        rank_flat[None, :] < rank_flat[:, None]
    )
    return jnp.sum(earlier.astype(jnp.int32), axis=1).reshape(route_ids.shape)


def dot32(spec, left, right):
    return jnp.einsum(spec, left, right, preferred_element_type=jnp.float32)


def greet(peers):
    barrier = pltpu.get_barrier_semaphore()
    for peer in peers:
        pl.semaphore_signal(barrier, inc=1, device_id=peer, device_id_type=MESH)
    pl.semaphore_wait(barrier, len(peers))


def send(source, target, send_sem, recv_sem, peer):
    copy = pltpu.make_async_remote_copy(
        source, target, send_sem, recv_sem, device_id=peer, device_id_type=MESH
    )
    copy.start()
    return copy


def comm_call(kernel, name, collective_id, out_shape, in_specs, out_specs, scratch_shapes, cost):
    return pl.pallas_call(
        kernel,
        out_shape=out_shape,
        in_specs=in_specs,
        out_specs=out_specs,
        scratch_shapes=scratch_shapes,
        compiler_params=pltpu.CompilerParams(
            collective_id=collective_id, has_side_effects=True, vmem_limit_bytes=48 * 2**20
        ),
        cost_estimate=pl.CostEstimate(flops=0, bytes_accessed=cost, transcendentals=0),
        name=name,
    )


def ctx_sum(values, collective_id):
    ctx = lax.axis_size("ctx")

    def kernel(own_ref, out_ref, held, send_sems, recv_sems):
        me, mine = lax.axis_index("ctx"), lax.axis_index("fsdp")
        peers = [(lax.rem(me + step, ctx), mine) for step in range(1, ctx)]
        greet(peers)
        copies = [
            send(own_ref, held.at[i], send_sems.at[i], recv_sems.at[i], peer)
            for i, peer in enumerate(peers)
        ]
        total = own_ref[...]
        for i, copy in enumerate(copies):
            copy.wait_recv()
            total = total + held[i]
        out_ref[...] = total
        for copy in copies:
            copy.wait_send()

    return comm_call(
        kernel,
        "ctx_sum",
        collective_id,
        jax.ShapeDtypeStruct(values.shape, values.dtype),
        [VMEM],
        VMEM,
        [
            pltpu.VMEM((ctx - 1,) + values.shape, values.dtype),
            DMA((ctx - 1,)),
            DMA((ctx - 1,)),
        ],
        20 * 2**20,
    )(values)


def mesh_sum(values, collective_id):
    ctx, fsdp = lax.axis_size("ctx"), lax.axis_size("fsdp")
    rows, part = values.shape[0], values.shape[1] // fsdp

    def kernel(own_ref, out_ref, parts, sums, held, part_send, part_recv, send_sems, recv_sems):
        me, mine = lax.axis_index("ctx"), lax.axis_index("fsdp")
        near = [lax.rem(mine + step, fsdp) for step in range(1, fsdp)]
        peers = [(lax.rem(me + step, ctx), mine) for step in range(1, ctx)]
        greet([(me, other) for other in near] + peers)

        def columns(index):
            return pl.ds(pl.multiple_of(index * part, part), part)

        copies = [
            send(
                own_ref.at[:, columns(other)],
                parts.at[i],
                part_send.at[i],
                part_recv.at[i],
                (me, other),
            )
            for i, other in enumerate(near)
        ]
        total = own_ref[:, columns(mine)]
        for i, copy in enumerate(copies):
            copy.wait_recv()
            total = total + parts[i]
        sums[...] = total
        wide = [
            send(sums, held.at[i], send_sems.at[i], recv_sems.at[i], peer)
            for i, peer in enumerate(peers)
        ]
        for i, copy in enumerate(wide):
            copy.wait_recv()
            total = total + held[i]
        out_ref[...] = total
        for copy in copies + wide:
            copy.wait_send()

    return comm_call(
        kernel,
        "mesh_sum",
        collective_id,
        jax.ShapeDtypeStruct((rows, part), values.dtype),
        [VMEM],
        VMEM,
        [
            pltpu.VMEM((fsdp - 1, rows, part), values.dtype),
            pltpu.VMEM((rows, part), values.dtype),
            pltpu.VMEM((ctx - 1, rows, part), values.dtype),
            DMA((fsdp - 1,)),
            DMA((fsdp - 1,)),
            DMA((ctx - 1,)),
            DMA((ctx - 1,)),
        ],
        30 * 2**20,
    )(values)


def heads_to_rows(values, collective_id):
    ctx, fsdp = lax.axis_size("ctx"), lax.axis_size("fsdp")
    rows, cols = values.shape[0] // ctx, values.shape[1]
    share = ctx // fsdp

    def kernel(own_ref, out_ref, send_sems, recv_sems):
        me, mine = lax.axis_index("ctx"), lax.axis_index("fsdp")
        keeper, place = me // share, lax.rem(me, share)
        own_keeper = (keeper == mine).astype(jnp.int32)
        barrier = pltpu.get_barrier_semaphore()
        for step in range(share * fsdp):
            source, stream = mine * share + step // fsdp, step % fsdp

            @pl.when(jnp.logical_or(source != me, stream != mine))
            def _():
                pl.semaphore_signal(
                    barrier, inc=1, device_id=(source, stream), device_id_type=MESH
                )

        pl.semaphore_wait(barrier, ctx - own_keeper)

        def block(index):
            return own_ref.at[pl.ds(pl.multiple_of(index * rows, rows), rows), :]

        def landing(stream, position):
            return out_ref.at[
                pl.ds(pl.multiple_of(stream * rows, rows), rows),
                pl.ds(pl.multiple_of(position * cols, cols), cols),
            ]

        slot = place * fsdp + mine

        def copy_to(step):
            other = lax.rem(me + step, ctx)
            return pltpu.make_async_remote_copy(
                block(other),
                landing(mine, place),
                send_sems.at[step],
                recv_sems.at[slot],
                device_id=(other, keeper),
                device_id_type=MESH,
            )

        kept = pltpu.make_async_copy(block(me), landing(mine, place), send_sems.at[0])
        for step in range(1, ctx):
            copy_to(step).start()

        @pl.when(own_keeper == 0)
        def _():
            copy_to(0).start()

        @pl.when(own_keeper == 1)
        def _():
            kept.start()
            kept.wait()

        for step in range(share * fsdp):

            @pl.when(
                jnp.logical_or(mine * share + step // fsdp != me, step % fsdp != mine)
            )
            def _():
                pltpu.make_async_copy(
                    block(0), landing(step % fsdp, step // fsdp), recv_sems.at[step]
                ).wait()

        for step in range(1, ctx):
            copy_to(step).wait_send()

        @pl.when(own_keeper == 0)
        def _():
            copy_to(0).wait_send()

    return comm_call(
        kernel,
        "heads_to_rows",
        collective_id,
        jax.ShapeDtypeStruct((fsdp * rows, share * cols), values.dtype),
        [ANY],
        ANY,
        [DMA((ctx,)), DMA((share * fsdp,))],
        40 * 2**20,
    )(values)


def rows_to_heads(values, collective_id):
    ctx, fsdp = lax.axis_size("ctx"), lax.axis_size("fsdp")
    share = ctx // fsdp
    rows, cols = values.shape[0] // fsdp, values.shape[1] // share

    def kernel(own_ref, out_ref, send_sems, recv_sems):
        me, mine = lax.axis_index("ctx"), lax.axis_index("fsdp")
        keeper, place = me // share, lax.rem(me, share)
        own_keeper = (keeper == mine).astype(jnp.int32)
        barrier = pltpu.get_barrier_semaphore()
        for step in range(ctx):
            source = lax.rem(me + step, ctx)

            @pl.when(jnp.logical_or(source != me, keeper != mine))
            def _():
                pl.semaphore_signal(
                    barrier, inc=1, device_id=(source, keeper), device_id_type=MESH
                )

        pl.semaphore_wait(barrier, share * fsdp - own_keeper)

        def block(stream, position):
            return own_ref.at[
                pl.ds(pl.multiple_of(stream * rows, rows), rows),
                pl.ds(pl.multiple_of(position * cols, cols), cols),
            ]

        def landing(index):
            return out_ref.at[pl.ds(pl.multiple_of(index * rows, rows), rows), :]

        def copy_to(step):
            return pltpu.make_async_remote_copy(
                block(step % fsdp, step // fsdp),
                landing(me),
                send_sems.at[step],
                recv_sems.at[me],
                device_id=(mine * share + step // fsdp, step % fsdp),
                device_id_type=MESH,
            )

        def is_far(step):
            return jnp.logical_or(mine * share + step // fsdp != me, step % fsdp != mine)

        for step in range(share * fsdp):
            pl.when(is_far(step))(copy_to(step).start)

        @pl.when(own_keeper == 1)
        def _():
            kept = pltpu.make_async_copy(block(mine, place), landing(me), recv_sems.at[me])
            kept.start()
            kept.wait()

        for step in range(ctx):
            source = lax.rem(me + step, ctx)

            @pl.when(jnp.logical_or(source != me, keeper != mine))
            def _():
                pltpu.make_async_copy(block(0, 0), landing(source), recv_sems.at[source]).wait()

        for step in range(share * fsdp):
            pl.when(is_far(step))(copy_to(step).wait_send)

    return comm_call(
        kernel,
        "rows_to_heads",
        collective_id,
        jax.ShapeDtypeStruct((ctx * rows, cols), values.dtype),
        [ANY],
        ANY,
        [DMA((share * fsdp,)), DMA((ctx,))],
        40 * 2**20,
    )(values)


def deal_columns(values, collective_id):
    ctx = lax.axis_size("ctx")
    kinds = values.shape[0]

    def kernel(own_ref, out_ref, send_sems, recv_sems):
        me, mine = lax.axis_index("ctx"), lax.axis_index("fsdp")
        greet([(lax.rem(me + step, ctx), mine) for step in range(1, ctx)])

        def copy_to(kind):
            index = kind * ctx + me
            return pltpu.make_async_remote_copy(
                own_ref.at[kind],
                out_ref.at[lax.rem(index, kinds)],
                send_sems.at[kind],
                recv_sems.at[lax.rem(index, kinds)],
                device_id=(index // kinds, mine),
                device_id_type=MESH,
            )

        def keep(kind):
            slot = lax.rem(kind * ctx + me, kinds)
            return pltpu.make_async_copy(own_ref.at[kind], out_ref.at[slot], send_sems.at[kind])

        def is_far(kind):
            return (kind * ctx + me) // kinds != me

        for kind in range(kinds):
            pl.when(is_far(kind))(copy_to(kind).start)
            pl.when(jnp.logical_not(is_far(kind)))(keep(kind).start)
        for kind in range(kinds):
            pl.when(is_far(kind))(copy_to(kind).wait_send)
            pl.when(jnp.logical_not(is_far(kind)))(keep(kind).wait)
        for slot in range(kinds):

            @pl.when(lax.rem(me * kinds + slot, ctx) != me)
            def _():
                pltpu.make_async_copy(
                    own_ref.at[slot], out_ref.at[slot], recv_sems.at[slot]
                ).wait()

    return comm_call(
        kernel,
        "deal_columns",
        collective_id,
        jax.ShapeDtypeStruct(values.shape, values.dtype),
        [ANY],
        ANY,
        [DMA((kinds,)), DMA((kinds,))],
        40 * 2**20,
    )(values)


def swap(values, axis, bit):
    return lax.ppermute(values, axis, [(i, i ^ bit) for i in range(lax.axis_size(axis))])


def halved(values, dim, axis, bit):
    own = (lax.axis_index(axis) // bit) % 2
    given = lax.dynamic_index_in_dim(values, 1 - own, dim, keepdims=False).astype(jnp.bfloat16)
    kept = lax.dynamic_index_in_dim(values, own, dim, keepdims=False)
    return kept.astype(jnp.float32) + swap(given, axis, bit).astype(jnp.float32)


def scatter_sum(values, dim, axis, bits):
    count = len(bits)
    shape = values.shape
    values = values.reshape(
        shape[:dim] + (2,) * count + (shape[dim] // 2**count,) + shape[dim + 1 :]
    )
    for left in range(count - 1, -1, -1):
        values = halved(values, dim + left, axis, bits[count - 1 - left])
    return values


def reduce_then_gather(partial, extras, out_shapes, chunk_math, name, collective_id):
    fsdp = lax.axis_size("fsdp")
    rows, width = partial.shape[0] // fsdp, partial.shape[1]
    chunks = 4
    size = rows // chunks
    count = len(extras)

    def kernel(*refs):
        part_ref, extra_refs = refs[0], refs[1 : 1 + count]
        all_ref, out_refs = refs[1 + count], refs[2 + count : 2 + count + len(out_shapes)]
        near_own, near_far, far_sum, far_own, sems = refs[2 + count + len(out_shapes) :]
        me, mine = lax.axis_index("ctx"), lax.axis_index("fsdp")
        flip = 1 - 2 * lax.rem(mine, 2)
        core = mine + flip
        chip = lax.rem(mine + 2, fsdp)
        diagonal = lax.rem(core + 2, fsdp)
        greet([(me, core), (me, chip)])

        def span(block, i):
            return pl.ds(pl.multiple_of(block * rows + i * size, size), size)

        def sem(kind, i):
            return sems.at[2 * kind, i], sems.at[2 * kind + 1, i]

        copies = []
        from_core_far, from_core_own, from_chip = [], [], []
        for i in range(chunks):
            copy = send(
                part_ref.at[span(diagonal, i), :], near_far.at[i], *sem(0, i), (me, core)
            )
            from_core_far.append(copy)
        for i in range(chunks):
            copy = send(part_ref.at[span(core, i), :], near_own.at[i], *sem(1, i), (me, core))
            from_core_own.append(copy)
        for i in range(chunks):
            from_core_far[i].wait_recv()
            both = part_ref[span(chip, i), :].astype(jnp.float32) + near_far[i].astype(jnp.float32)
            far_sum[i] = both.astype(jnp.bfloat16)
            from_chip.append(send(far_sum.at[i], far_own.at[i], *sem(2, i), (me, chip)))
        to_chip = []
        for i in range(chunks):
            from_core_own[i].wait_recv()
            from_chip[i].wait_recv()
            total = (
                part_ref[span(mine, i), :].astype(jnp.float32)
                + near_own[i].astype(jnp.float32)
                + far_own[i].astype(jnp.float32)
            )
            all_ref[span(mine, i), :] = chunk_math(
                i, pl.ds(i * size, size), total, extra_refs, out_refs
            ).astype(jnp.bfloat16)
            own = all_ref.at[span(mine, i), :]
            to_chip.append(send(own, own, *sem(3, i), (me, chip)))
            copies.append(send(own, own, *sem(4, i), (me, core)))
        for i in range(chunks):
            to_chip[i].wait_recv()
            other = all_ref.at[span(chip, i), :]
            copies.append(send(other, other, *sem(5, i), (me, core)))
        for copy in copies:
            copy.wait_recv()
        for copy in from_core_far + from_core_own + from_chip + to_chip + copies:
            copy.wait_send()

    return comm_call(
        kernel,
        name,
        collective_id,
        [jax.ShapeDtypeStruct(partial.shape, jnp.bfloat16)] + out_shapes,
        [VMEM] * (1 + count),
        [VMEM] * (1 + len(out_shapes)),
        [
            pltpu.VMEM((chunks, size, width), jnp.bfloat16),
            pltpu.VMEM((chunks, size, width), jnp.bfloat16),
            pltpu.VMEM((chunks, size, width), jnp.bfloat16),
            pltpu.VMEM((chunks, size, width), jnp.bfloat16),
            DMA((12, chunks)),
        ],
        100 * 2**20,
    )(partial, *extras)


def norm_chunk(index, span, total, extra_refs, out_refs):
    tokens_ref, gain_ref = extra_refs
    mixed = tokens_ref[span, :].astype(jnp.float32) + total
    out_refs[0][span, :] = mixed
    return mixed * rms_unit(mixed) * gain_ref[...]


def norm_back_chunk(index, span, total, extra_refs, out_refs):
    mixed_ref, gain_ref, dy_ref = extra_refs
    mixed = mixed_ref[span, :]
    scale = rms_unit(mixed)
    unit = mixed * scale
    pulled = total * gain_ref[...]
    grad = dy_ref[span, :].astype(jnp.float32) + scale * (
        pulled - unit * jnp.mean(unit * pulled, axis=-1, keepdims=True)
    )
    out_refs[0][span, :] = grad
    gain_grad = jnp.sum(total * unit, axis=0, keepdims=True)
    if index == 0:
        out_refs[1][...] = gain_grad
    else:
        out_refs[1][...] += gain_grad
    return grad


ROUTER_ROWS = 16


def one_hot(slots, capacity):
    return lax.broadcasted_iota(jnp.int32, (capacity, slots.shape[1]), 0) == slots


def run_experts(group, dy_all, slots, router, w_gate, w_up, w_down, blocks, capacity):
    experts, width, units = w_gate.shape
    total = group.shape[0]
    rows = total // blocks
    held = blocks * capacity
    f32, bf16 = jnp.float32, jnp.bfloat16

    def kernel(
        group_ref,
        dy_ref,
        slots_ref,
        router_ref,
        gate_ref,
        up_ref,
        down_ref,
        moved_ref,
        grad_ref,
        g_router_ref,
        slot_ref,
        disp,
        ins,
        dys,
        probs,
        prob_grad,
    ):
        expert = pl.program_id(0)

        def block_rows(b):
            return pl.ds(b * rows, rows)

        @pl.when(expert == 0)
        def _():
            logits = lax.dot_general(
                router_ref[...],
                group_ref[...],
                (((1,), (1,)), ((), ())),
                preferred_element_type=f32,
            )
            real = lax.broadcasted_iota(jnp.int32, logits.shape, 0) < experts
            logits = jnp.where(real, logits, MASKED)
            weights = jnp.exp(logits - jnp.max(logits, axis=0, keepdims=True))
            probs[...] = weights / jnp.sum(weights, axis=0, keepdims=True)
            prob_grad[...] = jnp.zeros_like(prob_grad)
            for b in range(blocks):
                for e in range(experts):
                    disp[b, pl.ds(e * capacity, capacity), :] = (
                        one_hot(slots_ref[pl.ds(e, 1), block_rows(b)], capacity)
                        .astype(f32)
                        .astype(bf16)
                    )
                for source, target in ((group_ref, ins), (dy_ref, dys)):
                    picked = jnp.dot(
                        disp[b], source[block_rows(b), :], preferred_element_type=f32
                    ).astype(bf16)
                    for e in range(experts):
                        target[e, pl.ds(b * capacity, capacity), :] = picked[
                            e * capacity : (e + 1) * capacity
                        ]

        expert_in, slot_dy = ins[expert], dys[expert]
        gate_matrix, up_matrix, down_matrix = gate_ref[0], up_ref[0], down_ref[0]
        gate_pre = jnp.dot(expert_in, gate_matrix, preferred_element_type=f32)
        up_pre = jnp.dot(expert_in, up_matrix, preferred_element_type=f32)
        raw_grad = lax.dot_general(
            slot_dy, down_matrix, (((1,), (1,)), ((), ())), preferred_element_type=f32
        )
        own_probs = probs[pl.ds(expert, 1), :]
        own_slots = slots_ref[pl.ds(expert, 1), :]
        hots = [
            one_hot(own_slots[:, b * rows : (b + 1) * rows], capacity) for b in range(blocks)
        ]
        value = jnp.concatenate(
            [
                jnp.sum(
                    jnp.where(hots[b], own_probs[:, b * rows : (b + 1) * rows], 0.0),
                    axis=1,
                    keepdims=True,
                )
                for b in range(blocks)
            ],
            axis=0,
        )
        sigma = 1.0 / (1.0 + jnp.exp(-gate_pre))
        silu = gate_pre * sigma
        hidden = (silu * up_pre).astype(bf16)
        hidden_f = hidden.astype(f32)
        value_grad = jnp.sum(hidden_f * raw_grad, axis=1, keepdims=True)
        hidden_grad = raw_grad * value
        gate_low = (hidden_grad * up_pre * sigma * (1.0 + gate_pre * (1.0 - sigma))).astype(bf16)
        up_low = (hidden_grad * silu).astype(bf16)
        scaled = (hidden_f * value).astype(bf16)
        slot_ref[0, 0] = scaled
        slot_ref[1, 0] = gate_low
        slot_ref[2, 0] = up_low
        for b in range(blocks):
            prob_grad[expert, :, block_rows(b)] = jnp.sum(
                jnp.where(hots[b], value_grad[b * capacity : (b + 1) * capacity], 0.0),
                axis=0,
                keepdims=True,
            )
        dys[expert] = jnp.dot(scaled, down_matrix, preferred_element_type=f32).astype(bf16)
        ins[expert] = (
            lax.dot_general(
                gate_low, gate_matrix, (((1,), (1,)), ((), ())), preferred_element_type=f32
            )
            + lax.dot_general(
                up_low, up_matrix, (((1,), (1,)), ((), ())), preferred_element_type=f32
            )
        ).astype(bf16)

        @pl.when(expert == experts - 1)
        def _():
            grads = jnp.concatenate([prob_grad[e] for e in range(ROUTER_ROWS)], axis=0)
            weights = probs[...]
            logit_grad = (
                weights * (grads - jnp.sum(weights * grads, axis=0, keepdims=True))
            ).astype(bf16)
            g_router_ref[...] = jnp.dot(logit_grad, group_ref[...], preferred_element_type=f32)
            for b in range(blocks):
                for source, target in ((dys, moved_ref), (ins, grad_ref)):
                    gathered = jnp.concatenate(
                        [source[e, pl.ds(b * capacity, capacity), :] for e in range(experts)],
                        axis=0,
                    )
                    back = lax.dot_general(
                        disp[b], gathered, (((0,), (0,)), ((), ())), preferred_element_type=f32
                    )
                    if target is grad_ref:
                        back = back + lax.dot_general(
                            logit_grad[:, b * rows : (b + 1) * rows],
                            router_ref[...],
                            (((0,), (0,)), ((), ())),
                            preferred_element_type=f32,
                        )
                    target[block_rows(b), :] = back.astype(bf16)

    def whole(shape):
        return pl.BlockSpec(shape, lambda e: (0,) * len(shape))

    def by_expert(shape):
        return pl.BlockSpec((1,) + shape, lambda e: (e, 0, 0))

    return pl.pallas_call(
        kernel,
        grid=(experts,),
        out_shape=[
            jax.ShapeDtypeStruct((total, width), bf16),
            jax.ShapeDtypeStruct((total, width), bf16),
            jax.ShapeDtypeStruct((ROUTER_ROWS, width), f32),
            jax.ShapeDtypeStruct((3, experts, held, units), bf16),
        ],
        in_specs=[
            whole((total, width)),
            whole((total, width)),
            whole((ROUTER_ROWS, total)),
            whole((ROUTER_ROWS, width)),
            by_expert((width, units)),
            by_expert((width, units)),
            by_expert((units, width)),
        ],
        out_specs=[
            whole((total, width)),
            whole((total, width)),
            whole((ROUTER_ROWS, width)),
            pl.BlockSpec((3, 1, held, units), lambda e: (0, e, 0, 0)),
        ],
        scratch_shapes=[
            pltpu.VMEM((blocks, experts * capacity, rows), bf16),
            pltpu.VMEM((experts, held, width), bf16),
            pltpu.VMEM((experts, held, width), bf16),
            pltpu.VMEM((ROUTER_ROWS, total), f32),
            pltpu.VMEM((ROUTER_ROWS, 1, total), f32),
        ],
        compiler_params=pltpu.CompilerParams(vmem_limit_bytes=60 * 2**20),
        cost_estimate=pl.CostEstimate(
            flops=30 * 10**9, bytes_accessed=30 * 2**20, transcendentals=10**6
        ),
        name="run_experts",
    )(group, dy_all, slots, router, w_gate, w_up, w_down)


def expert_grads(slot_own, slot_other, in_own, in_other, dy_own, dy_other, slots_own, slots_other, blocks, capacity):
    _, experts, held, units = slot_own.shape
    total, half = in_own.shape
    rows = total // blocks
    ctx = lax.axis_size("ctx")
    runs = ctx // 4
    cols = half // (2 * runs)
    f32, bf16 = jnp.float32, jnp.bfloat16

    def kernel(
        own_ref,
        other_ref,
        in_own_ref,
        in_other_ref,
        dy_own_ref,
        dy_other_ref,
        slots_own_ref,
        slots_other_ref,
        out_ref,
        ins,
        dys,
    ):
        expert = pl.program_id(0)

        @pl.when(expert == 0)
        def _():
            for side, slots_ref, in_ref, dy_ref in (
                (0, slots_own_ref, in_own_ref, dy_own_ref),
                (1, slots_other_ref, in_other_ref, dy_other_ref),
            ):
                for b in range(blocks):
                    span = pl.ds(b * rows, rows)
                    disp = jnp.concatenate(
                        [
                            one_hot(slots_ref[pl.ds(e, 1), span], capacity).astype(f32)
                            for e in range(experts)
                        ],
                        axis=0,
                    ).astype(bf16)
                    for source, target in ((in_ref, ins), (dy_ref, dys)):
                        picked = jnp.dot(
                            disp, source[span, :], preferred_element_type=f32
                        ).astype(bf16)
                        for e in range(experts):
                            target[e, pl.ds(side * held + b * capacity, capacity), :] = picked[
                                e * capacity : (e + 1) * capacity
                            ]

        keep_low = (lax.axis_index("ctx") // 2) % 2
        stacked = [jnp.concatenate([own_ref[m, 0], other_ref[m, 0]], axis=0) for m in range(3)]
        for low in range(2):
            kept = jnp.where(keep_low == low, 1, 0)
            for run in range(runs):
                span = pl.ds((run * 2 + low) * cols, cols)
                in_part, dy_part = ins[expert, :, span], dys[expert, :, span]
                contract = (((0,), (0,)), ((), ()))
                for m, (left, right) in enumerate(
                    ((stacked[0], dy_part), (in_part, stacked[1]), (in_part, stacked[2]))
                ):
                    out_ref[m, pl.ds(kept, 1), 0, run] = lax.dot_general(
                        left, right, contract, preferred_element_type=f32
                    ).astype(bf16)[None]

    def whole(shape):
        return pl.BlockSpec(shape, lambda e: (0,) * len(shape))

    slot_spec = pl.BlockSpec((3, 1, held, units), lambda e: (0, e, 0, 0))
    return pl.pallas_call(
        kernel,
        grid=(experts,),
        out_shape=jax.ShapeDtypeStruct((3, 2, experts, runs, units, cols), bf16),
        in_specs=[slot_spec, slot_spec]
        + [whole((total, half))] * 4
        + [whole((ROUTER_ROWS, total))] * 2,
        out_specs=pl.BlockSpec((3, 2, 1, runs, units, cols), lambda e: (0, 0, e, 0, 0, 0)),
        scratch_shapes=[
            pltpu.VMEM((experts, 2 * held, half), bf16),
            pltpu.VMEM((experts, 2 * held, half), bf16),
        ],
        compiler_params=pltpu.CompilerParams(vmem_limit_bytes=60 * 2**20),
        cost_estimate=pl.CostEstimate(
            flops=20 * 10**9, bytes_accessed=30 * 2**20, transcendentals=0
        ),
        name="expert_grads",
    )(slot_own, slot_other, in_own, in_other, dy_own, dy_other, slots_own, slots_other)


def pick_half(values, parity_flip):
    ctx = lax.axis_size("ctx")
    total, width = values.shape
    cols = width // ctx

    def kernel(in_ref, out_ref):
        parity = lax.rem(lax.axis_index("ctx") + parity_flip, 2)
        for run in range(ctx // 2):
            start = pl.multiple_of((2 * run + parity) * cols, cols)
            out_ref[:, pl.ds(run * cols, cols)] = in_ref[:, pl.ds(start, cols)]

    return pl.pallas_call(
        kernel,
        out_shape=jax.ShapeDtypeStruct((total, width // 2), values.dtype),
        in_specs=[VMEM],
        out_specs=VMEM,
        cost_estimate=pl.CostEstimate(flops=0, bytes_accessed=2**22, transcendentals=0),
        name="pick_half",
    )(values)


def roll_half(values):
    return pltpu.roll(values, values.shape[1] // 2, 1)


def allowed_keys(first_ref, last_ref, span, places):
    return (places >= first_ref[span, :]) & (places <= last_ref[span, :])


def attend(projected, scales, gains, cosine, sine_part, first, last, places, cols):
    total = projected.shape[0]
    head_dim = cosine.shape[1]
    heads = cols // head_dim
    size = math.gcd(total, 256)
    score_scale = head_dim ** (-0.5)
    f32, bf16 = jnp.float32, jnp.bfloat16

    def kernel(
        lin_ref,
        scales_ref,
        gains_ref,
        cos_ref,
        sin_ref,
        first_ref,
        last_ref,
        places_ref,
        low_ref,
        attended_ref,
        attended_low_ref,
        top_ref,
    ):
        for kind in range(3):
            for h in range(heads):
                span = pl.ds(kind * cols + h * head_dim, head_dim)
                values = lin_ref[:, span]
                if kind < 2:
                    values = values * scales_ref[:, kind : kind + 1] * gains_ref[:, span]
                    values = values * cos_ref[...] + roll_half(values) * sin_ref[...]
                low_ref[:, span] = values.astype(bf16)
        for h in range(heads):
            head = pl.ds(h * head_dim, head_dim)
            keys = low_ref[:, pl.ds(cols + h * head_dim, head_dim)]
            values = low_ref[:, pl.ds(2 * cols + h * head_dim, head_dim)]

            def step(b, carry):
                span = pl.ds(pl.multiple_of(b * size, size), size)
                scores = lax.dot_general(
                    low_ref[span, head],
                    keys,
                    (((1,), (1,)), ((), ())),
                    preferred_element_type=f32,
                )
                allowed = allowed_keys(first_ref, last_ref, span, places_ref[...])
                scores = jnp.where(allowed, scores * score_scale, MASKED)
                top = jnp.max(scores, axis=1, keepdims=True)
                weights = jnp.exp(scores - top)
                sums = jnp.sum(weights, axis=1, keepdims=True)
                probs = (weights * (1.0 / sums)).astype(bf16)
                attended = jnp.dot(probs, values, preferred_element_type=f32)
                attended_ref[span, head] = attended
                attended_low_ref[span, head] = attended.astype(bf16)
                top_ref[span, head] = jnp.broadcast_to(top + jnp.log(sums), (size, head_dim))
                return carry

            lax.fori_loop(0, total // size, step, 0)

    return pl.pallas_call(
        kernel,
        out_shape=[
            jax.ShapeDtypeStruct((total, 3 * cols), bf16),
            jax.ShapeDtypeStruct((total, cols), f32),
            jax.ShapeDtypeStruct((total, cols), bf16),
            jax.ShapeDtypeStruct((total, cols), f32),
        ],
        in_specs=[VMEM] * 8,
        out_specs=[VMEM] * 4,
        compiler_params=pltpu.CompilerParams(vmem_limit_bytes=56 * 2**20),
        cost_estimate=pl.CostEstimate(
            flops=2 * 10**9, bytes_accessed=20 * 2**20, transcendentals=2 * 10**6
        ),
        name="attend",
    )(projected, scales, gains, cosine, sine_part, first, last, places)


def attend_back(
    output_grad, low, attended, top, projected, scales, gains, cosine, sine_part, first, last, places
):
    total, cols = output_grad.shape
    head_dim = cosine.shape[1]
    heads = cols // head_dim
    size = math.gcd(total, 256)
    score_scale = head_dim ** (-0.5)
    f32, bf16 = jnp.float32, jnp.bfloat16
    contract_rows = (((0,), (0,)), ((), ()))

    def kernel(
        grad_ref,
        low_ref,
        attended_ref,
        top_ref,
        lin_ref,
        scales_ref,
        gains_ref,
        cos_ref,
        sin_ref,
        first_ref,
        last_ref,
        places_ref,
        back_ref,
        value_ref,
        gain_ref,
        sums_ref,
        query_grad,
        key_grad,
        value_grad,
    ):
        totals = [jnp.zeros((total, 1), f32) for _ in range(2)]
        for h in range(heads):
            head = pl.ds(h * head_dim, head_dim)
            keys = low_ref[:, pl.ds(cols + h * head_dim, head_dim)]
            values = low_ref[:, pl.ds(2 * cols + h * head_dim, head_dim)]
            key_grad[...] = jnp.zeros_like(key_grad)
            value_grad[...] = jnp.zeros_like(value_grad)

            def step(b, carry):
                span = pl.ds(pl.multiple_of(b * size, size), size)
                queries, grads = low_ref[span, head], grad_ref[span, head]
                scores = lax.dot_general(
                    queries, keys, (((1,), (1,)), ((), ())), preferred_element_type=f32
                )
                allowed = allowed_keys(first_ref, last_ref, span, places_ref[...])
                scores = jnp.where(allowed, scores * score_scale, MASKED)
                probs = jnp.exp(scores - top_ref[span, head][:, :1])
                prob_grad = lax.dot_general(
                    grads, values, (((1,), (1,)), ((), ())), preferred_element_type=f32
                )
                delta = jnp.sum(
                    grads.astype(f32) * attended_ref[span, head], axis=1, keepdims=True
                )
                score_grad = (probs * (prob_grad - delta)).astype(bf16)
                query_grad[span, :] = (
                    jnp.dot(score_grad, keys, preferred_element_type=f32) * score_scale
                )
                key_grad[...] += lax.dot_general(
                    score_grad, queries, contract_rows, preferred_element_type=f32
                )
                value_grad[...] += lax.dot_general(
                    probs.astype(bf16), grads, contract_rows, preferred_element_type=f32
                )
                return carry

            lax.fori_loop(0, total // size, step, 0)
            value_ref[:, head] = value_grad[...].astype(bf16)
            for kind, grad in ((0, query_grad[...]), (1, key_grad[...] * score_scale)):
                span = pl.ds(kind * cols + h * head_dim, head_dim)
                unit = lin_ref[:, span] * scales_ref[:, kind : kind + 1]
                grad = grad * cos_ref[...] - roll_half(grad) * sin_ref[...]
                gain_ref[kind, :, head] = jnp.sum(grad * unit, axis=0, keepdims=True)
                grad = grad * gains_ref[:, span]
                back_ref[kind, :, head] = grad
                totals[kind] = totals[kind] + jnp.sum(grad * unit, axis=1, keepdims=True)
        for kind in range(2):
            sums_ref[:, kind : kind + 1] = totals[kind]

    return pl.pallas_call(
        kernel,
        out_shape=[
            jax.ShapeDtypeStruct((2, total, cols), f32),
            jax.ShapeDtypeStruct((total, cols), bf16),
            jax.ShapeDtypeStruct((2, 1, cols), f32),
            jax.ShapeDtypeStruct((total, 2), f32),
        ],
        in_specs=[VMEM] * 12,
        out_specs=[VMEM] * 4,
        scratch_shapes=[pltpu.VMEM((total, head_dim), f32)] * 3,
        compiler_params=pltpu.CompilerParams(vmem_limit_bytes=56 * 2**20),
        cost_estimate=pl.CostEstimate(flops=0, bytes_accessed=2**20, transcendentals=0),
        name="attend_back",
    )(
        output_grad,
        low,
        attended,
        top,
        projected,
        scales,
        gains,
        cosine,
        sine_part,
        first,
        last,
        places,
    )


def on_device_heads(
    tokens,
    doc_lengths,
    routes,
    slot_order,
    attn_gain,
    w_qkv,
    q_gain,
    k_gain,
    w_out,
    ffn_gain,
    w_router,
    w_gate,
    w_up,
    w_down,
    cotangent,
):
    rows, width = tokens.shape[1], tokens.shape[2]
    ctx, fsdp = lax.axis_size("ctx"), lax.axis_size("fsdp")
    me = lax.axis_index("ctx")
    head_dim = width // HEADS
    cols = HEADS // ctx * head_dim
    part = width // fsdp
    total = rows * ctx
    lengths = doc_lengths[0]
    bf16, f32 = jnp.bfloat16, jnp.float32

    tokens_all = lax.all_gather(tokens[0], "ctx", axis=0, tiled=True)
    small = jnp.concatenate(
        [jnp.stack([attn_gain, q_gain, k_gain, ffn_gain]), w_router.T], axis=0
    )
    small = lax.all_gather(small, "fsdp", axis=1, tiled=True)
    gain_one, gain_query, gain_key, gain_two = (small[i].astype(f32) for i in range(4))
    router_weight = small[4:]
    own_cols = jnp.concatenate(
        [
            lax.dynamic_slice_in_dim(w_qkv, kind * width + me * cols, cols, 1)
            for kind in range(3)
        ],
        axis=1,
    )
    qkv_weight = lax.all_gather(own_cols, "fsdp", axis=0, tiled=True)
    dy_all = lax.all_gather(cotangent[0], "fsdp", axis=0, tiled=True)
    pairs_all = lax.all_gather(jnp.stack([routes[0], slot_order[0]]), "fsdp", axis=0)

    stream_pos = dealt_position(jnp.arange(total, dtype=jnp.int32), rows, ctx)
    stream_doc, stream_inner = document_info(stream_pos, lengths)
    cosine, sine_part = rope_tables(stream_inner, head_dim)
    turn_tables = (
        jnp.concatenate([cosine, cosine], axis=1),
        jnp.concatenate([-sine_part, sine_part], axis=1),
    )
    sight = (
        (stream_pos - stream_inner).reshape(total, 1),
        stream_pos.reshape(total, 1),
        stream_pos.reshape(1, total),
    )
    inputs_all = tokens_all.astype(f32)
    unit_all = inputs_all * rms_unit(inputs_all)
    normed_all = (unit_all * gain_one).astype(bf16)
    projected = dot32("td,de->te", normed_all, qkv_weight)
    squares = jnp.sum((projected * projected)[:, : 2 * cols].reshape(total, 2, cols), axis=2).T
    squares = ctx_sum(squares.reshape(-1, 128), 1).reshape(2, total)
    scales = lax.rsqrt(squares / width + EPSILON).T
    own_gains = [
        lax.dynamic_slice_in_dim(gain, me * cols, cols, 0) for gain in (gain_query, gain_key)
    ]
    own_gains = jnp.concatenate(own_gains).reshape(1, 2 * cols)
    low, attended, attended_low, tops = attend(
        projected, scales, own_gains, *turn_tables, *sight, cols
    )

    attended_part = heads_to_rows(attended_low, 2)
    mixed_part = dot32("td,de->te", attended_part, w_out).astype(bf16)
    inputs = tokens[0].astype(f32)
    row_gain_two = gain_two.reshape(1, width)
    group, mixed = reduce_then_gather(
        mixed_part,
        [tokens[0], row_gain_two],
        [jax.ShapeDtypeStruct((rows, width), f32)],
        norm_chunk,
        "mix_and_norm",
        6,
    )

    experts = w_gate.shape[0]
    top = routes.shape[2]
    capacity = rows * top // experts
    expert_ids = jnp.arange(experts, dtype=jnp.int32)
    slots = jax.vmap(slot_of_pairs)(pairs_all[:, 0], pairs_all[:, 1])
    chosen = pairs_all[:, 0][:, :, :, None] == expert_ids
    slot_by_expert = jnp.sum(jnp.where(chosen, slots[..., None] + 1, 0), axis=2) - 1
    slot_by_expert = jnp.pad(
        slot_by_expert.reshape(fsdp * rows, experts).T,
        ((0, ROUTER_ROWS - experts), (0, 0)),
        constant_values=-1,
    )
    router_rows = jnp.pad(router_weight, ((0, ROUTER_ROWS - experts), (0, 0)))
    moved_part, group_grad, g_router, slot_pack = run_experts(
        group, dy_all, slot_by_expert, router_rows, w_gate, w_up, w_down, fsdp, capacity
    )
    moved = lax.psum_scatter(moved_part, "fsdp", scatter_dimension=0, tiled=True)
    activations = (mixed + moved.astype(f32)).astype(bf16)

    packed = expert_grads(
        slot_pack,
        swap(slot_pack, "ctx", 1),
        pick_half(group, 0),
        swap(pick_half(group, 1), "ctx", 1),
        pick_half(dy_all, 0),
        swap(pick_half(dy_all, 1), "ctx", 1),
        slot_by_expert,
        swap(slot_by_expert, "ctx", 1),
        fsdp,
        capacity,
    )
    high_bits = [2**i for i in range(1, ctx.bit_length() - 1)]

    mixed_all, mixed_grad, g_ffn_gain = reduce_then_gather(
        group_grad,
        [mixed, row_gain_two, cotangent[0]],
        [jax.ShapeDtypeStruct((rows, width), f32), jax.ShapeDtypeStruct((1, width), f32)],
        norm_back_chunk,
        "norm_back",
        7,
    )
    g_ffn_gain = g_ffn_gain[0]
    output_part = dot32("te,de->td", mixed_all, w_out).astype(bf16)
    g_out = dot32("td,te->de", attended_part, mixed_all).astype(bf16)
    output_grad, packed = lax.optimization_barrier((rows_to_heads(output_part, 3), packed))

    def finish(kind):
        values = packed[kind, 1].astype(f32) + swap(packed[kind, 0], "ctx", 2).astype(f32)
        for bit in high_bits[1:]:
            left = values.shape[1] // 2
            values = halved(values.reshape((experts, left, 2) + values.shape[2:]), 2, "ctx", bit)
        return values[:, 0]

    down_parts, gate_parts, up_parts = (finish(kind) for kind in range(3))

    back, value_grad, own_g_gains, inner_sums = attend_back(
        output_grad, low, attended, tops, projected, scales, own_gains, *turn_tables, *sight
    )
    inner_sums = ctx_sum(inner_sums.T.reshape(-1, 128), 1).reshape(2, total).T / width

    def norm_back(kind):
        scale = scales[:, kind : kind + 1]
        unit = projected[:, kind * cols : (kind + 1) * cols] * scale
        return (scale * (back[kind] - unit * inner_sums[:, kind : kind + 1])).astype(bf16)

    proj_grad = jnp.concatenate([norm_back(0), norm_back(1), value_grad], axis=1)
    g_qkv = dot32("td,te->de", normed_all, proj_grad).astype(bf16)
    normed_grad_part = dot32("te,de->td", proj_grad, qkv_weight)
    g_attn_gain = jnp.sum(normed_grad_part * unit_all, axis=0)
    normed_grad = lax.psum_scatter(
        normed_grad_part.astype(bf16), "ctx", scatter_dimension=0, tiled=True
    ).astype(f32)
    scale_one = rms_unit(inputs)
    unit_one = inputs * scale_one
    pulled_one = normed_grad * gain_one
    input_grad = mixed_grad + scale_one * (
        pulled_one - unit_one * jnp.mean(unit_one * pulled_one, axis=-1, keepdims=True)
    )

    out_part = scatter_sum(g_out, 1, "ctx", [1] + high_bits)
    qkv_shard = scatter_sum(g_qkv, 0, "fsdp", [2**i for i in range(fsdp.bit_length() - 1)])
    qkv_shard = qkv_shard.astype(bf16).reshape(part, 3, cols).transpose(1, 0, 2)
    qkv_part = deal_columns(qkv_shard, 4).transpose(1, 0, 2).reshape(part, 3 * cols).astype(f32)

    def placed_cols(values):
        return lax.dynamic_update_slice_in_dim(jnp.zeros((width,), f32), values, me * cols, 0)

    sums = jnp.concatenate(
        [
            jnp.stack([g_attn_gain, placed_cols(own_g_gains[0, 0]), placed_cols(own_g_gains[1, 0]), g_ffn_gain]),
            g_router[:experts],
        ],
        axis=0,
    )
    sums = mesh_sum(jnp.pad(sums, ((0, -sums.shape[0] % 8), (0, 0))), 5)
    return (
        activations[None],
        input_grad[None],
        sums[0],
        qkv_part,
        sums[1],
        sums[2],
        out_part,
        sums[3],
        sums[4 : 4 + experts].T,
        gate_parts,
        up_parts,
        down_parts,
    )


def solution(mesh):
    in_specs = (
        P("fsdp", "ctx", None),
        P("fsdp", None),
        P("fsdp", "ctx", None),
        P("fsdp", "ctx", None),
        P("fsdp"),
        P("fsdp", None),
        P("fsdp"),
        P("fsdp"),
        P("fsdp", None),
        P("fsdp"),
        P("fsdp", None),
        P(None, None, "fsdp"),
        P(None, None, "fsdp"),
        P(None, "fsdp", None),
        P("fsdp", "ctx", None),
    )
    out_specs = (
        P("fsdp", "ctx", None),
        P("fsdp", "ctx", None),
        P("fsdp"),
        P("fsdp", "ctx"),
        P("fsdp"),
        P("fsdp"),
        P("fsdp", "ctx"),
        P("fsdp"),
        P("fsdp", None),
        P(None, "ctx", "fsdp"),
        P(None, "ctx", "fsdp"),
        P(None, "fsdp", "ctx"),
    )
    ctx, fsdp = mesh.shape["ctx"], mesh.shape["fsdp"]
    by_heads = HEADS % ctx == 0 and ctx == 8 and fsdp == 4
    body = on_device_heads if by_heads else on_device
    return jax.shard_map(
        body, mesh=mesh, in_specs=in_specs, out_specs=out_specs, check_vma=False
    )
```

```python
import math

import jax
import jax.numpy as jnp
from jax import lax
from jax.experimental import pallas as pl
from jax.experimental.pallas import tpu as pltpu
from jax.sharding import PartitionSpec as P

HEADS = 16
MESH = pl.DeviceIdType.MESH
ANY = pl.BlockSpec(memory_space=pl.ANY)
VMEM = pl.BlockSpec(memory_space=pltpu.VMEM)
DMA = pltpu.SemaphoreType.DMA

EPSILON = 1e-05
ROPE_BASE = 10000.0
MASKED = -1e30


def rms_scale(values, gain_vector):
    return (
        values
        * lax.rsqrt(jnp.mean(values * values, axis=-1, keepdims=True) + EPSILON)
        * gain_vector
    )


def rotate(values, inner_pos):
    half_dim = values.shape[-1] // 2
    freq_table = ROPE_BASE ** (-2.0 * jnp.arange(half_dim, dtype=jnp.float32) / values.shape[-1])
    angles = inner_pos.astype(jnp.float32)[:, None] * freq_table[None, :]
    cosine = jnp.cos(angles)[:, None, :]
    sine_part = jnp.sin(angles)[:, None, :]
    first_half = values[..., :half_dim]
    second_half = values[..., half_dim:]
    return jnp.concatenate(
        [
            first_half * cosine - second_half * sine_part,
            second_half * cosine + first_half * sine_part,
        ],
        axis=-1,
    )


def dealt_position(flat_index, per_device, device_count):
    device_index = flat_index // per_device
    within = flat_index % per_device
    half_rows = per_device // 2
    return jnp.where(
        within < half_rows,
        device_index * half_rows + within,
        (2 * device_count - 1 - device_index) * half_rows + within - half_rows,
    )


def document_info(positions, lengths):
    doc_ends = jnp.sum(jnp.where(jnp.arange(lengths.shape[0])[:, None] >= jnp.arange(lengths.shape[0])[None, :], lengths[None, :], 0), axis=1)
    passed = doc_ends[None, :] <= positions[:, None]
    doc_ids = jnp.sum(passed.astype(jnp.int32), axis=1)
    inner_pos = positions - jnp.sum(jnp.where(passed, lengths[None, :], 0), axis=1)
    return (doc_ids, inner_pos)


def slot_table(route_ids, order_ids, capacity, expert_count):
    pair_count = route_ids.shape[0] * route_ids.shape[1]
    expert_flat = route_ids.reshape(pair_count)
    rank_flat = order_ids.reshape(pair_count)
    earlier = (expert_flat[None, :] == expert_flat[:, None]) & (
        rank_flat[None, :] < rank_flat[:, None]
    )
    slot_index = jnp.sum(earlier.astype(jnp.int32), axis=1)
    placed = jnp.where(
        slot_index < capacity, expert_flat * capacity + slot_index, expert_count * capacity
    )
    source = (
        jnp.full((expert_count * capacity + 1,), pair_count, jnp.int32)
        .at[placed]
        .set(jnp.arange(pair_count, dtype=jnp.int32))
    )
    return (placed, source[: expert_count * capacity])


def masked_scores(query_block, key_block, query_pos, query_doc, key_pos, key_doc, score_scale):
    scores = (
        jnp.einsum("qhd,khd->hqk", query_block, key_block, preferred_element_type=jnp.float32)
        * score_scale
    )
    allowed = (query_doc[:, None] == key_doc[None, :]) & (key_pos[None, :] <= query_pos[:, None])
    return jnp.where(allowed[None], scores, MASKED)


def silu_parts(hidden_grad, slot_gate, slot_up):
    sigma = jax.nn.sigmoid(slot_gate)
    gate_grad_low = (hidden_grad * slot_up * sigma * (1.0 + slot_gate * (1.0 - sigma))).astype(
        jnp.bfloat16
    )
    up_grad_low = (hidden_grad * slot_gate * sigma).astype(jnp.bfloat16)
    return (gate_grad_low, up_grad_low)


def on_device(
    tokens,
    doc_lengths,
    routes,
    slot_order,
    attn_gain,
    w_qkv,
    q_gain,
    k_gain,
    w_out,
    ffn_gain,
    w_router,
    w_gate,
    w_up,
    w_down,
    cotangent,
):
    row_count = tokens.shape[1]
    model_width = tokens.shape[2]
    head_count = HEADS
    head_dim = model_width // head_count
    score_scale = head_dim ** (-0.5)
    ctx_count = lax.axis_size("ctx")
    ctx_index = lax.axis_index("ctx")
    total_rows = row_count * ctx_count
    lengths = doc_lengths[0]
    local_pos = dealt_position(
        ctx_index * row_count + jnp.arange(row_count, dtype=jnp.int32), row_count, ctx_count
    )
    local_doc, local_inner = document_info(local_pos, lengths)
    stream_pos = dealt_position(jnp.arange(total_rows, dtype=jnp.int32), row_count, ctx_count)
    stream_doc, stream_inner = document_info(stream_pos, lengths)
    block_rows = math.gcd(total_rows, 512)
    block_count = total_rows // block_rows
    block_ids = jnp.arange(block_count, dtype=jnp.int32)
    gain_one, qkv_weight, gain_query, gain_key, out_weight = (
        lax.all_gather(attn_gain, "fsdp", axis=0, tiled=True),
        lax.all_gather(w_qkv, "fsdp", axis=0, tiled=True),
        lax.all_gather(q_gain, "fsdp", axis=0, tiled=True),
        lax.all_gather(k_gain, "fsdp", axis=0, tiled=True),
        lax.all_gather(w_out, "fsdp", axis=0, tiled=True),
    )
    gain_two, router_weight, gate_weight, up_weight, down_weight = (
        lax.all_gather(ffn_gain, "fsdp", axis=0, tiled=True),
        lax.all_gather(w_router, "fsdp", axis=0, tiled=True),
        lax.all_gather(w_gate, "fsdp", axis=2, tiled=True),
        lax.all_gather(w_up, "fsdp", axis=2, tiled=True),
        lax.all_gather(w_down, "fsdp", axis=1, tiled=True),
    )
    inputs = tokens[0].astype(jnp.float32)
    normed_f, norm_one_pull = jax.vjp(rms_scale, inputs, gain_one.astype(jnp.float32))
    normed_low = normed_f.astype(jnp.bfloat16)
    projected = jnp.dot(normed_low, qkv_weight, preferred_element_type=jnp.float32)
    query_lin = projected[:, :model_width]
    key_lin = projected[:, model_width : 2 * model_width]
    value_low = (
        projected[:, 2 * model_width :]
        .astype(jnp.bfloat16)
        .reshape(row_count, head_count, head_dim)
    )

    def head_shape(values, gain_vector):
        return rotate(
            rms_scale(values, gain_vector).reshape(row_count, head_count, head_dim), local_inner
        )

    query_f, query_pull = jax.vjp(head_shape, query_lin, gain_query.astype(jnp.float32))
    key_f, key_pull = jax.vjp(head_shape, key_lin, gain_key.astype(jnp.float32))
    query_low = query_f.astype(jnp.bfloat16)
    key_low = key_f.astype(jnp.bfloat16)
    keys_all, values_all = (
        lax.all_gather(key_low, "ctx", axis=0, tiled=True),
        lax.all_gather(value_low, "ctx", axis=0, tiled=True),
    )

    def key_slice(block_index):
        first_row = block_index * block_rows
        return (
            lax.dynamic_slice_in_dim(keys_all, first_row, block_rows, 0),
            lax.dynamic_slice_in_dim(values_all, first_row, block_rows, 0),
            lax.dynamic_slice_in_dim(stream_pos, first_row, block_rows, 0),
            lax.dynamic_slice_in_dim(stream_doc, first_row, block_rows, 0),
        )

    def stats_step(carry, block_index):
        running_top, running_total = carry
        key_block, value_block, key_pos, key_doc = key_slice(block_index)
        scores = masked_scores(
            query_low, key_block, local_pos, local_doc, key_pos, key_doc, score_scale
        )
        new_top = jnp.maximum(running_top, jnp.max(scores, axis=-1))
        running_total = running_total * jnp.exp(running_top - new_top) + jnp.sum(
            jnp.exp(scores - new_top[..., None]), axis=-1
        )
        return ((new_top, running_total), None)

    start_stats = (
        jnp.full((head_count, row_count), MASKED, jnp.float32),
        jnp.zeros((head_count, row_count), jnp.float32),
    )
    (score_top, score_total), _ = lax.scan(stats_step, start_stats, block_ids)
    log_total = score_top + jnp.log(score_total)

    def output_step(accum, block_index):
        key_block, value_block, key_pos, key_doc = key_slice(block_index)
        scores = masked_scores(
            query_low, key_block, local_pos, local_doc, key_pos, key_doc, score_scale
        )
        prob_block = jnp.exp(scores - log_total[..., None]).astype(jnp.bfloat16)
        return (
            accum
            + jnp.einsum(
                "hqk,khd->qhd", prob_block, value_block, preferred_element_type=jnp.float32
            ),
            None,
        )

    attended_f, _ = lax.scan(
        output_step, jnp.zeros((row_count, head_count, head_dim), jnp.float32), block_ids
    )
    attended_low = attended_f.reshape(row_count, model_width).astype(jnp.bfloat16)
    mixed = inputs + jnp.dot(attended_low, out_weight, preferred_element_type=jnp.float32)
    normed_two_f, norm_two_pull = jax.vjp(rms_scale, mixed, gain_two.astype(jnp.float32))
    normed_two = normed_two_f.astype(jnp.bfloat16)
    expert_count = gate_weight.shape[0]
    route_ids = routes[0]
    top_count = route_ids.shape[1]
    pair_count = row_count * top_count
    capacity = pair_count // expert_count
    logits = jnp.dot(normed_two, router_weight, preferred_element_type=jnp.float32)
    router_probs = jax.nn.softmax(logits, axis=-1)
    chosen = (
        route_ids[:, :, None] == jnp.arange(expert_count, dtype=jnp.int32)[None, None, :]
    ).astype(jnp.float32)
    gate_values = jnp.sum(chosen * router_probs[:, None, :], axis=-1)
    placed, source = slot_table(route_ids, slot_order[0], capacity, expert_count)
    padded_in = jnp.concatenate([normed_two, jnp.zeros((1, model_width), jnp.bfloat16)], axis=0)
    expert_in = padded_in[source // top_count].reshape(expert_count, capacity, model_width)
    gate_pre = jnp.einsum(
        "ecd,edh->ech", expert_in, gate_weight, preferred_element_type=jnp.float32
    )
    up_pre = jnp.einsum("ecd,edh->ech", expert_in, up_weight, preferred_element_type=jnp.float32)
    hidden_low = (jax.nn.silu(gate_pre) * up_pre).astype(jnp.bfloat16)
    expert_out = jnp.einsum(
        "ech,ehd->ecd", hidden_low, down_weight, preferred_element_type=jnp.float32
    )
    out_padded = jnp.concatenate(
        [
            expert_out.reshape(expert_count * capacity, model_width),
            jnp.zeros((1, model_width), jnp.float32),
        ],
        axis=0,
    )
    per_pair = out_padded[placed].reshape(row_count, top_count, model_width)
    layer_out = mixed + jnp.sum(gate_values[:, :, None] * per_pair, axis=1)
    out_grad = cotangent[0].astype(jnp.float32)
    gate_grad = jnp.sum(out_grad[:, None, :] * per_pair, axis=-1)
    pair_grad = (gate_values[:, :, None] * out_grad[:, None, :]).reshape(pair_count, model_width)
    pair_padded = jnp.concatenate([pair_grad, jnp.zeros((1, model_width), jnp.float32)], axis=0)
    slot_grad = (
        pair_padded[source].reshape(expert_count, capacity, model_width).astype(jnp.bfloat16)
    )

    def expert_step(carry, pieces):
        slot_in, slot_hidden, slot_dy, slot_gate, slot_up, gate_matrix, up_matrix, down_matrix = (
            pieces
        )
        hidden_grad = jnp.einsum(
            "cd,hd->ch", slot_dy, down_matrix, preferred_element_type=jnp.float32
        )
        gate_grad_low, up_grad_low = silu_parts(hidden_grad, slot_gate, slot_up)
        in_grad = jnp.einsum(
            "ch,dh->cd", gate_grad_low, gate_matrix, preferred_element_type=jnp.float32
        ) + jnp.einsum("ch,dh->cd", up_grad_low, up_matrix, preferred_element_type=jnp.float32)
        gate_term = jnp.einsum(
            "cd,ch->dh", slot_in, gate_grad_low, preferred_element_type=jnp.float32
        )
        up_term = jnp.einsum("cd,ch->dh", slot_in, up_grad_low, preferred_element_type=jnp.float32)
        down_term = jnp.einsum(
            "ch,cd->hd", slot_hidden, slot_dy, preferred_element_type=jnp.float32
        )
        gate_shard, up_shard, down_shard = (
            lax.psum_scatter(
                gate_term.astype(jnp.bfloat16), "fsdp", scatter_dimension=1, tiled=True
            ).astype(jnp.float32),
            lax.psum_scatter(
                up_term.astype(jnp.bfloat16), "fsdp", scatter_dimension=1, tiled=True
            ).astype(jnp.float32),
            lax.psum_scatter(
                down_term.astype(jnp.bfloat16), "fsdp", scatter_dimension=0, tiled=True
            ).astype(jnp.float32),
        )
        gate_part, up_part, down_part = (
            lax.psum_scatter(
                gate_shard.astype(jnp.bfloat16), "ctx", scatter_dimension=0, tiled=True
            ).astype(jnp.float32),
            lax.psum_scatter(
                up_shard.astype(jnp.bfloat16), "ctx", scatter_dimension=0, tiled=True
            ).astype(jnp.float32),
            lax.psum_scatter(
                down_shard.astype(jnp.bfloat16), "ctx", scatter_dimension=1, tiled=True
            ).astype(jnp.float32),
        )
        return (carry, (in_grad, gate_part, up_part, down_part))

    _, (expert_in_grad, gate_parts, up_parts, down_parts) = lax.scan(
        expert_step,
        None,
        (expert_in, hidden_low, slot_grad, gate_pre, up_pre, gate_weight, up_weight, down_weight),
    )
    in_padded = jnp.concatenate(
        [
            expert_in_grad.reshape(expert_count * capacity, model_width),
            jnp.zeros((1, model_width), jnp.float32),
        ],
        axis=0,
    )
    normed_two_grad = jnp.sum(in_padded[placed].reshape(row_count, top_count, model_width), axis=1)
    prob_grad_router = jnp.sum(chosen * gate_grad[:, :, None], axis=1)
    logit_grad = (
        router_probs
        * (prob_grad_router - jnp.sum(router_probs * prob_grad_router, axis=-1, keepdims=True))
    ).astype(jnp.bfloat16)
    normed_two_grad = normed_two_grad + jnp.einsum(
        "te,de->td", logit_grad, router_weight, preferred_element_type=jnp.float32
    )
    router_grad = jnp.einsum(
        "td,te->de", normed_two, logit_grad, preferred_element_type=jnp.float32
    )
    mixed_norm_grad, gain_two_grad = norm_two_pull(normed_two_grad)
    mixed_grad = out_grad + mixed_norm_grad
    mixed_low = mixed_grad.astype(jnp.bfloat16)
    out_weight_grad = jnp.einsum(
        "td,te->de", attended_low, mixed_low, preferred_element_type=jnp.float32
    )
    output_grad = (
        jnp.einsum("te,de->td", mixed_low, out_weight, preferred_element_type=jnp.float32)
        .astype(jnp.bfloat16)
        .reshape(row_count, head_count, head_dim)
    )
    row_delta = jnp.sum(output_grad.astype(jnp.float32) * attended_f, axis=-1).T

    def query_grad_step(accum, block_index):
        key_block, value_block, key_pos, key_doc = key_slice(block_index)
        scores = masked_scores(
            query_low, key_block, local_pos, local_doc, key_pos, key_doc, score_scale
        )
        prob_block = jnp.exp(scores - log_total[..., None])
        prob_grad = jnp.einsum(
            "qhd,khd->hqk", output_grad, value_block, preferred_element_type=jnp.float32
        )
        score_grad = (prob_block * (prob_grad - row_delta[..., None])).astype(jnp.bfloat16)
        return (
            accum
            + jnp.einsum("hqk,khd->qhd", score_grad, key_block, preferred_element_type=jnp.float32)
            * score_scale,
            None,
        )

    query_grad, _ = lax.scan(
        query_grad_step, jnp.zeros((row_count, head_count, head_dim), jnp.float32), block_ids
    )
    inner_rows = math.gcd(row_count * lax.axis_size("ctx"), 512)

    def piece_step(carry, piece_index):
        first_row = piece_index * inner_rows
        key_block = lax.dynamic_slice_in_dim(keys_all, first_row, inner_rows, 0)
        value_block = lax.dynamic_slice_in_dim(values_all, first_row, inner_rows, 0)
        key_pos = lax.dynamic_slice_in_dim(stream_pos, first_row, inner_rows, 0)
        key_doc = lax.dynamic_slice_in_dim(stream_doc, first_row, inner_rows, 0)
        scores = masked_scores(
            query_low, key_block, local_pos, local_doc, key_pos, key_doc, score_scale
        )
        prob_block = jnp.exp(scores - log_total[..., None])
        prob_grad = jnp.einsum(
            "qhd,khd->hqk", output_grad, value_block, preferred_element_type=jnp.float32
        )
        score_grad = (prob_block * (prob_grad - row_delta[..., None])).astype(jnp.bfloat16)
        value_part = jnp.einsum(
            "hqk,qhd->khd",
            prob_block.astype(jnp.bfloat16),
            output_grad,
            preferred_element_type=jnp.float32,
        )
        key_part = (
            jnp.einsum("hqk,qhd->khd", score_grad, query_low, preferred_element_type=jnp.float32)
            * score_scale
        )
        return (
            carry,
            jnp.concatenate(
                [
                    key_part.reshape(inner_rows, model_width),
                    value_part.reshape(inner_rows, model_width),
                ],
                axis=1,
            ),
        )

    _, stacked = lax.scan(
        piece_step,
        None,
        jnp.arange(row_count * lax.axis_size("ctx") // inner_rows, dtype=jnp.int32),
    )
    key_value_grad = lax.psum_scatter(
        stacked.reshape(row_count * lax.axis_size("ctx"), 2 * model_width).astype(jnp.bfloat16),
        "ctx",
        scatter_dimension=0,
        tiled=True,
    ).astype(jnp.float32)
    key_grad = key_value_grad[:, :model_width].reshape(row_count, head_count, head_dim)
    value_grad = key_value_grad[:, model_width:]
    query_lin_grad, gain_query_grad = query_pull(query_grad)
    key_lin_grad, gain_key_grad = key_pull(key_grad)
    proj_grad = jnp.concatenate(
        [
            query_lin_grad.astype(jnp.bfloat16),
            key_lin_grad.astype(jnp.bfloat16),
            value_grad.astype(jnp.bfloat16),
        ],
        axis=1,
    )
    qkv_weight_grad = jnp.einsum(
        "td,te->de", normed_low, proj_grad, preferred_element_type=jnp.float32
    )
    normed_grad = jnp.einsum("te,de->td", proj_grad, qkv_weight, preferred_element_type=jnp.float32)
    input_norm_grad, gain_one_grad = norm_one_pull(normed_grad)
    input_grad = mixed_grad + input_norm_grad
    qkv_shard, out_shard = (
        lax.psum_scatter(
            qkv_weight_grad.astype(jnp.bfloat16), "fsdp", scatter_dimension=0, tiled=True
        ).astype(jnp.float32),
        lax.psum_scatter(
            out_weight_grad.astype(jnp.bfloat16), "fsdp", scatter_dimension=0, tiled=True
        ).astype(jnp.float32),
    )
    qkv_part, out_part = (
        lax.psum_scatter(
            qkv_shard.astype(jnp.bfloat16), "ctx", scatter_dimension=1, tiled=True
        ).astype(jnp.float32),
        lax.psum_scatter(
            out_shard.astype(jnp.bfloat16), "ctx", scatter_dimension=1, tiled=True
        ).astype(jnp.float32),
    )
    gain_one_sum, gain_query_sum, gain_key_sum, gain_two_sum, router_sum = lax.psum(
        (gain_one_grad, gain_query_grad, gain_key_grad, gain_two_grad, router_grad), ("ctx", "fsdp")
    )
    shard_rows = model_width // lax.axis_size("fsdp")
    shard_start = lax.axis_index("fsdp") * shard_rows

    def own_rows(full_array):
        return lax.dynamic_slice_in_dim(full_array, shard_start, shard_rows, 0)

    return (
        layer_out.astype(jnp.bfloat16)[None],
        input_grad[None],
        own_rows(gain_one_sum),
        qkv_part,
        own_rows(gain_query_sum),
        own_rows(gain_key_sum),
        out_part,
        own_rows(gain_two_sum),
        own_rows(router_sum),
        gate_parts,
        up_parts,
        down_parts,
    )


def rms_unit(values):
    return lax.rsqrt(jnp.mean(values * values, axis=-1, keepdims=True) + EPSILON)


def rope_tables(inner_pos, head_dim):
    half_dim = head_dim // 2
    freq_table = ROPE_BASE ** (-2.0 * jnp.arange(half_dim, dtype=jnp.float32) / head_dim)
    angles = inner_pos.astype(jnp.float32)[:, None] * freq_table[None, :]
    return (jnp.cos(angles), jnp.sin(angles))


def slot_of_pairs(route_ids, order_ids):
    pair_count = route_ids.shape[0] * route_ids.shape[1]
    expert_flat = route_ids.reshape(pair_count)
    rank_flat = order_ids.reshape(pair_count)
    earlier = (expert_flat[None, :] == expert_flat[:, None]) & (
        rank_flat[None, :] < rank_flat[:, None]
    )
    return jnp.sum(earlier.astype(jnp.int32), axis=1).reshape(route_ids.shape)


def dot32(spec, left, right):
    return jnp.einsum(spec, left, right, preferred_element_type=jnp.float32)


def greet(peers):
    barrier = pltpu.get_barrier_semaphore()
    for peer in peers:
        pl.semaphore_signal(barrier, inc=1, device_id=peer, device_id_type=MESH)
    pl.semaphore_wait(barrier, len(peers))


def send(source, target, send_sem, recv_sem, peer):
    copy = pltpu.make_async_remote_copy(
        source, target, send_sem, recv_sem, device_id=peer, device_id_type=MESH
    )
    copy.start()
    return copy


def comm_call(kernel, name, collective_id, out_shape, in_specs, out_specs, scratch_shapes, cost):
    return pl.pallas_call(
        kernel,
        out_shape=out_shape,
        in_specs=in_specs,
        out_specs=out_specs,
        scratch_shapes=scratch_shapes,
        compiler_params=pltpu.CompilerParams(
            collective_id=collective_id, has_side_effects=True, vmem_limit_bytes=48 * 2**20
        ),
        cost_estimate=pl.CostEstimate(flops=0, bytes_accessed=cost, transcendentals=0),
        name=name,
    )


def ctx_sum(values, collective_id):
    ctx = lax.axis_size("ctx")

    def kernel(own_ref, out_ref, held, send_sems, recv_sems):
        me, mine = lax.axis_index("ctx"), lax.axis_index("fsdp")
        peers = [(lax.rem(me + step, ctx), mine) for step in range(1, ctx)]
        greet(peers)
        copies = [
            send(own_ref, held.at[i], send_sems.at[i], recv_sems.at[i], peer)
            for i, peer in enumerate(peers)
        ]
        total = own_ref[...]
        for i, copy in enumerate(copies):
            copy.wait_recv()
            total = total + held[i]
        out_ref[...] = total
        for copy in copies:
            copy.wait_send()

    return comm_call(
        kernel,
        "ctx_sum",
        collective_id,
        jax.ShapeDtypeStruct(values.shape, values.dtype),
        [VMEM],
        VMEM,
        [
            pltpu.VMEM((ctx - 1,) + values.shape, values.dtype),
            DMA((ctx - 1,)),
            DMA((ctx - 1,)),
        ],
        20 * 2**20,
    )(values)


def heads_to_rows(values, collective_id):
    ctx, fsdp = lax.axis_size("ctx"), lax.axis_size("fsdp")
    rows, cols = values.shape[0] // ctx, values.shape[1]
    share = ctx // fsdp

    def kernel(own_ref, out_ref, send_sems, recv_sems):
        me, mine = lax.axis_index("ctx"), lax.axis_index("fsdp")
        keeper, place = me // share, lax.rem(me, share)
        own_keeper = (keeper == mine).astype(jnp.int32)
        barrier = pltpu.get_barrier_semaphore()
        for step in range(share * fsdp):
            source, stream = mine * share + step // fsdp, step % fsdp

            @pl.when(jnp.logical_or(source != me, stream != mine))
            def _():
                pl.semaphore_signal(
                    barrier, inc=1, device_id=(source, stream), device_id_type=MESH
                )

        pl.semaphore_wait(barrier, ctx - own_keeper)

        def block(index):
            return own_ref.at[pl.ds(pl.multiple_of(index * rows, rows), rows), :]

        def landing(stream, position):
            return out_ref.at[
                pl.ds(pl.multiple_of(stream * rows, rows), rows),
                pl.ds(pl.multiple_of(position * cols, cols), cols),
            ]

        slot = place * fsdp + mine

        def copy_to(step):
            other = lax.rem(me + step, ctx)
            return pltpu.make_async_remote_copy(
                block(other),
                landing(mine, place),
                send_sems.at[step],
                recv_sems.at[slot],
                device_id=(other, keeper),
                device_id_type=MESH,
            )

        kept = pltpu.make_async_copy(block(me), landing(mine, place), send_sems.at[0])
        for step in range(1, ctx):
            copy_to(step).start()

        @pl.when(own_keeper == 0)
        def _():
            copy_to(0).start()

        @pl.when(own_keeper == 1)
        def _():
            kept.start()
            kept.wait()

        for step in range(share * fsdp):

            @pl.when(
                jnp.logical_or(mine * share + step // fsdp != me, step % fsdp != mine)
            )
            def _():
                pltpu.make_async_copy(
                    block(0), landing(step % fsdp, step // fsdp), recv_sems.at[step]
                ).wait()

        for step in range(1, ctx):
            copy_to(step).wait_send()

        @pl.when(own_keeper == 0)
        def _():
            copy_to(0).wait_send()

    return comm_call(
        kernel,
        "heads_to_rows",
        collective_id,
        jax.ShapeDtypeStruct((fsdp * rows, share * cols), values.dtype),
        [ANY],
        ANY,
        [DMA((ctx,)), DMA((share * fsdp,))],
        40 * 2**20,
    )(values)


def rows_to_heads(values, collective_id):
    ctx, fsdp = lax.axis_size("ctx"), lax.axis_size("fsdp")
    share = ctx // fsdp
    rows, cols = values.shape[0] // fsdp, values.shape[1] // share

    def kernel(own_ref, out_ref, send_sems, recv_sems):
        me, mine = lax.axis_index("ctx"), lax.axis_index("fsdp")
        keeper, place = me // share, lax.rem(me, share)
        own_keeper = (keeper == mine).astype(jnp.int32)
        barrier = pltpu.get_barrier_semaphore()
        for step in range(ctx):
            source = lax.rem(me + step, ctx)

            @pl.when(jnp.logical_or(source != me, keeper != mine))
            def _():
                pl.semaphore_signal(
                    barrier, inc=1, device_id=(source, keeper), device_id_type=MESH
                )

        pl.semaphore_wait(barrier, share * fsdp - own_keeper)

        def block(stream, position):
            return own_ref.at[
                pl.ds(pl.multiple_of(stream * rows, rows), rows),
                pl.ds(pl.multiple_of(position * cols, cols), cols),
            ]

        def landing(index):
            return out_ref.at[pl.ds(pl.multiple_of(index * rows, rows), rows), :]

        def copy_to(step):
            return pltpu.make_async_remote_copy(
                block(step % fsdp, step // fsdp),
                landing(me),
                send_sems.at[step],
                recv_sems.at[me],
                device_id=(mine * share + step // fsdp, step % fsdp),
                device_id_type=MESH,
            )

        def is_far(step):
            return jnp.logical_or(mine * share + step // fsdp != me, step % fsdp != mine)

        for step in range(share * fsdp):
            pl.when(is_far(step))(copy_to(step).start)

        @pl.when(own_keeper == 1)
        def _():
            kept = pltpu.make_async_copy(block(mine, place), landing(me), recv_sems.at[me])
            kept.start()
            kept.wait()

        for step in range(ctx):
            source = lax.rem(me + step, ctx)

            @pl.when(jnp.logical_or(source != me, keeper != mine))
            def _():
                pltpu.make_async_copy(block(0, 0), landing(source), recv_sems.at[source]).wait()

        for step in range(share * fsdp):
            pl.when(is_far(step))(copy_to(step).wait_send)

    return comm_call(
        kernel,
        "rows_to_heads",
        collective_id,
        jax.ShapeDtypeStruct((ctx * rows, cols), values.dtype),
        [ANY],
        ANY,
        [DMA((share * fsdp,)), DMA((ctx,))],
        40 * 2**20,
    )(values)


def swap(values, axis, bit):
    return lax.ppermute(values, axis, [(i, i ^ bit) for i in range(lax.axis_size(axis))])


def reduce_then_gather(partial, extras, out_shapes, chunk_math, name, collective_id):
    fsdp = lax.axis_size("fsdp")
    rows, width = partial.shape[0] // fsdp, partial.shape[1]
    chunks = 4
    size = rows // chunks
    count = len(extras)

    def kernel(*refs):
        part_ref, extra_refs = refs[0], refs[1 : 1 + count]
        all_ref, out_refs = refs[1 + count], refs[2 + count : 2 + count + len(out_shapes)]
        near_own, near_far, far_sum, far_own, sems = refs[2 + count + len(out_shapes) :]
        me, mine = lax.axis_index("ctx"), lax.axis_index("fsdp")
        flip = 1 - 2 * lax.rem(mine, 2)
        core = mine + flip
        chip = lax.rem(mine + 2, fsdp)
        diagonal = lax.rem(core + 2, fsdp)
        greet([(me, core), (me, chip)])

        def span(block, i):
            return pl.ds(pl.multiple_of(block * rows + i * size, size), size)

        def sem(kind, i):
            return sems.at[2 * kind, i], sems.at[2 * kind + 1, i]

        copies = []
        from_core_far, from_core_own, from_chip = [], [], []
        for i in range(chunks):
            copy = send(
                part_ref.at[span(diagonal, i), :], near_far.at[i], *sem(0, i), (me, core)
            )
            from_core_far.append(copy)
        for i in range(chunks):
            copy = send(part_ref.at[span(core, i), :], near_own.at[i], *sem(1, i), (me, core))
            from_core_own.append(copy)
        for i in range(chunks):
            from_core_far[i].wait_recv()
            both = part_ref[span(chip, i), :].astype(jnp.float32) + near_far[i].astype(jnp.float32)
            far_sum[i] = both.astype(jnp.bfloat16)
            from_chip.append(send(far_sum.at[i], far_own.at[i], *sem(2, i), (me, chip)))
        to_chip = []
        for i in range(chunks):
            from_core_own[i].wait_recv()
            from_chip[i].wait_recv()
            total = (
                part_ref[span(mine, i), :].astype(jnp.float32)
                + near_own[i].astype(jnp.float32)
                + far_own[i].astype(jnp.float32)
            )
            all_ref[span(mine, i), :] = chunk_math(
                i, pl.ds(i * size, size), total, extra_refs, out_refs
            ).astype(jnp.bfloat16)
            own = all_ref.at[span(mine, i), :]
            to_chip.append(send(own, own, *sem(3, i), (me, chip)))
            copies.append(send(own, own, *sem(4, i), (me, core)))
        for i in range(chunks):
            to_chip[i].wait_recv()
            other = all_ref.at[span(chip, i), :]
            copies.append(send(other, other, *sem(5, i), (me, core)))
        for copy in copies:
            copy.wait_recv()
        for copy in from_core_far + from_core_own + from_chip + to_chip + copies:
            copy.wait_send()

    return comm_call(
        kernel,
        name,
        collective_id,
        [jax.ShapeDtypeStruct(partial.shape, jnp.bfloat16)] + out_shapes,
        [VMEM] * (1 + count),
        [VMEM] * (1 + len(out_shapes)),
        [
            pltpu.VMEM((chunks, size, width), jnp.bfloat16),
            pltpu.VMEM((chunks, size, width), jnp.bfloat16),
            pltpu.VMEM((chunks, size, width), jnp.bfloat16),
            pltpu.VMEM((chunks, size, width), jnp.bfloat16),
            DMA((12, chunks)),
        ],
        100 * 2**20,
    )(partial, *extras)


def norm_chunk(index, span, total, extra_refs, out_refs):
    tokens_ref, gain_ref = extra_refs
    mixed = tokens_ref[span, :].astype(jnp.float32) + total
    out_refs[0][span, :] = mixed
    return mixed * rms_unit(mixed) * gain_ref[...]


def norm_back_chunk(index, span, total, extra_refs, out_refs):
    mixed_ref, gain_ref, dy_ref = extra_refs
    mixed = mixed_ref[span, :]
    scale = rms_unit(mixed)
    unit = mixed * scale
    pulled = total * gain_ref[...]
    grad = dy_ref[span, :].astype(jnp.float32) + scale * (
        pulled - unit * jnp.mean(unit * pulled, axis=-1, keepdims=True)
    )
    out_refs[0][span, :] = grad
    gain_grad = jnp.sum(total * unit, axis=0, keepdims=True)
    if index == 0:
        out_refs[1][...] = gain_grad
    else:
        out_refs[1][...] += gain_grad
    return grad


ROUTER_ROWS = 16


def one_hot(slots, capacity):
    return lax.broadcasted_iota(jnp.int32, (capacity, slots.shape[1]), 0) == slots


def run_experts(group, dy_all, slots, router, w_gate, w_up, w_down, blocks, capacity):
    experts, width, units = w_gate.shape
    total = group.shape[0]
    rows = total // blocks
    held = blocks * capacity
    f32, bf16 = jnp.float32, jnp.bfloat16

    def kernel(
        group_ref,
        dy_ref,
        slots_ref,
        router_ref,
        gate_ref,
        up_ref,
        down_ref,
        moved_ref,
        grad_ref,
        g_router_ref,
        slot_ref,
        disp,
        ins,
        dys,
        probs,
        prob_grad,
    ):
        expert = pl.program_id(0)

        def block_rows(b):
            return pl.ds(b * rows, rows)

        @pl.when(expert == 0)
        def _():
            logits = lax.dot_general(
                router_ref[...],
                group_ref[...],
                (((1,), (1,)), ((), ())),
                preferred_element_type=f32,
            )
            real = lax.broadcasted_iota(jnp.int32, logits.shape, 0) < experts
            logits = jnp.where(real, logits, MASKED)
            weights = jnp.exp(logits - jnp.max(logits, axis=0, keepdims=True))
            probs[...] = weights / jnp.sum(weights, axis=0, keepdims=True)
            prob_grad[...] = jnp.zeros_like(prob_grad)
            for b in range(blocks):
                for e in range(experts):
                    disp[b, pl.ds(e * capacity, capacity), :] = (
                        one_hot(slots_ref[pl.ds(e, 1), block_rows(b)], capacity)
                        .astype(f32)
                        .astype(bf16)
                    )
                for source, target in ((group_ref, ins), (dy_ref, dys)):
                    picked = jnp.dot(
                        disp[b], source[block_rows(b), :], preferred_element_type=f32
                    ).astype(bf16)
                    for e in range(experts):
                        target[e, pl.ds(b * capacity, capacity), :] = picked[
                            e * capacity : (e + 1) * capacity
                        ]

        expert_in, slot_dy = ins[expert], dys[expert]
        gate_matrix, up_matrix, down_matrix = gate_ref[0], up_ref[0], down_ref[0]
        gate_pre = jnp.dot(expert_in, gate_matrix, preferred_element_type=f32)
        up_pre = jnp.dot(expert_in, up_matrix, preferred_element_type=f32)
        raw_grad = lax.dot_general(
            slot_dy, down_matrix, (((1,), (1,)), ((), ())), preferred_element_type=f32
        )
        own_probs = probs[pl.ds(expert, 1), :]
        own_slots = slots_ref[pl.ds(expert, 1), :]
        hots = [
            one_hot(own_slots[:, b * rows : (b + 1) * rows], capacity) for b in range(blocks)
        ]
        value = jnp.concatenate(
            [
                jnp.sum(
                    jnp.where(hots[b], own_probs[:, b * rows : (b + 1) * rows], 0.0),
                    axis=1,
                    keepdims=True,
                )
                for b in range(blocks)
            ],
            axis=0,
        )
        sigma = 1.0 / (1.0 + jnp.exp(-gate_pre))
        silu = gate_pre * sigma
        hidden = (silu * up_pre).astype(bf16)
        hidden_f = hidden.astype(f32)
        value_grad = jnp.sum(hidden_f * raw_grad, axis=1, keepdims=True)
        hidden_grad = raw_grad * value
        gate_low = (hidden_grad * up_pre * sigma * (1.0 + gate_pre * (1.0 - sigma))).astype(bf16)
        up_low = (hidden_grad * silu).astype(bf16)
        scaled = (hidden_f * value).astype(bf16)
        slot_ref[0, 0] = scaled
        slot_ref[1, 0] = gate_low
        slot_ref[2, 0] = up_low
        for b in range(blocks):
            prob_grad[expert, :, block_rows(b)] = jnp.sum(
                jnp.where(hots[b], value_grad[b * capacity : (b + 1) * capacity], 0.0),
                axis=0,
                keepdims=True,
            )
        dys[expert] = jnp.dot(scaled, down_matrix, preferred_element_type=f32).astype(bf16)
        ins[expert] = (
            lax.dot_general(
                gate_low, gate_matrix, (((1,), (1,)), ((), ())), preferred_element_type=f32
            )
            + lax.dot_general(
                up_low, up_matrix, (((1,), (1,)), ((), ())), preferred_element_type=f32
            )
        ).astype(bf16)

        @pl.when(expert == experts - 1)
        def _():
            grads = jnp.concatenate([prob_grad[e] for e in range(ROUTER_ROWS)], axis=0)
            weights = probs[...]
            logit_grad = (
                weights * (grads - jnp.sum(weights * grads, axis=0, keepdims=True))
            ).astype(bf16)
            g_router_ref[...] = jnp.dot(logit_grad, group_ref[...], preferred_element_type=f32)
            for b in range(blocks):
                for source, target in ((dys, moved_ref), (ins, grad_ref)):
                    gathered = jnp.concatenate(
                        [source[e, pl.ds(b * capacity, capacity), :] for e in range(experts)],
                        axis=0,
                    )
                    back = lax.dot_general(
                        disp[b], gathered, (((0,), (0,)), ((), ())), preferred_element_type=f32
                    )
                    if target is grad_ref:
                        back = back + lax.dot_general(
                            logit_grad[:, b * rows : (b + 1) * rows],
                            router_ref[...],
                            (((0,), (0,)), ((), ())),
                            preferred_element_type=f32,
                        )
                    target[block_rows(b), :] = back.astype(bf16)

    def whole(shape):
        return pl.BlockSpec(shape, lambda e: (0,) * len(shape))

    def by_expert(shape):
        return pl.BlockSpec((1,) + shape, lambda e: (e, 0, 0))

    return pl.pallas_call(
        kernel,
        grid=(experts,),
        out_shape=[
            jax.ShapeDtypeStruct((total, width), bf16),
            jax.ShapeDtypeStruct((total, width), bf16),
            jax.ShapeDtypeStruct((ROUTER_ROWS, width), f32),
            jax.ShapeDtypeStruct((3, experts, held, units), bf16),
        ],
        in_specs=[
            whole((total, width)),
            whole((total, width)),
            whole((ROUTER_ROWS, total)),
            whole((ROUTER_ROWS, width)),
            by_expert((width, units)),
            by_expert((width, units)),
            by_expert((units, width)),
        ],
        out_specs=[
            whole((total, width)),
            whole((total, width)),
            whole((ROUTER_ROWS, width)),
            pl.BlockSpec((3, 1, held, units), lambda e: (0, e, 0, 0)),
        ],
        scratch_shapes=[
            pltpu.VMEM((blocks, experts * capacity, rows), bf16),
            pltpu.VMEM((experts, held, width), bf16),
            pltpu.VMEM((experts, held, width), bf16),
            pltpu.VMEM((ROUTER_ROWS, total), f32),
            pltpu.VMEM((ROUTER_ROWS, 1, total), f32),
        ],
        compiler_params=pltpu.CompilerParams(vmem_limit_bytes=60 * 2**20),
        cost_estimate=pl.CostEstimate(
            flops=30 * 10**9, bytes_accessed=30 * 2**20, transcendentals=10**6
        ),
        name="run_experts",
    )(group, dy_all, slots, router, w_gate, w_up, w_down)


def expert_grads(slot_own, slot_other, in_own, in_other, dy_own, dy_other, slots_own, slots_other, blocks, capacity):
    _, experts, held, units = slot_own.shape
    total, half = in_own.shape
    rows = total // blocks
    ctx = lax.axis_size("ctx")
    runs = ctx // 4
    cols = half // (2 * runs)
    f32, bf16 = jnp.float32, jnp.bfloat16

    def kernel(
        own_ref,
        other_ref,
        in_own_ref,
        in_other_ref,
        dy_own_ref,
        dy_other_ref,
        slots_own_ref,
        slots_other_ref,
        out_ref,
        ins,
        dys,
    ):
        expert = pl.program_id(0)

        @pl.when(expert == 0)
        def _():
            for side, slots_ref, in_ref, dy_ref in (
                (0, slots_own_ref, in_own_ref, dy_own_ref),
                (1, slots_other_ref, in_other_ref, dy_other_ref),
            ):
                for b in range(blocks):
                    span = pl.ds(b * rows, rows)
                    disp = jnp.concatenate(
                        [
                            one_hot(slots_ref[pl.ds(e, 1), span], capacity).astype(f32)
                            for e in range(experts)
                        ],
                        axis=0,
                    ).astype(bf16)
                    for source, target in ((in_ref, ins), (dy_ref, dys)):
                        picked = jnp.dot(
                            disp, source[span, :], preferred_element_type=f32
                        ).astype(bf16)
                        for e in range(experts):
                            target[e, pl.ds(side * held + b * capacity, capacity), :] = picked[
                                e * capacity : (e + 1) * capacity
                            ]

        keep_low = (lax.axis_index("ctx") // 2) % 2
        stacked = [jnp.concatenate([own_ref[m, 0], other_ref[m, 0]], axis=0) for m in range(3)]
        for low in range(2):
            kept = jnp.where(keep_low == low, 1, 0)
            for run in range(runs):
                span = pl.ds((run * 2 + low) * cols, cols)
                in_part, dy_part = ins[expert, :, span], dys[expert, :, span]
                contract = (((0,), (0,)), ((), ()))
                for m, (left, right) in enumerate(
                    ((stacked[0], dy_part), (in_part, stacked[1]), (in_part, stacked[2]))
                ):
                    out_ref[m, pl.ds(kept, 1), 0, run] = lax.dot_general(
                        left, right, contract, preferred_element_type=f32
                    ).astype(bf16)[None]

    def whole(shape):
        return pl.BlockSpec(shape, lambda e: (0,) * len(shape))

    slot_spec = pl.BlockSpec((3, 1, held, units), lambda e: (0, e, 0, 0))
    return pl.pallas_call(
        kernel,
        grid=(experts,),
        out_shape=jax.ShapeDtypeStruct((3, 2, experts, runs, units, cols), bf16),
        in_specs=[slot_spec, slot_spec]
        + [whole((total, half))] * 4
        + [whole((ROUTER_ROWS, total))] * 2,
        out_specs=pl.BlockSpec((3, 2, 1, runs, units, cols), lambda e: (0, 0, e, 0, 0, 0)),
        scratch_shapes=[
            pltpu.VMEM((experts, 2 * held, half), bf16),
            pltpu.VMEM((experts, 2 * held, half), bf16),
        ],
        compiler_params=pltpu.CompilerParams(vmem_limit_bytes=60 * 2**20),
        cost_estimate=pl.CostEstimate(
            flops=20 * 10**9, bytes_accessed=30 * 2**20, transcendentals=0
        ),
        name="expert_grads",
    )(slot_own, slot_other, in_own, in_other, dy_own, dy_other, slots_own, slots_other)


def pick_half(values, parity_flip):
    ctx = lax.axis_size("ctx")
    total, width = values.shape
    cols = width // ctx

    def kernel(in_ref, out_ref):
        parity = lax.rem(lax.axis_index("ctx") + parity_flip, 2)
        for run in range(ctx // 2):
            start = pl.multiple_of((2 * run + parity) * cols, cols)
            out_ref[:, pl.ds(run * cols, cols)] = in_ref[:, pl.ds(start, cols)]

    return pl.pallas_call(
        kernel,
        out_shape=jax.ShapeDtypeStruct((total, width // 2), values.dtype),
        in_specs=[VMEM],
        out_specs=VMEM,
        cost_estimate=pl.CostEstimate(flops=0, bytes_accessed=2**22, transcendentals=0),
        name="pick_half",
    )(values)


def roll_half(values):
    return pltpu.roll(values, values.shape[1] // 2, 1)


def allowed_keys(first_ref, last_ref, span, places):
    return (places >= first_ref[span, :]) & (places <= last_ref[span, :])


def attend(projected, scales, gains, cosine, sine_part, first, last, places, cols):
    total = projected.shape[0]
    head_dim = cosine.shape[1]
    heads = cols // head_dim
    size = math.gcd(total, 256)
    score_scale = head_dim ** (-0.5)
    f32, bf16 = jnp.float32, jnp.bfloat16

    def kernel(
        lin_ref,
        scales_ref,
        gains_ref,
        cos_ref,
        sin_ref,
        first_ref,
        last_ref,
        places_ref,
        low_ref,
        attended_ref,
        attended_low_ref,
        top_ref,
    ):
        for kind in range(3):
            for h in range(heads):
                span = pl.ds(kind * cols + h * head_dim, head_dim)
                values = lin_ref[:, span]
                if kind < 2:
                    values = values * scales_ref[:, kind : kind + 1] * gains_ref[:, span]
                    values = values * cos_ref[...] + roll_half(values) * sin_ref[...]
                low_ref[:, span] = values.astype(bf16)
        for h in range(heads):
            head = pl.ds(h * head_dim, head_dim)
            keys = low_ref[:, pl.ds(cols + h * head_dim, head_dim)]
            values = low_ref[:, pl.ds(2 * cols + h * head_dim, head_dim)]

            def step(b, carry):
                span = pl.ds(pl.multiple_of(b * size, size), size)
                scores = lax.dot_general(
                    low_ref[span, head],
                    keys,
                    (((1,), (1,)), ((), ())),
                    preferred_element_type=f32,
                )
                allowed = allowed_keys(first_ref, last_ref, span, places_ref[...])
                scores = jnp.where(allowed, scores * score_scale, MASKED)
                top = jnp.max(scores, axis=1, keepdims=True)
                weights = jnp.exp(scores - top)
                sums = jnp.sum(weights, axis=1, keepdims=True)
                probs = (weights * (1.0 / sums)).astype(bf16)
                attended = jnp.dot(probs, values, preferred_element_type=f32)
                attended_ref[span, head] = attended
                attended_low_ref[span, head] = attended.astype(bf16)
                top_ref[span, head] = jnp.broadcast_to(top + jnp.log(sums), (size, head_dim))
                return carry

            lax.fori_loop(0, total // size, step, 0)

    return pl.pallas_call(
        kernel,
        out_shape=[
            jax.ShapeDtypeStruct((total, 3 * cols), bf16),
            jax.ShapeDtypeStruct((total, cols), f32),
            jax.ShapeDtypeStruct((total, cols), bf16),
            jax.ShapeDtypeStruct((total, cols), f32),
        ],
        in_specs=[VMEM] * 8,
        out_specs=[VMEM] * 4,
        compiler_params=pltpu.CompilerParams(vmem_limit_bytes=56 * 2**20),
        cost_estimate=pl.CostEstimate(
            flops=2 * 10**9, bytes_accessed=20 * 2**20, transcendentals=2 * 10**6
        ),
        name="attend",
    )(projected, scales, gains, cosine, sine_part, first, last, places)


def attend_back(
    output_grad, low, attended, top, projected, scales, gains, cosine, sine_part, first, last, places
):
    total, cols = output_grad.shape
    head_dim = cosine.shape[1]
    heads = cols // head_dim
    size = math.gcd(total, 256)
    score_scale = head_dim ** (-0.5)
    f32, bf16 = jnp.float32, jnp.bfloat16
    contract_rows = (((0,), (0,)), ((), ()))

    def kernel(
        grad_ref,
        low_ref,
        attended_ref,
        top_ref,
        lin_ref,
        scales_ref,
        gains_ref,
        cos_ref,
        sin_ref,
        first_ref,
        last_ref,
        places_ref,
        back_ref,
        value_ref,
        gain_ref,
        sums_ref,
        query_grad,
        key_grad,
        value_grad,
    ):
        totals = [jnp.zeros((total, 1), f32) for _ in range(2)]
        for h in range(heads):
            head = pl.ds(h * head_dim, head_dim)
            keys = low_ref[:, pl.ds(cols + h * head_dim, head_dim)]
            values = low_ref[:, pl.ds(2 * cols + h * head_dim, head_dim)]
            key_grad[...] = jnp.zeros_like(key_grad)
            value_grad[...] = jnp.zeros_like(value_grad)

            def step(b, carry):
                span = pl.ds(pl.multiple_of(b * size, size), size)
                queries, grads = low_ref[span, head], grad_ref[span, head]
                scores = lax.dot_general(
                    queries, keys, (((1,), (1,)), ((), ())), preferred_element_type=f32
                )
                allowed = allowed_keys(first_ref, last_ref, span, places_ref[...])
                scores = jnp.where(allowed, scores * score_scale, MASKED)
                probs = jnp.exp(scores - top_ref[span, head][:, :1])
                prob_grad = lax.dot_general(
                    grads, values, (((1,), (1,)), ((), ())), preferred_element_type=f32
                )
                delta = jnp.sum(
                    grads.astype(f32) * attended_ref[span, head], axis=1, keepdims=True
                )
                score_grad = (probs * (prob_grad - delta)).astype(bf16)
                query_grad[span, :] = (
                    jnp.dot(score_grad, keys, preferred_element_type=f32) * score_scale
                )
                key_grad[...] += lax.dot_general(
                    score_grad, queries, contract_rows, preferred_element_type=f32
                )
                value_grad[...] += lax.dot_general(
                    probs.astype(bf16), grads, contract_rows, preferred_element_type=f32
                )
                return carry

            lax.fori_loop(0, total // size, step, 0)
            value_ref[:, head] = value_grad[...].astype(bf16)
            for kind, grad in ((0, query_grad[...]), (1, key_grad[...] * score_scale)):
                span = pl.ds(kind * cols + h * head_dim, head_dim)
                unit = lin_ref[:, span] * scales_ref[:, kind : kind + 1]
                grad = grad * cos_ref[...] - roll_half(grad) * sin_ref[...]
                gain_ref[kind, :, head] = jnp.sum(grad * unit, axis=0, keepdims=True)
                grad = grad * gains_ref[:, span]
                back_ref[kind, :, head] = grad
                totals[kind] = totals[kind] + jnp.sum(grad * unit, axis=1, keepdims=True)
        for kind in range(2):
            sums_ref[:, kind : kind + 1] = totals[kind]

    return pl.pallas_call(
        kernel,
        out_shape=[
            jax.ShapeDtypeStruct((2, total, cols), f32),
            jax.ShapeDtypeStruct((total, cols), bf16),
            jax.ShapeDtypeStruct((2, 1, cols), f32),
            jax.ShapeDtypeStruct((total, 2), f32),
        ],
        in_specs=[VMEM] * 12,
        out_specs=[VMEM] * 4,
        scratch_shapes=[pltpu.VMEM((total, head_dim), f32)] * 3,
        compiler_params=pltpu.CompilerParams(vmem_limit_bytes=56 * 2**20),
        cost_estimate=pl.CostEstimate(flops=0, bytes_accessed=2**20, transcendentals=0),
        name="attend_back",
    )(
        output_grad,
        low,
        attended,
        top,
        projected,
        scales,
        gains,
        cosine,
        sine_part,
        first,
        last,
        places,
    )


def flipped(index, bit):
    return index + bit * (1 - 2 * lax.rem(index // bit, 2))


def add_into(target, *sources):
    step = target.shape[0] if len(target.shape) == 3 else target.shape[0] // 64

    def body(i, carry):
        span = i if len(target.shape) == 3 else pl.ds(pl.multiple_of(i * 64, 64), 64)
        total = sources[0][span].astype(jnp.float32)
        for source in sources[1:]:
            total = total + source[span].astype(jnp.float32)
        target[span] = total.astype(target.dtype)
        return carry

    lax.fori_loop(0, step, body, 0)


def finish_sums(packed, normed_part, out_part, qkv_part, small, tokens, mixed_grad, gain, collective_id):
    ctx, fsdp = lax.axis_size("ctx"), lax.axis_size("fsdp")
    kinds, _, experts, _, units, cols = packed.shape
    rows, width = tokens.shape
    part = out_part.shape[0]
    f32, bf16 = jnp.float32, jnp.bfloat16
    small_rows, small_cols = small.shape[0], small.shape[1] // fsdp
    copies_most = 64

    def kernel(
        packed_ref,
        normed_ref,
        g_out_ref,
        g_qkv_ref,
        small_ref,
        tokens_ref,
        mixed_ref,
        gain_ref,
        grads_ref,
        input_ref,
        out_ref,
        qkv_ref,
        sums_ref,
        kept,
        kept_low,
        kept_high,
        normed_own,
        normed_x,
        normed_low,
        normed_high,
        out_own,
        out_x,
        out_low,
        out_high,
        qkv_own,
        qkv_core,
        qkv_chip,
        qkv_sum,
        dealt,
        small_parts,
        small_sum,
        small_held,
        sends,
        recvs,
        locals_,
        deal_sems,
    ):
        me, mine = lax.axis_index("ctx"), lax.axis_index("fsdp")
        x, low, high = lax.rem(me, 2), lax.rem(me // 2, 2), me // 4
        to_x, to_low, to_high = ((flipped(me, bit), mine) for bit in (1, 2, 4))
        core, chip = flipped(mine, 1), flipped(mine, 2)
        diagonal = flipped(core, 2)
        ctx_peers = [(lax.rem(me + step, ctx), mine) for step in range(1, ctx)]
        near = [lax.rem(mine + step, fsdp) for step in range(1, fsdp)]
        greet(ctx_peers + [(me, other) for other in near])
        used, used_local, all_sends, loads = [0], [0], [], {}

        def push(source, target, peer):
            i = used[0]
            used[0] += 1
            copy = send(source, target, sends.at[i], recvs.at[i], peer)
            all_sends.append(copy)
            return copy

        def load(source, target):
            i = used_local[0]
            used_local[0] += 1
            copy = pltpu.make_async_copy(source, target, locals_.at[i])
            copy.start()
            return copy

        def normed_block(a, b, other):
            side = 1 - x if other else x
            block = (high + a - 2 * a * high) * 4 + (low + b - 2 * b * low) * 2 + side
            return normed_ref.at[pl.ds(pl.multiple_of(block * rows, rows), rows), :]

        def out_block(a, b, other):
            side = 1 - x if other else x
            block = (high + a - 2 * a * high) * 4 + (low + b - 2 * b * low) * 2 + side
            return g_out_ref.at[:, pl.ds(pl.multiple_of(block * cols, cols), cols)]

        def run(a):
            return high + a - 2 * a * high

        def qkv_block(index):
            return g_qkv_ref.at[pl.ds(pl.multiple_of(index * part, part), part), :]

        def columns(index):
            return pl.ds(pl.multiple_of(index * small_cols, small_cols), small_cols)

        order = ((1, 1), (0, 1), (1, 0), (0, 0))
        small_copies = [
            push(small_ref.at[:, columns(other)], small_parts.at[i], (me, other))
            for i, other in enumerate(near)
        ]
        normed_copies = {
            ab: push(normed_block(*ab, True), normed_x.at[ab[0], ab[1]], to_x) for ab in order
        }

        def push_low(kind, a):
            return push(packed_ref.at[kind, 0, :, run(a)], kept_low.at[kind, a], to_low)

        low_copies = {(0, a): push_low(0, a) for a in (1, 0)}
        qkv_copies = [
            push(qkv_block(diagonal), qkv_core.at[1], (me, core)),
            push(qkv_block(core), qkv_core.at[0], (me, core)),
        ]
        qkv_loads = [
            load(qkv_block(chip), qkv_own.at[1]),
            load(qkv_block(mine), qkv_own.at[0]),
        ]
        normed_loads = {
            ab: load(normed_block(*ab, False), normed_own.at[ab[0], ab[1]]) for ab in order
        }
        kept_loads = {
            (kind, a): load(packed_ref.at[kind, 1, :, run(a)], kept.at[kind, a])
            for kind in range(kinds)
            for a in (1, 0)
        }
        out_loads = {ab: load(out_block(*ab, False), out_own.at[ab[0], ab[1]]) for ab in order}

        total = small_ref[:, columns(mine)]
        for i, copy in enumerate(small_copies):
            copy.wait_recv()
            total = total + small_parts[i]
        small_sum[...] = total
        small_wide = [push(small_sum, small_held.at[i], peer) for i, peer in enumerate(ctx_peers)]

        qkv_copies[0].wait_recv()
        qkv_loads[0].wait()
        add_into(qkv_core.at[1], qkv_own.at[1], qkv_core.at[1])
        chip_copy = push(qkv_core.at[1], qkv_chip, (me, chip))

        def to_low_side(copies, loads, own, from_x, from_low, a):
            copies[a, 1].wait_recv()
            loads[a, 1].wait()
            add_into(from_x.at[a, 1], own.at[a, 1], from_x.at[a, 1])
            return push(from_x.at[a, 1], from_low.at[a], to_low)

        def to_high_side(copies, loads, lows, own, from_x, from_low, from_high):
            copies[1, 0].wait_recv()
            loads[1, 0].wait()
            lows[1].wait_recv()
            add_into(from_x.at[1, 0], own.at[1, 0], from_x.at[1, 0], from_low.at[1])
            return push(from_x.at[1, 0], from_high, to_high)

        def experts_high(kind):
            low_copies[kind, 1].wait_recv()
            kept_loads[kind, 1].wait()
            add_into(kept_low.at[kind, 1], kept.at[kind, 1], kept_low.at[kind, 1])
            return push(kept_low.at[kind, 1], kept_high.at[kind], to_high)

        normed_args = (normed_copies, normed_loads)
        normed_lows = {1: to_low_side(*normed_args, normed_own, normed_x, normed_low, 1)}
        high_copies = {0: experts_high(0)}
        low_copies.update({(1, a): push_low(1, a) for a in (1, 0)})
        normed_lows[0] = to_low_side(*normed_args, normed_own, normed_x, normed_low, 0)
        out_copies = {ab: push(out_block(*ab, True), out_x.at[ab[0], ab[1]], to_x) for ab in order}

        qkv_copies[1].wait_recv()
        qkv_loads[1].wait()
        chip_copy.wait_recv()
        add_into(qkv_sum, qkv_own.at[0], qkv_core.at[0], qkv_chip)

        def deal(kind):
            index = kind * ctx + me
            return pltpu.make_async_remote_copy(
                qkv_sum.at[:, pl.ds(kind * cols, cols)],
                dealt.at[lax.rem(index, kinds)],
                deal_sems.at[0, kind],
                deal_sems.at[1, lax.rem(index, kinds)],
                device_id=(index // kinds, mine),
                device_id_type=MESH,
            )

        def keep(kind):
            return pltpu.make_async_copy(
                qkv_sum.at[:, pl.ds(kind * cols, cols)],
                dealt.at[lax.rem(kind * ctx + me, kinds)],
                deal_sems.at[0, kind],
            )

        def is_far(kind):
            return (kind * ctx + me) // kinds != me

        for kind in range(kinds):
            pl.when(is_far(kind))(deal(kind).start)
            pl.when(jnp.logical_not(is_far(kind)))(keep(kind).start)

        normed_high_copy = to_high_side(
            *normed_args, normed_lows, normed_own, normed_x, normed_low, normed_high
        )
        high_copies[1] = experts_high(1)
        low_copies.update({(2, a): push_low(2, a) for a in (1, 0)})
        out_args = (out_copies, out_loads)
        out_lows = {a: to_low_side(*out_args, out_own, out_x, out_low, a) for a in (1, 0)}

        def experts_end(kind):
            low_copies[kind, 0].wait_recv()
            kept_loads[kind, 0].wait()
            high_copies[kind].wait_recv()
            add_into(grads_ref.at[kind], kept.at[kind, 0], kept_low.at[kind, 0], kept_high.at[kind])

        experts_end(0)

        normed_copies[0, 0].wait_recv()
        normed_loads[0, 0].wait()
        normed_lows[0].wait_recv()
        normed_high_copy.wait_recv()

        def norm_step(i, carry):
            span = pl.ds(pl.multiple_of(i * 16, 16), 16)
            grad = (
                normed_own[0, 0, span, :].astype(f32)
                + normed_x[0, 0, span, :].astype(f32)
                + normed_low[0, span, :].astype(f32)
                + normed_high[span, :].astype(f32)
            )
            values = tokens_ref[span, :].astype(f32)
            scale = rms_unit(values)
            unit = values * scale
            pulled = grad * gain_ref[...]
            input_ref[span, :] = mixed_ref[span, :] + scale * (
                pulled - unit * jnp.mean(unit * pulled, axis=-1, keepdims=True)
            )
            return carry

        lax.fori_loop(0, rows // 16, norm_step, 0)

        out_high_copy = to_high_side(*out_args, out_lows, out_own, out_x, out_low, out_high)
        high_copies[2] = experts_high(2)
        experts_end(1)

        total = small_sum[...]
        for i, copy in enumerate(small_wide):
            copy.wait_recv()
            total = total + small_held[i]
        sums_ref[...] = total

        for kind in range(kinds):
            pl.when(is_far(kind))(deal(kind).wait_send)
            pl.when(jnp.logical_not(is_far(kind)))(keep(kind).wait)
        for slot in range(kinds):

            @pl.when(lax.rem(me * kinds + slot, ctx) != me)
            def _():
                pltpu.make_async_copy(
                    dealt.at[slot], dealt.at[slot], deal_sems.at[1, slot]
                ).wait()

            add_into(qkv_ref.at[:, pl.ds(slot * cols, cols)], dealt.at[slot])

        out_copies[0, 0].wait_recv()
        out_loads[0, 0].wait()
        out_lows[0].wait_recv()
        out_high_copy.wait_recv()
        add_into(out_ref, out_own.at[0, 0], out_x.at[0, 0], out_low.at[0], out_high)
        experts_end(2)
        for copy in all_sends:
            copy.wait_send()

    def block(*shape):
        return pltpu.VMEM(shape, bf16)

    gradient = (experts, units, cols)
    return comm_call(
        kernel,
        "finish_sums",
        collective_id,
        [
            jax.ShapeDtypeStruct((kinds,) + gradient, f32),
            jax.ShapeDtypeStruct((rows, width), f32),
            jax.ShapeDtypeStruct((part, cols), f32),
            jax.ShapeDtypeStruct((part, kinds * cols), f32),
            jax.ShapeDtypeStruct((small_rows, small_cols), f32),
        ],
        [ANY] * 4 + [VMEM] * 4,
        [VMEM] * 5,
        [
            block(kinds, 2, *gradient),
            block(kinds, 2, *gradient),
            block(kinds, *gradient),
            block(2, 2, rows, width),
            block(2, 2, rows, width),
            block(2, rows, width),
            block(rows, width),
            block(2, 2, part, cols),
            block(2, 2, part, cols),
            block(2, part, cols),
            block(part, cols),
            block(2, part, kinds * cols),
            block(2, part, kinds * cols),
            block(part, kinds * cols),
            block(part, kinds * cols),
            block(kinds, part, cols),
            pltpu.VMEM((fsdp - 1, small_rows, small_cols), f32),
            pltpu.VMEM((small_rows, small_cols), f32),
            pltpu.VMEM((ctx - 1, small_rows, small_cols), f32),
            DMA((copies_most,)),
            DMA((copies_most,)),
            DMA((32,)),
            DMA((2, kinds)),
        ],
        700 * 2**20,
    )(packed, normed_part, out_part, qkv_part, small, tokens, mixed_grad, gain)


def on_device_heads(
    tokens,
    doc_lengths,
    routes,
    slot_order,
    attn_gain,
    w_qkv,
    q_gain,
    k_gain,
    w_out,
    ffn_gain,
    w_router,
    w_gate,
    w_up,
    w_down,
    cotangent,
):
    rows, width = tokens.shape[1], tokens.shape[2]
    ctx, fsdp = lax.axis_size("ctx"), lax.axis_size("fsdp")
    me = lax.axis_index("ctx")
    head_dim = width // HEADS
    cols = HEADS // ctx * head_dim
    part = width // fsdp
    total = rows * ctx
    lengths = doc_lengths[0]
    bf16, f32 = jnp.bfloat16, jnp.float32

    tokens_all = lax.all_gather(tokens[0], "ctx", axis=0, tiled=True)
    small = jnp.concatenate(
        [jnp.stack([attn_gain, q_gain, k_gain, ffn_gain]), w_router.T], axis=0
    )
    small = lax.all_gather(small, "fsdp", axis=1, tiled=True)
    gain_one, gain_query, gain_key, gain_two = (small[i].astype(f32) for i in range(4))
    router_weight = small[4:]
    own_cols = jnp.concatenate(
        [
            lax.dynamic_slice_in_dim(w_qkv, kind * width + me * cols, cols, 1)
            for kind in range(3)
        ],
        axis=1,
    )
    qkv_weight = lax.all_gather(own_cols, "fsdp", axis=0, tiled=True)
    dy_all = lax.all_gather(cotangent[0], "fsdp", axis=0, tiled=True)
    pairs_all = lax.all_gather(jnp.stack([routes[0], slot_order[0]]), "fsdp", axis=0)

    stream_pos = dealt_position(jnp.arange(total, dtype=jnp.int32), rows, ctx)
    stream_doc, stream_inner = document_info(stream_pos, lengths)
    cosine, sine_part = rope_tables(stream_inner, head_dim)
    turn_tables = (
        jnp.concatenate([cosine, cosine], axis=1),
        jnp.concatenate([-sine_part, sine_part], axis=1),
    )
    sight = (
        (stream_pos - stream_inner).reshape(total, 1),
        stream_pos.reshape(total, 1),
        stream_pos.reshape(1, total),
    )
    inputs_all = tokens_all.astype(f32)
    unit_all = inputs_all * rms_unit(inputs_all)
    normed_all = (unit_all * gain_one).astype(bf16)
    projected = dot32("td,de->te", normed_all, qkv_weight)
    squares = jnp.sum((projected * projected)[:, : 2 * cols].reshape(total, 2, cols), axis=2).T
    squares = ctx_sum(squares.reshape(-1, 128), 1).reshape(2, total)
    scales = lax.rsqrt(squares / width + EPSILON).T
    own_gains = [
        lax.dynamic_slice_in_dim(gain, me * cols, cols, 0) for gain in (gain_query, gain_key)
    ]
    own_gains = jnp.concatenate(own_gains).reshape(1, 2 * cols)
    low, attended, attended_low, tops = attend(
        projected, scales, own_gains, *turn_tables, *sight, cols
    )

    attended_part = heads_to_rows(attended_low, 2)
    mixed_part = dot32("td,de->te", attended_part, w_out).astype(bf16)
    inputs = tokens[0].astype(f32)
    row_gain_two = gain_two.reshape(1, width)
    group, mixed = reduce_then_gather(
        mixed_part,
        [tokens[0], row_gain_two],
        [jax.ShapeDtypeStruct((rows, width), f32)],
        norm_chunk,
        "mix_and_norm",
        6,
    )

    experts = w_gate.shape[0]
    top = routes.shape[2]
    capacity = rows * top // experts
    expert_ids = jnp.arange(experts, dtype=jnp.int32)
    slots = jax.vmap(slot_of_pairs)(pairs_all[:, 0], pairs_all[:, 1])
    chosen = pairs_all[:, 0][:, :, :, None] == expert_ids
    slot_by_expert = jnp.sum(jnp.where(chosen, slots[..., None] + 1, 0), axis=2) - 1
    slot_by_expert = jnp.pad(
        slot_by_expert.reshape(fsdp * rows, experts).T,
        ((0, ROUTER_ROWS - experts), (0, 0)),
        constant_values=-1,
    )
    router_rows = jnp.pad(router_weight, ((0, ROUTER_ROWS - experts), (0, 0)))
    moved_part, group_grad, g_router, slot_pack = run_experts(
        group, dy_all, slot_by_expert, router_rows, w_gate, w_up, w_down, fsdp, capacity
    )
    moved = lax.psum_scatter(moved_part, "fsdp", scatter_dimension=0, tiled=True)
    activations = (mixed + moved.astype(f32)).astype(bf16)

    packed = expert_grads(
        slot_pack,
        swap(slot_pack, "ctx", 1),
        pick_half(group, 0),
        swap(pick_half(group, 1), "ctx", 1),
        pick_half(dy_all, 0),
        swap(pick_half(dy_all, 1), "ctx", 1),
        slot_by_expert,
        swap(slot_by_expert, "ctx", 1),
        fsdp,
        capacity,
    )
    mixed_all, mixed_grad, g_ffn_gain = reduce_then_gather(
        group_grad,
        [mixed, row_gain_two, cotangent[0]],
        [jax.ShapeDtypeStruct((rows, width), f32), jax.ShapeDtypeStruct((1, width), f32)],
        norm_back_chunk,
        "norm_back",
        7,
    )
    g_ffn_gain = g_ffn_gain[0]
    output_part = dot32("te,de->td", mixed_all, w_out).astype(bf16)
    g_out = dot32("td,te->de", attended_part, mixed_all).astype(bf16)
    output_grad, packed = lax.optimization_barrier((rows_to_heads(output_part, 3), packed))

    back, value_grad, own_g_gains, inner_sums = attend_back(
        output_grad, low, attended, tops, projected, scales, own_gains, *turn_tables, *sight
    )
    inner_sums = ctx_sum(inner_sums.T.reshape(-1, 128), 1).reshape(2, total).T / width

    def norm_back(kind):
        scale = scales[:, kind : kind + 1]
        unit = projected[:, kind * cols : (kind + 1) * cols] * scale
        return (scale * (back[kind] - unit * inner_sums[:, kind : kind + 1])).astype(bf16)

    proj_grad = jnp.concatenate([norm_back(0), norm_back(1), value_grad], axis=1)
    g_qkv = dot32("td,te->de", normed_all, proj_grad).astype(bf16)
    normed_grad_part = dot32("te,de->td", proj_grad, qkv_weight)
    g_attn_gain = jnp.sum(normed_grad_part * unit_all, axis=0)
    def placed_cols(values):
        return lax.dynamic_update_slice_in_dim(jnp.zeros((width,), f32), values, me * cols, 0)

    sums = jnp.concatenate(
        [
            jnp.stack([g_attn_gain, placed_cols(own_g_gains[0, 0]), placed_cols(own_g_gains[1, 0]), g_ffn_gain]),
            g_router[:experts],
        ],
        axis=0,
    )
    grads, input_grad, out_part, qkv_part, sums = finish_sums(
        packed,
        normed_grad_part.astype(bf16),
        g_out,
        g_qkv,
        jnp.pad(sums, ((0, -sums.shape[0] % 8), (0, 0))),
        tokens[0],
        mixed_grad,
        gain_one.reshape(1, width),
        8,
    )
    return (
        activations[None],
        input_grad[None],
        sums[0],
        qkv_part,
        sums[1],
        sums[2],
        out_part,
        sums[3],
        sums[4 : 4 + experts].T,
        grads[1],
        grads[2],
        grads[0],
    )


def solution(mesh):
    in_specs = (
        P("fsdp", "ctx", None),
        P("fsdp", None),
        P("fsdp", "ctx", None),
        P("fsdp", "ctx", None),
        P("fsdp"),
        P("fsdp", None),
        P("fsdp"),
        P("fsdp"),
        P("fsdp", None),
        P("fsdp"),
        P("fsdp", None),
        P(None, None, "fsdp"),
        P(None, None, "fsdp"),
        P(None, "fsdp", None),
        P("fsdp", "ctx", None),
    )
    out_specs = (
        P("fsdp", "ctx", None),
        P("fsdp", "ctx", None),
        P("fsdp"),
        P("fsdp", "ctx"),
        P("fsdp"),
        P("fsdp"),
        P("fsdp", "ctx"),
        P("fsdp"),
        P("fsdp", None),
        P(None, "ctx", "fsdp"),
        P(None, "ctx", "fsdp"),
        P(None, "fsdp", "ctx"),
    )
    ctx, fsdp = mesh.shape["ctx"], mesh.shape["fsdp"]
    by_heads = HEADS % ctx == 0 and ctx == 8 and fsdp == 4
    body = on_device_heads if by_heads else on_device
    return jax.shard_map(
        body, mesh=mesh, in_specs=in_specs, out_specs=out_specs, check_vma=False
    )
```

```python
import math

import jax
import jax.numpy as jnp
from jax import lax
from jax.experimental import pallas as pl
from jax.experimental.pallas import tpu as pltpu
from jax.sharding import PartitionSpec as P

HEADS = 16
MESH = pl.DeviceIdType.MESH
ANY = pl.BlockSpec(memory_space=pl.ANY)
VMEM = pl.BlockSpec(memory_space=pltpu.VMEM)
DMA = pltpu.SemaphoreType.DMA

EPSILON = 1e-05
ROPE_BASE = 10000.0
MASKED = -1e30


def rms_scale(values, gain_vector):
    return (
        values
        * lax.rsqrt(jnp.mean(values * values, axis=-1, keepdims=True) + EPSILON)
        * gain_vector
    )


def rotate(values, inner_pos):
    half_dim = values.shape[-1] // 2
    freq_table = ROPE_BASE ** (-2.0 * jnp.arange(half_dim, dtype=jnp.float32) / values.shape[-1])
    angles = inner_pos.astype(jnp.float32)[:, None] * freq_table[None, :]
    cosine = jnp.cos(angles)[:, None, :]
    sine_part = jnp.sin(angles)[:, None, :]
    first_half = values[..., :half_dim]
    second_half = values[..., half_dim:]
    return jnp.concatenate(
        [
            first_half * cosine - second_half * sine_part,
            second_half * cosine + first_half * sine_part,
        ],
        axis=-1,
    )


def dealt_position(flat_index, per_device, device_count):
    device_index = flat_index // per_device
    within = flat_index % per_device
    half_rows = per_device // 2
    return jnp.where(
        within < half_rows,
        device_index * half_rows + within,
        (2 * device_count - 1 - device_index) * half_rows + within - half_rows,
    )


def document_info(positions, lengths):
    doc_ends = jnp.sum(jnp.where(jnp.arange(lengths.shape[0])[:, None] >= jnp.arange(lengths.shape[0])[None, :], lengths[None, :], 0), axis=1)
    passed = doc_ends[None, :] <= positions[:, None]
    doc_ids = jnp.sum(passed.astype(jnp.int32), axis=1)
    inner_pos = positions - jnp.sum(jnp.where(passed, lengths[None, :], 0), axis=1)
    return (doc_ids, inner_pos)


def slot_table(route_ids, order_ids, capacity, expert_count):
    pair_count = route_ids.shape[0] * route_ids.shape[1]
    expert_flat = route_ids.reshape(pair_count)
    rank_flat = order_ids.reshape(pair_count)
    earlier = (expert_flat[None, :] == expert_flat[:, None]) & (
        rank_flat[None, :] < rank_flat[:, None]
    )
    slot_index = jnp.sum(earlier.astype(jnp.int32), axis=1)
    placed = jnp.where(
        slot_index < capacity, expert_flat * capacity + slot_index, expert_count * capacity
    )
    source = (
        jnp.full((expert_count * capacity + 1,), pair_count, jnp.int32)
        .at[placed]
        .set(jnp.arange(pair_count, dtype=jnp.int32))
    )
    return (placed, source[: expert_count * capacity])


def masked_scores(query_block, key_block, query_pos, query_doc, key_pos, key_doc, score_scale):
    scores = (
        jnp.einsum("qhd,khd->hqk", query_block, key_block, preferred_element_type=jnp.float32)
        * score_scale
    )
    allowed = (query_doc[:, None] == key_doc[None, :]) & (key_pos[None, :] <= query_pos[:, None])
    return jnp.where(allowed[None], scores, MASKED)


def silu_parts(hidden_grad, slot_gate, slot_up):
    sigma = jax.nn.sigmoid(slot_gate)
    gate_grad_low = (hidden_grad * slot_up * sigma * (1.0 + slot_gate * (1.0 - sigma))).astype(
        jnp.bfloat16
    )
    up_grad_low = (hidden_grad * slot_gate * sigma).astype(jnp.bfloat16)
    return (gate_grad_low, up_grad_low)


def on_device(
    tokens,
    doc_lengths,
    routes,
    slot_order,
    attn_gain,
    w_qkv,
    q_gain,
    k_gain,
    w_out,
    ffn_gain,
    w_router,
    w_gate,
    w_up,
    w_down,
    cotangent,
):
    row_count = tokens.shape[1]
    model_width = tokens.shape[2]
    head_count = HEADS
    head_dim = model_width // head_count
    score_scale = head_dim ** (-0.5)
    ctx_count = lax.axis_size("ctx")
    ctx_index = lax.axis_index("ctx")
    total_rows = row_count * ctx_count
    lengths = doc_lengths[0]
    local_pos = dealt_position(
        ctx_index * row_count + jnp.arange(row_count, dtype=jnp.int32), row_count, ctx_count
    )
    local_doc, local_inner = document_info(local_pos, lengths)
    stream_pos = dealt_position(jnp.arange(total_rows, dtype=jnp.int32), row_count, ctx_count)
    stream_doc, stream_inner = document_info(stream_pos, lengths)
    block_rows = math.gcd(total_rows, 512)
    block_count = total_rows // block_rows
    block_ids = jnp.arange(block_count, dtype=jnp.int32)
    gain_one, qkv_weight, gain_query, gain_key, out_weight = (
        lax.all_gather(attn_gain, "fsdp", axis=0, tiled=True),
        lax.all_gather(w_qkv, "fsdp", axis=0, tiled=True),
        lax.all_gather(q_gain, "fsdp", axis=0, tiled=True),
        lax.all_gather(k_gain, "fsdp", axis=0, tiled=True),
        lax.all_gather(w_out, "fsdp", axis=0, tiled=True),
    )
    gain_two, router_weight, gate_weight, up_weight, down_weight = (
        lax.all_gather(ffn_gain, "fsdp", axis=0, tiled=True),
        lax.all_gather(w_router, "fsdp", axis=0, tiled=True),
        lax.all_gather(w_gate, "fsdp", axis=2, tiled=True),
        lax.all_gather(w_up, "fsdp", axis=2, tiled=True),
        lax.all_gather(w_down, "fsdp", axis=1, tiled=True),
    )
    inputs = tokens[0].astype(jnp.float32)
    normed_f, norm_one_pull = jax.vjp(rms_scale, inputs, gain_one.astype(jnp.float32))
    normed_low = normed_f.astype(jnp.bfloat16)
    projected = jnp.dot(normed_low, qkv_weight, preferred_element_type=jnp.float32)
    query_lin = projected[:, :model_width]
    key_lin = projected[:, model_width : 2 * model_width]
    value_low = (
        projected[:, 2 * model_width :]
        .astype(jnp.bfloat16)
        .reshape(row_count, head_count, head_dim)
    )

    def head_shape(values, gain_vector):
        return rotate(
            rms_scale(values, gain_vector).reshape(row_count, head_count, head_dim), local_inner
        )

    query_f, query_pull = jax.vjp(head_shape, query_lin, gain_query.astype(jnp.float32))
    key_f, key_pull = jax.vjp(head_shape, key_lin, gain_key.astype(jnp.float32))
    query_low = query_f.astype(jnp.bfloat16)
    key_low = key_f.astype(jnp.bfloat16)
    keys_all, values_all = (
        lax.all_gather(key_low, "ctx", axis=0, tiled=True),
        lax.all_gather(value_low, "ctx", axis=0, tiled=True),
    )

    def key_slice(block_index):
        first_row = block_index * block_rows
        return (
            lax.dynamic_slice_in_dim(keys_all, first_row, block_rows, 0),
            lax.dynamic_slice_in_dim(values_all, first_row, block_rows, 0),
            lax.dynamic_slice_in_dim(stream_pos, first_row, block_rows, 0),
            lax.dynamic_slice_in_dim(stream_doc, first_row, block_rows, 0),
        )

    def stats_step(carry, block_index):
        running_top, running_total = carry
        key_block, value_block, key_pos, key_doc = key_slice(block_index)
        scores = masked_scores(
            query_low, key_block, local_pos, local_doc, key_pos, key_doc, score_scale
        )
        new_top = jnp.maximum(running_top, jnp.max(scores, axis=-1))
        running_total = running_total * jnp.exp(running_top - new_top) + jnp.sum(
            jnp.exp(scores - new_top[..., None]), axis=-1
        )
        return ((new_top, running_total), None)

    start_stats = (
        jnp.full((head_count, row_count), MASKED, jnp.float32),
        jnp.zeros((head_count, row_count), jnp.float32),
    )
    (score_top, score_total), _ = lax.scan(stats_step, start_stats, block_ids)
    log_total = score_top + jnp.log(score_total)

    def output_step(accum, block_index):
        key_block, value_block, key_pos, key_doc = key_slice(block_index)
        scores = masked_scores(
            query_low, key_block, local_pos, local_doc, key_pos, key_doc, score_scale
        )
        prob_block = jnp.exp(scores - log_total[..., None]).astype(jnp.bfloat16)
        return (
            accum
            + jnp.einsum(
                "hqk,khd->qhd", prob_block, value_block, preferred_element_type=jnp.float32
            ),
            None,
        )

    attended_f, _ = lax.scan(
        output_step, jnp.zeros((row_count, head_count, head_dim), jnp.float32), block_ids
    )
    attended_low = attended_f.reshape(row_count, model_width).astype(jnp.bfloat16)
    mixed = inputs + jnp.dot(attended_low, out_weight, preferred_element_type=jnp.float32)
    normed_two_f, norm_two_pull = jax.vjp(rms_scale, mixed, gain_two.astype(jnp.float32))
    normed_two = normed_two_f.astype(jnp.bfloat16)
    expert_count = gate_weight.shape[0]
    route_ids = routes[0]
    top_count = route_ids.shape[1]
    pair_count = row_count * top_count
    capacity = pair_count // expert_count
    logits = jnp.dot(normed_two, router_weight, preferred_element_type=jnp.float32)
    router_probs = jax.nn.softmax(logits, axis=-1)
    chosen = (
        route_ids[:, :, None] == jnp.arange(expert_count, dtype=jnp.int32)[None, None, :]
    ).astype(jnp.float32)
    gate_values = jnp.sum(chosen * router_probs[:, None, :], axis=-1)
    placed, source = slot_table(route_ids, slot_order[0], capacity, expert_count)
    padded_in = jnp.concatenate([normed_two, jnp.zeros((1, model_width), jnp.bfloat16)], axis=0)
    expert_in = padded_in[source // top_count].reshape(expert_count, capacity, model_width)
    gate_pre = jnp.einsum(
        "ecd,edh->ech", expert_in, gate_weight, preferred_element_type=jnp.float32
    )
    up_pre = jnp.einsum("ecd,edh->ech", expert_in, up_weight, preferred_element_type=jnp.float32)
    hidden_low = (jax.nn.silu(gate_pre) * up_pre).astype(jnp.bfloat16)
    expert_out = jnp.einsum(
        "ech,ehd->ecd", hidden_low, down_weight, preferred_element_type=jnp.float32
    )
    out_padded = jnp.concatenate(
        [
            expert_out.reshape(expert_count * capacity, model_width),
            jnp.zeros((1, model_width), jnp.float32),
        ],
        axis=0,
    )
    per_pair = out_padded[placed].reshape(row_count, top_count, model_width)
    layer_out = mixed + jnp.sum(gate_values[:, :, None] * per_pair, axis=1)
    out_grad = cotangent[0].astype(jnp.float32)
    gate_grad = jnp.sum(out_grad[:, None, :] * per_pair, axis=-1)
    pair_grad = (gate_values[:, :, None] * out_grad[:, None, :]).reshape(pair_count, model_width)
    pair_padded = jnp.concatenate([pair_grad, jnp.zeros((1, model_width), jnp.float32)], axis=0)
    slot_grad = (
        pair_padded[source].reshape(expert_count, capacity, model_width).astype(jnp.bfloat16)
    )

    def expert_step(carry, pieces):
        slot_in, slot_hidden, slot_dy, slot_gate, slot_up, gate_matrix, up_matrix, down_matrix = (
            pieces
        )
        hidden_grad = jnp.einsum(
            "cd,hd->ch", slot_dy, down_matrix, preferred_element_type=jnp.float32
        )
        gate_grad_low, up_grad_low = silu_parts(hidden_grad, slot_gate, slot_up)
        in_grad = jnp.einsum(
            "ch,dh->cd", gate_grad_low, gate_matrix, preferred_element_type=jnp.float32
        ) + jnp.einsum("ch,dh->cd", up_grad_low, up_matrix, preferred_element_type=jnp.float32)
        gate_term = jnp.einsum(
            "cd,ch->dh", slot_in, gate_grad_low, preferred_element_type=jnp.float32
        )
        up_term = jnp.einsum("cd,ch->dh", slot_in, up_grad_low, preferred_element_type=jnp.float32)
        down_term = jnp.einsum(
            "ch,cd->hd", slot_hidden, slot_dy, preferred_element_type=jnp.float32
        )
        gate_shard, up_shard, down_shard = (
            lax.psum_scatter(
                gate_term.astype(jnp.bfloat16), "fsdp", scatter_dimension=1, tiled=True
            ).astype(jnp.float32),
            lax.psum_scatter(
                up_term.astype(jnp.bfloat16), "fsdp", scatter_dimension=1, tiled=True
            ).astype(jnp.float32),
            lax.psum_scatter(
                down_term.astype(jnp.bfloat16), "fsdp", scatter_dimension=0, tiled=True
            ).astype(jnp.float32),
        )
        gate_part, up_part, down_part = (
            lax.psum_scatter(
                gate_shard.astype(jnp.bfloat16), "ctx", scatter_dimension=0, tiled=True
            ).astype(jnp.float32),
            lax.psum_scatter(
                up_shard.astype(jnp.bfloat16), "ctx", scatter_dimension=0, tiled=True
            ).astype(jnp.float32),
            lax.psum_scatter(
                down_shard.astype(jnp.bfloat16), "ctx", scatter_dimension=1, tiled=True
            ).astype(jnp.float32),
        )
        return (carry, (in_grad, gate_part, up_part, down_part))

    _, (expert_in_grad, gate_parts, up_parts, down_parts) = lax.scan(
        expert_step,
        None,
        (expert_in, hidden_low, slot_grad, gate_pre, up_pre, gate_weight, up_weight, down_weight),
    )
    in_padded = jnp.concatenate(
        [
            expert_in_grad.reshape(expert_count * capacity, model_width),
            jnp.zeros((1, model_width), jnp.float32),
        ],
        axis=0,
    )
    normed_two_grad = jnp.sum(in_padded[placed].reshape(row_count, top_count, model_width), axis=1)
    prob_grad_router = jnp.sum(chosen * gate_grad[:, :, None], axis=1)
    logit_grad = (
        router_probs
        * (prob_grad_router - jnp.sum(router_probs * prob_grad_router, axis=-1, keepdims=True))
    ).astype(jnp.bfloat16)
    normed_two_grad = normed_two_grad + jnp.einsum(
        "te,de->td", logit_grad, router_weight, preferred_element_type=jnp.float32
    )
    router_grad = jnp.einsum(
        "td,te->de", normed_two, logit_grad, preferred_element_type=jnp.float32
    )
    mixed_norm_grad, gain_two_grad = norm_two_pull(normed_two_grad)
    mixed_grad = out_grad + mixed_norm_grad
    mixed_low = mixed_grad.astype(jnp.bfloat16)
    out_weight_grad = jnp.einsum(
        "td,te->de", attended_low, mixed_low, preferred_element_type=jnp.float32
    )
    output_grad = (
        jnp.einsum("te,de->td", mixed_low, out_weight, preferred_element_type=jnp.float32)
        .astype(jnp.bfloat16)
        .reshape(row_count, head_count, head_dim)
    )
    row_delta = jnp.sum(output_grad.astype(jnp.float32) * attended_f, axis=-1).T

    def query_grad_step(accum, block_index):
        key_block, value_block, key_pos, key_doc = key_slice(block_index)
        scores = masked_scores(
            query_low, key_block, local_pos, local_doc, key_pos, key_doc, score_scale
        )
        prob_block = jnp.exp(scores - log_total[..., None])
        prob_grad = jnp.einsum(
            "qhd,khd->hqk", output_grad, value_block, preferred_element_type=jnp.float32
        )
        score_grad = (prob_block * (prob_grad - row_delta[..., None])).astype(jnp.bfloat16)
        return (
            accum
            + jnp.einsum("hqk,khd->qhd", score_grad, key_block, preferred_element_type=jnp.float32)
            * score_scale,
            None,
        )

    query_grad, _ = lax.scan(
        query_grad_step, jnp.zeros((row_count, head_count, head_dim), jnp.float32), block_ids
    )
    inner_rows = math.gcd(row_count * lax.axis_size("ctx"), 512)

    def piece_step(carry, piece_index):
        first_row = piece_index * inner_rows
        key_block = lax.dynamic_slice_in_dim(keys_all, first_row, inner_rows, 0)
        value_block = lax.dynamic_slice_in_dim(values_all, first_row, inner_rows, 0)
        key_pos = lax.dynamic_slice_in_dim(stream_pos, first_row, inner_rows, 0)
        key_doc = lax.dynamic_slice_in_dim(stream_doc, first_row, inner_rows, 0)
        scores = masked_scores(
            query_low, key_block, local_pos, local_doc, key_pos, key_doc, score_scale
        )
        prob_block = jnp.exp(scores - log_total[..., None])
        prob_grad = jnp.einsum(
            "qhd,khd->hqk", output_grad, value_block, preferred_element_type=jnp.float32
        )
        score_grad = (prob_block * (prob_grad - row_delta[..., None])).astype(jnp.bfloat16)
        value_part = jnp.einsum(
            "hqk,qhd->khd",
            prob_block.astype(jnp.bfloat16),
            output_grad,
            preferred_element_type=jnp.float32,
        )
        key_part = (
            jnp.einsum("hqk,qhd->khd", score_grad, query_low, preferred_element_type=jnp.float32)
            * score_scale
        )
        return (
            carry,
            jnp.concatenate(
                [
                    key_part.reshape(inner_rows, model_width),
                    value_part.reshape(inner_rows, model_width),
                ],
                axis=1,
            ),
        )

    _, stacked = lax.scan(
        piece_step,
        None,
        jnp.arange(row_count * lax.axis_size("ctx") // inner_rows, dtype=jnp.int32),
    )
    key_value_grad = lax.psum_scatter(
        stacked.reshape(row_count * lax.axis_size("ctx"), 2 * model_width).astype(jnp.bfloat16),
        "ctx",
        scatter_dimension=0,
        tiled=True,
    ).astype(jnp.float32)
    key_grad = key_value_grad[:, :model_width].reshape(row_count, head_count, head_dim)
    value_grad = key_value_grad[:, model_width:]
    query_lin_grad, gain_query_grad = query_pull(query_grad)
    key_lin_grad, gain_key_grad = key_pull(key_grad)
    proj_grad = jnp.concatenate(
        [
            query_lin_grad.astype(jnp.bfloat16),
            key_lin_grad.astype(jnp.bfloat16),
            value_grad.astype(jnp.bfloat16),
        ],
        axis=1,
    )
    qkv_weight_grad = jnp.einsum(
        "td,te->de", normed_low, proj_grad, preferred_element_type=jnp.float32
    )
    normed_grad = jnp.einsum("te,de->td", proj_grad, qkv_weight, preferred_element_type=jnp.float32)
    input_norm_grad, gain_one_grad = norm_one_pull(normed_grad)
    input_grad = mixed_grad + input_norm_grad
    qkv_shard, out_shard = (
        lax.psum_scatter(
            qkv_weight_grad.astype(jnp.bfloat16), "fsdp", scatter_dimension=0, tiled=True
        ).astype(jnp.float32),
        lax.psum_scatter(
            out_weight_grad.astype(jnp.bfloat16), "fsdp", scatter_dimension=0, tiled=True
        ).astype(jnp.float32),
    )
    qkv_part, out_part = (
        lax.psum_scatter(
            qkv_shard.astype(jnp.bfloat16), "ctx", scatter_dimension=1, tiled=True
        ).astype(jnp.float32),
        lax.psum_scatter(
            out_shard.astype(jnp.bfloat16), "ctx", scatter_dimension=1, tiled=True
        ).astype(jnp.float32),
    )
    gain_one_sum, gain_query_sum, gain_key_sum, gain_two_sum, router_sum = lax.psum(
        (gain_one_grad, gain_query_grad, gain_key_grad, gain_two_grad, router_grad), ("ctx", "fsdp")
    )
    shard_rows = model_width // lax.axis_size("fsdp")
    shard_start = lax.axis_index("fsdp") * shard_rows

    def own_rows(full_array):
        return lax.dynamic_slice_in_dim(full_array, shard_start, shard_rows, 0)

    return (
        layer_out.astype(jnp.bfloat16)[None],
        input_grad[None],
        own_rows(gain_one_sum),
        qkv_part,
        own_rows(gain_query_sum),
        own_rows(gain_key_sum),
        out_part,
        own_rows(gain_two_sum),
        own_rows(router_sum),
        gate_parts,
        up_parts,
        down_parts,
    )


def rms_unit(values):
    return lax.rsqrt(jnp.mean(values * values, axis=-1, keepdims=True) + EPSILON)


def rope_tables(inner_pos, head_dim):
    half_dim = head_dim // 2
    freq_table = ROPE_BASE ** (-2.0 * jnp.arange(half_dim, dtype=jnp.float32) / head_dim)
    angles = inner_pos.astype(jnp.float32)[:, None] * freq_table[None, :]
    return (jnp.cos(angles), jnp.sin(angles))


def dot32(spec, left, right):
    return jnp.einsum(spec, left, right, preferred_element_type=jnp.float32)


def greet(peers):
    barrier = pltpu.get_barrier_semaphore()
    for peer in peers:
        pl.semaphore_signal(barrier, inc=1, device_id=peer, device_id_type=MESH)
    pl.semaphore_wait(barrier, len(peers))


def send(source, target, send_sem, recv_sem, peer):
    copy = pltpu.make_async_remote_copy(
        source, target, send_sem, recv_sem, device_id=peer, device_id_type=MESH
    )
    copy.start()
    return copy


def comm_call(
    kernel, name, collective_id, out_shape, in_specs, out_specs, scratch_shapes, cost, vmem=16
):
    return pl.pallas_call(
        kernel,
        out_shape=out_shape,
        in_specs=in_specs,
        out_specs=out_specs,
        scratch_shapes=scratch_shapes,
        compiler_params=pltpu.CompilerParams(
            collective_id=collective_id, has_side_effects=True, vmem_limit_bytes=vmem * 2**20
        ),
        cost_estimate=pl.CostEstimate(flops=0, bytes_accessed=cost, transcendentals=0),
        name=name,
    )


def ctx_sum(values, collective_id):
    ctx = lax.axis_size("ctx")

    def kernel(own_ref, out_ref, held, send_sems, recv_sems):
        me, mine = lax.axis_index("ctx"), lax.axis_index("fsdp")
        peers = [(lax.rem(me + step, ctx), mine) for step in range(1, ctx)]
        greet(peers)
        copies = [
            send(own_ref, held.at[i], send_sems.at[i], recv_sems.at[i], peer)
            for i, peer in enumerate(peers)
        ]
        total = own_ref[...]
        for i, copy in enumerate(copies):
            copy.wait_recv()
            total = total + held[i]
        out_ref[...] = total
        for copy in copies:
            copy.wait_send()

    return comm_call(
        kernel,
        "ctx_sum",
        collective_id,
        jax.ShapeDtypeStruct(values.shape, values.dtype),
        [VMEM],
        VMEM,
        [
            pltpu.VMEM((ctx - 1,) + values.shape, values.dtype),
            DMA((ctx - 1,)),
            DMA((ctx - 1,)),
        ],
        20 * 2**20,
    )(values)


def heads_to_rows(values, collective_id):
    ctx, fsdp = lax.axis_size("ctx"), lax.axis_size("fsdp")
    rows, cols = values.shape[0] // ctx, values.shape[1]
    share = ctx // fsdp

    def kernel(own_ref, out_ref, send_sems, recv_sems):
        me, mine = lax.axis_index("ctx"), lax.axis_index("fsdp")
        keeper, place = me // share, lax.rem(me, share)
        own_keeper = (keeper == mine).astype(jnp.int32)
        barrier = pltpu.get_barrier_semaphore()
        for step in range(share * fsdp):
            source, stream = mine * share + step // fsdp, step % fsdp

            @pl.when(jnp.logical_or(source != me, stream != mine))
            def _():
                pl.semaphore_signal(
                    barrier, inc=1, device_id=(source, stream), device_id_type=MESH
                )

        pl.semaphore_wait(barrier, ctx - own_keeper)

        def block(index):
            return own_ref.at[pl.ds(pl.multiple_of(index * rows, rows), rows), :]

        def landing(stream, position):
            return out_ref.at[
                pl.ds(pl.multiple_of(stream * rows, rows), rows),
                pl.ds(pl.multiple_of(position * cols, cols), cols),
            ]

        slot = place * fsdp + mine

        def copy_to(step):
            other = lax.rem(me + step, ctx)
            return pltpu.make_async_remote_copy(
                block(other),
                landing(mine, place),
                send_sems.at[step],
                recv_sems.at[slot],
                device_id=(other, keeper),
                device_id_type=MESH,
            )

        kept = pltpu.make_async_copy(block(me), landing(mine, place), send_sems.at[0])
        for step in range(1, ctx):
            copy_to(step).start()

        @pl.when(own_keeper == 0)
        def _():
            copy_to(0).start()

        @pl.when(own_keeper == 1)
        def _():
            kept.start()
            kept.wait()

        for step in range(share * fsdp):

            @pl.when(
                jnp.logical_or(mine * share + step // fsdp != me, step % fsdp != mine)
            )
            def _():
                pltpu.make_async_copy(
                    block(0), landing(step % fsdp, step // fsdp), recv_sems.at[step]
                ).wait()

        for step in range(1, ctx):
            copy_to(step).wait_send()

        @pl.when(own_keeper == 0)
        def _():
            copy_to(0).wait_send()

    return comm_call(
        kernel,
        "heads_to_rows",
        collective_id,
        jax.ShapeDtypeStruct((fsdp * rows, share * cols), values.dtype),
        [ANY],
        ANY,
        [DMA((ctx,)), DMA((share * fsdp,))],
        40 * 2**20,
    )(values)


def rows_to_heads(values, collective_id):
    ctx, fsdp = lax.axis_size("ctx"), lax.axis_size("fsdp")
    share = ctx // fsdp
    rows, cols = values.shape[0] // fsdp, values.shape[1] // share

    def kernel(own_ref, out_ref, stage, stage_send, stage_recv, send_sems, recv_sems, done_sem):
        me, mine = lax.axis_index("ctx"), lax.axis_index("fsdp")
        ctx_peers = [(lax.rem(me + step, ctx), mine) for step in range(1, ctx)]
        greet(ctx_peers + [(me, lax.rem(mine + step, fsdp)) for step in range(1, fsdp)])

        def block(stream):
            return own_ref.at[pl.ds(pl.multiple_of(stream * rows, rows), rows), :]

        def landing(index):
            return out_ref.at[pl.ds(pl.multiple_of(index * rows, rows), rows), :]

        steps = [2, 3, 1]
        staged = {
            step: send(
                block(lax.rem(mine + step, fsdp)),
                stage.at[fsdp - step],
                stage_send.at[step],
                stage_recv.at[fsdp - step],
                (me, lax.rem(mine + step, fsdp)),
            )
            for step in steps
        }

        def piece(step, place):
            span = pl.ds(place * cols, cols)
            if step == 0:
                return own_ref.at[pl.ds(pl.multiple_of(mine * rows, rows), rows), span]
            return stage.at[step, :, span]

        def target(step, place):
            return lax.rem(mine + step, fsdp) * share + place

        def copy_to(step, place):
            return pltpu.make_async_remote_copy(
                piece(step, place),
                landing(me),
                send_sems.at[step * share + place],
                recv_sems.at[me],
                device_id=(target(step, place), mine),
                device_id_type=MESH,
            )

        def keep(step, place):
            return pltpu.make_async_copy(
                piece(step, place), landing(me), send_sems.at[step * share + place]
            )

        for step in [0, 1, 2, 3]:
            if step > 0:
                staged[fsdp - step].wait_recv()
            for place in range(share):
                far = target(step, place) != me
                pl.when(far)(copy_to(step, place).start)
                pl.when(jnp.logical_not(far))(keep(step, place).start)
        for step in range(1, ctx):
            source = lax.rem(me + step, ctx)
            pltpu.make_async_copy(
                piece(0, 0), landing(source), recv_sems.at[source]
            ).wait()
        for step in range(fsdp):
            for place in range(share):
                far = target(step, place) != me
                pl.when(far)(copy_to(step, place).wait_send)
                pl.when(jnp.logical_not(far))(keep(step, place).wait)
        for copy in staged.values():
            copy.wait_send()
        for peer in ctx_peers:
            pl.semaphore_signal(done_sem, inc=1, device_id=peer, device_id_type=MESH)
        pl.semaphore_wait(done_sem, ctx - 1)

    return comm_call(
        kernel,
        "rows_to_heads",
        collective_id,
        jax.ShapeDtypeStruct((ctx * rows, cols), values.dtype),
        [ANY],
        ANY,
        [
            pltpu.VMEM((fsdp, rows, share * cols), values.dtype),
            DMA((fsdp,)),
            DMA((fsdp,)),
            DMA((ctx,)),
            DMA((ctx,)),
            pltpu.SemaphoreType.REGULAR,
        ],
        2**20,
    )(values)


def swap(values, axis, bit):
    return lax.ppermute(values, axis, [(i, i ^ bit) for i in range(lax.axis_size(axis))])


def reduce_then_gather(partial, extras, out_shapes, chunk_math, name, collective_id, crossed, bulk):
    ctx, fsdp = lax.axis_size("ctx"), lax.axis_size("fsdp")
    rows, width = partial.shape[0] // fsdp, partial.shape[1]
    chunks = 4
    size = rows // chunks
    count = len(extras)
    cols = width // ctx
    if crossed:
        out_shapes = out_shapes + [jax.ShapeDtypeStruct((rows, width // 2), jnp.bfloat16)]
    bulk_count, out_count = len(bulk), len(out_shapes)

    def kernel(*refs):
        part_ref, extra_refs = refs[0], refs[1 : 1 + count]
        bulk_refs, refs = refs[1 + count : 1 + count + bulk_count], refs[1 + count + bulk_count :]
        all_ref, out_refs = refs[0], refs[1 : 1 + out_count]
        bulk_out_refs, refs = refs[1 + out_count : 1 + out_count + bulk_count], refs[1 + out_count :]
        near_own, near_far, far_sum, far_own, sems, cross_sems, bulk_sems = refs[bulk_count:]
        me, mine = lax.axis_index("ctx"), lax.axis_index("fsdp")
        flip = 1 - 2 * lax.rem(mine, 2)
        core = mine + flip
        chip = lax.rem(mine + 2, fsdp)
        diagonal = lax.rem(core + 2, fsdp)
        to_x = (flipped(me, 1), mine)
        greet([(me, core), (me, chip)] + ([to_x] if crossed or bulk else []))

        def span(block, i):
            return pl.ds(pl.multiple_of(block * rows + i * size, size), size)

        def sem(kind, i):
            return sems.at[2 * kind, i], sems.at[2 * kind + 1, i]

        copies = []
        from_core_far, from_core_own, from_chip = [], [], []
        exchanged = [
            send(source, target, bulk_sems.at[0, i], bulk_sems.at[1, i], to_x)
            for i, (source, target) in enumerate(zip(bulk_refs, bulk_out_refs))
        ]
        for i in range(chunks):
            copy = send(
                part_ref.at[span(diagonal, i), :], near_far.at[i], *sem(0, i), (me, core)
            )
            from_core_far.append(copy)
        for i in range(chunks):
            copy = send(part_ref.at[span(core, i), :], near_own.at[i], *sem(1, i), (me, core))
            from_core_own.append(copy)
        for i in range(chunks):
            from_core_far[i].wait_recv()
            both = part_ref[span(chip, i), :].astype(jnp.float32) + near_far[i].astype(jnp.float32)
            far_sum[i] = both.astype(jnp.bfloat16)
            from_chip.append(send(far_sum.at[i], far_own.at[i], *sem(2, i), (me, chip)))
        to_chip = []
        for i in range(chunks):
            from_core_own[i].wait_recv()
            from_chip[i].wait_recv()
            total = (
                part_ref[span(mine, i), :].astype(jnp.float32)
                + near_own[i].astype(jnp.float32)
                + far_own[i].astype(jnp.float32)
            )
            all_ref[span(mine, i), :] = chunk_math(
                i, pl.ds(i * size, size), total, extra_refs, out_refs
            ).astype(jnp.bfloat16)
            own = all_ref.at[span(mine, i), :]
            to_chip.append(send(own, own, *sem(3, i), (me, chip)))
            copies.append(send(own, own, *sem(4, i), (me, core)))
            for run in range(ctx // 2 if crossed else 0):
                start = pl.multiple_of((2 * run + 1 - lax.rem(me, 2)) * cols, cols)
                copies.append(
                    send(
                        all_ref.at[span(mine, i), pl.ds(start, cols)],
                        out_refs[-1].at[pl.ds(i * size, size), pl.ds(run * cols, cols)],
                        cross_sems.at[0, i, run],
                        cross_sems.at[1, i, run],
                        to_x,
                    )
                )
        for i in range(chunks):
            to_chip[i].wait_recv()
            other = all_ref.at[span(chip, i), :]
            copies.append(send(other, other, *sem(5, i), (me, core)))
        for copy in copies + exchanged:
            copy.wait_recv()
        for copy in from_core_far + from_core_own + from_chip + to_chip + copies + exchanged:
            copy.wait_send()

    return comm_call(
        kernel,
        name,
        collective_id,
        [jax.ShapeDtypeStruct(partial.shape, jnp.bfloat16)]
        + out_shapes
        + [jax.ShapeDtypeStruct(values.shape, values.dtype) for values in bulk],
        [VMEM] * (1 + count) + [ANY] * bulk_count,
        [VMEM] * (1 + out_count) + [ANY] * bulk_count,
        [
            pltpu.VMEM((chunks, size, width), jnp.bfloat16),
            pltpu.VMEM((chunks, size, width), jnp.bfloat16),
            pltpu.VMEM((chunks, size, width), jnp.bfloat16),
            pltpu.VMEM((chunks, size, width), jnp.bfloat16),
            DMA((12, chunks)),
            DMA((2, chunks, ctx // 2)),
            DMA((2, max(1, bulk_count))),
        ],
        100 * 2**20,
    )(partial, *extras, *bulk)


def norm_chunk(index, span, total, extra_refs, out_refs):
    tokens_ref, gain_ref = extra_refs
    mixed = tokens_ref[span, :].astype(jnp.float32) + total
    out_refs[0][span, :] = mixed
    return mixed * rms_unit(mixed) * gain_ref[...]


def norm_back_chunk(index, span, total, extra_refs, out_refs):
    mixed_ref, gain_ref, dy_ref = extra_refs
    mixed = mixed_ref[span, :]
    scale = rms_unit(mixed)
    unit = mixed * scale
    pulled = total * gain_ref[...]
    grad = dy_ref[span, :].astype(jnp.float32) + scale * (
        pulled - unit * jnp.mean(unit * pulled, axis=-1, keepdims=True)
    )
    out_refs[0][span, :] = grad
    gain_grad = jnp.sum(total * unit, axis=0, keepdims=True)
    if index == 0:
        out_refs[1][...] = gain_grad
    else:
        out_refs[1][...] += gain_grad
    return grad


ROUTER_ROWS = 16


def one_hot(slots, capacity):
    return lax.broadcasted_iota(jnp.int32, (capacity, slots.shape[1]), 0) == slots


def slots_of(pairs, experts, top):
    count = len(pairs)
    blocks, _, rows = pairs[0].shape
    absent = float(rows * top)

    def kernel(*refs):
        for pairs_ref, out_ref in zip(refs[:count], refs[count:]):
            out_ref[...] = jnp.full(out_ref.shape, -1, jnp.int32)
            for b in range(blocks):
                rank_rows = []
                for expert in range(experts):
                    rank = jnp.full((1, rows), absent, jnp.float32)
                    for k in range(top):
                        rank = jnp.where(
                            pairs_ref[b, k : k + 1, :] == expert,
                            pairs_ref[b, top + k : top + k + 1, :].astype(jnp.float32),
                            rank,
                        )
                    rank_rows.append(rank)
                filler = jnp.full((rows - experts, rows), absent, jnp.float32)
                by_column = jnp.concatenate(rank_rows + [filler], axis=0).T
                for expert, rank in enumerate(rank_rows):
                    earlier = jnp.where(by_column[:, expert : expert + 1] < rank, 1.0, 0.0)
                    slot = jnp.where(rank < absent, jnp.sum(earlier, axis=0, keepdims=True), -1.0)
                    out_ref[expert : expert + 1, b * rows : (b + 1) * rows] = slot.astype(jnp.int32)

    shape = jax.ShapeDtypeStruct((ROUTER_ROWS, blocks * rows), jnp.int32)
    return pl.pallas_call(
        kernel,
        out_shape=[shape] * count,
        in_specs=[VMEM] * count,
        out_specs=[VMEM] * count,
        cost_estimate=pl.CostEstimate(flops=10**7, bytes_accessed=2**20, transcendentals=0),
        name="slots_of",
    )(*pairs)


def run_experts(group, dy_all, slots, router, w_gate, w_up, w_down, blocks, capacity):
    experts, width, units = w_gate.shape
    total = group.shape[0]
    rows = total // blocks
    held = blocks * capacity
    f32, bf16 = jnp.float32, jnp.bfloat16

    def kernel(
        group_ref,
        dy_ref,
        slots_ref,
        router_ref,
        gate_ref,
        up_ref,
        down_ref,
        moved_ref,
        grad_ref,
        g_router_ref,
        scaled_ref,
        gate_low_ref,
        up_low_ref,
        disp,
        ins,
        dys,
        probs,
        prob_grad,
    ):
        expert = pl.program_id(0)

        def block_rows(b):
            return pl.ds(b * rows, rows)

        @pl.when(expert == 0)
        def _():
            logits = lax.dot_general(
                router_ref[...],
                group_ref[...],
                (((1,), (1,)), ((), ())),
                preferred_element_type=f32,
            )
            real = lax.broadcasted_iota(jnp.int32, logits.shape, 0) < experts
            logits = jnp.where(real, logits, MASKED)
            weights = jnp.exp(logits - jnp.max(logits, axis=0, keepdims=True))
            probs[...] = weights / jnp.sum(weights, axis=0, keepdims=True)
            prob_grad[...] = jnp.zeros_like(prob_grad)
            for b in range(blocks):
                for e in range(experts):
                    disp[b, pl.ds(e * capacity, capacity), :] = (
                        one_hot(slots_ref[pl.ds(e, 1), block_rows(b)], capacity)
                        .astype(f32)
                        .astype(bf16)
                    )
                for source, target in ((group_ref, ins), (dy_ref, dys)):
                    picked = jnp.dot(
                        disp[b], source[block_rows(b), :], preferred_element_type=f32
                    ).astype(bf16)
                    for e in range(experts):
                        target[e, pl.ds(b * capacity, capacity), :] = picked[
                            e * capacity : (e + 1) * capacity
                        ]

        expert_in, slot_dy = ins[expert], dys[expert]
        gate_matrix, up_matrix, down_matrix = gate_ref[0], up_ref[0], down_ref[0]
        gate_pre = jnp.dot(expert_in, gate_matrix, preferred_element_type=f32)
        up_pre = jnp.dot(expert_in, up_matrix, preferred_element_type=f32)
        raw_grad = lax.dot_general(
            slot_dy, down_matrix, (((1,), (1,)), ((), ())), preferred_element_type=f32
        )
        own_probs = probs[pl.ds(expert, 1), :]
        own_slots = slots_ref[pl.ds(expert, 1), :]
        hots = [
            one_hot(own_slots[:, b * rows : (b + 1) * rows], capacity) for b in range(blocks)
        ]
        value = jnp.concatenate(
            [
                jnp.sum(
                    jnp.where(hots[b], own_probs[:, b * rows : (b + 1) * rows], 0.0),
                    axis=1,
                    keepdims=True,
                )
                for b in range(blocks)
            ],
            axis=0,
        )
        sigma = 1.0 / (1.0 + jnp.exp(-gate_pre))
        silu = gate_pre * sigma
        hidden = (silu * up_pre).astype(bf16)
        hidden_f = hidden.astype(f32)
        value_grad = jnp.sum(hidden_f * raw_grad, axis=1, keepdims=True)
        hidden_grad = raw_grad * value
        gate_low = (hidden_grad * up_pre * sigma * (1.0 + gate_pre * (1.0 - sigma))).astype(bf16)
        up_low = (hidden_grad * silu).astype(bf16)
        scaled = (hidden_f * value).astype(bf16)
        scaled_ref[0] = scaled
        gate_low_ref[0] = gate_low
        up_low_ref[0] = up_low
        for b in range(blocks):
            prob_grad[expert, :, block_rows(b)] = jnp.sum(
                jnp.where(hots[b], value_grad[b * capacity : (b + 1) * capacity], 0.0),
                axis=0,
                keepdims=True,
            )
        dys[expert] = jnp.dot(scaled, down_matrix, preferred_element_type=f32).astype(bf16)
        ins[expert] = (
            lax.dot_general(
                gate_low, gate_matrix, (((1,), (1,)), ((), ())), preferred_element_type=f32
            )
            + lax.dot_general(
                up_low, up_matrix, (((1,), (1,)), ((), ())), preferred_element_type=f32
            )
        ).astype(bf16)

        @pl.when(expert == experts - 1)
        def _():
            grads = jnp.concatenate([prob_grad[e] for e in range(ROUTER_ROWS)], axis=0)
            weights = probs[...]
            logit_grad = (
                weights * (grads - jnp.sum(weights * grads, axis=0, keepdims=True))
            ).astype(bf16)
            g_router_ref[...] = jnp.dot(logit_grad, group_ref[...], preferred_element_type=f32)
            for b in range(blocks):
                for source, target in ((dys, moved_ref), (ins, grad_ref)):
                    gathered = jnp.concatenate(
                        [source[e, pl.ds(b * capacity, capacity), :] for e in range(experts)],
                        axis=0,
                    )
                    back = lax.dot_general(
                        disp[b], gathered, (((0,), (0,)), ((), ())), preferred_element_type=f32
                    )
                    if target is grad_ref:
                        back = back + lax.dot_general(
                            logit_grad[:, b * rows : (b + 1) * rows],
                            router_ref[...],
                            (((0,), (0,)), ((), ())),
                            preferred_element_type=f32,
                        )
                    target[block_rows(b), :] = back.astype(bf16)

    def whole(shape):
        return pl.BlockSpec(shape, lambda e: (0,) * len(shape))

    def by_expert(shape):
        return pl.BlockSpec((1,) + shape, lambda e: (e, 0, 0))

    return pl.pallas_call(
        kernel,
        grid=(experts,),
        out_shape=[
            jax.ShapeDtypeStruct((total, width), bf16),
            jax.ShapeDtypeStruct((total, width), bf16),
            jax.ShapeDtypeStruct((ROUTER_ROWS, width), f32),
        ]
        + [jax.ShapeDtypeStruct((experts, held, units), bf16)] * 3,
        in_specs=[
            whole((total, width)),
            whole((total, width)),
            whole((ROUTER_ROWS, total)),
            whole((ROUTER_ROWS, width)),
            by_expert((width, units)),
            by_expert((width, units)),
            by_expert((units, width)),
        ],
        out_specs=[
            whole((total, width)),
            whole((total, width)),
            whole((ROUTER_ROWS, width)),
        ]
        + [by_expert((held, units))] * 3,
        scratch_shapes=[
            pltpu.VMEM((blocks, experts * capacity, rows), bf16),
            pltpu.VMEM((experts, held, width), bf16),
            pltpu.VMEM((experts, held, width), bf16),
            pltpu.VMEM((ROUTER_ROWS, total), f32),
            pltpu.VMEM((ROUTER_ROWS, 1, total), f32),
        ],
        compiler_params=pltpu.CompilerParams(vmem_limit_bytes=60 * 2**20),
        cost_estimate=pl.CostEstimate(
            flops=30 * 10**9, bytes_accessed=30 * 2**20, transcendentals=10**6
        ),
        name="run_experts",
    )(group, dy_all, slots, router, w_gate, w_up, w_down)


def expert_grads(slot_own, slot_other, rows_own, rows_other, slots_own, slots_other, capacity, slots_left):
    kinds = len(slot_own)
    experts, held, units = slot_own[0].shape
    total, half = rows_other.shape
    blocks = held // capacity
    rows = total // blocks
    ctx = lax.axis_size("ctx")
    cols = 2 * half // ctx
    f32, bf16 = jnp.float32, jnp.bfloat16

    def kernel(*refs):
        own_refs, other_refs = refs[:kinds], refs[kinds : 2 * kinds]
        rows_own_ref, rows_other_ref, slots_own_ref, slots_other_ref = refs[2 * kinds : 2 * kinds + 4]
        out_ref, held_rows = refs[2 * kinds + 4 :]
        expert = pl.program_id(0)
        me = lax.axis_index("ctx")

        def columns(side, run):
            if side == 1:
                return pl.ds(run * cols, cols)
            return pl.ds(pl.multiple_of((2 * run + lax.rem(me, 2)) * cols, cols), cols)

        @pl.when(expert == 0)
        def _():
            for side, slots_ref, source in (
                (0, slots_own_ref, rows_own_ref),
                (1, slots_other_ref, rows_other_ref),
            ):
                for b in range(blocks):
                    span = pl.ds(b * rows, rows)
                    disp = jnp.concatenate(
                        [
                            one_hot(slots_ref[pl.ds(e, 1), span], capacity).astype(f32)
                            for e in range(experts)
                        ],
                        axis=0,
                    ).astype(bf16)
                    for run in range(ctx // 2):
                        picked = jnp.dot(
                            disp, source[span, columns(side, run)], preferred_element_type=f32
                        ).astype(bf16)
                        for e in range(experts):
                            held_rows[
                                e,
                                pl.ds(side * held + b * capacity, capacity),
                                pl.ds(run * cols, cols),
                            ] = picked[e * capacity : (e + 1) * capacity]

        low, high = lax.rem(me // 2, 2), me // 4
        stacked = [
            jnp.concatenate([own[0], other[0]], axis=0) for own, other in zip(own_refs, other_refs)
        ]
        contract = (((0,), (0,)), ((), ()))
        for run in range(ctx // 2):
            kept = jnp.where(low == run % 2, 1, 0)
            far = jnp.where(high == run // 2, 0, 1)
            features = held_rows[expert, :, pl.ds(run * cols, cols)]
            for kind in range(kinds):
                pair = (stacked[kind], features) if slots_left else (features, stacked[kind])
                out_ref[kind, pl.ds(kept, 1), pl.ds(far, 1), 0] = lax.dot_general(
                    *pair, contract, preferred_element_type=f32
                ).astype(bf16)[None, None]

    def whole(shape):
        return pl.BlockSpec(shape, lambda e: (0,) * len(shape))

    slot_spec = pl.BlockSpec((1, held, units), lambda e: (e, 0, 0))
    return pl.pallas_call(
        kernel,
        grid=(experts,),
        out_shape=jax.ShapeDtypeStruct((kinds, 2, 2, experts, units, cols), bf16),
        in_specs=[slot_spec] * (2 * kinds)
        + [whole((total, 2 * half)), whole((total, half))]
        + [whole((ROUTER_ROWS, total))] * 2,
        out_specs=pl.BlockSpec((kinds, 2, 2, 1, units, cols), lambda e: (0, 0, 0, e, 0, 0)),
        scratch_shapes=[pltpu.VMEM((experts, 2 * held, half), bf16)],
        compiler_params=pltpu.CompilerParams(vmem_limit_bytes=60 * 2**20),
        cost_estimate=pl.CostEstimate(flops=0, bytes_accessed=2**20, transcendentals=0),
        name="expert_grads",
    )(*slot_own, *slot_other, rows_own, rows_other, slots_own, slots_other)


def pick_half(values, parity_flip):
    ctx = lax.axis_size("ctx")
    total, width = values.shape
    cols = width // ctx

    def kernel(in_ref, out_ref):
        parity = lax.rem(lax.axis_index("ctx") + parity_flip, 2)
        for run in range(ctx // 2):
            start = pl.multiple_of((2 * run + parity) * cols, cols)
            out_ref[:, pl.ds(run * cols, cols)] = in_ref[:, pl.ds(start, cols)]

    return pl.pallas_call(
        kernel,
        out_shape=jax.ShapeDtypeStruct((total, width // 2), values.dtype),
        in_specs=[VMEM],
        out_specs=VMEM,
        cost_estimate=pl.CostEstimate(flops=0, bytes_accessed=2**22, transcendentals=0),
        name="pick_half",
    )(values)


def roll_half(values):
    return pltpu.roll(values, values.shape[1] // 2, 1)


def allowed_keys(first_ref, last_ref, span, places):
    return (places >= first_ref[span, :]) & (places <= last_ref[span, :])


def attend(projected, scales, gains, cosine, sine_part, first, last, places, cols):
    total = projected.shape[0]
    head_dim = cosine.shape[1]
    heads = cols // head_dim
    size = math.gcd(total, 256)
    score_scale = head_dim ** (-0.5)
    f32, bf16 = jnp.float32, jnp.bfloat16

    def kernel(
        lin_ref,
        scales_ref,
        gains_ref,
        cos_ref,
        sin_ref,
        first_ref,
        last_ref,
        places_ref,
        low_ref,
        attended_ref,
        attended_low_ref,
        top_ref,
    ):
        for kind in range(3):
            for h in range(heads):
                span = pl.ds(kind * cols + h * head_dim, head_dim)
                values = lin_ref[:, span]
                if kind < 2:
                    values = values * scales_ref[:, kind : kind + 1] * gains_ref[:, span]
                    values = values * cos_ref[...] + roll_half(values) * sin_ref[...]
                low_ref[:, span] = values.astype(bf16)
        for h in range(heads):
            head = pl.ds(h * head_dim, head_dim)
            keys = low_ref[:, pl.ds(cols + h * head_dim, head_dim)]
            values = low_ref[:, pl.ds(2 * cols + h * head_dim, head_dim)]

            def step(b, carry):
                span = pl.ds(pl.multiple_of(b * size, size), size)
                scores = lax.dot_general(
                    low_ref[span, head],
                    keys,
                    (((1,), (1,)), ((), ())),
                    preferred_element_type=f32,
                )
                allowed = allowed_keys(first_ref, last_ref, span, places_ref[...])
                scores = jnp.where(allowed, scores * score_scale, MASKED)
                top = jnp.max(scores, axis=1, keepdims=True)
                weights = jnp.exp(scores - top)
                sums = jnp.sum(weights, axis=1, keepdims=True)
                probs = (weights * (1.0 / sums)).astype(bf16)
                attended = jnp.dot(probs, values, preferred_element_type=f32)
                attended_ref[span, head] = attended
                attended_low_ref[span, head] = attended.astype(bf16)
                top_ref[span, head] = jnp.broadcast_to(top + jnp.log(sums), (size, head_dim))
                return carry

            lax.fori_loop(0, total // size, step, 0)

    return pl.pallas_call(
        kernel,
        out_shape=[
            jax.ShapeDtypeStruct((total, 3 * cols), bf16),
            jax.ShapeDtypeStruct((total, cols), f32),
            jax.ShapeDtypeStruct((total, cols), bf16),
            jax.ShapeDtypeStruct((total, cols), f32),
        ],
        in_specs=[VMEM] * 8,
        out_specs=[VMEM] * 4,
        compiler_params=pltpu.CompilerParams(vmem_limit_bytes=60 * 2**20),
        cost_estimate=pl.CostEstimate(
            flops=2 * 10**9, bytes_accessed=20 * 2**20, transcendentals=2 * 10**6
        ),
        name="attend",
    )(projected, scales, gains, cosine, sine_part, first, last, places)


def attend_back(
    output_grad, low, attended, top, projected, scales, gains, cosine, sine_part, first, last, places
):
    total, cols = output_grad.shape
    head_dim = cosine.shape[1]
    heads = cols // head_dim
    size = math.gcd(total, 256)
    score_scale = head_dim ** (-0.5)
    f32, bf16 = jnp.float32, jnp.bfloat16
    contract_rows = (((0,), (0,)), ((), ()))

    def kernel(
        grad_ref,
        low_ref,
        attended_ref,
        top_ref,
        lin_ref,
        scales_ref,
        gains_ref,
        cos_ref,
        sin_ref,
        first_ref,
        last_ref,
        places_ref,
        back_ref,
        value_ref,
        gain_ref,
        sums_ref,
        query_grad,
        key_grad,
        value_grad,
    ):
        totals = [jnp.zeros((total, 1), f32) for _ in range(2)]
        for h in range(heads):
            head = pl.ds(h * head_dim, head_dim)
            keys = low_ref[:, pl.ds(cols + h * head_dim, head_dim)]
            values = low_ref[:, pl.ds(2 * cols + h * head_dim, head_dim)]
            key_grad[...] = jnp.zeros_like(key_grad)
            value_grad[...] = jnp.zeros_like(value_grad)

            def step(b, carry):
                span = pl.ds(pl.multiple_of(b * size, size), size)
                queries, grads = low_ref[span, head], grad_ref[span, head]
                scores = lax.dot_general(
                    queries, keys, (((1,), (1,)), ((), ())), preferred_element_type=f32
                )
                allowed = allowed_keys(first_ref, last_ref, span, places_ref[...])
                scores = jnp.where(allowed, scores * score_scale, MASKED)
                probs = jnp.exp(scores - top_ref[span, head][:, :1])
                prob_grad = lax.dot_general(
                    grads, values, (((1,), (1,)), ((), ())), preferred_element_type=f32
                )
                delta = jnp.sum(
                    grads.astype(f32) * attended_ref[span, head], axis=1, keepdims=True
                )
                score_grad = (probs * (prob_grad - delta)).astype(bf16)
                query_grad[span, :] = (
                    jnp.dot(score_grad, keys, preferred_element_type=f32) * score_scale
                )
                key_grad[...] += lax.dot_general(
                    score_grad, queries, contract_rows, preferred_element_type=f32
                )
                value_grad[...] += lax.dot_general(
                    probs.astype(bf16), grads, contract_rows, preferred_element_type=f32
                )
                return carry

            lax.fori_loop(0, total // size, step, 0)
            value_ref[:, head] = value_grad[...].astype(bf16)
            for kind, grad in ((0, query_grad[...]), (1, key_grad[...] * score_scale)):
                span = pl.ds(kind * cols + h * head_dim, head_dim)
                unit = lin_ref[:, span] * scales_ref[:, kind : kind + 1]
                grad = grad * cos_ref[...] - roll_half(grad) * sin_ref[...]
                gain_ref[kind, :, head] = jnp.sum(grad * unit, axis=0, keepdims=True)
                grad = grad * gains_ref[:, span]
                back_ref[kind, :, head] = grad
                totals[kind] = totals[kind] + jnp.sum(grad * unit, axis=1, keepdims=True)
        for kind in range(2):
            sums_ref[:, kind : kind + 1] = totals[kind]

    return pl.pallas_call(
        kernel,
        out_shape=[
            jax.ShapeDtypeStruct((2, total, cols), f32),
            jax.ShapeDtypeStruct((total, cols), bf16),
            jax.ShapeDtypeStruct((2, 1, cols), f32),
            jax.ShapeDtypeStruct((total, 2), f32),
        ],
        in_specs=[VMEM] * 12,
        out_specs=[VMEM] * 4,
        scratch_shapes=[pltpu.VMEM((total, head_dim), f32)] * 3,
        compiler_params=pltpu.CompilerParams(vmem_limit_bytes=60 * 2**20),
        cost_estimate=pl.CostEstimate(flops=0, bytes_accessed=2**20, transcendentals=0),
        name="attend_back",
    )(
        output_grad,
        low,
        attended,
        top,
        projected,
        scales,
        gains,
        cosine,
        sine_part,
        first,
        last,
        places,
    )


def flipped(index, bit):
    return index + bit * (1 - 2 * lax.rem(index // bit, 2))


def add_into(target, *sources):
    step = target.shape[0] if len(target.shape) == 3 else target.shape[0] // 64

    def body(i, carry):
        span = i if len(target.shape) == 3 else pl.ds(pl.multiple_of(i * 64, 64), 64)
        total = sources[0][span].astype(jnp.float32)
        for source in sources[1:]:
            total = total + source[span].astype(jnp.float32)
        target[span] = total.astype(target.dtype)
        return carry

    lax.fori_loop(0, step, body, 0)


def finish_sums(downs, ups, low_far, low_own, gate_far, normed_part, out_part, qkv_part, small, tokens, mixed_grad, gain, collective_id):
    ctx, fsdp = lax.axis_size("ctx"), lax.axis_size("fsdp")
    experts, units, cols = low_far.shape
    kinds = 3
    rows, width = tokens.shape
    part = out_part.shape[0]
    f32, bf16 = jnp.float32, jnp.bfloat16
    small_rows, small_cols = small.shape[0], small.shape[1] // fsdp
    copies_most = 64

    def kernel(
        downs_ref,
        ups_ref,
        low_far_ref,
        low_own_ref,
        gate_far_ref,
        normed_ref,
        g_out_ref,
        g_qkv_ref,
        small_ref,
        tokens_ref,
        mixed_ref,
        gain_ref,
        down_ref,
        gate_ref,
        up_ref,
        input_ref,
        out_ref,
        qkv_ref,
        sums_ref,
        kept,
        kept_low,
        kept_high,
        normed_own,
        normed_x,
        normed_low,
        normed_high,
        out_own,
        out_x,
        out_low,
        out_high,
        qkv_own,
        qkv_core,
        qkv_chip,
        qkv_sum,
        dealt,
        small_parts,
        small_sum,
        small_held,
        sends,
        recvs,
        locals_,
        deal_sems,
    ):
        me, mine = lax.axis_index("ctx"), lax.axis_index("fsdp")
        x, low, high = lax.rem(me, 2), lax.rem(me // 2, 2), me // 4
        to_x, to_low, to_high = ((flipped(me, bit), mine) for bit in (1, 2, 4))
        core, chip = flipped(mine, 1), flipped(mine, 2)
        diagonal = flipped(core, 2)
        ctx_peers = [(lax.rem(me + step, ctx), mine) for step in range(1, ctx)]
        near = [lax.rem(mine + step, fsdp) for step in range(1, fsdp)]
        greet(ctx_peers + [(me, other) for other in near])
        used, used_local, all_sends, loads = [0], [0], [], {}

        def push(source, target, peer):
            i = used[0]
            used[0] += 1
            copy = send(source, target, sends.at[i], recvs.at[i], peer)
            all_sends.append(copy)
            return copy

        def load(source, target):
            i = used_local[0]
            used_local[0] += 1
            copy = pltpu.make_async_copy(source, target, locals_.at[i])
            copy.start()
            return copy

        def normed_block(a, b, other):
            side = 1 - x if other else x
            block = (high + a - 2 * a * high) * 4 + (low + b - 2 * b * low) * 2 + side
            return normed_ref.at[pl.ds(pl.multiple_of(block * rows, rows), rows), :]

        def out_block(a, b, other):
            side = 1 - x if other else x
            block = (high + a - 2 * a * high) * 4 + (low + b - 2 * b * low) * 2 + side
            return g_out_ref.at[:, pl.ds(pl.multiple_of(block * cols, cols), cols)]

        def qkv_block(index):
            return g_qkv_ref.at[pl.ds(pl.multiple_of(index * part, part), part), :]

        def columns(index):
            return pl.ds(pl.multiple_of(index * small_cols, small_cols), small_cols)

        order = ((1, 1), (0, 1), (1, 0), (0, 0))
        small_copies = [
            push(small_ref.at[:, columns(other)], small_parts.at[i], (me, other))
            for i, other in enumerate(near)
        ]
        normed_copies = {
            ab: push(normed_block(*ab, True), normed_x.at[ab[0], ab[1]], to_x) for ab in order
        }

        def push_low(kind, a):
            return push(ups_ref.at[kind - 1, 0, a], kept_low.at[kind, a], to_low)

        low_copies = {(2, 1): push_low(2, 1)}
        early = {
            (0, 1): load(low_far_ref, kept_low.at[0, 1]),
            (1, 1): load(gate_far_ref, kept_low.at[1, 1]),
            (0, 0): load(low_own_ref, kept_low.at[0, 0]),
        }
        kept_loads = {
            (kind, a): load(
                downs_ref.at[0, 1, a] if kind == 0 else ups_ref.at[kind - 1, 1, a],
                kept.at[kind, a],
            )
            for a in (1, 0)
            for kind in range(kinds)
        }
        qkv_copies = [
            push(qkv_block(diagonal), qkv_core.at[1], (me, core)),
            push(qkv_block(core), qkv_core.at[0], (me, core)),
        ]
        qkv_loads = [
            load(qkv_block(chip), qkv_own.at[1]),
            load(qkv_block(mine), qkv_own.at[0]),
        ]
        normed_loads = {
            ab: load(normed_block(*ab, False), normed_own.at[ab[0], ab[1]]) for ab in order
        }
        out_loads = {ab: load(out_block(*ab, False), out_own.at[ab[0], ab[1]]) for ab in order}

        total = small_ref[:, columns(mine)]
        for i, copy in enumerate(small_copies):
            copy.wait_recv()
            total = total + small_parts[i]
        small_sum[...] = total
        small_wide = [push(small_sum, small_held.at[i], peer) for i, peer in enumerate(ctx_peers)]

        qkv_copies[0].wait_recv()
        qkv_loads[0].wait()
        add_into(qkv_core.at[1], qkv_own.at[1], qkv_core.at[1])
        chip_copy = push(qkv_core.at[1], qkv_chip, (me, chip))

        def to_low_side(copies, loads, own, from_x, from_low, a):
            copies[a, 1].wait_recv()
            loads[a, 1].wait()
            add_into(from_x.at[a, 1], own.at[a, 1], from_x.at[a, 1])
            return push(from_x.at[a, 1], from_low.at[a], to_low)

        def to_high_side(copies, loads, lows, own, from_x, from_low, from_high):
            copies[1, 0].wait_recv()
            loads[1, 0].wait()
            lows[1].wait_recv()
            add_into(from_x.at[1, 0], own.at[1, 0], from_x.at[1, 0], from_low.at[1])
            return push(from_x.at[1, 0], from_high, to_high)

        def arrived(kind, a):
            if (kind, a) in early:
                early[kind, a].wait()
            else:
                low_copies[kind, a].wait_recv()

        def experts_high(kind):
            arrived(kind, 1)
            kept_loads[kind, 1].wait()
            add_into(kept_low.at[kind, 1], kept.at[kind, 1], kept_low.at[kind, 1])
            return push(kept_low.at[kind, 1], kept_high.at[kind], to_high)

        high_copies = {0: experts_high(0)}
        normed_args = (normed_copies, normed_loads)
        normed_lows = {1: to_low_side(*normed_args, normed_own, normed_x, normed_low, 1)}
        high_copies[1] = experts_high(1)
        normed_lows[0] = to_low_side(*normed_args, normed_own, normed_x, normed_low, 0)
        out_copies = {ab: push(out_block(*ab, True), out_x.at[ab[0], ab[1]], to_x) for ab in order}

        qkv_copies[1].wait_recv()
        qkv_loads[1].wait()
        chip_copy.wait_recv()
        add_into(qkv_sum, qkv_own.at[0], qkv_core.at[0], qkv_chip)

        def deal(kind):
            index = kind * ctx + me
            return pltpu.make_async_remote_copy(
                qkv_sum.at[:, pl.ds(kind * cols, cols)],
                dealt.at[lax.rem(index, kinds)],
                deal_sems.at[0, kind],
                deal_sems.at[1, lax.rem(index, kinds)],
                device_id=(index // kinds, mine),
                device_id_type=MESH,
            )

        def keep(kind):
            return pltpu.make_async_copy(
                qkv_sum.at[:, pl.ds(kind * cols, cols)],
                dealt.at[lax.rem(kind * ctx + me, kinds)],
                deal_sems.at[0, kind],
            )

        def is_far(kind):
            return (kind * ctx + me) // kinds != me

        for kind in range(kinds):
            pl.when(is_far(kind))(deal(kind).start)
            pl.when(jnp.logical_not(is_far(kind)))(keep(kind).start)

        normed_high_copy = to_high_side(
            *normed_args, normed_lows, normed_own, normed_x, normed_low, normed_high
        )
        high_copies[2] = experts_high(2)
        low_copies.update({(kind, 0): push_low(kind, 0) for kind in (1, 2)})
        out_args = (out_copies, out_loads)
        out_lows = {a: to_low_side(*out_args, out_own, out_x, out_low, a) for a in (1, 0)}

        def experts_end(kind):
            arrived(kind, 0)
            kept_loads[kind, 0].wait()
            high_copies[kind].wait_recv()
            target = (down_ref, gate_ref, up_ref)[kind]
            add_into(target, kept.at[kind, 0], kept_low.at[kind, 0], kept_high.at[kind])

        experts_end(0)

        normed_copies[0, 0].wait_recv()
        normed_loads[0, 0].wait()
        normed_lows[0].wait_recv()
        normed_high_copy.wait_recv()

        def norm_step(i, carry):
            span = pl.ds(pl.multiple_of(i * 16, 16), 16)
            grad = (
                normed_own[0, 0, span, :].astype(f32)
                + normed_x[0, 0, span, :].astype(f32)
                + normed_low[0, span, :].astype(f32)
                + normed_high[span, :].astype(f32)
            )
            values = tokens_ref[span, :].astype(f32)
            scale = rms_unit(values)
            unit = values * scale
            pulled = grad * gain_ref[...]
            input_ref[span, :] = mixed_ref[span, :] + scale * (
                pulled - unit * jnp.mean(unit * pulled, axis=-1, keepdims=True)
            )
            return carry

        lax.fori_loop(0, rows // 16, norm_step, 0)

        out_high_copy = to_high_side(*out_args, out_lows, out_own, out_x, out_low, out_high)
        experts_end(1)

        total = small_sum[...]
        for i, copy in enumerate(small_wide):
            copy.wait_recv()
            total = total + small_held[i]
        sums_ref[...] = total

        for kind in range(kinds):
            pl.when(is_far(kind))(deal(kind).wait_send)
            pl.when(jnp.logical_not(is_far(kind)))(keep(kind).wait)
        for slot in range(kinds):

            @pl.when(lax.rem(me * kinds + slot, ctx) != me)
            def _():
                pltpu.make_async_copy(
                    dealt.at[slot], dealt.at[slot], deal_sems.at[1, slot]
                ).wait()

            add_into(qkv_ref.at[:, pl.ds(slot * cols, cols)], dealt.at[slot])

        out_copies[0, 0].wait_recv()
        out_loads[0, 0].wait()
        out_lows[0].wait_recv()
        out_high_copy.wait_recv()
        add_into(out_ref, out_own.at[0, 0], out_x.at[0, 0], out_low.at[0], out_high)
        experts_end(2)
        for copy in all_sends:
            copy.wait_send()

    def block(*shape):
        return pltpu.VMEM(shape, bf16)

    gradient = (experts, units, cols)
    return comm_call(
        kernel,
        "finish_sums",
        collective_id,
        [
            jax.ShapeDtypeStruct(gradient, f32),
            jax.ShapeDtypeStruct(gradient, f32),
            jax.ShapeDtypeStruct(gradient, f32),
            jax.ShapeDtypeStruct((rows, width), f32),
            jax.ShapeDtypeStruct((part, cols), f32),
            jax.ShapeDtypeStruct((part, kinds * cols), f32),
            jax.ShapeDtypeStruct((small_rows, small_cols), f32),
        ],
        [ANY] * 8 + [VMEM] * 4,
        [VMEM] * 7,
        [
            block(kinds, 2, *gradient),
            block(kinds, 2, *gradient),
            block(kinds, *gradient),
            block(2, 2, rows, width),
            block(2, 2, rows, width),
            block(2, rows, width),
            block(rows, width),
            block(2, 2, part, cols),
            block(2, 2, part, cols),
            block(2, part, cols),
            block(part, cols),
            block(2, part, kinds * cols),
            block(2, part, kinds * cols),
            block(part, kinds * cols),
            block(part, kinds * cols),
            block(kinds, part, cols),
            pltpu.VMEM((fsdp - 1, small_rows, small_cols), f32),
            pltpu.VMEM((small_rows, small_cols), f32),
            pltpu.VMEM((ctx - 1, small_rows, small_cols), f32),
            DMA((copies_most,)),
            DMA((copies_most,)),
            DMA((32,)),
            DMA((2, kinds)),
        ],
        700 * 2**20,
        56,
    )(
        downs,
        ups,
        low_far,
        low_own,
        gate_far,
        normed_part,
        out_part,
        qkv_part,
        small,
        tokens,
        mixed_grad,
        gain,
    )


def gather_inputs(tokens, w_qkv, dy, row_arrays, blocks, collective_id):
    ctx, fsdp = lax.axis_size("ctx"), lax.axis_size("fsdp")
    rows, width = tokens.shape
    part = w_qkv.shape[0]
    kinds = 3
    cols = width // ctx
    line = ctx // 2
    row_count, block_count = len(row_arrays), len(blocks)
    small_count = row_count + block_count

    def kernel(*refs):
        tokens_ref, w_qkv_ref, dy_ref = refs[:3]
        small_refs = refs[3 : 3 + small_count]
        all_ref, weight_ref, dy_all_ref = refs[3 + small_count : 6 + small_count]
        small_all_refs = refs[6 + small_count : 6 + 2 * small_count]
        refs = refs[6 + 2 * small_count :]
        run_kernel(
            tokens_ref,
            w_qkv_ref,
            dy_ref,
            small_refs,
            all_ref,
            weight_ref,
            dy_all_ref,
            small_all_refs,
            *refs,
        )

    def run_kernel(
        tokens_ref,
        w_qkv_ref,
        dy_ref,
        small_refs,
        all_ref,
        weight_ref,
        dy_all_ref,
        small_all_refs,
        *refs,
    ):
        cross_refs, refs = refs[:block_count], refs[block_count:]
        sends, recvs, line_send, line_recv, cross_send, cross_recv, local_sems = refs
        me, mine = lax.axis_index("ctx"), lax.axis_index("fsdp")
        z, x = me // 2, lax.rem(me, 2)
        to_x = (flipped(me, 1), mine)
        core, chip = (me, flipped(mine, 1)), (me, flipped(mine, 2))
        greet(
            [(lax.rem(me + step, ctx), mine) for step in range(1, ctx)]
            + [(me, lax.rem(mine + step, fsdp)) for step in range(1, fsdp)]
            + [(to_x[0], lax.rem(mine + step, fsdp)) for step in range(1, fsdp)]
        )
        used, used_local, started, kept = [0], [0], [], []

        def push(source, target, peer):
            i = used[0]
            used[0] += 1
            copy = send(source, target, sends.at[i], recvs.at[i], peer)
            started.append(copy)
            return copy

        def load(source, target):
            i = used_local[0]
            used_local[0] += 1
            copy = pltpu.make_async_copy(source, target, local_sems.at[i])
            copy.start()
            kept.append(copy)

        def block(index):
            return all_ref.at[pl.ds(pl.multiple_of(index * rows, rows), rows), :]

        def by_part(ref, index, size):
            return ref.at[pl.ds(pl.multiple_of(index * size, size), size), :]

        def cross(source, away, side):
            index = 2 * (z - away if side == 0 else z + away) + x
            i = side * line + away
            return pltpu.make_async_remote_copy(
                block(index) if source is None else source,
                block(index),
                cross_send.at[i],
                cross_recv.at[i],
                device_id=to_x,
                device_id_type=MESH,
            )

        def along(source, away, side):
            index = 2 * (z - away if side == 0 else z + away) + x
            i = side * line + away
            return pltpu.make_async_remote_copy(
                block(index) if source is None else source,
                block(index),
                line_send.at[i],
                line_recv.at[i],
                device_id=(me + 2 if side == 0 else me - 2, mine),
                device_id_type=MESH,
            )

        def has(away, side):
            return z >= away if side == 0 else z + away < line

        def goes_on(away, side):
            return jnp.logical_and(has(away, side), z < line - 1 if side == 0 else z > 0)

        for side in range(2):
            pl.when(goes_on(0, side))(along(tokens_ref, 0, side).start)
        own_cross = cross(tokens_ref, 0, 0)
        own_cross.start()
        load(tokens_ref, block(me))

        weight_chip = []
        for kind in range(kinds):
            column = pl.ds(pl.multiple_of(kind * width + me * cols, cols), cols)
            target = by_part(weight_ref, mine, part).at[:, pl.ds(kind * cols, cols)]
            source = w_qkv_ref.at[:, column]
            weight_chip.append(push(source, target, chip))
            push(source, target, core)
            load(source, target)
        columns = pl.ds(pl.multiple_of(mine * part, part), part)
        for i, (source, target) in enumerate(zip(small_refs, small_all_refs)):
            if i < row_count:
                target = target.at[:, columns]
            else:
                target = target.at[mine]
            for step in range(1, fsdp):
                push(source, target, (me, lax.rem(mine + step, fsdp)))
            load(source, target)
        for source, target in zip(small_refs[row_count:], cross_refs):
            for step in range(fsdp):
                push(source, target.at[mine], (to_x[0], lax.rem(mine + step, fsdp)))
        dy_chip = push(dy_ref, by_part(dy_all_ref, mine, rows), chip)
        push(dy_ref, by_part(dy_all_ref, mine, rows), core)
        load(dy_ref, by_part(dy_all_ref, mine, rows))

        for away in range(1, line):
            for side in range(2):

                @pl.when(has(away, side))
                def _():
                    i = side * line + away - 1
                    index = 2 * (z - away if side == 0 else z + away) + x
                    pltpu.make_async_copy(tokens_ref, block(index), line_recv.at[i]).wait()
                    cross(None, away, side).start()

                if away < line - 1:
                    pl.when(goes_on(away, side))(along(None, away, side).start)
            if away == 1:
                for copy in weight_chip:
                    copy.wait_recv()
                far = by_part(weight_ref, flipped(mine, 2), part)
                push(far, far, core)
            if away == 2:
                dy_chip.wait_recv()
                far = by_part(dy_all_ref, flipped(mine, 2), rows)
                push(far, far, core)

        own_cross.wait_recv()
        for away in range(1, line):
            for side in range(2):
                pl.when(has(away, side))(cross(None, away, side).wait_recv)
        for copy in started:
            if copy is not dy_chip and not any(copy is other for other in weight_chip):
                copy.wait_recv()
        for copy in kept:
            copy.wait()
        for copy in started + [own_cross]:
            copy.wait_send()
        for away in range(line - 1):
            for side in range(2):
                pl.when(goes_on(away, side))(
                    along(tokens_ref if away == 0 else None, away, side).wait_send
                )
        for away in range(1, line):
            for side in range(2):
                pl.when(has(away, side))(cross(None, away, side).wait_send)

    return comm_call(
        kernel,
        "gather_inputs",
        collective_id,
        [
            jax.ShapeDtypeStruct((ctx * rows, width), tokens.dtype),
            jax.ShapeDtypeStruct((fsdp * part, kinds * cols), w_qkv.dtype),
            jax.ShapeDtypeStruct((fsdp * rows, width), dy.dtype),
        ]
        + [jax.ShapeDtypeStruct((row.shape[0], fsdp * part), row.dtype) for row in row_arrays]
        + [jax.ShapeDtypeStruct((fsdp,) + block.shape, block.dtype) for block in blocks + blocks],
        [ANY] * (3 + small_count),
        [ANY] * (3 + small_count + block_count),
        [
            DMA((56,)),
            DMA((56,)),
            DMA((2 * line,)),
            DMA((2 * line,)),
            DMA((2 * line,)),
            DMA((2 * line,)),
            DMA((16,)),
        ],
        150 * 2**20,
    )(tokens, w_qkv, dy, *row_arrays, *blocks)


def project(tokens, gain, weight):
    total, width = tokens.shape
    wide = weight.shape[1]
    cols = wide // 3
    size = math.gcd(total, 256)
    f32 = jnp.float32

    def kernel(tokens_ref, gain_ref, weight_ref, normed_ref, lin_ref, squares_ref):
        values = tokens_ref[...].astype(f32)
        normed = (values * rms_unit(values) * gain_ref[...]).astype(jnp.bfloat16)
        normed_ref[...] = normed
        lin = jnp.dot(normed, weight_ref[...], preferred_element_type=f32)
        lin_ref[...] = lin
        for kind in range(2):
            piece = lin[:, kind * cols : (kind + 1) * cols]
            squares_ref[:, kind : kind + 1] = jnp.sum(piece * piece, axis=1, keepdims=True)

    def by_rows(columns):
        return pl.BlockSpec((size, columns), lambda i: (i, 0))

    return pl.pallas_call(
        kernel,
        grid=(total // size,),
        out_shape=[
            jax.ShapeDtypeStruct((total, width), jnp.bfloat16),
            jax.ShapeDtypeStruct((total, wide), f32),
            jax.ShapeDtypeStruct((total, 2), f32),
        ],
        in_specs=[
            by_rows(width),
            pl.BlockSpec((1, width), lambda i: (0, 0)),
            pl.BlockSpec((width, wide), lambda i: (0, 0)),
        ],
        out_specs=[by_rows(width), by_rows(wide), by_rows(2)],
        compiler_params=pltpu.CompilerParams(vmem_limit_bytes=60 * 2**20),
        cost_estimate=pl.CostEstimate(
            flops=3 * 10**9, bytes_accessed=15 * 2**20, transcendentals=0
        ),
        name="project",
    )(tokens, gain, weight)


def project_back(back, projected, scales, inner_sums, value_grad, weight, normed, tokens):
    total, width = tokens.shape
    wide = weight.shape[1]
    cols = wide // 3
    size = math.gcd(total, 256)
    steps, runs = total // size, 4
    f32, bf16 = jnp.float32, jnp.bfloat16

    def kernel(
        back_ref,
        lin_ref,
        scales_ref,
        sums_ref,
        value_ref,
        weight_ref,
        normed_ref,
        tokens_ref,
        part_ref,
        g_qkv_ref,
        gain_ref,
        proj,
    ):
        i = pl.program_id(0)

        @pl.when(i == 0)
        def _():
            gain_ref[...] = jnp.zeros_like(gain_ref)

        @pl.when(i < steps)
        def _():
            pieces = []
            for kind in range(2):
                scale = scales_ref[:, kind : kind + 1]
                unit = lin_ref[:, kind * cols : (kind + 1) * cols] * scale
                grad = scale * (back_ref[kind] - unit * sums_ref[:, kind : kind + 1])
                pieces.append(grad.astype(bf16))
            grads = jnp.concatenate(pieces + [value_ref[...]], axis=1)
            proj[pl.ds(pl.multiple_of(i * size, size), size), :] = grads
            part = lax.dot_general(
                grads, weight_ref[...], (((1,), (1,)), ((), ())), preferred_element_type=f32
            )
            values = tokens_ref[...].astype(f32)
            gain_ref[...] += jnp.sum(part * (values * rms_unit(values)), axis=0, keepdims=True)
            part_ref[...] = part.astype(bf16)

        @pl.when(i >= steps)
        def _():
            g_qkv_ref[...] = lax.dot_general(
                normed_ref[...], proj[...], (((0,), (0,)), ((), ())), preferred_element_type=f32
            ).astype(bf16)

    def by_rows(columns):
        return pl.BlockSpec((size, columns), lambda i: (jnp.minimum(i, steps - 1), 0))

    def later(i):
        return jnp.maximum(i - steps, 0)

    return pl.pallas_call(
        kernel,
        grid=(steps + runs,),
        out_shape=[
            jax.ShapeDtypeStruct((total, width), bf16),
            jax.ShapeDtypeStruct((width, wide), bf16),
            jax.ShapeDtypeStruct((1, width), f32),
        ],
        in_specs=[
            pl.BlockSpec((2, size, cols), lambda i: (0, jnp.minimum(i, steps - 1), 0)),
            by_rows(wide),
            by_rows(2),
            by_rows(2),
            by_rows(cols),
            pl.BlockSpec((width, wide), lambda i: (0, 0)),
            pl.BlockSpec((total, width // runs), lambda i: (0, later(i))),
            by_rows(width),
        ],
        out_specs=[
            by_rows(width),
            pl.BlockSpec((width // runs, wide), lambda i: (later(i), 0)),
            pl.BlockSpec((1, width), lambda i: (0, 0)),
        ],
        scratch_shapes=[pltpu.VMEM((total, wide), bf16)],
        compiler_params=pltpu.CompilerParams(vmem_limit_bytes=60 * 2**20),
        cost_estimate=pl.CostEstimate(flops=0, bytes_accessed=2**20, transcendentals=0),
        name="project_back",
    )(back, projected, scales, inner_sums, value_grad, weight, normed, tokens)


def on_device_heads(
    tokens,
    doc_lengths,
    routes,
    slot_order,
    attn_gain,
    w_qkv,
    q_gain,
    k_gain,
    w_out,
    ffn_gain,
    w_router,
    w_gate,
    w_up,
    w_down,
    cotangent,
):
    rows, width = tokens.shape[1], tokens.shape[2]
    ctx, fsdp = lax.axis_size("ctx"), lax.axis_size("fsdp")
    me = lax.axis_index("ctx")
    head_dim = width // HEADS
    cols = HEADS // ctx * head_dim
    part = width // fsdp
    total = rows * ctx
    lengths = doc_lengths[0]
    bf16, f32 = jnp.bfloat16, jnp.float32

    experts, top = w_gate.shape[0], routes.shape[2]
    gains = [gain.reshape(1, part) for gain in (attn_gain, q_gain, k_gain, ffn_gain)]
    router_rows = jnp.pad(w_router.T, ((0, ROUTER_ROWS - experts), (0, 0)))
    pairs = jnp.concatenate([routes[0].T, slot_order[0].T], axis=0)
    pairs = jnp.pad(pairs, ((0, -pairs.shape[0] % 8), (0, 0)))
    tokens_all, qkv_weight, dy_all, *gains, router_rows, pairs_own, pairs_other = gather_inputs(
        tokens[0], w_qkv, cotangent[0], gains + [router_rows], [pairs], 9
    )
    row_gain_one, row_gain_two = gains[0].astype(f32), gains[3].astype(f32)
    gain_query, gain_key = gains[1][0].astype(f32), gains[2][0].astype(f32)
    cotangent, tokens_all = lax.optimization_barrier((cotangent, tokens_all))

    stream_pos = dealt_position(jnp.arange(total, dtype=jnp.int32), rows, ctx)
    stream_doc, stream_inner = document_info(stream_pos, lengths)
    cosine, sine_part = rope_tables(stream_inner, head_dim)
    turn_tables = (
        jnp.concatenate([cosine, cosine], axis=1),
        jnp.concatenate([-sine_part, sine_part], axis=1),
    )
    sight = (
        (stream_pos - stream_inner).reshape(total, 1),
        stream_pos.reshape(total, 1),
        stream_pos.reshape(1, total),
    )
    normed_all, projected, squares = project(tokens_all, row_gain_one, qkv_weight)
    squares = squares.T
    squares = ctx_sum(squares.reshape(-1, 128), 1).reshape(2, total)
    scales = lax.rsqrt(squares / width + EPSILON).T
    own_gains = [
        lax.dynamic_slice_in_dim(gain, me * cols, cols, 0) for gain in (gain_query, gain_key)
    ]
    own_gains = jnp.concatenate(own_gains).reshape(1, 2 * cols)
    low, attended, attended_low, tops = attend(
        projected, scales, own_gains, *turn_tables, *sight, cols
    )

    attended_part = heads_to_rows(attended_low, 2)
    mixed_part = dot32("td,de->te", attended_part, w_out).astype(bf16)
    inputs = tokens[0].astype(f32)
    group, mixed, crossed = reduce_then_gather(
        mixed_part,
        [tokens[0], row_gain_two],
        [jax.ShapeDtypeStruct((rows, width), f32)],
        norm_chunk,
        "mix_and_norm",
        6,
        True,
        [],
    )

    capacity = rows * top // experts
    slot_by_expert, slots_other = slots_of([pairs_own, pairs_other], experts, top)
    moved_part, group_grad, g_router, scaled, gate_low, up_low = run_experts(
        group, dy_all, slot_by_expert, router_rows, w_gate, w_up, w_down, fsdp, capacity
    )
    mixed_all, mixed_grad, g_ffn_gain, scaled_other, gate_other = reduce_then_gather(
        group_grad,
        [mixed, row_gain_two, cotangent[0]],
        [jax.ShapeDtypeStruct((rows, width), f32), jax.ShapeDtypeStruct((1, width), f32)],
        norm_back_chunk,
        "norm_back",
        7,
        False,
        [scaled, gate_low],
    )
    g_ffn_gain = g_ffn_gain[0]
    up_low, mixed_all = lax.optimization_barrier((up_low, mixed_all))
    up_other = swap(up_low, "ctx", 1)
    dy_other = lax.all_gather(
        swap(pick_half(cotangent[0], 1), "ctx", 1), "fsdp", axis=0, tiled=True
    )
    crossed = lax.all_gather(crossed, "fsdp", axis=0, tiled=True)
    downs = expert_grads(
        [scaled], [scaled_other], dy_all, dy_other, slot_by_expert, slots_other, capacity, True
    )
    downs, mixed_all = lax.optimization_barrier((downs, mixed_all))
    output_part = dot32("te,de->td", mixed_all, w_out).astype(bf16)
    g_out = dot32("td,te->de", attended_part, mixed_all).astype(bf16)
    output_grad = rows_to_heads(output_part, 3)
    output_grad, up_other, downs, moved_part = lax.optimization_barrier(
        (output_grad, up_other, downs, moved_part)
    )
    moved = lax.psum_scatter(moved_part, "fsdp", scatter_dimension=0, tiled=True)
    activations = (mixed + moved.astype(f32)).astype(bf16)
    low_far, low_own = swap(downs[0, 0, 1], "ctx", 2), swap(downs[0, 0, 0], "ctx", 2)
    ups = expert_grads(
        [gate_low, up_low], [gate_other, up_other], group, crossed, slot_by_expert, slots_other, capacity, False
    )
    output_grad, ups = lax.optimization_barrier((output_grad, ups))

    back, value_grad, own_g_gains, inner_sums = attend_back(
        output_grad, low, attended, tops, projected, scales, own_gains, *turn_tables, *sight
    )
    inner_sums, low_far, low_own = lax.optimization_barrier((inner_sums, low_far, low_own))
    inner_sums = ctx_sum(inner_sums.T.reshape(-1, 128), 1)
    inner_sums, ups = lax.optimization_barrier((inner_sums, ups))
    gate_far = swap(ups[0, 0, 1], "ctx", 2)
    inner_sums = inner_sums.reshape(2, total).T / width

    normed_grad_part, g_qkv, g_attn_gain = project_back(
        back, projected, scales, inner_sums, value_grad, qkv_weight, normed_all, tokens_all
    )
    g_attn_gain = g_attn_gain[0]

    def placed_cols(values):
        return lax.dynamic_update_slice_in_dim(jnp.zeros((width,), f32), values, me * cols, 0)

    sums = jnp.concatenate(
        [
            jnp.stack([g_attn_gain, placed_cols(own_g_gains[0, 0]), placed_cols(own_g_gains[1, 0]), g_ffn_gain]),
            g_router[:experts],
        ],
        axis=0,
    )
    down_parts, gate_parts, up_parts, input_grad, out_part, qkv_part, sums = finish_sums(
        downs,
        ups,
        low_far,
        low_own,
        gate_far,
        normed_grad_part,
        g_out,
        g_qkv,
        jnp.pad(sums, ((0, -sums.shape[0] % 8), (0, 0))),
        tokens[0],
        mixed_grad,
        row_gain_one,
        8,
    )
    return (
        activations[None],
        input_grad[None],
        sums[0],
        qkv_part,
        sums[1],
        sums[2],
        out_part,
        sums[3],
        sums[4 : 4 + experts].T,
        gate_parts,
        up_parts,
        down_parts,
    )


def solution(mesh):
    in_specs = (
        P("fsdp", "ctx", None),
        P("fsdp", None),
        P("fsdp", "ctx", None),
        P("fsdp", "ctx", None),
        P("fsdp"),
        P("fsdp", None),
        P("fsdp"),
        P("fsdp"),
        P("fsdp", None),
        P("fsdp"),
        P("fsdp", None),
        P(None, None, "fsdp"),
        P(None, None, "fsdp"),
        P(None, "fsdp", None),
        P("fsdp", "ctx", None),
    )
    out_specs = (
        P("fsdp", "ctx", None),
        P("fsdp", "ctx", None),
        P("fsdp"),
        P("fsdp", "ctx"),
        P("fsdp"),
        P("fsdp"),
        P("fsdp", "ctx"),
        P("fsdp"),
        P("fsdp", None),
        P(None, "ctx", "fsdp"),
        P(None, "ctx", "fsdp"),
        P(None, "fsdp", "ctx"),
    )
    ctx, fsdp = mesh.shape["ctx"], mesh.shape["fsdp"]
    by_heads = HEADS % ctx == 0 and ctx == 8 and fsdp == 4
    body = on_device_heads if by_heads else on_device
    return jax.shard_map(
        body, mesh=mesh, in_specs=in_specs, out_specs=out_specs, check_vma=False
    )
```

```python
import math

import jax
import jax.numpy as jnp
from jax import lax
from jax.experimental import pallas as pl
from jax.experimental.pallas import tpu as pltpu
from jax.sharding import PartitionSpec as P

HEADS = 16
MESH = pl.DeviceIdType.MESH
ANY = pl.BlockSpec(memory_space=pl.ANY)
HBM = pl.BlockSpec(memory_space=pltpu.HBM)
VMEM = pl.BlockSpec(memory_space=pltpu.VMEM)
DMA = pltpu.SemaphoreType.DMA

EPSILON = 1e-05
ROPE_BASE = 10000.0
MASKED = -1e30


def rms_scale(values, gain_vector):
    return (
        values
        * lax.rsqrt(jnp.mean(values * values, axis=-1, keepdims=True) + EPSILON)
        * gain_vector
    )


def rotate(values, inner_pos):
    half_dim = values.shape[-1] // 2
    freq_table = ROPE_BASE ** (-2.0 * jnp.arange(half_dim, dtype=jnp.float32) / values.shape[-1])
    angles = inner_pos.astype(jnp.float32)[:, None] * freq_table[None, :]
    cosine = jnp.cos(angles)[:, None, :]
    sine_part = jnp.sin(angles)[:, None, :]
    first_half = values[..., :half_dim]
    second_half = values[..., half_dim:]
    return jnp.concatenate(
        [
            first_half * cosine - second_half * sine_part,
            second_half * cosine + first_half * sine_part,
        ],
        axis=-1,
    )


def dealt_position(flat_index, per_device, device_count):
    device_index = flat_index // per_device
    within = flat_index % per_device
    half_rows = per_device // 2
    return jnp.where(
        within < half_rows,
        device_index * half_rows + within,
        (2 * device_count - 1 - device_index) * half_rows + within - half_rows,
    )


def document_info(positions, lengths):
    doc_ends = jnp.sum(jnp.where(jnp.arange(lengths.shape[0])[:, None] >= jnp.arange(lengths.shape[0])[None, :], lengths[None, :], 0), axis=1)
    passed = doc_ends[None, :] <= positions[:, None]
    doc_ids = jnp.sum(passed.astype(jnp.int32), axis=1)
    inner_pos = positions - jnp.sum(jnp.where(passed, lengths[None, :], 0), axis=1)
    return (doc_ids, inner_pos)


def slot_table(route_ids, order_ids, capacity, expert_count):
    pair_count = route_ids.shape[0] * route_ids.shape[1]
    expert_flat = route_ids.reshape(pair_count)
    rank_flat = order_ids.reshape(pair_count)
    earlier = (expert_flat[None, :] == expert_flat[:, None]) & (
        rank_flat[None, :] < rank_flat[:, None]
    )
    slot_index = jnp.sum(earlier.astype(jnp.int32), axis=1)
    placed = jnp.where(
        slot_index < capacity, expert_flat * capacity + slot_index, expert_count * capacity
    )
    source = (
        jnp.full((expert_count * capacity + 1,), pair_count, jnp.int32)
        .at[placed]
        .set(jnp.arange(pair_count, dtype=jnp.int32))
    )
    return (placed, source[: expert_count * capacity])


def masked_scores(query_block, key_block, query_pos, query_doc, key_pos, key_doc, score_scale):
    scores = (
        jnp.einsum("qhd,khd->hqk", query_block, key_block, preferred_element_type=jnp.float32)
        * score_scale
    )
    allowed = (query_doc[:, None] == key_doc[None, :]) & (key_pos[None, :] <= query_pos[:, None])
    return jnp.where(allowed[None], scores, MASKED)


def silu_parts(hidden_grad, slot_gate, slot_up):
    sigma = jax.nn.sigmoid(slot_gate)
    gate_grad_low = (hidden_grad * slot_up * sigma * (1.0 + slot_gate * (1.0 - sigma))).astype(
        jnp.bfloat16
    )
    up_grad_low = (hidden_grad * slot_gate * sigma).astype(jnp.bfloat16)
    return (gate_grad_low, up_grad_low)


def on_device(
    tokens,
    doc_lengths,
    routes,
    slot_order,
    attn_gain,
    w_qkv,
    q_gain,
    k_gain,
    w_out,
    ffn_gain,
    w_router,
    w_gate,
    w_up,
    w_down,
    cotangent,
):
    row_count = tokens.shape[1]
    model_width = tokens.shape[2]
    head_count = HEADS
    head_dim = model_width // head_count
    score_scale = head_dim ** (-0.5)
    ctx_count = lax.axis_size("ctx")
    ctx_index = lax.axis_index("ctx")
    total_rows = row_count * ctx_count
    lengths = doc_lengths[0]
    local_pos = dealt_position(
        ctx_index * row_count + jnp.arange(row_count, dtype=jnp.int32), row_count, ctx_count
    )
    local_doc, local_inner = document_info(local_pos, lengths)
    stream_pos = dealt_position(jnp.arange(total_rows, dtype=jnp.int32), row_count, ctx_count)
    stream_doc, stream_inner = document_info(stream_pos, lengths)
    block_rows = math.gcd(total_rows, 512)
    block_count = total_rows // block_rows
    block_ids = jnp.arange(block_count, dtype=jnp.int32)
    gain_one, qkv_weight, gain_query, gain_key, out_weight = (
        lax.all_gather(attn_gain, "fsdp", axis=0, tiled=True),
        lax.all_gather(w_qkv, "fsdp", axis=0, tiled=True),
        lax.all_gather(q_gain, "fsdp", axis=0, tiled=True),
        lax.all_gather(k_gain, "fsdp", axis=0, tiled=True),
        lax.all_gather(w_out, "fsdp", axis=0, tiled=True),
    )
    gain_two, router_weight, gate_weight, up_weight, down_weight = (
        lax.all_gather(ffn_gain, "fsdp", axis=0, tiled=True),
        lax.all_gather(w_router, "fsdp", axis=0, tiled=True),
        lax.all_gather(w_gate, "fsdp", axis=2, tiled=True),
        lax.all_gather(w_up, "fsdp", axis=2, tiled=True),
        lax.all_gather(w_down, "fsdp", axis=1, tiled=True),
    )
    inputs = tokens[0].astype(jnp.float32)
    normed_f, norm_one_pull = jax.vjp(rms_scale, inputs, gain_one.astype(jnp.float32))
    normed_low = normed_f.astype(jnp.bfloat16)
    projected = jnp.dot(normed_low, qkv_weight, preferred_element_type=jnp.float32)
    query_lin = projected[:, :model_width]
    key_lin = projected[:, model_width : 2 * model_width]
    value_low = (
        projected[:, 2 * model_width :]
        .astype(jnp.bfloat16)
        .reshape(row_count, head_count, head_dim)
    )

    def head_shape(values, gain_vector):
        return rotate(
            rms_scale(values, gain_vector).reshape(row_count, head_count, head_dim), local_inner
        )

    query_f, query_pull = jax.vjp(head_shape, query_lin, gain_query.astype(jnp.float32))
    key_f, key_pull = jax.vjp(head_shape, key_lin, gain_key.astype(jnp.float32))
    query_low = query_f.astype(jnp.bfloat16)
    key_low = key_f.astype(jnp.bfloat16)
    keys_all, values_all = (
        lax.all_gather(key_low, "ctx", axis=0, tiled=True),
        lax.all_gather(value_low, "ctx", axis=0, tiled=True),
    )

    def key_slice(block_index):
        first_row = block_index * block_rows
        return (
            lax.dynamic_slice_in_dim(keys_all, first_row, block_rows, 0),
            lax.dynamic_slice_in_dim(values_all, first_row, block_rows, 0),
            lax.dynamic_slice_in_dim(stream_pos, first_row, block_rows, 0),
            lax.dynamic_slice_in_dim(stream_doc, first_row, block_rows, 0),
        )

    def stats_step(carry, block_index):
        running_top, running_total = carry
        key_block, value_block, key_pos, key_doc = key_slice(block_index)
        scores = masked_scores(
            query_low, key_block, local_pos, local_doc, key_pos, key_doc, score_scale
        )
        new_top = jnp.maximum(running_top, jnp.max(scores, axis=-1))
        running_total = running_total * jnp.exp(running_top - new_top) + jnp.sum(
            jnp.exp(scores - new_top[..., None]), axis=-1
        )
        return ((new_top, running_total), None)

    start_stats = (
        jnp.full((head_count, row_count), MASKED, jnp.float32),
        jnp.zeros((head_count, row_count), jnp.float32),
    )
    (score_top, score_total), _ = lax.scan(stats_step, start_stats, block_ids)
    log_total = score_top + jnp.log(score_total)

    def output_step(accum, block_index):
        key_block, value_block, key_pos, key_doc = key_slice(block_index)
        scores = masked_scores(
            query_low, key_block, local_pos, local_doc, key_pos, key_doc, score_scale
        )
        prob_block = jnp.exp(scores - log_total[..., None]).astype(jnp.bfloat16)
        return (
            accum
            + jnp.einsum(
                "hqk,khd->qhd", prob_block, value_block, preferred_element_type=jnp.float32
            ),
            None,
        )

    attended_f, _ = lax.scan(
        output_step, jnp.zeros((row_count, head_count, head_dim), jnp.float32), block_ids
    )
    attended_low = attended_f.reshape(row_count, model_width).astype(jnp.bfloat16)
    mixed = inputs + jnp.dot(attended_low, out_weight, preferred_element_type=jnp.float32)
    normed_two_f, norm_two_pull = jax.vjp(rms_scale, mixed, gain_two.astype(jnp.float32))
    normed_two = normed_two_f.astype(jnp.bfloat16)
    expert_count = gate_weight.shape[0]
    route_ids = routes[0]
    top_count = route_ids.shape[1]
    pair_count = row_count * top_count
    capacity = pair_count // expert_count
    logits = jnp.dot(normed_two, router_weight, preferred_element_type=jnp.float32)
    router_probs = jax.nn.softmax(logits, axis=-1)
    chosen = (
        route_ids[:, :, None] == jnp.arange(expert_count, dtype=jnp.int32)[None, None, :]
    ).astype(jnp.float32)
    gate_values = jnp.sum(chosen * router_probs[:, None, :], axis=-1)
    placed, source = slot_table(route_ids, slot_order[0], capacity, expert_count)
    padded_in = jnp.concatenate([normed_two, jnp.zeros((1, model_width), jnp.bfloat16)], axis=0)
    expert_in = padded_in[source // top_count].reshape(expert_count, capacity, model_width)
    gate_pre = jnp.einsum(
        "ecd,edh->ech", expert_in, gate_weight, preferred_element_type=jnp.float32
    )
    up_pre = jnp.einsum("ecd,edh->ech", expert_in, up_weight, preferred_element_type=jnp.float32)
    hidden_low = (jax.nn.silu(gate_pre) * up_pre).astype(jnp.bfloat16)
    expert_out = jnp.einsum(
        "ech,ehd->ecd", hidden_low, down_weight, preferred_element_type=jnp.float32
    )
    out_padded = jnp.concatenate(
        [
            expert_out.reshape(expert_count * capacity, model_width),
            jnp.zeros((1, model_width), jnp.float32),
        ],
        axis=0,
    )
    per_pair = out_padded[placed].reshape(row_count, top_count, model_width)
    layer_out = mixed + jnp.sum(gate_values[:, :, None] * per_pair, axis=1)
    out_grad = cotangent[0].astype(jnp.float32)
    gate_grad = jnp.sum(out_grad[:, None, :] * per_pair, axis=-1)
    pair_grad = (gate_values[:, :, None] * out_grad[:, None, :]).reshape(pair_count, model_width)
    pair_padded = jnp.concatenate([pair_grad, jnp.zeros((1, model_width), jnp.float32)], axis=0)
    slot_grad = (
        pair_padded[source].reshape(expert_count, capacity, model_width).astype(jnp.bfloat16)
    )

    def expert_step(carry, pieces):
        slot_in, slot_hidden, slot_dy, slot_gate, slot_up, gate_matrix, up_matrix, down_matrix = (
            pieces
        )
        hidden_grad = jnp.einsum(
            "cd,hd->ch", slot_dy, down_matrix, preferred_element_type=jnp.float32
        )
        gate_grad_low, up_grad_low = silu_parts(hidden_grad, slot_gate, slot_up)
        in_grad = jnp.einsum(
            "ch,dh->cd", gate_grad_low, gate_matrix, preferred_element_type=jnp.float32
        ) + jnp.einsum("ch,dh->cd", up_grad_low, up_matrix, preferred_element_type=jnp.float32)
        gate_term = jnp.einsum(
            "cd,ch->dh", slot_in, gate_grad_low, preferred_element_type=jnp.float32
        )
        up_term = jnp.einsum("cd,ch->dh", slot_in, up_grad_low, preferred_element_type=jnp.float32)
        down_term = jnp.einsum(
            "ch,cd->hd", slot_hidden, slot_dy, preferred_element_type=jnp.float32
        )
        gate_shard, up_shard, down_shard = (
            lax.psum_scatter(
                gate_term.astype(jnp.bfloat16), "fsdp", scatter_dimension=1, tiled=True
            ).astype(jnp.float32),
            lax.psum_scatter(
                up_term.astype(jnp.bfloat16), "fsdp", scatter_dimension=1, tiled=True
            ).astype(jnp.float32),
            lax.psum_scatter(
                down_term.astype(jnp.bfloat16), "fsdp", scatter_dimension=0, tiled=True
            ).astype(jnp.float32),
        )
        gate_part, up_part, down_part = (
            lax.psum_scatter(
                gate_shard.astype(jnp.bfloat16), "ctx", scatter_dimension=0, tiled=True
            ).astype(jnp.float32),
            lax.psum_scatter(
                up_shard.astype(jnp.bfloat16), "ctx", scatter_dimension=0, tiled=True
            ).astype(jnp.float32),
            lax.psum_scatter(
                down_shard.astype(jnp.bfloat16), "ctx", scatter_dimension=1, tiled=True
            ).astype(jnp.float32),
        )
        return (carry, (in_grad, gate_part, up_part, down_part))

    _, (expert_in_grad, gate_parts, up_parts, down_parts) = lax.scan(
        expert_step,
        None,
        (expert_in, hidden_low, slot_grad, gate_pre, up_pre, gate_weight, up_weight, down_weight),
    )
    in_padded = jnp.concatenate(
        [
            expert_in_grad.reshape(expert_count * capacity, model_width),
            jnp.zeros((1, model_width), jnp.float32),
        ],
        axis=0,
    )
    normed_two_grad = jnp.sum(in_padded[placed].reshape(row_count, top_count, model_width), axis=1)
    prob_grad_router = jnp.sum(chosen * gate_grad[:, :, None], axis=1)
    logit_grad = (
        router_probs
        * (prob_grad_router - jnp.sum(router_probs * prob_grad_router, axis=-1, keepdims=True))
    ).astype(jnp.bfloat16)
    normed_two_grad = normed_two_grad + jnp.einsum(
        "te,de->td", logit_grad, router_weight, preferred_element_type=jnp.float32
    )
    router_grad = jnp.einsum(
        "td,te->de", normed_two, logit_grad, preferred_element_type=jnp.float32
    )
    mixed_norm_grad, gain_two_grad = norm_two_pull(normed_two_grad)
    mixed_grad = out_grad + mixed_norm_grad
    mixed_low = mixed_grad.astype(jnp.bfloat16)
    out_weight_grad = jnp.einsum(
        "td,te->de", attended_low, mixed_low, preferred_element_type=jnp.float32
    )
    output_grad = (
        jnp.einsum("te,de->td", mixed_low, out_weight, preferred_element_type=jnp.float32)
        .astype(jnp.bfloat16)
        .reshape(row_count, head_count, head_dim)
    )
    row_delta = jnp.sum(output_grad.astype(jnp.float32) * attended_f, axis=-1).T

    def query_grad_step(accum, block_index):
        key_block, value_block, key_pos, key_doc = key_slice(block_index)
        scores = masked_scores(
            query_low, key_block, local_pos, local_doc, key_pos, key_doc, score_scale
        )
        prob_block = jnp.exp(scores - log_total[..., None])
        prob_grad = jnp.einsum(
            "qhd,khd->hqk", output_grad, value_block, preferred_element_type=jnp.float32
        )
        score_grad = (prob_block * (prob_grad - row_delta[..., None])).astype(jnp.bfloat16)
        return (
            accum
            + jnp.einsum("hqk,khd->qhd", score_grad, key_block, preferred_element_type=jnp.float32)
            * score_scale,
            None,
        )

    query_grad, _ = lax.scan(
        query_grad_step, jnp.zeros((row_count, head_count, head_dim), jnp.float32), block_ids
    )
    inner_rows = math.gcd(row_count * lax.axis_size("ctx"), 512)

    def piece_step(carry, piece_index):
        first_row = piece_index * inner_rows
        key_block = lax.dynamic_slice_in_dim(keys_all, first_row, inner_rows, 0)
        value_block = lax.dynamic_slice_in_dim(values_all, first_row, inner_rows, 0)
        key_pos = lax.dynamic_slice_in_dim(stream_pos, first_row, inner_rows, 0)
        key_doc = lax.dynamic_slice_in_dim(stream_doc, first_row, inner_rows, 0)
        scores = masked_scores(
            query_low, key_block, local_pos, local_doc, key_pos, key_doc, score_scale
        )
        prob_block = jnp.exp(scores - log_total[..., None])
        prob_grad = jnp.einsum(
            "qhd,khd->hqk", output_grad, value_block, preferred_element_type=jnp.float32
        )
        score_grad = (prob_block * (prob_grad - row_delta[..., None])).astype(jnp.bfloat16)
        value_part = jnp.einsum(
            "hqk,qhd->khd",
            prob_block.astype(jnp.bfloat16),
            output_grad,
            preferred_element_type=jnp.float32,
        )
        key_part = (
            jnp.einsum("hqk,qhd->khd", score_grad, query_low, preferred_element_type=jnp.float32)
            * score_scale
        )
        return (
            carry,
            jnp.concatenate(
                [
                    key_part.reshape(inner_rows, model_width),
                    value_part.reshape(inner_rows, model_width),
                ],
                axis=1,
            ),
        )

    _, stacked = lax.scan(
        piece_step,
        None,
        jnp.arange(row_count * lax.axis_size("ctx") // inner_rows, dtype=jnp.int32),
    )
    key_value_grad = lax.psum_scatter(
        stacked.reshape(row_count * lax.axis_size("ctx"), 2 * model_width).astype(jnp.bfloat16),
        "ctx",
        scatter_dimension=0,
        tiled=True,
    ).astype(jnp.float32)
    key_grad = key_value_grad[:, :model_width].reshape(row_count, head_count, head_dim)
    value_grad = key_value_grad[:, model_width:]
    query_lin_grad, gain_query_grad = query_pull(query_grad)
    key_lin_grad, gain_key_grad = key_pull(key_grad)
    proj_grad = jnp.concatenate(
        [
            query_lin_grad.astype(jnp.bfloat16),
            key_lin_grad.astype(jnp.bfloat16),
            value_grad.astype(jnp.bfloat16),
        ],
        axis=1,
    )
    qkv_weight_grad = jnp.einsum(
        "td,te->de", normed_low, proj_grad, preferred_element_type=jnp.float32
    )
    normed_grad = jnp.einsum("te,de->td", proj_grad, qkv_weight, preferred_element_type=jnp.float32)
    input_norm_grad, gain_one_grad = norm_one_pull(normed_grad)
    input_grad = mixed_grad + input_norm_grad
    qkv_shard, out_shard = (
        lax.psum_scatter(
            qkv_weight_grad.astype(jnp.bfloat16), "fsdp", scatter_dimension=0, tiled=True
        ).astype(jnp.float32),
        lax.psum_scatter(
            out_weight_grad.astype(jnp.bfloat16), "fsdp", scatter_dimension=0, tiled=True
        ).astype(jnp.float32),
    )
    qkv_part, out_part = (
        lax.psum_scatter(
            qkv_shard.astype(jnp.bfloat16), "ctx", scatter_dimension=1, tiled=True
        ).astype(jnp.float32),
        lax.psum_scatter(
            out_shard.astype(jnp.bfloat16), "ctx", scatter_dimension=1, tiled=True
        ).astype(jnp.float32),
    )
    gain_one_sum, gain_query_sum, gain_key_sum, gain_two_sum, router_sum = lax.psum(
        (gain_one_grad, gain_query_grad, gain_key_grad, gain_two_grad, router_grad), ("ctx", "fsdp")
    )
    shard_rows = model_width // lax.axis_size("fsdp")
    shard_start = lax.axis_index("fsdp") * shard_rows

    def own_rows(full_array):
        return lax.dynamic_slice_in_dim(full_array, shard_start, shard_rows, 0)

    return (
        layer_out.astype(jnp.bfloat16)[None],
        input_grad[None],
        own_rows(gain_one_sum),
        qkv_part,
        own_rows(gain_query_sum),
        own_rows(gain_key_sum),
        out_part,
        own_rows(gain_two_sum),
        own_rows(router_sum),
        gate_parts,
        up_parts,
        down_parts,
    )


def rms_unit(values):
    return lax.rsqrt(jnp.mean(values * values, axis=-1, keepdims=True) + EPSILON)


def rope_tables(inner_pos, head_dim):
    half_dim = head_dim // 2
    freq_table = ROPE_BASE ** (-2.0 * jnp.arange(half_dim, dtype=jnp.float32) / head_dim)
    angles = inner_pos.astype(jnp.float32)[:, None] * freq_table[None, :]
    return (jnp.cos(angles), jnp.sin(angles))


def dot32(spec, left, right):
    return jnp.einsum(spec, left, right, preferred_element_type=jnp.float32)


def greet(peers):
    barrier = pltpu.get_barrier_semaphore()
    for peer in peers:
        pl.semaphore_signal(barrier, inc=1, device_id=peer, device_id_type=MESH)
    pl.semaphore_wait(barrier, len(peers))


def send(source, target, send_sem, recv_sem, peer):
    copy = pltpu.make_async_remote_copy(
        source, target, send_sem, recv_sem, device_id=peer, device_id_type=MESH
    )
    copy.start()
    return copy


def comm_call(
    kernel, name, collective_id, out_shape, in_specs, out_specs, scratch_shapes, cost, vmem=16
):
    return pl.pallas_call(
        kernel,
        out_shape=out_shape,
        in_specs=in_specs,
        out_specs=out_specs,
        scratch_shapes=scratch_shapes,
        compiler_params=pltpu.CompilerParams(
            collective_id=collective_id, has_side_effects=True, vmem_limit_bytes=vmem * 2**20
        ),
        cost_estimate=pl.CostEstimate(flops=0, bytes_accessed=cost, transcendentals=0),
        name=name,
    )


def ctx_sum(values, collective_id):
    ctx = lax.axis_size("ctx")

    def kernel(own_ref, out_ref, held, send_sems, recv_sems):
        me, mine = lax.axis_index("ctx"), lax.axis_index("fsdp")
        peers = [(lax.rem(me + step, ctx), mine) for step in range(1, ctx)]
        greet(peers)
        copies = [
            send(own_ref, held.at[i], send_sems.at[i], recv_sems.at[i], peer)
            for i, peer in enumerate(peers)
        ]
        total = own_ref[...]
        for i, copy in enumerate(copies):
            copy.wait_recv()
            total = total + held[i]
        out_ref[...] = total
        for copy in copies:
            copy.wait_send()

    return comm_call(
        kernel,
        "ctx_sum",
        collective_id,
        jax.ShapeDtypeStruct(values.shape, values.dtype),
        [VMEM],
        VMEM,
        [
            pltpu.VMEM((ctx - 1,) + values.shape, values.dtype),
            DMA((ctx - 1,)),
            DMA((ctx - 1,)),
        ],
        20 * 2**20,
    )(values)


def heads_to_rows(values, collective_id):
    ctx, fsdp = lax.axis_size("ctx"), lax.axis_size("fsdp")
    rows, cols = values.shape[0] // ctx, values.shape[1]
    share = ctx // fsdp

    def kernel(own_ref, out_ref, send_sems, recv_sems):
        me, mine = lax.axis_index("ctx"), lax.axis_index("fsdp")
        keeper, place = me // share, lax.rem(me, share)
        own_keeper = (keeper == mine).astype(jnp.int32)
        barrier = pltpu.get_barrier_semaphore()
        for step in range(share * fsdp):
            source, stream = mine * share + step // fsdp, step % fsdp

            @pl.when(jnp.logical_or(source != me, stream != mine))
            def _():
                pl.semaphore_signal(
                    barrier, inc=1, device_id=(source, stream), device_id_type=MESH
                )

        pl.semaphore_wait(barrier, ctx - own_keeper)

        def block(index):
            return own_ref.at[pl.ds(pl.multiple_of(index * rows, rows), rows), :]

        def landing(stream, position):
            return out_ref.at[
                pl.ds(pl.multiple_of(stream * rows, rows), rows),
                pl.ds(pl.multiple_of(position * cols, cols), cols),
            ]

        slot = place * fsdp + mine

        def copy_to(step):
            other = lax.rem(me + step, ctx)
            return pltpu.make_async_remote_copy(
                block(other),
                landing(mine, place),
                send_sems.at[step],
                recv_sems.at[slot],
                device_id=(other, keeper),
                device_id_type=MESH,
            )

        kept = pltpu.make_async_copy(block(me), landing(mine, place), send_sems.at[0])
        for step in range(1, ctx):
            copy_to(step).start()

        @pl.when(own_keeper == 0)
        def _():
            copy_to(0).start()

        @pl.when(own_keeper == 1)
        def _():
            kept.start()
            kept.wait()

        for step in range(share * fsdp):

            @pl.when(
                jnp.logical_or(mine * share + step // fsdp != me, step % fsdp != mine)
            )
            def _():
                pltpu.make_async_copy(
                    block(0), landing(step % fsdp, step // fsdp), recv_sems.at[step]
                ).wait()

        for step in range(1, ctx):
            copy_to(step).wait_send()

        @pl.when(own_keeper == 0)
        def _():
            copy_to(0).wait_send()

    return comm_call(
        kernel,
        "heads_to_rows",
        collective_id,
        jax.ShapeDtypeStruct((fsdp * rows, share * cols), values.dtype),
        [ANY],
        ANY,
        [DMA((ctx,)), DMA((share * fsdp,))],
        40 * 2**20,
    )(values)


def rows_to_heads(values, collective_id):
    ctx, fsdp = lax.axis_size("ctx"), lax.axis_size("fsdp")
    share = ctx // fsdp
    rows, cols = values.shape[0] // fsdp, values.shape[1] // share

    def kernel(own_ref, out_ref, stage, stage_send, stage_recv, send_sems, recv_sems, done_sem):
        me, mine = lax.axis_index("ctx"), lax.axis_index("fsdp")
        ctx_peers = [(lax.rem(me + step, ctx), mine) for step in range(1, ctx)]
        greet(ctx_peers + [(me, lax.rem(mine + step, fsdp)) for step in range(1, fsdp)])

        def block(stream):
            return own_ref.at[pl.ds(pl.multiple_of(stream * rows, rows), rows), :]

        def landing(index):
            return out_ref.at[pl.ds(pl.multiple_of(index * rows, rows), rows), :]

        steps = [2, 3, 1]
        staged = {
            step: send(
                block(lax.rem(mine + step, fsdp)),
                stage.at[fsdp - step],
                stage_send.at[step],
                stage_recv.at[fsdp - step],
                (me, lax.rem(mine + step, fsdp)),
            )
            for step in steps
        }

        def piece(step, place):
            span = pl.ds(place * cols, cols)
            if step == 0:
                return own_ref.at[pl.ds(pl.multiple_of(mine * rows, rows), rows), span]
            return stage.at[step, :, span]

        def target(step, place):
            return lax.rem(mine + step, fsdp) * share + place

        def copy_to(step, place):
            return pltpu.make_async_remote_copy(
                piece(step, place),
                landing(me),
                send_sems.at[step * share + place],
                recv_sems.at[me],
                device_id=(target(step, place), mine),
                device_id_type=MESH,
            )

        def keep(step, place):
            return pltpu.make_async_copy(
                piece(step, place), landing(me), send_sems.at[step * share + place]
            )

        for step in [0, 1, 2, 3]:
            if step > 0:
                staged[fsdp - step].wait_recv()
            for place in range(share):
                far = target(step, place) != me
                pl.when(far)(copy_to(step, place).start)
                pl.when(jnp.logical_not(far))(keep(step, place).start)
        for step in range(1, ctx):
            source = lax.rem(me + step, ctx)
            pltpu.make_async_copy(
                piece(0, 0), landing(source), recv_sems.at[source]
            ).wait()
        for step in range(fsdp):
            for place in range(share):
                far = target(step, place) != me
                pl.when(far)(copy_to(step, place).wait_send)
                pl.when(jnp.logical_not(far))(keep(step, place).wait)
        for copy in staged.values():
            copy.wait_send()
        for peer in ctx_peers:
            pl.semaphore_signal(done_sem, inc=1, device_id=peer, device_id_type=MESH)
        pl.semaphore_wait(done_sem, ctx - 1)

    return comm_call(
        kernel,
        "rows_to_heads",
        collective_id,
        jax.ShapeDtypeStruct((ctx * rows, cols), values.dtype),
        [ANY],
        ANY,
        [
            pltpu.VMEM((fsdp, rows, share * cols), values.dtype),
            DMA((fsdp,)),
            DMA((fsdp,)),
            DMA((ctx,)),
            DMA((ctx,)),
            pltpu.SemaphoreType.REGULAR,
        ],
        2**20,
    )(values)


def swap(values, flip):
    return lax.ppermute(values, "ctx", [(i, i ^ flip) for i in range(lax.axis_size("ctx"))])


def reduce_then_gather(partial, extras, out_shapes, chunk_math, name, collective_id, crossed, bulk):
    ctx, fsdp = lax.axis_size("ctx"), lax.axis_size("fsdp")
    rows, width = partial.shape[0] // fsdp, partial.shape[1]
    chunks = 4
    size = rows // chunks
    count = len(extras)
    cols = width // ctx
    if crossed:
        out_shapes = out_shapes + [jax.ShapeDtypeStruct((rows, width // 2), jnp.bfloat16)]
    bulk_count, out_count = len(bulk), len(out_shapes)

    def kernel(*refs):
        part_ref, extra_refs = refs[0], refs[1 : 1 + count]
        bulk_refs, refs = refs[1 + count : 1 + count + bulk_count], refs[1 + count + bulk_count :]
        all_ref, out_refs = refs[0], refs[1 : 1 + out_count]
        bulk_out_refs, refs = refs[1 + out_count : 1 + out_count + bulk_count], refs[1 + out_count :]
        near_own, near_far, far_sum, far_own, sems, cross_sems, bulk_sems = refs[bulk_count:]
        me, mine = lax.axis_index("ctx"), lax.axis_index("fsdp")
        flip = 1 - 2 * lax.rem(mine, 2)
        core = mine + flip
        chip = lax.rem(mine + 2, fsdp)
        diagonal = lax.rem(core + 2, fsdp)
        to_x = (flipped(me, 1), mine)
        greet([(me, core), (me, chip)] + ([to_x] if crossed or bulk else []))

        def span(block, i):
            return pl.ds(pl.multiple_of(block * rows + i * size, size), size)

        def sem(kind, i):
            return sems.at[2 * kind, i], sems.at[2 * kind + 1, i]

        copies = []
        from_core_far, from_core_own, from_chip = [], [], []
        exchanged = [
            send(source, target, bulk_sems.at[0, i], bulk_sems.at[1, i], to_x)
            for i, (source, target) in enumerate(zip(bulk_refs, bulk_out_refs))
        ]
        for i in range(chunks):
            copy = send(
                part_ref.at[span(diagonal, i), :], near_far.at[i], *sem(0, i), (me, core)
            )
            from_core_far.append(copy)
        for i in range(chunks):
            copy = send(part_ref.at[span(core, i), :], near_own.at[i], *sem(1, i), (me, core))
            from_core_own.append(copy)
        for i in range(chunks):
            from_core_far[i].wait_recv()
            both = part_ref[span(chip, i), :].astype(jnp.float32) + near_far[i].astype(jnp.float32)
            far_sum[i] = both.astype(jnp.bfloat16)
            from_chip.append(send(far_sum.at[i], far_own.at[i], *sem(2, i), (me, chip)))
        to_chip = []
        for i in range(chunks):
            from_core_own[i].wait_recv()
            from_chip[i].wait_recv()
            total = (
                part_ref[span(mine, i), :].astype(jnp.float32)
                + near_own[i].astype(jnp.float32)
                + far_own[i].astype(jnp.float32)
            )
            all_ref[span(mine, i), :] = chunk_math(
                i, pl.ds(i * size, size), total, extra_refs, out_refs
            ).astype(jnp.bfloat16)
            own = all_ref.at[span(mine, i), :]
            to_chip.append(send(own, own, *sem(3, i), (me, chip)))
            copies.append(send(own, own, *sem(4, i), (me, core)))
            for run in range(ctx // 2 if crossed else 0):
                start = pl.multiple_of((2 * run + 1 - lax.rem(me, 2)) * cols, cols)
                copies.append(
                    send(
                        all_ref.at[span(mine, i), pl.ds(start, cols)],
                        out_refs[-1].at[pl.ds(i * size, size), pl.ds(run * cols, cols)],
                        cross_sems.at[0, i, run],
                        cross_sems.at[1, i, run],
                        to_x,
                    )
                )
        for i in range(chunks):
            to_chip[i].wait_recv()
            other = all_ref.at[span(chip, i), :]
            copies.append(send(other, other, *sem(5, i), (me, core)))
        for copy in copies + exchanged:
            copy.wait_recv()
        for copy in from_core_far + from_core_own + from_chip + to_chip + copies + exchanged:
            copy.wait_send()

    return comm_call(
        kernel,
        name,
        collective_id,
        [jax.ShapeDtypeStruct(partial.shape, jnp.bfloat16)]
        + out_shapes
        + [jax.ShapeDtypeStruct(values.shape, values.dtype) for values in bulk],
        [VMEM] * (1 + count) + [ANY] * bulk_count,
        [VMEM] * (1 + out_count) + [ANY] * bulk_count,
        [
            pltpu.VMEM((chunks, size, width), jnp.bfloat16),
            pltpu.VMEM((chunks, size, width), jnp.bfloat16),
            pltpu.VMEM((chunks, size, width), jnp.bfloat16),
            pltpu.VMEM((chunks, size, width), jnp.bfloat16),
            DMA((12, chunks)),
            DMA((2, chunks, ctx // 2)),
            DMA((2, max(1, bulk_count))),
        ],
        100 * 2**20,
    )(partial, *extras, *bulk)


def norm_chunk(index, span, total, extra_refs, out_refs):
    tokens_ref, gain_ref = extra_refs
    mixed = tokens_ref[span, :].astype(jnp.float32) + total
    out_refs[0][span, :] = mixed
    return mixed * rms_unit(mixed) * gain_ref[...]


def norm_back_chunk(index, span, total, extra_refs, out_refs):
    mixed_ref, gain_ref, dy_ref = extra_refs
    mixed = mixed_ref[span, :]
    scale = rms_unit(mixed)
    unit = mixed * scale
    pulled = total * gain_ref[...]
    grad = dy_ref[span, :].astype(jnp.float32) + scale * (
        pulled - unit * jnp.mean(unit * pulled, axis=-1, keepdims=True)
    )
    out_refs[0][span, :] = grad
    gain_grad = jnp.sum(total * unit, axis=0, keepdims=True)
    if index == 0:
        out_refs[1][...] = gain_grad
    else:
        out_refs[1][...] += gain_grad
    return grad


ROUTER_ROWS = 16


def one_hot(slots, capacity):
    return lax.broadcasted_iota(jnp.int32, (capacity, slots.shape[1]), 0) == slots


def slots_of(pairs, experts, top):
    count = len(pairs)
    blocks, _, rows = pairs[0].shape
    absent = float(rows * top)

    def kernel(*refs):
        for pairs_ref, out_ref in zip(refs[:count], refs[count:]):
            out_ref[...] = jnp.full(out_ref.shape, -1, jnp.int32)
            for b in range(blocks):
                rank_rows = []
                for expert in range(experts):
                    rank = jnp.full((1, rows), absent, jnp.float32)
                    for k in range(top):
                        rank = jnp.where(
                            pairs_ref[b, k : k + 1, :] == expert,
                            pairs_ref[b, top + k : top + k + 1, :].astype(jnp.float32),
                            rank,
                        )
                    rank_rows.append(rank)
                filler = jnp.full((rows - experts, rows), absent, jnp.float32)
                by_column = jnp.concatenate(rank_rows + [filler], axis=0).T
                for expert, rank in enumerate(rank_rows):
                    earlier = jnp.where(by_column[:, expert : expert + 1] < rank, 1.0, 0.0)
                    slot = jnp.where(rank < absent, jnp.sum(earlier, axis=0, keepdims=True), -1.0)
                    out_ref[expert : expert + 1, b * rows : (b + 1) * rows] = slot.astype(jnp.int32)

    shape = jax.ShapeDtypeStruct((ROUTER_ROWS, blocks * rows), jnp.int32)
    return pl.pallas_call(
        kernel,
        out_shape=[shape] * count,
        in_specs=[VMEM] * count,
        out_specs=[VMEM] * count,
        cost_estimate=pl.CostEstimate(flops=10**7, bytes_accessed=2**20, transcendentals=0),
        name="slots_of",
    )(*pairs)


def run_experts(group, dy_all, slots, router, w_gate, w_up, w_down, blocks, capacity):
    experts, width, units = w_gate.shape
    total = group.shape[0]
    rows = total // blocks
    held = blocks * capacity
    f32, bf16 = jnp.float32, jnp.bfloat16

    def kernel(
        group_ref,
        dy_ref,
        slots_ref,
        router_ref,
        gate_ref,
        up_ref,
        down_ref,
        moved_ref,
        grad_ref,
        g_router_ref,
        scaled_ref,
        gate_low_ref,
        up_low_ref,
        disp,
        ins,
        dys,
        probs,
        prob_grad,
    ):
        expert = pl.program_id(0)

        def block_rows(b):
            return pl.ds(b * rows, rows)

        @pl.when(expert == 0)
        def _():
            logits = lax.dot_general(
                router_ref[...],
                group_ref[...],
                (((1,), (1,)), ((), ())),
                preferred_element_type=f32,
            )
            real = lax.broadcasted_iota(jnp.int32, logits.shape, 0) < experts
            logits = jnp.where(real, logits, MASKED)
            weights = jnp.exp(logits - jnp.max(logits, axis=0, keepdims=True))
            probs[...] = weights / jnp.sum(weights, axis=0, keepdims=True)
            prob_grad[...] = jnp.zeros_like(prob_grad)
            for b in range(blocks):
                for e in range(experts):
                    disp[b, pl.ds(e * capacity, capacity), :] = (
                        one_hot(slots_ref[pl.ds(e, 1), block_rows(b)], capacity)
                        .astype(f32)
                        .astype(bf16)
                    )
                for source, target in ((group_ref, ins), (dy_ref, dys)):
                    picked = jnp.dot(
                        disp[b], source[block_rows(b), :], preferred_element_type=f32
                    ).astype(bf16)
                    for e in range(experts):
                        target[e, pl.ds(b * capacity, capacity), :] = picked[
                            e * capacity : (e + 1) * capacity
                        ]

        expert_in, slot_dy = ins[expert], dys[expert]
        gate_matrix, up_matrix, down_matrix = gate_ref[0], up_ref[0], down_ref[0]
        gate_pre = jnp.dot(expert_in, gate_matrix, preferred_element_type=f32)
        up_pre = jnp.dot(expert_in, up_matrix, preferred_element_type=f32)
        raw_grad = lax.dot_general(
            slot_dy, down_matrix, (((1,), (1,)), ((), ())), preferred_element_type=f32
        )
        own_probs = probs[pl.ds(expert, 1), :]
        own_slots = slots_ref[pl.ds(expert, 1), :]
        hots = [
            one_hot(own_slots[:, b * rows : (b + 1) * rows], capacity) for b in range(blocks)
        ]
        value = jnp.concatenate(
            [
                jnp.sum(
                    jnp.where(hots[b], own_probs[:, b * rows : (b + 1) * rows], 0.0),
                    axis=1,
                    keepdims=True,
                )
                for b in range(blocks)
            ],
            axis=0,
        )
        sigma = 1.0 / (1.0 + jnp.exp(-gate_pre))
        silu = gate_pre * sigma
        hidden = (silu * up_pre).astype(bf16)
        hidden_f = hidden.astype(f32)
        value_grad = jnp.sum(hidden_f * raw_grad, axis=1, keepdims=True)
        hidden_grad = raw_grad * value
        gate_low = (hidden_grad * up_pre * sigma * (1.0 + gate_pre * (1.0 - sigma))).astype(bf16)
        up_low = (hidden_grad * silu).astype(bf16)
        scaled = (hidden_f * value).astype(bf16)
        scaled_ref[0] = scaled
        gate_low_ref[0] = gate_low
        up_low_ref[0] = up_low
        for b in range(blocks):
            prob_grad[expert, :, block_rows(b)] = jnp.sum(
                jnp.where(hots[b], value_grad[b * capacity : (b + 1) * capacity], 0.0),
                axis=0,
                keepdims=True,
            )
        dys[expert] = jnp.dot(scaled, down_matrix, preferred_element_type=f32).astype(bf16)
        ins[expert] = (
            lax.dot_general(
                gate_low, gate_matrix, (((1,), (1,)), ((), ())), preferred_element_type=f32
            )
            + lax.dot_general(
                up_low, up_matrix, (((1,), (1,)), ((), ())), preferred_element_type=f32
            )
        ).astype(bf16)

        @pl.when(expert == experts - 1)
        def _():
            grads = jnp.concatenate([prob_grad[e] for e in range(ROUTER_ROWS)], axis=0)
            weights = probs[...]
            logit_grad = (
                weights * (grads - jnp.sum(weights * grads, axis=0, keepdims=True))
            ).astype(bf16)
            g_router_ref[...] = jnp.dot(logit_grad, group_ref[...], preferred_element_type=f32)
            for b in range(blocks):
                for source, target in ((dys, moved_ref), (ins, grad_ref)):
                    gathered = jnp.concatenate(
                        [source[e, pl.ds(b * capacity, capacity), :] for e in range(experts)],
                        axis=0,
                    )
                    back = lax.dot_general(
                        disp[b], gathered, (((0,), (0,)), ((), ())), preferred_element_type=f32
                    )
                    if target is grad_ref:
                        back = back + lax.dot_general(
                            logit_grad[:, b * rows : (b + 1) * rows],
                            router_ref[...],
                            (((0,), (0,)), ((), ())),
                            preferred_element_type=f32,
                        )
                    target[block_rows(b), :] = back.astype(bf16)

    def whole(shape):
        return pl.BlockSpec(shape, lambda e: (0,) * len(shape))

    def by_expert(shape):
        return pl.BlockSpec((1,) + shape, lambda e: (e, 0, 0))

    return pl.pallas_call(
        kernel,
        grid=(experts,),
        out_shape=[
            jax.ShapeDtypeStruct((total, width), bf16),
            jax.ShapeDtypeStruct((total, width), bf16),
            jax.ShapeDtypeStruct((ROUTER_ROWS, width), f32),
        ]
        + [jax.ShapeDtypeStruct((experts, held, units), bf16)] * 3,
        in_specs=[
            whole((total, width)),
            whole((total, width)),
            whole((ROUTER_ROWS, total)),
            whole((ROUTER_ROWS, width)),
            by_expert((width, units)),
            by_expert((width, units)),
            by_expert((units, width)),
        ],
        out_specs=[
            whole((total, width)),
            whole((total, width)),
            whole((ROUTER_ROWS, width)),
        ]
        + [by_expert((held, units))] * 3,
        scratch_shapes=[
            pltpu.VMEM((blocks, experts * capacity, rows), bf16),
            pltpu.VMEM((experts, held, width), bf16),
            pltpu.VMEM((experts, held, width), bf16),
            pltpu.VMEM((ROUTER_ROWS, total), f32),
            pltpu.VMEM((ROUTER_ROWS, 1, total), f32),
        ],
        compiler_params=pltpu.CompilerParams(vmem_limit_bytes=56 * 2**20),
        cost_estimate=pl.CostEstimate(
            flops=30 * 10**9, bytes_accessed=30 * 2**20, transcendentals=10**6
        ),
        name="run_experts",
    )(group, dy_all, slots, router, w_gate, w_up, w_down)


def expert_grads(slot_own, slot_other, rows_own, rows_other, slots_own, slots_other, capacity):
    kinds = len(slot_own)
    experts, held, units = slot_own[0].shape
    total, half = rows_other.shape
    blocks = held // capacity
    rows = total // blocks
    ctx = lax.axis_size("ctx")
    cols = 2 * half // ctx
    f32, bf16 = jnp.float32, jnp.bfloat16

    def kernel(*refs):
        own_refs, other_refs = refs[:kinds], refs[kinds : 2 * kinds]
        rows_own_ref, rows_other_ref, slots_own_ref, slots_other_ref = refs[2 * kinds : 2 * kinds + 4]
        out_ref, held_rows = refs[2 * kinds + 4 :]
        expert = pl.program_id(0)
        me = lax.axis_index("ctx")

        def columns(side, run):
            if side == 1:
                return pl.ds(run * cols, cols)
            return pl.ds(pl.multiple_of((2 * run + lax.rem(me, 2)) * cols, cols), cols)

        @pl.when(expert == 0)
        def _():
            for side, slots_ref, source in (
                (0, slots_own_ref, rows_own_ref),
                (1, slots_other_ref, rows_other_ref),
            ):
                for b in range(blocks):
                    span = pl.ds(b * rows, rows)
                    disp = jnp.concatenate(
                        [
                            one_hot(slots_ref[pl.ds(e, 1), span], capacity).astype(f32)
                            for e in range(experts)
                        ],
                        axis=0,
                    ).astype(bf16)
                    for run in range(ctx // 2):
                        picked = jnp.dot(
                            disp, source[span, columns(side, run)], preferred_element_type=f32
                        ).astype(bf16)
                        for e in range(experts):
                            held_rows[
                                e,
                                pl.ds(side * held + b * capacity, capacity),
                                pl.ds(run * cols, cols),
                            ] = picked[e * capacity : (e + 1) * capacity]

        low, high = lax.rem(me // 2, 2), me // 4
        stacked = [
            jnp.concatenate([own[0], other[0]], axis=0) for own, other in zip(own_refs, other_refs)
        ]
        contract = (((0,), (0,)), ((), ()))
        for run in range(ctx // 2):
            kept = jnp.where(low == run % 2, 1, 0)
            far = jnp.where(high == run // 2, 0, 1)
            features = held_rows[expert, :, pl.ds(run * cols, cols)]
            for kind in range(kinds):
                out_ref[kind, pl.ds(kept, 1), pl.ds(far, 1), 0] = lax.dot_general(
                    features, stacked[kind], contract, preferred_element_type=f32
                ).astype(bf16)[None, None]

    def whole(shape):
        return pl.BlockSpec(shape, lambda e: (0,) * len(shape))

    slot_spec = pl.BlockSpec((1, held, units), lambda e: (e, 0, 0))
    return pl.pallas_call(
        kernel,
        grid=(experts,),
        out_shape=jax.ShapeDtypeStruct((kinds, 2, 2, experts, units, cols), bf16),
        in_specs=[slot_spec] * (2 * kinds)
        + [whole((total, 2 * half)), whole((total, half))]
        + [whole((ROUTER_ROWS, total))] * 2,
        out_specs=pl.BlockSpec((kinds, 2, 2, 1, units, cols), lambda e: (0, 0, 0, e, 0, 0)),
        scratch_shapes=[pltpu.VMEM((experts, 2 * held, half), bf16)],
        compiler_params=pltpu.CompilerParams(vmem_limit_bytes=60 * 2**20),
        cost_estimate=pl.CostEstimate(flops=0, bytes_accessed=2**20, transcendentals=0),
        name="expert_grads",
    )(*slot_own, *slot_other, rows_own, rows_other, slots_own, slots_other)


def down_grads(scaled, dy_parts, slots, capacity):
    count = len(scaled)
    experts, held, units = scaled[0].shape
    blocks, _, rows, wide = dy_parts.shape
    cols = wide // 2
    f32, bf16 = jnp.float32, jnp.bfloat16

    def kernel(*refs):
        scaled_refs, dy_ref, slots_refs = refs[:count], refs[count], refs[count + 1 : 2 * count + 1]
        out_ref, held_rows = refs[2 * count + 1 :]
        expert = pl.program_id(0)

        @pl.when(expert == 0)
        def _():
            for i, slots_ref in enumerate(slots_refs):
                for b in range(blocks):
                    span = pl.ds(b * rows, rows)
                    disp = jnp.concatenate(
                        [
                            one_hot(slots_ref[pl.ds(e, 1), span], capacity).astype(f32)
                            for e in range(experts)
                        ],
                        axis=0,
                    ).astype(bf16)
                    picked = jnp.dot(disp, dy_ref[b, i], preferred_element_type=f32).astype(bf16)
                    for e in range(experts):
                        held_rows[e, pl.ds(i * held + b * capacity, capacity), :] = picked[
                            e * capacity : (e + 1) * capacity
                        ]

        stacked = jnp.concatenate([ref[0] for ref in scaled_refs], axis=0)
        total = lax.dot_general(
            stacked, held_rows[expert], (((0,), (0,)), ((), ())), preferred_element_type=f32
        ).astype(bf16)
        side = lax.rem(lax.axis_index("ctx"), 2)
        for x in range(2):
            kept = jnp.where(side == x, 1, 0)
            out_ref[pl.ds(kept, 1), 0] = total[:, x * cols : (x + 1) * cols][None]

    def whole(shape):
        return pl.BlockSpec(shape, lambda e: (0,) * len(shape))

    return pl.pallas_call(
        kernel,
        grid=(experts,),
        out_shape=jax.ShapeDtypeStruct((2, experts, units, cols), bf16),
        in_specs=[pl.BlockSpec((1, held, units), lambda e: (e, 0, 0))] * count
        + [whole(dy_parts.shape)]
        + [whole(slots[0].shape)] * count,
        out_specs=pl.BlockSpec((2, 1, units, cols), lambda e: (0, e, 0, 0)),
        scratch_shapes=[pltpu.VMEM((experts, count * held, wide), bf16)],
        compiler_params=pltpu.CompilerParams(vmem_limit_bytes=60 * 2**20),
        cost_estimate=pl.CostEstimate(flops=0, bytes_accessed=2**20, transcendentals=0),
        name="down_grads",
    )(*scaled, dy_parts, *slots)


def roll_half(values):
    return pltpu.roll(values, values.shape[1] // 2, 1)


def allowed_keys(first_ref, last_ref, span, places):
    return (places >= first_ref[span, :]) & (places <= last_ref[span, :])


def attend(projected, scales, gains, cosine, sine_part, first, last, places, cols):
    total = projected.shape[0]
    head_dim = cosine.shape[1]
    heads = cols // head_dim
    size = math.gcd(total, 256)
    score_scale = head_dim ** (-0.5)
    f32, bf16 = jnp.float32, jnp.bfloat16

    def kernel(
        lin_ref,
        scales_ref,
        gains_ref,
        cos_ref,
        sin_ref,
        first_ref,
        last_ref,
        places_ref,
        low_ref,
        attended_ref,
        attended_low_ref,
        top_ref,
    ):
        for kind in range(3):
            for h in range(heads):
                span = pl.ds(kind * cols + h * head_dim, head_dim)
                values = lin_ref[:, span]
                if kind < 2:
                    values = values * scales_ref[:, kind : kind + 1] * gains_ref[:, span]
                    values = values * cos_ref[...] + roll_half(values) * sin_ref[...]
                low_ref[:, span] = values.astype(bf16)
        for h in range(heads):
            head = pl.ds(h * head_dim, head_dim)
            keys = low_ref[:, pl.ds(cols + h * head_dim, head_dim)]
            values = low_ref[:, pl.ds(2 * cols + h * head_dim, head_dim)]

            def step(b, carry):
                span = pl.ds(pl.multiple_of(b * size, size), size)
                scores = lax.dot_general(
                    low_ref[span, head],
                    keys,
                    (((1,), (1,)), ((), ())),
                    preferred_element_type=f32,
                )
                allowed = allowed_keys(first_ref, last_ref, span, places_ref[...])
                scores = jnp.where(allowed, scores * score_scale, MASKED)
                top = jnp.max(scores, axis=1, keepdims=True)
                weights = jnp.exp(scores - top)
                sums = jnp.sum(weights, axis=1, keepdims=True)
                probs = (weights * (1.0 / sums)).astype(bf16)
                attended = jnp.dot(probs, values, preferred_element_type=f32)
                attended_ref[span, head] = attended
                attended_low_ref[span, head] = attended.astype(bf16)
                top_ref[span, head] = jnp.broadcast_to(top + jnp.log(sums), (size, head_dim))
                return carry

            lax.fori_loop(0, total // size, step, 0)

    return pl.pallas_call(
        kernel,
        out_shape=[
            jax.ShapeDtypeStruct((total, 3 * cols), bf16),
            jax.ShapeDtypeStruct((total, cols), f32),
            jax.ShapeDtypeStruct((total, cols), bf16),
            jax.ShapeDtypeStruct((total, cols), f32),
        ],
        in_specs=[VMEM] * 8,
        out_specs=[VMEM] * 4,
        compiler_params=pltpu.CompilerParams(vmem_limit_bytes=24 * 2**20),
        cost_estimate=pl.CostEstimate(
            flops=2 * 10**9, bytes_accessed=20 * 2**20, transcendentals=2 * 10**6
        ),
        name="attend",
    )(projected, scales, gains, cosine, sine_part, first, last, places)


def attend_back(
    output_grad, low, attended, top, projected, scales, gains, cosine, sine_part, first, last, places
):
    total, cols = output_grad.shape
    head_dim = cosine.shape[1]
    heads = cols // head_dim
    size = math.gcd(total, 256)
    score_scale = head_dim ** (-0.5)
    f32, bf16 = jnp.float32, jnp.bfloat16
    contract_rows = (((0,), (0,)), ((), ()))

    def kernel(
        grad_ref,
        low_ref,
        attended_ref,
        top_ref,
        lin_ref,
        scales_ref,
        gains_ref,
        cos_ref,
        sin_ref,
        first_ref,
        last_ref,
        places_ref,
        back_ref,
        value_ref,
        gain_ref,
        sums_ref,
        query_grad,
        key_grad,
        value_grad,
    ):
        totals = [jnp.zeros((total, 1), f32) for _ in range(2)]
        for h in range(heads):
            head = pl.ds(h * head_dim, head_dim)
            keys = low_ref[:, pl.ds(cols + h * head_dim, head_dim)]
            values = low_ref[:, pl.ds(2 * cols + h * head_dim, head_dim)]
            key_grad[...] = jnp.zeros_like(key_grad)
            value_grad[...] = jnp.zeros_like(value_grad)

            def step(b, carry):
                span = pl.ds(pl.multiple_of(b * size, size), size)
                queries, grads = low_ref[span, head], grad_ref[span, head]
                scores = lax.dot_general(
                    queries, keys, (((1,), (1,)), ((), ())), preferred_element_type=f32
                )
                allowed = allowed_keys(first_ref, last_ref, span, places_ref[...])
                scores = jnp.where(allowed, scores * score_scale, MASKED)
                probs = jnp.exp(scores - top_ref[span, head][:, :1])
                prob_grad = lax.dot_general(
                    grads, values, (((1,), (1,)), ((), ())), preferred_element_type=f32
                )
                delta = jnp.sum(
                    grads.astype(f32) * attended_ref[span, head], axis=1, keepdims=True
                )
                score_grad = (probs * (prob_grad - delta)).astype(bf16)
                query_grad[span, :] = (
                    jnp.dot(score_grad, keys, preferred_element_type=f32) * score_scale
                )
                key_grad[...] += lax.dot_general(
                    score_grad, queries, contract_rows, preferred_element_type=f32
                )
                value_grad[...] += lax.dot_general(
                    probs.astype(bf16), grads, contract_rows, preferred_element_type=f32
                )
                return carry

            lax.fori_loop(0, total // size, step, 0)
            value_ref[:, head] = value_grad[...].astype(bf16)
            for kind, grad in ((0, query_grad[...]), (1, key_grad[...] * score_scale)):
                span = pl.ds(kind * cols + h * head_dim, head_dim)
                unit = lin_ref[:, span] * scales_ref[:, kind : kind + 1]
                grad = grad * cos_ref[...] - roll_half(grad) * sin_ref[...]
                gain_ref[kind, :, head] = jnp.sum(grad * unit, axis=0, keepdims=True)
                grad = grad * gains_ref[:, span]
                back_ref[kind, :, head] = grad
                totals[kind] = totals[kind] + jnp.sum(grad * unit, axis=1, keepdims=True)
        for kind in range(2):
            sums_ref[:, kind : kind + 1] = totals[kind]

    return pl.pallas_call(
        kernel,
        out_shape=[
            jax.ShapeDtypeStruct((2, total, cols), f32),
            jax.ShapeDtypeStruct((total, cols), bf16),
            jax.ShapeDtypeStruct((2, 1, cols), f32),
            jax.ShapeDtypeStruct((total, 2), f32),
        ],
        in_specs=[VMEM] * 12,
        out_specs=[VMEM] * 4,
        scratch_shapes=[pltpu.VMEM((total, head_dim), f32)] * 3,
        compiler_params=pltpu.CompilerParams(vmem_limit_bytes=60 * 2**20),
        cost_estimate=pl.CostEstimate(flops=0, bytes_accessed=2**20, transcendentals=0),
        name="attend_back",
    )(
        output_grad,
        low,
        attended,
        top,
        projected,
        scales,
        gains,
        cosine,
        sine_part,
        first,
        last,
        places,
    )


def flipped(index, bit):
    return index + bit * (1 - 2 * lax.rem(index // bit, 2))


def flipped_by(index, flip):
    for bit in (1, 2, 4):
        index = flipped(index, bit) if flip & bit else index
    return index


def add_into(target, *sources):
    step = target.shape[0] if len(target.shape) == 3 else target.shape[0] // 64

    def body(i, carry):
        span = i if len(target.shape) == 3 else pl.ds(pl.multiple_of(i * 64, 64), 64)
        total = sources[0][span].astype(jnp.float32)
        for source in sources[1:]:
            total = total + source[span].astype(jnp.float32)
        target[span] = total.astype(target.dtype)
        return carry

    lax.fori_loop(0, step, body, 0)


def finish_sums(downs, ups, gate_far, gate_own, up_far, normed_part, out_part, qkv_part, small, tokens, mixed_grad, gain, mixed, moved, collective_id):
    ctx, fsdp = lax.axis_size("ctx"), lax.axis_size("fsdp")
    experts, units, cols = gate_far.shape
    kinds = 3
    rows, width = tokens.shape
    part = out_part.shape[0]
    f32, bf16 = jnp.float32, jnp.bfloat16
    small_rows, small_cols = small.shape[0], small.shape[1] // fsdp
    copies_most = 64

    def kernel(
        downs_ref,
        ups_ref,
        gate_far_ref,
        gate_own_ref,
        up_far_ref,
        normed_ref,
        g_out_ref,
        g_qkv_ref,
        small_ref,
        tokens_ref,
        mixed_ref,
        gain_ref,
        forward_ref,
        moved_ref,
        down_ref,
        gate_ref,
        up_ref,
        input_ref,
        out_ref,
        qkv_ref,
        sums_ref,
        result_ref,
        kept,
        kept_low,
        kept_high,
        normed_own,
        normed_x,
        normed_low,
        normed_high,
        out_own,
        out_x,
        out_low,
        out_high,
        qkv_own,
        qkv_core,
        qkv_chip,
        qkv_sum,
        dealt,
        small_parts,
        small_sum,
        small_held,
        sends,
        recvs,
        locals_,
        deal_sems,
    ):
        me, mine = lax.axis_index("ctx"), lax.axis_index("fsdp")
        x, low, high = lax.rem(me, 2), lax.rem(me // 2, 2), me // 4
        to_x, to_low, to_high = ((flipped(me, bit), mine) for bit in (1, 2, 4))
        core, chip = flipped(mine, 1), flipped(mine, 2)
        diagonal = flipped(core, 2)
        ctx_peers = [(lax.rem(me + step, ctx), mine) for step in range(1, ctx)]
        near = [lax.rem(mine + step, fsdp) for step in range(1, fsdp)]
        greet(ctx_peers + [(me, other) for other in near])
        used, used_local, all_sends, loads = [0], [0], [], {}

        def push(source, target, peer):
            i = used[0]
            used[0] += 1
            copy = send(source, target, sends.at[i], recvs.at[i], peer)
            all_sends.append(copy)
            return copy

        def load(source, target):
            i = used_local[0]
            used_local[0] += 1
            copy = pltpu.make_async_copy(source, target, locals_.at[i])
            copy.start()
            return copy

        def normed_block(a, b, other):
            side = 1 - x if other else x
            block = (high + a - 2 * a * high) * 4 + (low + b - 2 * b * low) * 2 + side
            return normed_ref.at[pl.ds(pl.multiple_of(block * rows, rows), rows), :]

        def out_block(a, b, other):
            side = 1 - x if other else x
            block = (high + a - 2 * a * high) * 4 + (low + b - 2 * b * low) * 2 + side
            return g_out_ref.at[:, pl.ds(pl.multiple_of(block * cols, cols), cols)]

        def qkv_block(index):
            return g_qkv_ref.at[pl.ds(pl.multiple_of(index * part, part), part), :]

        def columns(index):
            return pl.ds(pl.multiple_of(index * small_cols, small_cols), small_cols)

        order = ((1, 1), (0, 1), (1, 0), (0, 0))
        small_copies = [
            push(small_ref.at[:, columns(other)], small_parts.at[i], (me, other))
            for i, other in enumerate(near)
        ]
        normed_copies = {
            ab: push(normed_block(*ab, True), normed_x.at[ab[0], ab[1]], to_x) for ab in order
        }

        def push_low(kind, a):
            return push(ups_ref.at[kind - 1, 0, a], kept_low.at[kind, a], to_low)

        low_copies = {
            (2, 0): push_low(2, 0),
            (0, 0): push(downs_ref.at[0], kept_low.at[0, 0], to_x),
        }
        early = {
            (1, 1): load(gate_far_ref, kept_low.at[1, 1]),
            (2, 1): load(up_far_ref, kept_low.at[2, 1]),
            (1, 0): load(gate_own_ref, kept_low.at[1, 0]),
        }
        kept_loads = {
            (kind, a): load(
                downs_ref.at[1] if kind == 0 else ups_ref.at[kind - 1, 1, a], kept.at[kind, a]
            )
            for kind, a in ((1, 1), (2, 1), (0, 0), (1, 0), (2, 0))
        }
        qkv_copies = [
            push(qkv_block(diagonal), qkv_core.at[1], (me, core)),
            push(qkv_block(core), qkv_core.at[0], (me, core)),
        ]
        qkv_loads = [
            load(qkv_block(chip), qkv_own.at[1]),
            load(qkv_block(mine), qkv_own.at[0]),
        ]
        normed_loads = {
            ab: load(normed_block(*ab, False), normed_own.at[ab[0], ab[1]]) for ab in order
        }
        out_loads = {ab: load(out_block(*ab, False), out_own.at[ab[0], ab[1]]) for ab in order}

        total = small_ref[:, columns(mine)]
        for i, copy in enumerate(small_copies):
            copy.wait_recv()
            total = total + small_parts[i]
        small_sum[...] = total
        small_wide = [push(small_sum, small_held.at[i], peer) for i, peer in enumerate(ctx_peers)]

        qkv_copies[0].wait_recv()
        qkv_loads[0].wait()
        add_into(qkv_core.at[1], qkv_own.at[1], qkv_core.at[1])
        chip_copy = push(qkv_core.at[1], qkv_chip, (me, chip))

        def to_low_side(copies, loads, own, from_x, from_low, a):
            copies[a, 1].wait_recv()
            loads[a, 1].wait()
            add_into(from_x.at[a, 1], own.at[a, 1], from_x.at[a, 1])
            return push(from_x.at[a, 1], from_low.at[a], to_low)

        def to_high_side(copies, loads, lows, own, from_x, from_low, from_high):
            copies[1, 0].wait_recv()
            loads[1, 0].wait()
            lows[1].wait_recv()
            add_into(from_x.at[1, 0], own.at[1, 0], from_x.at[1, 0], from_low.at[1])
            return push(from_x.at[1, 0], from_high, to_high)

        def arrived(kind, a):
            if (kind, a) in early:
                early[kind, a].wait()
            else:
                low_copies[kind, a].wait_recv()

        def experts_high(kind):
            arrived(kind, 1)
            kept_loads[kind, 1].wait()
            add_into(kept_low.at[kind, 1], kept.at[kind, 1], kept_low.at[kind, 1])
            return push(kept_low.at[kind, 1], kept_high.at[kind], to_high)

        high_copies = {1: experts_high(1)}
        normed_args = (normed_copies, normed_loads)
        normed_lows = {1: to_low_side(*normed_args, normed_own, normed_x, normed_low, 1)}
        high_copies[2] = experts_high(2)
        normed_lows[0] = to_low_side(*normed_args, normed_own, normed_x, normed_low, 0)
        out_copies = {ab: push(out_block(*ab, True), out_x.at[ab[0], ab[1]], to_x) for ab in order}

        qkv_copies[1].wait_recv()
        qkv_loads[1].wait()
        chip_copy.wait_recv()
        add_into(qkv_sum, qkv_own.at[0], qkv_core.at[0], qkv_chip)

        def deal(kind):
            index = kind * ctx + me
            return pltpu.make_async_remote_copy(
                qkv_sum.at[:, pl.ds(kind * cols, cols)],
                dealt.at[lax.rem(index, kinds)],
                deal_sems.at[0, kind],
                deal_sems.at[1, lax.rem(index, kinds)],
                device_id=(index // kinds, mine),
                device_id_type=MESH,
            )

        def keep(kind):
            return pltpu.make_async_copy(
                qkv_sum.at[:, pl.ds(kind * cols, cols)],
                dealt.at[lax.rem(kind * ctx + me, kinds)],
                deal_sems.at[0, kind],
            )

        def is_far(kind):
            return (kind * ctx + me) // kinds != me

        for kind in range(kinds):
            pl.when(is_far(kind))(deal(kind).start)
            pl.when(jnp.logical_not(is_far(kind)))(keep(kind).start)

        normed_high_copy = to_high_side(
            *normed_args, normed_lows, normed_own, normed_x, normed_low, normed_high
        )
        out_args = (out_copies, out_loads)
        out_lows = {a: to_low_side(*out_args, out_own, out_x, out_low, a) for a in (1, 0)}

        def experts_end(kind):
            arrived(kind, 0)
            kept_loads[kind, 0].wait()
            sources = [kept.at[kind, 0], kept_low.at[kind, 0]]
            if kind > 0:
                high_copies[kind].wait_recv()
                sources.append(kept_high.at[kind])
            add_into((down_ref, gate_ref, up_ref)[kind], *sources)

        experts_end(0)

        normed_copies[0, 0].wait_recv()
        normed_loads[0, 0].wait()
        normed_lows[0].wait_recv()
        normed_high_copy.wait_recv()

        def norm_step(i, carry):
            span = pl.ds(pl.multiple_of(i * 16, 16), 16)
            grad = (
                normed_own[0, 0, span, :].astype(f32)
                + normed_x[0, 0, span, :].astype(f32)
                + normed_low[0, span, :].astype(f32)
                + normed_high[span, :].astype(f32)
            )
            values = tokens_ref[span, :].astype(f32)
            scale = rms_unit(values)
            unit = values * scale
            pulled = grad * gain_ref[...]
            input_ref[span, :] = mixed_ref[span, :] + scale * (
                pulled - unit * jnp.mean(unit * pulled, axis=-1, keepdims=True)
            )
            result_ref[span, :] = (forward_ref[span, :] + moved_ref[span, :].astype(f32)).astype(bf16)
            return carry

        lax.fori_loop(0, rows // 16, norm_step, 0)

        out_high_copy = to_high_side(*out_args, out_lows, out_own, out_x, out_low, out_high)
        experts_end(1)

        total = small_sum[...]
        for i, copy in enumerate(small_wide):
            copy.wait_recv()
            total = total + small_held[i]
        sums_ref[...] = total

        for kind in range(kinds):
            pl.when(is_far(kind))(deal(kind).wait_send)
            pl.when(jnp.logical_not(is_far(kind)))(keep(kind).wait)
        for slot in range(kinds):

            @pl.when(lax.rem(me * kinds + slot, ctx) != me)
            def _():
                pltpu.make_async_copy(
                    dealt.at[slot], dealt.at[slot], deal_sems.at[1, slot]
                ).wait()

            add_into(qkv_ref.at[:, pl.ds(slot * cols, cols)], dealt.at[slot])

        out_copies[0, 0].wait_recv()
        out_loads[0, 0].wait()
        out_lows[0].wait_recv()
        out_high_copy.wait_recv()
        add_into(out_ref, out_own.at[0, 0], out_x.at[0, 0], out_low.at[0], out_high)
        experts_end(2)
        for copy in all_sends:
            copy.wait_send()

    def block(*shape):
        return pltpu.VMEM(shape, bf16)

    gradient = (experts, units, cols)
    return comm_call(
        kernel,
        "finish_sums",
        collective_id,
        [
            jax.ShapeDtypeStruct(gradient, f32),
            jax.ShapeDtypeStruct(gradient, f32),
            jax.ShapeDtypeStruct(gradient, f32),
            jax.ShapeDtypeStruct((rows, width), f32),
            jax.ShapeDtypeStruct((part, cols), f32),
            jax.ShapeDtypeStruct((part, kinds * cols), f32),
            jax.ShapeDtypeStruct((small_rows, small_cols), f32),
            jax.ShapeDtypeStruct((rows, width), bf16),
        ],
        [ANY] * 8 + [VMEM] * 6,
        [VMEM] * 8,
        [
            block(kinds, 2, *gradient),
            block(kinds, 2, *gradient),
            block(kinds, *gradient),
            block(2, 2, rows, width),
            block(2, 2, rows, width),
            block(2, rows, width),
            block(rows, width),
            block(2, 2, part, cols),
            block(2, 2, part, cols),
            block(2, part, cols),
            block(part, cols),
            block(2, part, kinds * cols),
            block(2, part, kinds * cols),
            block(part, kinds * cols),
            block(part, kinds * cols),
            block(kinds, part, cols),
            pltpu.VMEM((fsdp - 1, small_rows, small_cols), f32),
            pltpu.VMEM((small_rows, small_cols), f32),
            pltpu.VMEM((ctx - 1, small_rows, small_cols), f32),
            DMA((copies_most,)),
            DMA((copies_most,)),
            DMA((32,)),
            DMA((2, kinds)),
        ],
        700 * 2**20,
        56,
    )(
        downs,
        ups,
        gate_far,
        gate_own,
        up_far,
        normed_part,
        out_part,
        qkv_part,
        small,
        tokens,
        mixed_grad,
        gain,
        mixed,
        moved,
    )


def gather_inputs(tokens, w_qkv, dy, row_arrays, block, flips, collective_id):
    ctx, fsdp = lax.axis_size("ctx"), lax.axis_size("fsdp")
    rows, width = tokens.shape
    part = w_qkv.shape[0]
    kinds = 3
    cols = width // ctx
    line = ctx // 2
    chunks = 2
    size = rows // chunks
    row_count, flip_count = len(row_arrays), len(flips)
    small_count = row_count + 1

    def kernel(*refs):
        tokens_ref, w_qkv_ref, dy_ref = refs[:3]
        small_refs = refs[3 : 3 + small_count]
        all_ref, weight_ref, dy_all_ref = refs[3 + small_count : 6 + small_count]
        small_all_refs = refs[6 + small_count : 6 + 2 * small_count]
        refs = refs[6 + 2 * small_count :]
        run_kernel(
            tokens_ref,
            w_qkv_ref,
            dy_ref,
            small_refs,
            all_ref,
            weight_ref,
            dy_all_ref,
            small_all_refs,
            *refs,
        )

    def run_kernel(
        tokens_ref,
        w_qkv_ref,
        dy_ref,
        small_refs,
        all_ref,
        weight_ref,
        dy_all_ref,
        small_all_refs,
        *refs,
    ):
        flip_refs, dy_line_ref, refs = refs[:flip_count], refs[flip_count], refs[flip_count + 1 :]
        sends, recvs, line_send, line_recv, cross_send, cross_recv, local_sems = refs
        me, mine = lax.axis_index("ctx"), lax.axis_index("fsdp")
        z, x = me // 2, lax.rem(me, 2)
        to_x = (flipped(me, 1), mine)
        core, chip = (me, flipped(mine, 1)), (me, flipped(mine, 2))
        others = [flipped_by(me, flip) for flip in flips]
        greet(
            [(lax.rem(me + step, ctx), mine) for step in range(1, ctx)]
            + [(me, lax.rem(mine + step, fsdp)) for step in range(1, fsdp)]
            + [(other, lax.rem(mine + step, fsdp)) for other in others for step in range(1, fsdp)]
        )
        used, used_local, started, kept = [0], [0], [], []

        def push(source, target, peer):
            i = used[0]
            used[0] += 1
            copy = send(source, target, sends.at[i], recvs.at[i], peer)
            started.append(copy)
            return copy

        def load(source, target):
            i = used_local[0]
            used_local[0] += 1
            copy = pltpu.make_async_copy(source, target, local_sems.at[i])
            copy.start()
            kept.append(copy)

        def token_block(index):
            return all_ref.at[pl.ds(pl.multiple_of(index * rows, rows), rows), :]

        def token_chunk(index, chunk):
            start = pl.multiple_of(index * rows + chunk * size, size)
            return all_ref.at[pl.ds(start, size), :]

        def taken(own, index, chunk):
            return tokens_ref.at[pl.ds(chunk * size, size), :] if own else token_chunk(index, chunk)

        def by_part(ref, index, count):
            return ref.at[pl.ds(pl.multiple_of(index * count, count), count), :]

        def cross(away, side, chunk):
            index = 2 * (z - away if side == 0 else z + away) + x
            i = side * line + away
            return pltpu.make_async_remote_copy(
                taken(away == 0, index, chunk),
                token_chunk(index, chunk),
                cross_send.at[i, chunk],
                cross_recv.at[i, chunk],
                device_id=to_x,
                device_id_type=MESH,
            )

        def along(away, side, chunk):
            index = 2 * (z - away if side == 0 else z + away) + x
            i = side * line + away
            return pltpu.make_async_remote_copy(
                taken(away == 0, index, chunk),
                token_chunk(index, chunk),
                line_send.at[i, chunk],
                line_recv.at[i, chunk],
                device_id=(me + 2 if side == 0 else me - 2, mine),
                device_id_type=MESH,
            )

        def has(away, side):
            return z >= away if side == 0 else z + away < line

        def goes_on(away, side):
            return jnp.logical_and(has(away, side), z < line - 1 if side == 0 else z > 0)

        for chunk in range(chunks):
            for side in range(2):
                pl.when(goes_on(0, side))(along(0, side, chunk).start)
            cross(0, 0, chunk).start()
        load(tokens_ref, token_block(me))

        weight_chip = []
        for kind in range(kinds):
            column = pl.ds(pl.multiple_of(kind * width + me * cols, cols), cols)
            target = by_part(weight_ref, mine, part).at[:, pl.ds(kind * cols, cols)]
            source = w_qkv_ref.at[:, column]
            weight_chip.append(push(source, target, chip))
            push(source, target, core)
            load(source, target)
        columns = pl.ds(pl.multiple_of(mine * part, part), part)
        for i, (source, target) in enumerate(zip(small_refs, small_all_refs)):
            if i < row_count:
                target = target.at[:, columns]
            else:
                target = target.at[mine]
            for step in range(1, fsdp):
                push(source, target, (me, lax.rem(mine + step, fsdp)))
            load(source, target)
        dy_chip = push(dy_ref, by_part(dy_all_ref, mine, rows), chip)
        push(dy_ref, by_part(dy_all_ref, mine, rows), core)
        load(dy_ref, by_part(dy_all_ref, mine, rows))

        for away in range(1, line):
            for chunk in range(chunks):
                for side in range(2):

                    @pl.when(has(away, side))
                    def _():
                        index = 2 * (z - away if side == 0 else z + away) + x
                        pltpu.make_async_copy(
                            taken(True, index, chunk),
                            token_chunk(index, chunk),
                            line_recv.at[side * line + away - 1, chunk],
                        ).wait()
                        cross(away, side, chunk).start()

                    if away < line - 1:
                        pl.when(goes_on(away, side))(along(away, side, chunk).start)
            if away == 1:
                for copy in weight_chip:
                    copy.wait_recv()
                far = by_part(weight_ref, flipped(mine, 2), part)
                push(far, far, core)
            if away == 2:
                dy_chip.wait_recv()
                far = by_part(dy_all_ref, flipped(mine, 2), rows)
                push(far, far, core)
        for other, target in zip(others, flip_refs):
            for step in range(fsdp):
                push(small_refs[-1], target.at[mine], (other, lax.rem(mine + step, fsdp)))
        for i in range(line):
            wide = 2 * cols
            to = flipped_by(me, 2 * i)
            source = dy_ref.at[:, pl.ds(pl.multiple_of(to // 2 * wide, wide), wide)]
            if i == 0:
                load(source, dy_line_ref.at[0])
            else:
                push(source, dy_line_ref.at[i], (to, mine))

        every = [(side, chunk) for side in range(2) for chunk in range(chunks)]
        for chunk in range(chunks):
            cross(0, 0, chunk).wait_recv()
        for away in range(1, line):
            for side, chunk in every:
                pl.when(has(away, side))(cross(away, side, chunk).wait_recv)
        for copy in started:
            if copy is not dy_chip and not any(copy is other for other in weight_chip):
                copy.wait_recv()
        for copy in kept:
            copy.wait()
        for copy in started:
            copy.wait_send()
        for chunk in range(chunks):
            cross(0, 0, chunk).wait_send()
        for away in range(line - 1):
            for side, chunk in every:
                pl.when(goes_on(away, side))(along(away, side, chunk).wait_send)
        for away in range(1, line):
            for side, chunk in every:
                pl.when(has(away, side))(cross(away, side, chunk).wait_send)

    return comm_call(
        kernel,
        "gather_inputs",
        collective_id,
        [
            jax.ShapeDtypeStruct((ctx * rows, width), tokens.dtype),
            jax.ShapeDtypeStruct((fsdp * part, kinds * cols), w_qkv.dtype),
            jax.ShapeDtypeStruct((fsdp * rows, width), dy.dtype),
        ]
        + [jax.ShapeDtypeStruct((row.shape[0], fsdp * part), row.dtype) for row in row_arrays]
        + [jax.ShapeDtypeStruct((fsdp,) + block.shape, block.dtype)] * (1 + flip_count)
        + [jax.ShapeDtypeStruct((line, rows, 2 * cols), dy.dtype)],
        [HBM] * (3 + small_count),
        [HBM] * (4 + small_count + flip_count),
        [
            DMA((64,)),
            DMA((64,)),
            DMA((2 * line, chunks)),
            DMA((2 * line, chunks)),
            DMA((2 * line, chunks)),
            DMA((2 * line, chunks)),
            DMA((16,)),
        ],
        150 * 2**20,
    )(tokens, w_qkv, dy, *row_arrays, block)


def project(tokens, gain, weight):
    total, width = tokens.shape
    wide = weight.shape[1]
    cols = wide // 3
    size = math.gcd(total, 256)
    f32 = jnp.float32

    def kernel(tokens_ref, gain_ref, weight_ref, normed_ref, lin_ref, squares_ref):
        values = tokens_ref[...].astype(f32)
        normed = (values * rms_unit(values) * gain_ref[...]).astype(jnp.bfloat16)
        normed_ref[...] = normed
        lin = jnp.dot(normed, weight_ref[...], preferred_element_type=f32)
        lin_ref[...] = lin
        for kind in range(2):
            piece = lin[:, kind * cols : (kind + 1) * cols]
            squares_ref[:, kind : kind + 1] = jnp.sum(piece * piece, axis=1, keepdims=True)

    def by_rows(columns):
        return pl.BlockSpec((size, columns), lambda i: (i, 0))

    return pl.pallas_call(
        kernel,
        grid=(total // size,),
        out_shape=[
            jax.ShapeDtypeStruct((total, width), jnp.bfloat16),
            jax.ShapeDtypeStruct((total, wide), f32),
            jax.ShapeDtypeStruct((total, 2), f32),
        ],
        in_specs=[
            by_rows(width),
            pl.BlockSpec((1, width), lambda i: (0, 0)),
            pl.BlockSpec((width, wide), lambda i: (0, 0)),
        ],
        out_specs=[by_rows(width), by_rows(wide), by_rows(2)],
        compiler_params=pltpu.CompilerParams(vmem_limit_bytes=24 * 2**20),
        cost_estimate=pl.CostEstimate(
            flops=3 * 10**9, bytes_accessed=15 * 2**20, transcendentals=0
        ),
        name="project",
    )(tokens, gain, weight)


def project_back(back, projected, scales, inner_sums, value_grad, weight, normed, tokens):
    total, width = tokens.shape
    wide = weight.shape[1]
    cols = wide // 3
    size = math.gcd(total, 256)
    steps, runs = total // size, 4
    f32, bf16 = jnp.float32, jnp.bfloat16

    def kernel(
        back_ref,
        lin_ref,
        scales_ref,
        sums_ref,
        value_ref,
        weight_ref,
        normed_ref,
        tokens_ref,
        part_ref,
        g_qkv_ref,
        gain_ref,
        proj,
    ):
        i = pl.program_id(0)

        @pl.when(i == 0)
        def _():
            gain_ref[...] = jnp.zeros_like(gain_ref)

        @pl.when(i < steps)
        def _():
            pieces = []
            for kind in range(2):
                scale = scales_ref[:, kind : kind + 1]
                unit = lin_ref[:, kind * cols : (kind + 1) * cols] * scale
                grad = scale * (back_ref[kind] - unit * sums_ref[:, kind : kind + 1])
                pieces.append(grad.astype(bf16))
            grads = jnp.concatenate(pieces + [value_ref[...]], axis=1)
            proj[pl.ds(pl.multiple_of(i * size, size), size), :] = grads
            part = lax.dot_general(
                grads, weight_ref[...], (((1,), (1,)), ((), ())), preferred_element_type=f32
            )
            values = tokens_ref[...].astype(f32)
            gain_ref[...] += jnp.sum(part * (values * rms_unit(values)), axis=0, keepdims=True)
            part_ref[...] = part.astype(bf16)

        @pl.when(i >= steps)
        def _():
            g_qkv_ref[...] = lax.dot_general(
                normed_ref[...], proj[...], (((0,), (0,)), ((), ())), preferred_element_type=f32
            ).astype(bf16)

    def by_rows(columns):
        return pl.BlockSpec((size, columns), lambda i: (jnp.minimum(i, steps - 1), 0))

    def later(i):
        return jnp.maximum(i - steps, 0)

    return pl.pallas_call(
        kernel,
        grid=(steps + runs,),
        out_shape=[
            jax.ShapeDtypeStruct((total, width), bf16),
            jax.ShapeDtypeStruct((width, wide), bf16),
            jax.ShapeDtypeStruct((1, width), f32),
        ],
        in_specs=[
            pl.BlockSpec((2, size, cols), lambda i: (0, jnp.minimum(i, steps - 1), 0)),
            by_rows(wide),
            by_rows(2),
            by_rows(2),
            by_rows(cols),
            pl.BlockSpec((width, wide), lambda i: (0, 0)),
            pl.BlockSpec((total, width // runs), lambda i: (0, later(i))),
            by_rows(width),
        ],
        out_specs=[
            by_rows(width),
            pl.BlockSpec((width // runs, wide), lambda i: (later(i), 0)),
            pl.BlockSpec((1, width), lambda i: (0, 0)),
        ],
        scratch_shapes=[pltpu.VMEM((total, wide), bf16)],
        compiler_params=pltpu.CompilerParams(vmem_limit_bytes=60 * 2**20),
        cost_estimate=pl.CostEstimate(flops=0, bytes_accessed=2**20, transcendentals=0),
        name="project_back",
    )(back, projected, scales, inner_sums, value_grad, weight, normed, tokens)


def on_device_heads(
    tokens,
    doc_lengths,
    routes,
    slot_order,
    attn_gain,
    w_qkv,
    q_gain,
    k_gain,
    w_out,
    ffn_gain,
    w_router,
    w_gate,
    w_up,
    w_down,
    cotangent,
):
    rows, width = tokens.shape[1], tokens.shape[2]
    ctx, fsdp = lax.axis_size("ctx"), lax.axis_size("fsdp")
    me = lax.axis_index("ctx")
    head_dim = width // HEADS
    cols = HEADS // ctx * head_dim
    part = width // fsdp
    total = rows * ctx
    lengths = doc_lengths[0]
    bf16, f32 = jnp.bfloat16, jnp.float32

    experts, top = w_gate.shape[0], routes.shape[2]
    gains = jnp.concatenate([attn_gain, q_gain, k_gain, ffn_gain]).reshape(4, part)
    router_rows = jnp.pad(w_router.T, ((0, ROUTER_ROWS - experts), (0, 0)))
    pairs = jnp.concatenate([routes[0].T, slot_order[0].T], axis=0)
    pairs = jnp.pad(pairs, ((0, -pairs.shape[0] % 8), (0, 0)))
    tokens_all, qkv_weight, dy_all, gains, router_rows, *pairs, dy_parts = gather_inputs(
        tokens[0], w_qkv, cotangent[0], [gains, router_rows], pairs, [1, 2, 4, 6], 9
    )
    row_gain_one, gain_query, gain_key, row_gain_two = (
        gains[i : i + 1].astype(f32) for i in range(4)
    )
    flips = [0, 2, 4, 6]
    dy_parts = lax.all_gather(dy_parts, "fsdp", axis=0)

    stream_pos = dealt_position(jnp.arange(total, dtype=jnp.int32), rows, ctx)
    stream_doc, stream_inner = document_info(stream_pos, lengths)
    cosine, sine_part = rope_tables(stream_inner, head_dim)
    turn_tables = (
        jnp.concatenate([cosine, cosine], axis=1),
        jnp.concatenate([-sine_part, sine_part], axis=1),
    )
    sight = (
        (stream_pos - stream_inner).reshape(total, 1),
        stream_pos.reshape(total, 1),
        stream_pos.reshape(1, total),
    )
    normed_all, projected, squares = project(tokens_all, row_gain_one, qkv_weight)
    squares = squares.T
    squares = ctx_sum(squares.reshape(-1, 128), 1).reshape(2, total)
    scales = lax.rsqrt(squares / width + EPSILON).T
    own_gains = [
        lax.dynamic_slice_in_dim(gain, me * cols, cols, 1) for gain in (gain_query, gain_key)
    ]
    own_gains = jnp.concatenate(own_gains, axis=1)
    low, attended, attended_low, tops = attend(
        projected, scales, own_gains, *turn_tables, *sight, cols
    )

    attended_part = heads_to_rows(attended_low, 2)
    mixed_part = dot32("td,de->te", attended_part, w_out).astype(bf16)
    inputs = tokens[0].astype(f32)
    group, mixed, crossed = reduce_then_gather(
        mixed_part,
        [tokens[0], row_gain_two],
        [jax.ShapeDtypeStruct((rows, width), f32)],
        norm_chunk,
        "mix_and_norm",
        6,
        True,
        [],
    )

    capacity = rows * top // experts
    slot_by_expert, slots_other, *slots_line = slots_of(pairs, experts, top)
    moved_part, group_grad, g_router, scaled, gate_low, up_low = run_experts(
        group, dy_all, slot_by_expert, router_rows, w_gate, w_up, w_down, fsdp, capacity
    )
    scaled_line = [scaled] + [swap(scaled, flip) for flip in flips[1:]]
    mixed_all, mixed_grad, g_ffn_gain, gate_other, up_other = reduce_then_gather(
        group_grad,
        [mixed, row_gain_two, cotangent[0]],
        [jax.ShapeDtypeStruct((rows, width), f32), jax.ShapeDtypeStruct((1, width), f32)],
        norm_back_chunk,
        "norm_back",
        7,
        False,
        [gate_low, up_low],
    )
    g_ffn_gain = g_ffn_gain[0]
    crossed = lax.all_gather(crossed, "fsdp", axis=0, tiled=True)
    ups = expert_grads(
        [gate_low, up_low], [gate_other, up_other], group, crossed, slot_by_expert, slots_other, capacity
    )
    ups, mixed_all = lax.optimization_barrier((ups, mixed_all))
    output_part = dot32("te,de->td", mixed_all, w_out).astype(bf16)
    output_grad = rows_to_heads(output_part, 3)
    output_grad, moved_part, ups, mixed_all, *scaled_line = lax.optimization_barrier(
        (output_grad, moved_part, ups, mixed_all, *scaled_line)
    )
    moved = lax.psum_scatter(moved_part, "fsdp", scatter_dimension=0, tiled=True)
    gate_far, gate_own = swap(ups[0, 0, 1], 2), swap(ups[0, 0, 0], 2)
    downs = down_grads(scaled_line, dy_parts, [slot_by_expert] + slots_line, capacity)
    g_out = dot32("td,te->de", attended_part, mixed_all).astype(bf16)
    output_grad, ups, downs, g_out = lax.optimization_barrier((output_grad, ups, downs, g_out))

    back, value_grad, own_g_gains, inner_sums = attend_back(
        output_grad, low, attended, tops, projected, scales, own_gains, *turn_tables, *sight
    )
    inner_sums, gate_far, gate_own = lax.optimization_barrier((inner_sums, gate_far, gate_own))
    inner_sums = ctx_sum(inner_sums.T.reshape(-1, 128), 1)
    inner_sums, ups = lax.optimization_barrier((inner_sums, ups))
    up_far = swap(ups[1, 0, 1], 2)
    inner_sums = inner_sums.reshape(2, total).T / width

    normed_grad_part, g_qkv, g_attn_gain = project_back(
        back, projected, scales, inner_sums, value_grad, qkv_weight, normed_all, tokens_all
    )
    g_attn_gain = g_attn_gain[0]

    def placed_cols(values):
        return lax.dynamic_update_slice_in_dim(jnp.zeros((width,), f32), values, me * cols, 0)

    sums = jnp.concatenate(
        [
            jnp.stack([g_attn_gain, placed_cols(own_g_gains[0, 0]), placed_cols(own_g_gains[1, 0]), g_ffn_gain]),
            g_router[:experts],
        ],
        axis=0,
    )
    down_parts, gate_parts, up_parts, input_grad, out_part, qkv_part, sums, activations = finish_sums(
        downs,
        ups,
        gate_far,
        gate_own,
        up_far,
        normed_grad_part,
        g_out,
        g_qkv,
        jnp.pad(sums, ((0, -sums.shape[0] % 8), (0, 0))),
        tokens[0],
        mixed_grad,
        row_gain_one,
        mixed,
        moved,
        8,
    )
    return (
        activations[None],
        input_grad[None],
        sums[0],
        qkv_part,
        sums[1],
        sums[2],
        out_part,
        sums[3],
        sums[4 : 4 + experts].T,
        gate_parts,
        up_parts,
        down_parts,
    )


def solution(mesh):
    in_specs = (
        P("fsdp", "ctx", None),
        P("fsdp", None),
        P("fsdp", "ctx", None),
        P("fsdp", "ctx", None),
        P("fsdp"),
        P("fsdp", None),
        P("fsdp"),
        P("fsdp"),
        P("fsdp", None),
        P("fsdp"),
        P("fsdp", None),
        P(None, None, "fsdp"),
        P(None, None, "fsdp"),
        P(None, "fsdp", None),
        P("fsdp", "ctx", None),
    )
    out_specs = (
        P("fsdp", "ctx", None),
        P("fsdp", "ctx", None),
        P("fsdp"),
        P("fsdp", "ctx"),
        P("fsdp"),
        P("fsdp"),
        P("fsdp", "ctx"),
        P("fsdp"),
        P("fsdp", None),
        P(None, "ctx", "fsdp"),
        P(None, "ctx", "fsdp"),
        P(None, "fsdp", "ctx"),
    )
    ctx, fsdp = mesh.shape["ctx"], mesh.shape["fsdp"]
    by_heads = HEADS % ctx == 0 and ctx == 8 and fsdp == 4
    body = on_device_heads if by_heads else on_device
    return jax.shard_map(
        body, mesh=mesh, in_specs=in_specs, out_specs=out_specs, check_vma=False
    )
```

```python
import math

import jax
import jax.numpy as jnp
from jax import lax
from jax.experimental import pallas as pl
from jax.experimental.pallas import tpu as pltpu
from jax.sharding import PartitionSpec as P

HEADS = 16
MESH = pl.DeviceIdType.MESH
ANY = pl.BlockSpec(memory_space=pl.ANY)
VMEM = pl.BlockSpec(memory_space=pltpu.VMEM)
DMA = pltpu.SemaphoreType.DMA

EPSILON = 1e-05
ROPE_BASE = 10000.0
MASKED = -1e30


def rms_scale(values, gain_vector):
    return (
        values
        * lax.rsqrt(jnp.mean(values * values, axis=-1, keepdims=True) + EPSILON)
        * gain_vector
    )


def rotate(values, inner_pos):
    half_dim = values.shape[-1] // 2
    freq_table = ROPE_BASE ** (-2.0 * jnp.arange(half_dim, dtype=jnp.float32) / values.shape[-1])
    angles = inner_pos.astype(jnp.float32)[:, None] * freq_table[None, :]
    cosine = jnp.cos(angles)[:, None, :]
    sine_part = jnp.sin(angles)[:, None, :]
    first_half = values[..., :half_dim]
    second_half = values[..., half_dim:]
    return jnp.concatenate(
        [
            first_half * cosine - second_half * sine_part,
            second_half * cosine + first_half * sine_part,
        ],
        axis=-1,
    )


def dealt_position(flat_index, per_device, device_count):
    device_index = flat_index // per_device
    within = flat_index % per_device
    half_rows = per_device // 2
    return jnp.where(
        within < half_rows,
        device_index * half_rows + within,
        (2 * device_count - 1 - device_index) * half_rows + within - half_rows,
    )


def document_info(positions, lengths):
    doc_ends = jnp.sum(jnp.where(jnp.arange(lengths.shape[0])[:, None] >= jnp.arange(lengths.shape[0])[None, :], lengths[None, :], 0), axis=1)
    passed = doc_ends[None, :] <= positions[:, None]
    doc_ids = jnp.sum(passed.astype(jnp.int32), axis=1)
    inner_pos = positions - jnp.sum(jnp.where(passed, lengths[None, :], 0), axis=1)
    return (doc_ids, inner_pos)


def slot_table(route_ids, order_ids, capacity, expert_count):
    pair_count = route_ids.shape[0] * route_ids.shape[1]
    expert_flat = route_ids.reshape(pair_count)
    rank_flat = order_ids.reshape(pair_count)
    earlier = (expert_flat[None, :] == expert_flat[:, None]) & (
        rank_flat[None, :] < rank_flat[:, None]
    )
    slot_index = jnp.sum(earlier.astype(jnp.int32), axis=1)
    placed = jnp.where(
        slot_index < capacity, expert_flat * capacity + slot_index, expert_count * capacity
    )
    source = (
        jnp.full((expert_count * capacity + 1,), pair_count, jnp.int32)
        .at[placed]
        .set(jnp.arange(pair_count, dtype=jnp.int32))
    )
    return (placed, source[: expert_count * capacity])


def masked_scores(query_block, key_block, query_pos, query_doc, key_pos, key_doc, score_scale):
    scores = (
        jnp.einsum("qhd,khd->hqk", query_block, key_block, preferred_element_type=jnp.float32)
        * score_scale
    )
    allowed = (query_doc[:, None] == key_doc[None, :]) & (key_pos[None, :] <= query_pos[:, None])
    return jnp.where(allowed[None], scores, MASKED)


def silu_parts(hidden_grad, slot_gate, slot_up):
    sigma = jax.nn.sigmoid(slot_gate)
    gate_grad_low = (hidden_grad * slot_up * sigma * (1.0 + slot_gate * (1.0 - sigma))).astype(
        jnp.bfloat16
    )
    up_grad_low = (hidden_grad * slot_gate * sigma).astype(jnp.bfloat16)
    return (gate_grad_low, up_grad_low)


def on_device(
    tokens,
    doc_lengths,
    routes,
    slot_order,
    attn_gain,
    w_qkv,
    q_gain,
    k_gain,
    w_out,
    ffn_gain,
    w_router,
    w_gate,
    w_up,
    w_down,
    cotangent,
):
    row_count = tokens.shape[1]
    model_width = tokens.shape[2]
    head_count = HEADS
    head_dim = model_width // head_count
    score_scale = head_dim ** (-0.5)
    ctx_count = lax.axis_size("ctx")
    ctx_index = lax.axis_index("ctx")
    total_rows = row_count * ctx_count
    lengths = doc_lengths[0]
    local_pos = dealt_position(
        ctx_index * row_count + jnp.arange(row_count, dtype=jnp.int32), row_count, ctx_count
    )
    local_doc, local_inner = document_info(local_pos, lengths)
    stream_pos = dealt_position(jnp.arange(total_rows, dtype=jnp.int32), row_count, ctx_count)
    stream_doc, stream_inner = document_info(stream_pos, lengths)
    block_rows = math.gcd(total_rows, 512)
    block_count = total_rows // block_rows
    block_ids = jnp.arange(block_count, dtype=jnp.int32)
    gain_one, qkv_weight, gain_query, gain_key, out_weight = (
        lax.all_gather(attn_gain, "fsdp", axis=0, tiled=True),
        lax.all_gather(w_qkv, "fsdp", axis=0, tiled=True),
        lax.all_gather(q_gain, "fsdp", axis=0, tiled=True),
        lax.all_gather(k_gain, "fsdp", axis=0, tiled=True),
        lax.all_gather(w_out, "fsdp", axis=0, tiled=True),
    )
    gain_two, router_weight, gate_weight, up_weight, down_weight = (
        lax.all_gather(ffn_gain, "fsdp", axis=0, tiled=True),
        lax.all_gather(w_router, "fsdp", axis=0, tiled=True),
        lax.all_gather(w_gate, "fsdp", axis=2, tiled=True),
        lax.all_gather(w_up, "fsdp", axis=2, tiled=True),
        lax.all_gather(w_down, "fsdp", axis=1, tiled=True),
    )
    inputs = tokens[0].astype(jnp.float32)
    normed_f, norm_one_pull = jax.vjp(rms_scale, inputs, gain_one.astype(jnp.float32))
    normed_low = normed_f.astype(jnp.bfloat16)
    projected = jnp.dot(normed_low, qkv_weight, preferred_element_type=jnp.float32)
    query_lin = projected[:, :model_width]
    key_lin = projected[:, model_width : 2 * model_width]
    value_low = (
        projected[:, 2 * model_width :]
        .astype(jnp.bfloat16)
        .reshape(row_count, head_count, head_dim)
    )

    def head_shape(values, gain_vector):
        return rotate(
            rms_scale(values, gain_vector).reshape(row_count, head_count, head_dim), local_inner
        )

    query_f, query_pull = jax.vjp(head_shape, query_lin, gain_query.astype(jnp.float32))
    key_f, key_pull = jax.vjp(head_shape, key_lin, gain_key.astype(jnp.float32))
    query_low = query_f.astype(jnp.bfloat16)
    key_low = key_f.astype(jnp.bfloat16)
    keys_all, values_all = (
        lax.all_gather(key_low, "ctx", axis=0, tiled=True),
        lax.all_gather(value_low, "ctx", axis=0, tiled=True),
    )

    def key_slice(block_index):
        first_row = block_index * block_rows
        return (
            lax.dynamic_slice_in_dim(keys_all, first_row, block_rows, 0),
            lax.dynamic_slice_in_dim(values_all, first_row, block_rows, 0),
            lax.dynamic_slice_in_dim(stream_pos, first_row, block_rows, 0),
            lax.dynamic_slice_in_dim(stream_doc, first_row, block_rows, 0),
        )

    def stats_step(carry, block_index):
        running_top, running_total = carry
        key_block, value_block, key_pos, key_doc = key_slice(block_index)
        scores = masked_scores(
            query_low, key_block, local_pos, local_doc, key_pos, key_doc, score_scale
        )
        new_top = jnp.maximum(running_top, jnp.max(scores, axis=-1))
        running_total = running_total * jnp.exp(running_top - new_top) + jnp.sum(
            jnp.exp(scores - new_top[..., None]), axis=-1
        )
        return ((new_top, running_total), None)

    start_stats = (
        jnp.full((head_count, row_count), MASKED, jnp.float32),
        jnp.zeros((head_count, row_count), jnp.float32),
    )
    (score_top, score_total), _ = lax.scan(stats_step, start_stats, block_ids)
    log_total = score_top + jnp.log(score_total)

    def output_step(accum, block_index):
        key_block, value_block, key_pos, key_doc = key_slice(block_index)
        scores = masked_scores(
            query_low, key_block, local_pos, local_doc, key_pos, key_doc, score_scale
        )
        prob_block = jnp.exp(scores - log_total[..., None]).astype(jnp.bfloat16)
        return (
            accum
            + jnp.einsum(
                "hqk,khd->qhd", prob_block, value_block, preferred_element_type=jnp.float32
            ),
            None,
        )

    attended_f, _ = lax.scan(
        output_step, jnp.zeros((row_count, head_count, head_dim), jnp.float32), block_ids
    )
    attended_low = attended_f.reshape(row_count, model_width).astype(jnp.bfloat16)
    mixed = inputs + jnp.dot(attended_low, out_weight, preferred_element_type=jnp.float32)
    normed_two_f, norm_two_pull = jax.vjp(rms_scale, mixed, gain_two.astype(jnp.float32))
    normed_two = normed_two_f.astype(jnp.bfloat16)
    expert_count = gate_weight.shape[0]
    route_ids = routes[0]
    top_count = route_ids.shape[1]
    pair_count = row_count * top_count
    capacity = pair_count // expert_count
    logits = jnp.dot(normed_two, router_weight, preferred_element_type=jnp.float32)
    router_probs = jax.nn.softmax(logits, axis=-1)
    chosen = (
        route_ids[:, :, None] == jnp.arange(expert_count, dtype=jnp.int32)[None, None, :]
    ).astype(jnp.float32)
    gate_values = jnp.sum(chosen * router_probs[:, None, :], axis=-1)
    placed, source = slot_table(route_ids, slot_order[0], capacity, expert_count)
    padded_in = jnp.concatenate([normed_two, jnp.zeros((1, model_width), jnp.bfloat16)], axis=0)
    expert_in = padded_in[source // top_count].reshape(expert_count, capacity, model_width)
    gate_pre = jnp.einsum(
        "ecd,edh->ech", expert_in, gate_weight, preferred_element_type=jnp.float32
    )
    up_pre = jnp.einsum("ecd,edh->ech", expert_in, up_weight, preferred_element_type=jnp.float32)
    hidden_low = (jax.nn.silu(gate_pre) * up_pre).astype(jnp.bfloat16)
    expert_out = jnp.einsum(
        "ech,ehd->ecd", hidden_low, down_weight, preferred_element_type=jnp.float32
    )
    out_padded = jnp.concatenate(
        [
            expert_out.reshape(expert_count * capacity, model_width),
            jnp.zeros((1, model_width), jnp.float32),
        ],
        axis=0,
    )
    per_pair = out_padded[placed].reshape(row_count, top_count, model_width)
    layer_out = mixed + jnp.sum(gate_values[:, :, None] * per_pair, axis=1)
    out_grad = cotangent[0].astype(jnp.float32)
    gate_grad = jnp.sum(out_grad[:, None, :] * per_pair, axis=-1)
    pair_grad = (gate_values[:, :, None] * out_grad[:, None, :]).reshape(pair_count, model_width)
    pair_padded = jnp.concatenate([pair_grad, jnp.zeros((1, model_width), jnp.float32)], axis=0)
    slot_grad = (
        pair_padded[source].reshape(expert_count, capacity, model_width).astype(jnp.bfloat16)
    )

    def expert_step(carry, pieces):
        slot_in, slot_hidden, slot_dy, slot_gate, slot_up, gate_matrix, up_matrix, down_matrix = (
            pieces
        )
        hidden_grad = jnp.einsum(
            "cd,hd->ch", slot_dy, down_matrix, preferred_element_type=jnp.float32
        )
        gate_grad_low, up_grad_low = silu_parts(hidden_grad, slot_gate, slot_up)
        in_grad = jnp.einsum(
            "ch,dh->cd", gate_grad_low, gate_matrix, preferred_element_type=jnp.float32
        ) + jnp.einsum("ch,dh->cd", up_grad_low, up_matrix, preferred_element_type=jnp.float32)
        gate_term = jnp.einsum(
            "cd,ch->dh", slot_in, gate_grad_low, preferred_element_type=jnp.float32
        )
        up_term = jnp.einsum("cd,ch->dh", slot_in, up_grad_low, preferred_element_type=jnp.float32)
        down_term = jnp.einsum(
            "ch,cd->hd", slot_hidden, slot_dy, preferred_element_type=jnp.float32
        )
        gate_shard, up_shard, down_shard = (
            lax.psum_scatter(
                gate_term.astype(jnp.bfloat16), "fsdp", scatter_dimension=1, tiled=True
            ).astype(jnp.float32),
            lax.psum_scatter(
                up_term.astype(jnp.bfloat16), "fsdp", scatter_dimension=1, tiled=True
            ).astype(jnp.float32),
            lax.psum_scatter(
                down_term.astype(jnp.bfloat16), "fsdp", scatter_dimension=0, tiled=True
            ).astype(jnp.float32),
        )
        gate_part, up_part, down_part = (
            lax.psum_scatter(
                gate_shard.astype(jnp.bfloat16), "ctx", scatter_dimension=0, tiled=True
            ).astype(jnp.float32),
            lax.psum_scatter(
                up_shard.astype(jnp.bfloat16), "ctx", scatter_dimension=0, tiled=True
            ).astype(jnp.float32),
            lax.psum_scatter(
                down_shard.astype(jnp.bfloat16), "ctx", scatter_dimension=1, tiled=True
            ).astype(jnp.float32),
        )
        return (carry, (in_grad, gate_part, up_part, down_part))

    _, (expert_in_grad, gate_parts, up_parts, down_parts) = lax.scan(
        expert_step,
        None,
        (expert_in, hidden_low, slot_grad, gate_pre, up_pre, gate_weight, up_weight, down_weight),
    )
    in_padded = jnp.concatenate(
        [
            expert_in_grad.reshape(expert_count * capacity, model_width),
            jnp.zeros((1, model_width), jnp.float32),
        ],
        axis=0,
    )
    normed_two_grad = jnp.sum(in_padded[placed].reshape(row_count, top_count, model_width), axis=1)
    prob_grad_router = jnp.sum(chosen * gate_grad[:, :, None], axis=1)
    logit_grad = (
        router_probs
        * (prob_grad_router - jnp.sum(router_probs * prob_grad_router, axis=-1, keepdims=True))
    ).astype(jnp.bfloat16)
    normed_two_grad = normed_two_grad + jnp.einsum(
        "te,de->td", logit_grad, router_weight, preferred_element_type=jnp.float32
    )
    router_grad = jnp.einsum(
        "td,te->de", normed_two, logit_grad, preferred_element_type=jnp.float32
    )
    mixed_norm_grad, gain_two_grad = norm_two_pull(normed_two_grad)
    mixed_grad = out_grad + mixed_norm_grad
    mixed_low = mixed_grad.astype(jnp.bfloat16)
    out_weight_grad = jnp.einsum(
        "td,te->de", attended_low, mixed_low, preferred_element_type=jnp.float32
    )
    output_grad = (
        jnp.einsum("te,de->td", mixed_low, out_weight, preferred_element_type=jnp.float32)
        .astype(jnp.bfloat16)
        .reshape(row_count, head_count, head_dim)
    )
    row_delta = jnp.sum(output_grad.astype(jnp.float32) * attended_f, axis=-1).T

    def query_grad_step(accum, block_index):
        key_block, value_block, key_pos, key_doc = key_slice(block_index)
        scores = masked_scores(
            query_low, key_block, local_pos, local_doc, key_pos, key_doc, score_scale
        )
        prob_block = jnp.exp(scores - log_total[..., None])
        prob_grad = jnp.einsum(
            "qhd,khd->hqk", output_grad, value_block, preferred_element_type=jnp.float32
        )
        score_grad = (prob_block * (prob_grad - row_delta[..., None])).astype(jnp.bfloat16)
        return (
            accum
            + jnp.einsum("hqk,khd->qhd", score_grad, key_block, preferred_element_type=jnp.float32)
            * score_scale,
            None,
        )

    query_grad, _ = lax.scan(
        query_grad_step, jnp.zeros((row_count, head_count, head_dim), jnp.float32), block_ids
    )
    inner_rows = math.gcd(row_count * lax.axis_size("ctx"), 512)

    def piece_step(carry, piece_index):
        first_row = piece_index * inner_rows
        key_block = lax.dynamic_slice_in_dim(keys_all, first_row, inner_rows, 0)
        value_block = lax.dynamic_slice_in_dim(values_all, first_row, inner_rows, 0)
        key_pos = lax.dynamic_slice_in_dim(stream_pos, first_row, inner_rows, 0)
        key_doc = lax.dynamic_slice_in_dim(stream_doc, first_row, inner_rows, 0)
        scores = masked_scores(
            query_low, key_block, local_pos, local_doc, key_pos, key_doc, score_scale
        )
        prob_block = jnp.exp(scores - log_total[..., None])
        prob_grad = jnp.einsum(
            "qhd,khd->hqk", output_grad, value_block, preferred_element_type=jnp.float32
        )
        score_grad = (prob_block * (prob_grad - row_delta[..., None])).astype(jnp.bfloat16)
        value_part = jnp.einsum(
            "hqk,qhd->khd",
            prob_block.astype(jnp.bfloat16),
            output_grad,
            preferred_element_type=jnp.float32,
        )
        key_part = (
            jnp.einsum("hqk,qhd->khd", score_grad, query_low, preferred_element_type=jnp.float32)
            * score_scale
        )
        return (
            carry,
            jnp.concatenate(
                [
                    key_part.reshape(inner_rows, model_width),
                    value_part.reshape(inner_rows, model_width),
                ],
                axis=1,
            ),
        )

    _, stacked = lax.scan(
        piece_step,
        None,
        jnp.arange(row_count * lax.axis_size("ctx") // inner_rows, dtype=jnp.int32),
    )
    key_value_grad = lax.psum_scatter(
        stacked.reshape(row_count * lax.axis_size("ctx"), 2 * model_width).astype(jnp.bfloat16),
        "ctx",
        scatter_dimension=0,
        tiled=True,
    ).astype(jnp.float32)
    key_grad = key_value_grad[:, :model_width].reshape(row_count, head_count, head_dim)
    value_grad = key_value_grad[:, model_width:]
    query_lin_grad, gain_query_grad = query_pull(query_grad)
    key_lin_grad, gain_key_grad = key_pull(key_grad)
    proj_grad = jnp.concatenate(
        [
            query_lin_grad.astype(jnp.bfloat16),
            key_lin_grad.astype(jnp.bfloat16),
            value_grad.astype(jnp.bfloat16),
        ],
        axis=1,
    )
    qkv_weight_grad = jnp.einsum(
        "td,te->de", normed_low, proj_grad, preferred_element_type=jnp.float32
    )
    normed_grad = jnp.einsum("te,de->td", proj_grad, qkv_weight, preferred_element_type=jnp.float32)
    input_norm_grad, gain_one_grad = norm_one_pull(normed_grad)
    input_grad = mixed_grad + input_norm_grad
    qkv_shard, out_shard = (
        lax.psum_scatter(
            qkv_weight_grad.astype(jnp.bfloat16), "fsdp", scatter_dimension=0, tiled=True
        ).astype(jnp.float32),
        lax.psum_scatter(
            out_weight_grad.astype(jnp.bfloat16), "fsdp", scatter_dimension=0, tiled=True
        ).astype(jnp.float32),
    )
    qkv_part, out_part = (
        lax.psum_scatter(
            qkv_shard.astype(jnp.bfloat16), "ctx", scatter_dimension=1, tiled=True
        ).astype(jnp.float32),
        lax.psum_scatter(
            out_shard.astype(jnp.bfloat16), "ctx", scatter_dimension=1, tiled=True
        ).astype(jnp.float32),
    )
    gain_one_sum, gain_query_sum, gain_key_sum, gain_two_sum, router_sum = lax.psum(
        (gain_one_grad, gain_query_grad, gain_key_grad, gain_two_grad, router_grad), ("ctx", "fsdp")
    )
    shard_rows = model_width // lax.axis_size("fsdp")
    shard_start = lax.axis_index("fsdp") * shard_rows

    def own_rows(full_array):
        return lax.dynamic_slice_in_dim(full_array, shard_start, shard_rows, 0)

    return (
        layer_out.astype(jnp.bfloat16)[None],
        input_grad[None],
        own_rows(gain_one_sum),
        qkv_part,
        own_rows(gain_query_sum),
        own_rows(gain_key_sum),
        out_part,
        own_rows(gain_two_sum),
        own_rows(router_sum),
        gate_parts,
        up_parts,
        down_parts,
    )


def rms_unit(values):
    return lax.rsqrt(jnp.mean(values * values, axis=-1, keepdims=True) + EPSILON)


def rope_tables(inner_pos, head_dim):
    half_dim = head_dim // 2
    freq_table = ROPE_BASE ** (-2.0 * jnp.arange(half_dim, dtype=jnp.float32) / head_dim)
    angles = inner_pos.astype(jnp.float32)[:, None] * freq_table[None, :]
    return (jnp.cos(angles), jnp.sin(angles))


def dot32(spec, left, right):
    return jnp.einsum(spec, left, right, preferred_element_type=jnp.float32)


def greet(peers):
    barrier = pltpu.get_barrier_semaphore()
    for peer in peers:
        pl.semaphore_signal(barrier, inc=1, device_id=peer, device_id_type=MESH)
    pl.semaphore_wait(barrier, len(peers))


def send(source, target, send_sem, recv_sem, peer):
    copy = pltpu.make_async_remote_copy(
        source, target, send_sem, recv_sem, device_id=peer, device_id_type=MESH
    )
    copy.start()
    return copy


def comm_call(
    kernel, name, collective_id, out_shape, in_specs, out_specs, scratch_shapes, cost, vmem=16
):
    return pl.pallas_call(
        kernel,
        out_shape=out_shape,
        in_specs=in_specs,
        out_specs=out_specs,
        scratch_shapes=scratch_shapes,
        compiler_params=pltpu.CompilerParams(
            collective_id=collective_id, has_side_effects=True, vmem_limit_bytes=vmem * 2**20
        ),
        cost_estimate=pl.CostEstimate(flops=0, bytes_accessed=cost, transcendentals=0),
        name=name,
    )


def ctx_sum(values, collective_id):
    ctx = lax.axis_size("ctx")

    def kernel(own_ref, out_ref, held, send_sems, recv_sems):
        me, mine = lax.axis_index("ctx"), lax.axis_index("fsdp")
        peers = [(lax.rem(me + step, ctx), mine) for step in range(1, ctx)]
        greet(peers)
        copies = [
            send(own_ref, held.at[i], send_sems.at[i], recv_sems.at[i], peer)
            for i, peer in enumerate(peers)
        ]
        total = own_ref[...]
        for i, copy in enumerate(copies):
            copy.wait_recv()
            total = total + held[i]
        out_ref[...] = total
        for copy in copies:
            copy.wait_send()

    return comm_call(
        kernel,
        "ctx_sum",
        collective_id,
        jax.ShapeDtypeStruct(values.shape, values.dtype),
        [VMEM],
        VMEM,
        [
            pltpu.VMEM((ctx - 1,) + values.shape, values.dtype),
            DMA((ctx - 1,)),
            DMA((ctx - 1,)),
        ],
        20 * 2**20,
    )(values)


def heads_to_rows(values, collective_id):
    ctx, fsdp = lax.axis_size("ctx"), lax.axis_size("fsdp")
    rows, cols = values.shape[0] // ctx, values.shape[1]
    share = ctx // fsdp

    def kernel(own_ref, out_ref, send_sems, recv_sems):
        me, mine = lax.axis_index("ctx"), lax.axis_index("fsdp")
        keeper, place = me // share, lax.rem(me, share)
        own_keeper = (keeper == mine).astype(jnp.int32)
        barrier = pltpu.get_barrier_semaphore()
        for step in range(share * fsdp):
            source, stream = mine * share + step // fsdp, step % fsdp

            @pl.when(jnp.logical_or(source != me, stream != mine))
            def _():
                pl.semaphore_signal(
                    barrier, inc=1, device_id=(source, stream), device_id_type=MESH
                )

        pl.semaphore_wait(barrier, ctx - own_keeper)

        def block(index):
            return own_ref.at[pl.ds(pl.multiple_of(index * rows, rows), rows), :]

        def landing(stream, position):
            return out_ref.at[
                pl.ds(pl.multiple_of(stream * rows, rows), rows),
                pl.ds(pl.multiple_of(position * cols, cols), cols),
            ]

        slot = place * fsdp + mine

        def copy_to(step):
            other = lax.rem(me + step, ctx)
            return pltpu.make_async_remote_copy(
                block(other),
                landing(mine, place),
                send_sems.at[step],
                recv_sems.at[slot],
                device_id=(other, keeper),
                device_id_type=MESH,
            )

        kept = pltpu.make_async_copy(block(me), landing(mine, place), send_sems.at[0])
        for step in range(1, ctx):
            copy_to(step).start()

        @pl.when(own_keeper == 0)
        def _():
            copy_to(0).start()

        @pl.when(own_keeper == 1)
        def _():
            kept.start()
            kept.wait()

        for step in range(share * fsdp):

            @pl.when(
                jnp.logical_or(mine * share + step // fsdp != me, step % fsdp != mine)
            )
            def _():
                pltpu.make_async_copy(
                    block(0), landing(step % fsdp, step // fsdp), recv_sems.at[step]
                ).wait()

        for step in range(1, ctx):
            copy_to(step).wait_send()

        @pl.when(own_keeper == 0)
        def _():
            copy_to(0).wait_send()

    return comm_call(
        kernel,
        "heads_to_rows",
        collective_id,
        jax.ShapeDtypeStruct((fsdp * rows, share * cols), values.dtype),
        [ANY],
        ANY,
        [DMA((ctx,)), DMA((share * fsdp,))],
        40 * 2**20,
    )(values)


def rows_to_heads(values, collective_id):
    ctx, fsdp = lax.axis_size("ctx"), lax.axis_size("fsdp")
    share = ctx // fsdp
    rows, cols = values.shape[0] // fsdp, values.shape[1] // share

    def kernel(own_ref, out_ref, stage, stage_send, stage_recv, send_sems, recv_sems, done_sem):
        me, mine = lax.axis_index("ctx"), lax.axis_index("fsdp")
        ctx_peers = [(lax.rem(me + step, ctx), mine) for step in range(1, ctx)]
        greet(ctx_peers + [(me, lax.rem(mine + step, fsdp)) for step in range(1, fsdp)])

        def block(stream):
            return own_ref.at[pl.ds(pl.multiple_of(stream * rows, rows), rows), :]

        def landing(index):
            return out_ref.at[pl.ds(pl.multiple_of(index * rows, rows), rows), :]

        steps = [2, 3, 1]
        staged = {
            step: send(
                block(lax.rem(mine + step, fsdp)),
                stage.at[fsdp - step],
                stage_send.at[step],
                stage_recv.at[fsdp - step],
                (me, lax.rem(mine + step, fsdp)),
            )
            for step in steps
        }

        def piece(step, place):
            span = pl.ds(place * cols, cols)
            if step == 0:
                return own_ref.at[pl.ds(pl.multiple_of(mine * rows, rows), rows), span]
            return stage.at[step, :, span]

        def target(step, place):
            return lax.rem(mine + step, fsdp) * share + place

        def copy_to(step, place):
            return pltpu.make_async_remote_copy(
                piece(step, place),
                landing(me),
                send_sems.at[step * share + place],
                recv_sems.at[me],
                device_id=(target(step, place), mine),
                device_id_type=MESH,
            )

        def keep(step, place):
            return pltpu.make_async_copy(
                piece(step, place), landing(me), send_sems.at[step * share + place]
            )

        for step in [0, 1, 2, 3]:
            if step > 0:
                staged[fsdp - step].wait_recv()
            for place in range(share):
                far = target(step, place) != me
                pl.when(far)(copy_to(step, place).start)
                pl.when(jnp.logical_not(far))(keep(step, place).start)
        for step in range(1, ctx):
            source = lax.rem(me + step, ctx)
            pltpu.make_async_copy(
                piece(0, 0), landing(source), recv_sems.at[source]
            ).wait()
        for step in range(fsdp):
            for place in range(share):
                far = target(step, place) != me
                pl.when(far)(copy_to(step, place).wait_send)
                pl.when(jnp.logical_not(far))(keep(step, place).wait)
        for copy in staged.values():
            copy.wait_send()
        for peer in ctx_peers:
            pl.semaphore_signal(done_sem, inc=1, device_id=peer, device_id_type=MESH)
        pl.semaphore_wait(done_sem, ctx - 1)

    return comm_call(
        kernel,
        "rows_to_heads",
        collective_id,
        jax.ShapeDtypeStruct((ctx * rows, cols), values.dtype),
        [ANY],
        ANY,
        [
            pltpu.VMEM((fsdp, rows, share * cols), values.dtype),
            DMA((fsdp,)),
            DMA((fsdp,)),
            DMA((ctx,)),
            DMA((ctx,)),
            pltpu.SemaphoreType.REGULAR,
        ],
        2**20,
    )(values)


def swap(values, flip):
    return lax.ppermute(values, "ctx", [(i, i ^ flip) for i in range(lax.axis_size("ctx"))])


def reduce_then_gather(partial, extras, out_shapes, chunk_math, name, collective_id, crossed, bulk):
    ctx, fsdp = lax.axis_size("ctx"), lax.axis_size("fsdp")
    rows, width = partial.shape[0] // fsdp, partial.shape[1]
    chunks = 4
    size = rows // chunks
    count = len(extras)
    cols = width // ctx
    if crossed:
        out_shapes = out_shapes + [jax.ShapeDtypeStruct((rows, width // 2), jnp.bfloat16)]
    bulk_count, out_count = len(bulk), len(out_shapes)

    def kernel(*refs):
        part_ref, extra_refs = refs[0], refs[1 : 1 + count]
        bulk_refs, refs = refs[1 + count : 1 + count + bulk_count], refs[1 + count + bulk_count :]
        all_ref, out_refs = refs[0], refs[1 : 1 + out_count]
        bulk_out_refs, refs = refs[1 + out_count : 1 + out_count + bulk_count], refs[1 + out_count :]
        near_own, near_far, far_sum, far_own, sems, cross_sems, bulk_sems = refs[bulk_count:]
        me, mine = lax.axis_index("ctx"), lax.axis_index("fsdp")
        flip = 1 - 2 * lax.rem(mine, 2)
        core = mine + flip
        chip = lax.rem(mine + 2, fsdp)
        diagonal = lax.rem(core + 2, fsdp)
        to_x = (flipped(me, 1), mine)
        greet([(me, core), (me, chip)] + ([to_x] if crossed or bulk else []))

        def span(block, i):
            return pl.ds(pl.multiple_of(block * rows + i * size, size), size)

        def sem(kind, i):
            return sems.at[2 * kind, i], sems.at[2 * kind + 1, i]

        copies = []
        from_core_far, from_core_own, from_chip = [], [], []
        exchanged = [
            send(source, target, bulk_sems.at[0, i], bulk_sems.at[1, i], to_x)
            for i, (source, target) in enumerate(zip(bulk_refs, bulk_out_refs))
        ]
        for i in range(chunks):
            copy = send(
                part_ref.at[span(diagonal, i), :], near_far.at[i], *sem(0, i), (me, core)
            )
            from_core_far.append(copy)
        for i in range(chunks):
            copy = send(part_ref.at[span(core, i), :], near_own.at[i], *sem(1, i), (me, core))
            from_core_own.append(copy)
        for i in range(chunks):
            from_core_far[i].wait_recv()
            both = part_ref[span(chip, i), :].astype(jnp.float32) + near_far[i].astype(jnp.float32)
            far_sum[i] = both.astype(jnp.bfloat16)
            from_chip.append(send(far_sum.at[i], far_own.at[i], *sem(2, i), (me, chip)))
        to_chip = []
        for i in range(chunks):
            from_core_own[i].wait_recv()
            from_chip[i].wait_recv()
            total = (
                part_ref[span(mine, i), :].astype(jnp.float32)
                + near_own[i].astype(jnp.float32)
                + far_own[i].astype(jnp.float32)
            )
            all_ref[span(mine, i), :] = chunk_math(
                i, pl.ds(i * size, size), total, extra_refs, out_refs
            ).astype(jnp.bfloat16)
            own = all_ref.at[span(mine, i), :]
            to_chip.append(send(own, own, *sem(3, i), (me, chip)))
            copies.append(send(own, own, *sem(4, i), (me, core)))
            for run in range(ctx // 2 if crossed else 0):
                start = pl.multiple_of((2 * run + 1 - lax.rem(me, 2)) * cols, cols)
                copies.append(
                    send(
                        all_ref.at[span(mine, i), pl.ds(start, cols)],
                        out_refs[-1].at[pl.ds(i * size, size), pl.ds(run * cols, cols)],
                        cross_sems.at[0, i, run],
                        cross_sems.at[1, i, run],
                        to_x,
                    )
                )
        for i in range(chunks):
            to_chip[i].wait_recv()
            other = all_ref.at[span(chip, i), :]
            copies.append(send(other, other, *sem(5, i), (me, core)))
        for copy in copies + exchanged:
            copy.wait_recv()
        for copy in from_core_far + from_core_own + from_chip + to_chip + copies + exchanged:
            copy.wait_send()

    return comm_call(
        kernel,
        name,
        collective_id,
        [jax.ShapeDtypeStruct(partial.shape, jnp.bfloat16)]
        + out_shapes
        + [jax.ShapeDtypeStruct(values.shape, values.dtype) for values in bulk],
        [VMEM] * (1 + count) + [ANY] * bulk_count,
        [VMEM] * (1 + out_count) + [ANY] * bulk_count,
        [
            pltpu.VMEM((chunks, size, width), jnp.bfloat16),
            pltpu.VMEM((chunks, size, width), jnp.bfloat16),
            pltpu.VMEM((chunks, size, width), jnp.bfloat16),
            pltpu.VMEM((chunks, size, width), jnp.bfloat16),
            DMA((12, chunks)),
            DMA((2, chunks, ctx // 2)),
            DMA((2, max(1, bulk_count))),
        ],
        100 * 2**20,
    )(partial, *extras, *bulk)


def norm_chunk(index, span, total, extra_refs, out_refs):
    tokens_ref, gain_ref = extra_refs
    mixed = tokens_ref[span, :].astype(jnp.float32) + total
    out_refs[0][span, :] = mixed
    return mixed * rms_unit(mixed) * gain_ref[...]


def norm_back_chunk(index, span, total, extra_refs, out_refs):
    mixed_ref, gain_ref, dy_ref = extra_refs
    mixed = mixed_ref[span, :]
    scale = rms_unit(mixed)
    unit = mixed * scale
    pulled = total * gain_ref[...]
    grad = dy_ref[span, :].astype(jnp.float32) + scale * (
        pulled - unit * jnp.mean(unit * pulled, axis=-1, keepdims=True)
    )
    out_refs[0][span, :] = grad
    gain_grad = jnp.sum(total * unit, axis=0, keepdims=True)
    if index == 0:
        out_refs[1][...] = gain_grad
    else:
        out_refs[1][...] += gain_grad
    return grad


ROUTER_ROWS = 16


def one_hot(slots, capacity):
    return lax.broadcasted_iota(jnp.int32, (capacity, slots.shape[1]), 0) == slots


def slots_of(pairs, experts, top):
    count = len(pairs)
    blocks, _, rows = pairs[0].shape
    absent = float(rows * top)

    def kernel(*refs):
        for pairs_ref, out_ref in zip(refs[:count], refs[count:]):
            out_ref[...] = jnp.full(out_ref.shape, -1, jnp.int32)
            for b in range(blocks):
                rank_rows = []
                for expert in range(experts):
                    rank = jnp.full((1, rows), absent, jnp.float32)
                    for k in range(top):
                        rank = jnp.where(
                            pairs_ref[b, k : k + 1, :] == expert,
                            pairs_ref[b, top + k : top + k + 1, :].astype(jnp.float32),
                            rank,
                        )
                    rank_rows.append(rank)
                filler = jnp.full((rows - experts, rows), absent, jnp.float32)
                by_column = jnp.concatenate(rank_rows + [filler], axis=0).T
                for expert, rank in enumerate(rank_rows):
                    earlier = jnp.where(by_column[:, expert : expert + 1] < rank, 1.0, 0.0)
                    slot = jnp.where(rank < absent, jnp.sum(earlier, axis=0, keepdims=True), -1.0)
                    out_ref[expert : expert + 1, b * rows : (b + 1) * rows] = slot.astype(jnp.int32)

    shape = jax.ShapeDtypeStruct((ROUTER_ROWS, blocks * rows), jnp.int32)
    return pl.pallas_call(
        kernel,
        out_shape=[shape] * count,
        in_specs=[VMEM] * count,
        out_specs=[VMEM] * count,
        cost_estimate=pl.CostEstimate(flops=10**7, bytes_accessed=2**20, transcendentals=0),
        name="slots_of",
    )(*pairs)


def run_experts(group, dy_all, slots, router, w_gate, w_up, w_down, blocks, capacity):
    experts, width, units = w_gate.shape
    total = group.shape[0]
    rows = total // blocks
    held = blocks * capacity
    f32, bf16 = jnp.float32, jnp.bfloat16

    def kernel(
        group_ref,
        dy_ref,
        slots_ref,
        router_ref,
        gate_ref,
        up_ref,
        down_ref,
        moved_ref,
        grad_ref,
        g_router_ref,
        scaled_ref,
        gate_low_ref,
        up_low_ref,
        disp,
        ins,
        dys,
        probs,
        prob_grad,
    ):
        expert = pl.program_id(0)

        def block_rows(b):
            return pl.ds(b * rows, rows)

        @pl.when(expert == 0)
        def _():
            logits = lax.dot_general(
                router_ref[...],
                group_ref[...],
                (((1,), (1,)), ((), ())),
                preferred_element_type=f32,
            )
            real = lax.broadcasted_iota(jnp.int32, logits.shape, 0) < experts
            logits = jnp.where(real, logits, MASKED)
            weights = jnp.exp(logits - jnp.max(logits, axis=0, keepdims=True))
            probs[...] = weights / jnp.sum(weights, axis=0, keepdims=True)
            prob_grad[...] = jnp.zeros_like(prob_grad)
            for b in range(blocks):
                for e in range(experts):
                    disp[b, pl.ds(e * capacity, capacity), :] = (
                        one_hot(slots_ref[pl.ds(e, 1), block_rows(b)], capacity)
                        .astype(f32)
                        .astype(bf16)
                    )
                for source, target in ((group_ref, ins), (dy_ref, dys)):
                    picked = jnp.dot(
                        disp[b], source[block_rows(b), :], preferred_element_type=f32
                    ).astype(bf16)
                    for e in range(experts):
                        target[e, pl.ds(b * capacity, capacity), :] = picked[
                            e * capacity : (e + 1) * capacity
                        ]

        expert_in, slot_dy = ins[expert], dys[expert]
        gate_matrix, up_matrix, down_matrix = gate_ref[0], up_ref[0], down_ref[0]
        gate_pre = jnp.dot(expert_in, gate_matrix, preferred_element_type=f32)
        up_pre = jnp.dot(expert_in, up_matrix, preferred_element_type=f32)
        raw_grad = lax.dot_general(
            slot_dy, down_matrix, (((1,), (1,)), ((), ())), preferred_element_type=f32
        )
        own_probs = probs[pl.ds(expert, 1), :]
        own_slots = slots_ref[pl.ds(expert, 1), :]
        hots = [
            one_hot(own_slots[:, b * rows : (b + 1) * rows], capacity) for b in range(blocks)
        ]
        value = jnp.concatenate(
            [
                jnp.sum(
                    jnp.where(hots[b], own_probs[:, b * rows : (b + 1) * rows], 0.0),
                    axis=1,
                    keepdims=True,
                )
                for b in range(blocks)
            ],
            axis=0,
        )
        sigma = 1.0 / (1.0 + jnp.exp(-gate_pre))
        silu = gate_pre * sigma
        hidden = (silu * up_pre).astype(bf16)
        hidden_f = hidden.astype(f32)
        value_grad = jnp.sum(hidden_f * raw_grad, axis=1, keepdims=True)
        hidden_grad = raw_grad * value
        gate_low = (hidden_grad * up_pre * sigma * (1.0 + gate_pre * (1.0 - sigma))).astype(bf16)
        up_low = (hidden_grad * silu).astype(bf16)
        scaled = (hidden_f * value).astype(bf16)
        scaled_ref[0] = scaled
        gate_low_ref[0] = gate_low
        up_low_ref[0] = up_low
        for b in range(blocks):
            prob_grad[expert, :, block_rows(b)] = jnp.sum(
                jnp.where(hots[b], value_grad[b * capacity : (b + 1) * capacity], 0.0),
                axis=0,
                keepdims=True,
            )
        dys[expert] = jnp.dot(scaled, down_matrix, preferred_element_type=f32).astype(bf16)
        ins[expert] = (
            lax.dot_general(
                gate_low, gate_matrix, (((1,), (1,)), ((), ())), preferred_element_type=f32
            )
            + lax.dot_general(
                up_low, up_matrix, (((1,), (1,)), ((), ())), preferred_element_type=f32
            )
        ).astype(bf16)

        @pl.when(expert == experts - 1)
        def _():
            grads = jnp.concatenate([prob_grad[e] for e in range(ROUTER_ROWS)], axis=0)
            weights = probs[...]
            logit_grad = (
                weights * (grads - jnp.sum(weights * grads, axis=0, keepdims=True))
            ).astype(bf16)
            g_router_ref[...] = jnp.dot(logit_grad, group_ref[...], preferred_element_type=f32)
            for b in range(blocks):
                for source, target in ((dys, moved_ref), (ins, grad_ref)):
                    gathered = jnp.concatenate(
                        [source[e, pl.ds(b * capacity, capacity), :] for e in range(experts)],
                        axis=0,
                    )
                    back = lax.dot_general(
                        disp[b], gathered, (((0,), (0,)), ((), ())), preferred_element_type=f32
                    )
                    if target is grad_ref:
                        back = back + lax.dot_general(
                            logit_grad[:, b * rows : (b + 1) * rows],
                            router_ref[...],
                            (((0,), (0,)), ((), ())),
                            preferred_element_type=f32,
                        )
                    target[block_rows(b), :] = back.astype(bf16)

    def whole(shape):
        return pl.BlockSpec(shape, lambda e: (0,) * len(shape))

    def by_expert(shape):
        return pl.BlockSpec((1,) + shape, lambda e: (e, 0, 0))

    return pl.pallas_call(
        kernel,
        grid=(experts,),
        out_shape=[
            jax.ShapeDtypeStruct((total, width), bf16),
            jax.ShapeDtypeStruct((total, width), bf16),
            jax.ShapeDtypeStruct((ROUTER_ROWS, width), f32),
        ]
        + [jax.ShapeDtypeStruct((experts, held, units), bf16)] * 3,
        in_specs=[
            whole((total, width)),
            whole((total, width)),
            whole((ROUTER_ROWS, total)),
            whole((ROUTER_ROWS, width)),
            by_expert((width, units)),
            by_expert((width, units)),
            by_expert((units, width)),
        ],
        out_specs=[
            whole((total, width)),
            whole((total, width)),
            whole((ROUTER_ROWS, width)),
        ]
        + [by_expert((held, units))] * 3,
        scratch_shapes=[
            pltpu.VMEM((blocks, experts * capacity, rows), bf16),
            pltpu.VMEM((experts, held, width), bf16),
            pltpu.VMEM((experts, held, width), bf16),
            pltpu.VMEM((ROUTER_ROWS, total), f32),
            pltpu.VMEM((ROUTER_ROWS, 1, total), f32),
        ],
        compiler_params=pltpu.CompilerParams(vmem_limit_bytes=60 * 2**20),
        cost_estimate=pl.CostEstimate(
            flops=30 * 10**9, bytes_accessed=30 * 2**20, transcendentals=10**6
        ),
        name="run_experts",
    )(group, dy_all, slots, router, w_gate, w_up, w_down)


def expert_grads(slot_own, slot_other, rows_own, rows_other, slots_own, slots_other, capacity):
    kinds = len(slot_own)
    experts, held, units = slot_own[0].shape
    total, half = rows_other.shape
    blocks = held // capacity
    rows = total // blocks
    ctx = lax.axis_size("ctx")
    cols = 2 * half // ctx
    f32, bf16 = jnp.float32, jnp.bfloat16

    def kernel(*refs):
        own_refs, other_refs = refs[:kinds], refs[kinds : 2 * kinds]
        rows_own_ref, rows_other_ref, slots_own_ref, slots_other_ref = refs[2 * kinds : 2 * kinds + 4]
        out_refs, held_rows = refs[2 * kinds + 4 : -1], refs[-1]
        expert = pl.program_id(0)
        me = lax.axis_index("ctx")

        def columns(side, run):
            if side == 1:
                return pl.ds(run * cols, cols)
            return pl.ds(pl.multiple_of((2 * run + lax.rem(me, 2)) * cols, cols), cols)

        @pl.when(expert == 0)
        def _():
            for side, slots_ref, source in (
                (0, slots_own_ref, rows_own_ref),
                (1, slots_other_ref, rows_other_ref),
            ):
                for b in range(blocks):
                    span = pl.ds(b * rows, rows)
                    disp = jnp.concatenate(
                        [
                            one_hot(slots_ref[pl.ds(e, 1), span], capacity).astype(f32)
                            for e in range(experts)
                        ],
                        axis=0,
                    ).astype(bf16)
                    for run in range(ctx // 2):
                        picked = jnp.dot(
                            disp, source[span, columns(side, run)], preferred_element_type=f32
                        ).astype(bf16)
                        for e in range(experts):
                            held_rows[
                                e,
                                pl.ds(side * held + b * capacity, capacity),
                                pl.ds(run * cols, cols),
                            ] = picked[e * capacity : (e + 1) * capacity]

        low, high = lax.rem(me // 2, 2), me // 4
        stacked = [
            jnp.concatenate([own[0], other[0]], axis=0) for own, other in zip(own_refs, other_refs)
        ]
        contract = (((0,), (0,)), ((), ()))
        for run in range(ctx // 2):
            given = jnp.where(low == run % 2, 0, 2)
            place = given + jnp.where(high == run // 2, 0, 1)
            features = held_rows[expert, :, pl.ds(run * cols, cols)]
            for kind in range(kinds):
                total = lax.dot_general(
                    features, stacked[kind], contract, preferred_element_type=f32
                ).astype(bf16)
                for i in range(4):

                    @pl.when(place == i)
                    def _():
                        out_refs[4 * kind + i][0] = total

    def whole(shape):
        return pl.BlockSpec(shape, lambda e: (0,) * len(shape))

    slot_spec = pl.BlockSpec((1, held, units), lambda e: (e, 0, 0))
    return pl.pallas_call(
        kernel,
        grid=(experts,),
        out_shape=[jax.ShapeDtypeStruct((experts, units, cols), bf16)] * (4 * kinds),
        in_specs=[slot_spec] * (2 * kinds)
        + [whole((total, 2 * half)), whole((total, half))]
        + [whole((ROUTER_ROWS, total))] * 2,
        out_specs=[pl.BlockSpec((1, units, cols), lambda e: (e, 0, 0))] * (4 * kinds),
        scratch_shapes=[pltpu.VMEM((experts, 2 * held, half), bf16)],
        compiler_params=pltpu.CompilerParams(vmem_limit_bytes=60 * 2**20),
        cost_estimate=pl.CostEstimate(flops=0, bytes_accessed=2**20, transcendentals=0),
        name="expert_grads",
    )(*slot_own, *slot_other, rows_own, rows_other, slots_own, slots_other)


def down_grads(scaled, dy_parts, slots, capacity):
    count = len(scaled)
    experts, held, units = scaled[0].shape
    blocks, _, rows, wide = dy_parts.shape
    cols = wide // 2
    f32, bf16 = jnp.float32, jnp.bfloat16

    def kernel(*refs):
        scaled_refs, dy_ref, slots_refs = refs[:count], refs[count], refs[count + 1 : 2 * count + 1]
        out_ref, held_rows = refs[2 * count + 1 :]
        expert = pl.program_id(0)

        @pl.when(expert == 0)
        def _():
            for i, slots_ref in enumerate(slots_refs):
                for b in range(blocks):
                    span = pl.ds(b * rows, rows)
                    disp = jnp.concatenate(
                        [
                            one_hot(slots_ref[pl.ds(e, 1), span], capacity).astype(f32)
                            for e in range(experts)
                        ],
                        axis=0,
                    ).astype(bf16)
                    picked = jnp.dot(disp, dy_ref[b, i], preferred_element_type=f32).astype(bf16)
                    for e in range(experts):
                        held_rows[e, pl.ds(i * held + b * capacity, capacity), :] = picked[
                            e * capacity : (e + 1) * capacity
                        ]

        stacked = jnp.concatenate([ref[0] for ref in scaled_refs], axis=0)
        total = lax.dot_general(
            stacked, held_rows[expert], (((0,), (0,)), ((), ())), preferred_element_type=f32
        ).astype(bf16)
        side = lax.rem(lax.axis_index("ctx"), 2)
        for x in range(2):
            kept = jnp.where(side == x, 1, 0)
            out_ref[pl.ds(kept, 1), 0] = total[:, x * cols : (x + 1) * cols][None]

    def whole(shape):
        return pl.BlockSpec(shape, lambda e: (0,) * len(shape))

    return pl.pallas_call(
        kernel,
        grid=(experts,),
        out_shape=jax.ShapeDtypeStruct((2, experts, units, cols), bf16),
        in_specs=[pl.BlockSpec((1, held, units), lambda e: (e, 0, 0))] * count
        + [whole(dy_parts.shape)]
        + [whole(slots[0].shape)] * count,
        out_specs=pl.BlockSpec((2, 1, units, cols), lambda e: (0, e, 0, 0)),
        scratch_shapes=[pltpu.VMEM((experts, count * held, wide), bf16)],
        compiler_params=pltpu.CompilerParams(vmem_limit_bytes=60 * 2**20),
        cost_estimate=pl.CostEstimate(flops=0, bytes_accessed=2**20, transcendentals=0),
        name="down_grads",
    )(*scaled, dy_parts, *slots)


def roll_half(values):
    return pltpu.roll(values, values.shape[1] // 2, 1)


def allowed_keys(first_ref, last_ref, span, places):
    return (places >= first_ref[span, :]) & (places <= last_ref[span, :])


def attend(projected, scales, gains, cosine, sine_part, first, last, places, cols):
    total = projected.shape[0]
    head_dim = cosine.shape[1]
    heads = cols // head_dim
    size = math.gcd(total, 256)
    score_scale = head_dim ** (-0.5)
    f32, bf16 = jnp.float32, jnp.bfloat16

    def kernel(
        lin_ref,
        scales_ref,
        gains_ref,
        cos_ref,
        sin_ref,
        first_ref,
        last_ref,
        places_ref,
        low_ref,
        attended_ref,
        attended_low_ref,
        top_ref,
    ):
        for kind in range(3):
            for h in range(heads):
                span = pl.ds(kind * cols + h * head_dim, head_dim)
                values = lin_ref[:, span]
                if kind < 2:
                    values = values * scales_ref[:, kind : kind + 1] * gains_ref[:, span]
                    values = values * cos_ref[...] + roll_half(values) * sin_ref[...]
                low_ref[:, span] = values.astype(bf16)
        for h in range(heads):
            head = pl.ds(h * head_dim, head_dim)
            keys = low_ref[:, pl.ds(cols + h * head_dim, head_dim)]
            values = low_ref[:, pl.ds(2 * cols + h * head_dim, head_dim)]

            def step(b, carry):
                span = pl.ds(pl.multiple_of(b * size, size), size)
                scores = lax.dot_general(
                    low_ref[span, head],
                    keys,
                    (((1,), (1,)), ((), ())),
                    preferred_element_type=f32,
                )
                allowed = allowed_keys(first_ref, last_ref, span, places_ref[...])
                scores = jnp.where(allowed, scores * score_scale, MASKED)
                top = jnp.max(scores, axis=1, keepdims=True)
                weights = jnp.exp(scores - top)
                sums = jnp.sum(weights, axis=1, keepdims=True)
                probs = (weights * (1.0 / sums)).astype(bf16)
                attended = jnp.dot(probs, values, preferred_element_type=f32)
                attended_ref[span, head] = attended
                attended_low_ref[span, head] = attended.astype(bf16)
                top_ref[span, head] = jnp.broadcast_to(top + jnp.log(sums), (size, head_dim))
                return carry

            lax.fori_loop(0, total // size, step, 0)

    return pl.pallas_call(
        kernel,
        out_shape=[
            jax.ShapeDtypeStruct((total, 3 * cols), bf16),
            jax.ShapeDtypeStruct((total, cols), f32),
            jax.ShapeDtypeStruct((total, cols), bf16),
            jax.ShapeDtypeStruct((total, cols), f32),
        ],
        in_specs=[VMEM] * 8,
        out_specs=[VMEM] * 4,
        compiler_params=pltpu.CompilerParams(vmem_limit_bytes=24 * 2**20),
        cost_estimate=pl.CostEstimate(
            flops=2 * 10**9, bytes_accessed=20 * 2**20, transcendentals=2 * 10**6
        ),
        name="attend",
    )(projected, scales, gains, cosine, sine_part, first, last, places)


def attend_back(
    output_grad, low, attended, top, projected, scales, gains, cosine, sine_part, first, last, places
):
    total, cols = output_grad.shape
    head_dim = cosine.shape[1]
    heads = cols // head_dim
    size = math.gcd(total, 256)
    score_scale = head_dim ** (-0.5)
    f32, bf16 = jnp.float32, jnp.bfloat16
    contract_rows = (((0,), (0,)), ((), ()))

    def kernel(
        grad_ref,
        low_ref,
        attended_ref,
        top_ref,
        lin_ref,
        scales_ref,
        gains_ref,
        cos_ref,
        sin_ref,
        first_ref,
        last_ref,
        places_ref,
        back_ref,
        value_ref,
        gain_ref,
        sums_ref,
        query_grad,
        key_grad,
        value_grad,
    ):
        totals = [jnp.zeros((total, 1), f32) for _ in range(2)]
        for h in range(heads):
            head = pl.ds(h * head_dim, head_dim)
            keys = low_ref[:, pl.ds(cols + h * head_dim, head_dim)]
            values = low_ref[:, pl.ds(2 * cols + h * head_dim, head_dim)]
            key_grad[...] = jnp.zeros_like(key_grad)
            value_grad[...] = jnp.zeros_like(value_grad)

            def step(b, carry):
                span = pl.ds(pl.multiple_of(b * size, size), size)
                queries, grads = low_ref[span, head], grad_ref[span, head]
                scores = lax.dot_general(
                    queries, keys, (((1,), (1,)), ((), ())), preferred_element_type=f32
                )
                allowed = allowed_keys(first_ref, last_ref, span, places_ref[...])
                scores = jnp.where(allowed, scores * score_scale, MASKED)
                probs = jnp.exp(scores - top_ref[span, head][:, :1])
                prob_grad = lax.dot_general(
                    grads, values, (((1,), (1,)), ((), ())), preferred_element_type=f32
                )
                delta = jnp.sum(
                    grads.astype(f32) * attended_ref[span, head], axis=1, keepdims=True
                )
                score_grad = (probs * (prob_grad - delta)).astype(bf16)
                query_grad[span, :] = (
                    jnp.dot(score_grad, keys, preferred_element_type=f32) * score_scale
                )
                key_grad[...] += lax.dot_general(
                    score_grad, queries, contract_rows, preferred_element_type=f32
                )
                value_grad[...] += lax.dot_general(
                    probs.astype(bf16), grads, contract_rows, preferred_element_type=f32
                )
                return carry

            lax.fori_loop(0, total // size, step, 0)
            value_ref[:, head] = value_grad[...].astype(bf16)
            for kind, grad in ((0, query_grad[...]), (1, key_grad[...] * score_scale)):
                span = pl.ds(kind * cols + h * head_dim, head_dim)
                unit = lin_ref[:, span] * scales_ref[:, kind : kind + 1]
                grad = grad * cos_ref[...] - roll_half(grad) * sin_ref[...]
                gain_ref[kind, :, head] = jnp.sum(grad * unit, axis=0, keepdims=True)
                grad = grad * gains_ref[:, span]
                back_ref[kind, :, head] = grad
                totals[kind] = totals[kind] + jnp.sum(grad * unit, axis=1, keepdims=True)
        for kind in range(2):
            sums_ref[:, kind : kind + 1] = totals[kind]

    return pl.pallas_call(
        kernel,
        out_shape=[
            jax.ShapeDtypeStruct((2, total, cols), f32),
            jax.ShapeDtypeStruct((total, cols), bf16),
            jax.ShapeDtypeStruct((2, 1, cols), f32),
            jax.ShapeDtypeStruct((total, 2), f32),
        ],
        in_specs=[VMEM] * 12,
        out_specs=[VMEM] * 4,
        scratch_shapes=[pltpu.VMEM((total, head_dim), f32)] * 3,
        compiler_params=pltpu.CompilerParams(vmem_limit_bytes=60 * 2**20),
        cost_estimate=pl.CostEstimate(flops=0, bytes_accessed=2**20, transcendentals=0),
        name="attend_back",
    )(
        output_grad,
        low,
        attended,
        top,
        projected,
        scales,
        gains,
        cosine,
        sine_part,
        first,
        last,
        places,
    )


def flipped(index, bit):
    return index + bit * (1 - 2 * lax.rem(index // bit, 2))


def flipped_by(index, flip):
    for bit in (1, 2, 4):
        index = flipped(index, bit) if flip & bit else index
    return index


def add_into(target, *sources):
    step = target.shape[0] if len(target.shape) == 3 else target.shape[0] // 64

    def body(i, carry):
        span = i if len(target.shape) == 3 else pl.ds(pl.multiple_of(i * 64, 64), 64)
        total = sources[0][span].astype(jnp.float32)
        for source in sources[1:]:
            total = total + source[span].astype(jnp.float32)
        target[span] = total.astype(target.dtype)
        return carry

    lax.fori_loop(0, step, body, 0)


def finish_sums(downs, ups, gate_far, gate_own, up_far, normed_part, out_part, qkv_part, small, tokens, mixed_grad, gain, mixed, moved, collective_id):
    ctx, fsdp = lax.axis_size("ctx"), lax.axis_size("fsdp")
    experts, units, cols = gate_far.shape
    kinds = 3
    rows, width = tokens.shape
    part = out_part.shape[0]
    f32, bf16 = jnp.float32, jnp.bfloat16
    small_rows, small_cols = small.shape[0], small.shape[1] // fsdp
    copies_most = 64

    def kernel(
        downs_ref,
        gate_near_ref,
        gate_high_ref,
        up_near_ref,
        up_high_ref,
        up_low_ref,
        gate_far_ref,
        gate_own_ref,
        up_far_ref,
        normed_ref,
        g_out_ref,
        g_qkv_ref,
        small_ref,
        tokens_ref,
        mixed_ref,
        gain_ref,
        forward_ref,
        moved_ref,
        down_ref,
        gate_ref,
        up_ref,
        input_ref,
        out_ref,
        qkv_ref,
        sums_ref,
        result_ref,
        kept,
        kept_low,
        kept_high,
        normed_own,
        normed_x,
        normed_low,
        normed_high,
        out_own,
        out_x,
        out_low,
        out_high,
        qkv_own,
        qkv_core,
        qkv_chip,
        qkv_sum,
        dealt,
        small_parts,
        small_sum,
        small_held,
        sends,
        recvs,
        locals_,
        deal_sems,
    ):
        me, mine = lax.axis_index("ctx"), lax.axis_index("fsdp")
        x, low, high = lax.rem(me, 2), lax.rem(me // 2, 2), me // 4
        to_x, to_low, to_high = ((flipped(me, bit), mine) for bit in (1, 2, 4))
        core, chip = flipped(mine, 1), flipped(mine, 2)
        diagonal = flipped(core, 2)
        ctx_peers = [(lax.rem(me + step, ctx), mine) for step in range(1, ctx)]
        near = [lax.rem(mine + step, fsdp) for step in range(1, fsdp)]
        greet(ctx_peers + [(me, other) for other in near])
        used, used_local, all_sends, loads = [0], [0], [], {}

        def push(source, target, peer):
            i = used[0]
            used[0] += 1
            copy = send(source, target, sends.at[i], recvs.at[i], peer)
            all_sends.append(copy)
            return copy

        def load(source, target):
            i = used_local[0]
            used_local[0] += 1
            copy = pltpu.make_async_copy(source, target, locals_.at[i])
            copy.start()
            return copy

        def normed_block(a, b, other):
            side = 1 - x if other else x
            block = (high + a - 2 * a * high) * 4 + (low + b - 2 * b * low) * 2 + side
            return normed_ref.at[pl.ds(pl.multiple_of(block * rows, rows), rows), :]

        def out_block(a, b, other):
            side = 1 - x if other else x
            block = (high + a - 2 * a * high) * 4 + (low + b - 2 * b * low) * 2 + side
            return g_out_ref.at[:, pl.ds(pl.multiple_of(block * cols, cols), cols)]

        def qkv_block(index):
            return g_qkv_ref.at[pl.ds(pl.multiple_of(index * part, part), part), :]

        def columns(index):
            return pl.ds(pl.multiple_of(index * small_cols, small_cols), small_cols)

        order = ((1, 1), (0, 1), (1, 0), (0, 0))
        small_copies = [
            push(small_ref.at[:, columns(other)], small_parts.at[i], (me, other))
            for i, other in enumerate(near)
        ]
        normed_copies = {
            ab: push(normed_block(*ab, True), normed_x.at[ab[0], ab[1]], to_x) for ab in order
        }

        low_copies = {
            (2, 0): push(up_low_ref, kept_low.at[2, 0], to_low),
            (0, 0): push(downs_ref.at[0], kept_low.at[0, 0], to_x),
        }
        early = {
            (1, 1): load(gate_far_ref, kept_low.at[1, 1]),
            (2, 1): load(up_far_ref, kept_low.at[2, 1]),
            (1, 0): load(gate_own_ref, kept_low.at[1, 0]),
        }
        kept_loads = {
            place: load(source, kept.at[place])
            for place, source in (
                ((1, 1), gate_high_ref),
                ((2, 1), up_high_ref),
                ((0, 0), downs_ref.at[1]),
                ((1, 0), gate_near_ref),
                ((2, 0), up_near_ref),
            )
        }
        qkv_copies = [
            push(qkv_block(diagonal), qkv_core.at[1], (me, core)),
            push(qkv_block(core), qkv_core.at[0], (me, core)),
        ]
        qkv_loads = [
            load(qkv_block(chip), qkv_own.at[1]),
            load(qkv_block(mine), qkv_own.at[0]),
        ]
        normed_loads = {
            ab: load(normed_block(*ab, False), normed_own.at[ab[0], ab[1]]) for ab in order
        }
        out_loads = {ab: load(out_block(*ab, False), out_own.at[ab[0], ab[1]]) for ab in order}

        total = small_ref[:, columns(mine)]
        for i, copy in enumerate(small_copies):
            copy.wait_recv()
            total = total + small_parts[i]
        small_sum[...] = total
        small_wide = [push(small_sum, small_held.at[i], peer) for i, peer in enumerate(ctx_peers)]

        qkv_copies[0].wait_recv()
        qkv_loads[0].wait()
        add_into(qkv_core.at[1], qkv_own.at[1], qkv_core.at[1])
        chip_copy = push(qkv_core.at[1], qkv_chip, (me, chip))

        def to_low_side(copies, loads, own, from_x, from_low, a):
            copies[a, 1].wait_recv()
            loads[a, 1].wait()
            add_into(from_x.at[a, 1], own.at[a, 1], from_x.at[a, 1])
            return push(from_x.at[a, 1], from_low.at[a], to_low)

        def to_high_side(copies, loads, lows, own, from_x, from_low, from_high):
            copies[1, 0].wait_recv()
            loads[1, 0].wait()
            lows[1].wait_recv()
            add_into(from_x.at[1, 0], own.at[1, 0], from_x.at[1, 0], from_low.at[1])
            return push(from_x.at[1, 0], from_high, to_high)

        def arrived(kind, a):
            if (kind, a) in early:
                early[kind, a].wait()
            else:
                low_copies[kind, a].wait_recv()

        def experts_high(kind):
            arrived(kind, 1)
            kept_loads[kind, 1].wait()
            add_into(kept_low.at[kind, 1], kept.at[kind, 1], kept_low.at[kind, 1])
            return push(kept_low.at[kind, 1], kept_high.at[kind], to_high)

        high_copies = {1: experts_high(1)}
        normed_args = (normed_copies, normed_loads)
        normed_lows = {1: to_low_side(*normed_args, normed_own, normed_x, normed_low, 1)}
        high_copies[2] = experts_high(2)
        normed_lows[0] = to_low_side(*normed_args, normed_own, normed_x, normed_low, 0)
        out_copies = {ab: push(out_block(*ab, True), out_x.at[ab[0], ab[1]], to_x) for ab in order}

        qkv_copies[1].wait_recv()
        qkv_loads[1].wait()
        chip_copy.wait_recv()
        add_into(qkv_sum, qkv_own.at[0], qkv_core.at[0], qkv_chip)

        def deal(kind):
            index = kind * ctx + me
            return pltpu.make_async_remote_copy(
                qkv_sum.at[:, pl.ds(kind * cols, cols)],
                dealt.at[lax.rem(index, kinds)],
                deal_sems.at[0, kind],
                deal_sems.at[1, lax.rem(index, kinds)],
                device_id=(index // kinds, mine),
                device_id_type=MESH,
            )

        def keep(kind):
            return pltpu.make_async_copy(
                qkv_sum.at[:, pl.ds(kind * cols, cols)],
                dealt.at[lax.rem(kind * ctx + me, kinds)],
                deal_sems.at[0, kind],
            )

        def is_far(kind):
            return (kind * ctx + me) // kinds != me

        for kind in range(kinds):
            pl.when(is_far(kind))(deal(kind).start)
            pl.when(jnp.logical_not(is_far(kind)))(keep(kind).start)

        normed_high_copy = to_high_side(
            *normed_args, normed_lows, normed_own, normed_x, normed_low, normed_high
        )
        out_args = (out_copies, out_loads)
        out_lows = {a: to_low_side(*out_args, out_own, out_x, out_low, a) for a in (1, 0)}

        def experts_end(kind):
            arrived(kind, 0)
            kept_loads[kind, 0].wait()
            sources = [kept.at[kind, 0], kept_low.at[kind, 0]]
            if kind > 0:
                high_copies[kind].wait_recv()
                sources.append(kept_high.at[kind])
            add_into((down_ref, gate_ref, up_ref)[kind], *sources)

        experts_end(0)

        normed_copies[0, 0].wait_recv()
        normed_loads[0, 0].wait()
        normed_lows[0].wait_recv()
        normed_high_copy.wait_recv()

        def norm_step(i, carry):
            span = pl.ds(pl.multiple_of(i * 16, 16), 16)
            grad = (
                normed_own[0, 0, span, :].astype(f32)
                + normed_x[0, 0, span, :].astype(f32)
                + normed_low[0, span, :].astype(f32)
                + normed_high[span, :].astype(f32)
            )
            values = tokens_ref[span, :].astype(f32)
            scale = rms_unit(values)
            unit = values * scale
            pulled = grad * gain_ref[...]
            input_ref[span, :] = mixed_ref[span, :] + scale * (
                pulled - unit * jnp.mean(unit * pulled, axis=-1, keepdims=True)
            )
            result_ref[span, :] = (forward_ref[span, :] + moved_ref[span, :].astype(f32)).astype(bf16)
            return carry

        lax.fori_loop(0, rows // 16, norm_step, 0)

        out_high_copy = to_high_side(*out_args, out_lows, out_own, out_x, out_low, out_high)
        experts_end(1)

        total = small_sum[...]
        for i, copy in enumerate(small_wide):
            copy.wait_recv()
            total = total + small_held[i]
        sums_ref[...] = total

        for kind in range(kinds):
            pl.when(is_far(kind))(deal(kind).wait_send)
            pl.when(jnp.logical_not(is_far(kind)))(keep(kind).wait)
        for slot in range(kinds):

            @pl.when(lax.rem(me * kinds + slot, ctx) != me)
            def _():
                pltpu.make_async_copy(
                    dealt.at[slot], dealt.at[slot], deal_sems.at[1, slot]
                ).wait()

            add_into(qkv_ref.at[:, pl.ds(slot * cols, cols)], dealt.at[slot])

        out_copies[0, 0].wait_recv()
        out_loads[0, 0].wait()
        out_lows[0].wait_recv()
        out_high_copy.wait_recv()
        add_into(out_ref, out_own.at[0, 0], out_x.at[0, 0], out_low.at[0], out_high)
        experts_end(2)
        for copy in all_sends:
            copy.wait_send()

    def block(*shape):
        return pltpu.VMEM(shape, bf16)

    gradient = (experts, units, cols)
    return comm_call(
        kernel,
        "finish_sums",
        collective_id,
        [
            jax.ShapeDtypeStruct(gradient, f32),
            jax.ShapeDtypeStruct(gradient, f32),
            jax.ShapeDtypeStruct(gradient, f32),
            jax.ShapeDtypeStruct((rows, width), f32),
            jax.ShapeDtypeStruct((part, cols), f32),
            jax.ShapeDtypeStruct((part, kinds * cols), f32),
            jax.ShapeDtypeStruct((small_rows, small_cols), f32),
            jax.ShapeDtypeStruct((rows, width), bf16),
        ],
        [ANY] * 12 + [VMEM] * 6,
        [VMEM] * 8,
        [
            block(kinds, 2, *gradient),
            block(kinds, 2, *gradient),
            block(kinds, *gradient),
            block(2, 2, rows, width),
            block(2, 2, rows, width),
            block(2, rows, width),
            block(rows, width),
            block(2, 2, part, cols),
            block(2, 2, part, cols),
            block(2, part, cols),
            block(part, cols),
            block(2, part, kinds * cols),
            block(2, part, kinds * cols),
            block(part, kinds * cols),
            block(part, kinds * cols),
            block(kinds, part, cols),
            pltpu.VMEM((fsdp - 1, small_rows, small_cols), f32),
            pltpu.VMEM((small_rows, small_cols), f32),
            pltpu.VMEM((ctx - 1, small_rows, small_cols), f32),
            DMA((copies_most,)),
            DMA((copies_most,)),
            DMA((32,)),
            DMA((2, kinds)),
        ],
        700 * 2**20,
        56,
    )(
        downs,
        *ups,
        gate_far,
        gate_own,
        up_far,
        normed_part,
        out_part,
        qkv_part,
        small,
        tokens,
        mixed_grad,
        gain,
        mixed,
        moved,
    )


def gather_inputs(tokens, w_qkv, dy, row_arrays, block, flips, collective_id):
    ctx, fsdp = lax.axis_size("ctx"), lax.axis_size("fsdp")
    rows, width = tokens.shape
    part = w_qkv.shape[0]
    kinds = 3
    cols = width // ctx
    line = ctx // 2
    chunks = 2
    size = rows // chunks
    row_count, flip_count = len(row_arrays), len(flips)
    small_count = row_count + 1

    def kernel(*refs):
        tokens_ref, w_qkv_ref, dy_ref = refs[:3]
        small_refs = refs[3 : 3 + small_count]
        all_ref, weight_ref, dy_all_ref = refs[3 + small_count : 6 + small_count]
        small_all_refs = refs[6 + small_count : 6 + 2 * small_count]
        refs = refs[6 + 2 * small_count :]
        run_kernel(
            tokens_ref,
            w_qkv_ref,
            dy_ref,
            small_refs,
            all_ref,
            weight_ref,
            dy_all_ref,
            small_all_refs,
            *refs,
        )

    def run_kernel(
        tokens_ref,
        w_qkv_ref,
        dy_ref,
        small_refs,
        all_ref,
        weight_ref,
        dy_all_ref,
        small_all_refs,
        *refs,
    ):
        flip_refs, dy_line_ref, refs = refs[:flip_count], refs[flip_count], refs[flip_count + 1 :]
        stage, weight_stage, dy_stage, sends, recvs, line_send, line_recv, cross_send, cross_recv, *refs = refs
        local_sems, line_out, cross_out = refs
        me, mine = lax.axis_index("ctx"), lax.axis_index("fsdp")
        z, x = me // 2, lax.rem(me, 2)
        to_x = (flipped(me, 1), mine)
        core, chip = (me, flipped(mine, 1)), (me, flipped(mine, 2))
        others = [flipped_by(me, flip) for flip in flips]
        greet(
            [(lax.rem(me + step, ctx), mine) for step in range(1, ctx)]
            + [(me, lax.rem(mine + step, fsdp)) for step in range(1, fsdp)]
            + [(other, lax.rem(mine + step, fsdp)) for other in others for step in range(1, fsdp)]
        )
        used, used_local, started, kept = [0], [0], [], []

        def push(source, target, peer):
            i = used[0]
            used[0] += 1
            copy = send(source, target, sends.at[i], recvs.at[i], peer)
            started.append(copy)
            return copy

        def load(source, target):
            i = used_local[0]
            used_local[0] += 1
            copy = pltpu.make_async_copy(source, target, local_sems.at[i])
            copy.start()
            kept.append(copy)

        def token_block(index):
            return all_ref.at[pl.ds(pl.multiple_of(index * rows, rows), rows), :]

        def token_chunk(index, chunk):
            start = pl.multiple_of(index * rows + chunk * size, size)
            return stage.at[pl.ds(start, size), :]

        def put(away, side, chunk, crossed):
            index = 2 * (z - away if side == 0 else z + away) + (1 - x if crossed else x)
            start = pl.multiple_of(index * rows + chunk * size, size)
            return pltpu.make_async_copy(
                stage.at[pl.ds(start, size), :],
                all_ref.at[pl.ds(start, size), :],
                (cross_out if crossed else line_out).at[side * line + away, chunk],
            )

        def taken(own, index, chunk):
            return tokens_ref.at[pl.ds(chunk * size, size), :] if own else token_chunk(index, chunk)

        def by_part(ref, index, count):
            return ref.at[pl.ds(pl.multiple_of(index * count, count), count), :]

        def cross(away, side, chunk):
            index = 2 * (z - away if side == 0 else z + away) + x
            i = side * line + away
            return pltpu.make_async_remote_copy(
                taken(away == 0, index, chunk),
                token_chunk(index, chunk),
                cross_send.at[i, chunk],
                cross_recv.at[i, chunk],
                device_id=to_x,
                device_id_type=MESH,
            )

        def along(away, side, chunk):
            index = 2 * (z - away if side == 0 else z + away) + x
            i = side * line + away
            return pltpu.make_async_remote_copy(
                taken(away == 0, index, chunk),
                token_chunk(index, chunk),
                line_send.at[i, chunk],
                line_recv.at[i, chunk],
                device_id=(me + 2 if side == 0 else me - 2, mine),
                device_id_type=MESH,
            )

        def has(away, side):
            return z >= away if side == 0 else z + away < line

        def goes_on(away, side):
            return jnp.logical_and(has(away, side), z < line - 1 if side == 0 else z > 0)

        for chunk in range(chunks):
            for side in range(2):
                pl.when(goes_on(0, side))(along(0, side, chunk).start)
            cross(0, 0, chunk).start()
        load(tokens_ref, token_block(me))

        own_weight = by_part(weight_stage, mine, part)
        pieces = []
        for kind in range(kinds):
            column = pl.ds(pl.multiple_of(kind * width + me * cols, cols), cols)
            target = own_weight.at[:, pl.ds(kind * cols, cols)]
            pieces.append(
                pltpu.make_async_copy(w_qkv_ref.at[:, column], target, local_sems.at[23 - kind])
            )
            pieces[-1].start()
        load(dy_ref, dy_stage)
        dy_loaded = kept.pop()
        for piece in pieces:
            piece.wait()
        weight_chip = [push(own_weight, own_weight, chip)]
        weight_core = [push(own_weight, own_weight, core)]
        load(own_weight, by_part(weight_ref, mine, part))
        columns = pl.ds(pl.multiple_of(mine * part, part), part)
        for i, (source, target) in enumerate(zip(small_refs, small_all_refs)):
            if i < row_count:
                target = target.at[:, columns]
            else:
                target = target.at[mine]
            for step in range(1, fsdp):
                push(source, target, (me, lax.rem(mine + step, fsdp)))
            load(source, target)
        dy_chip = push(dy_ref, by_part(dy_all_ref, mine, rows), chip)
        push(dy_ref, by_part(dy_all_ref, mine, rows), core)
        load(dy_ref, by_part(dy_all_ref, mine, rows))

        for away in range(1, line):
            for chunk in range(chunks):
                for side in range(2):

                    @pl.when(has(away, side))
                    def _():
                        index = 2 * (z - away if side == 0 else z + away) + x
                        pltpu.make_async_copy(
                            taken(True, index, chunk),
                            token_chunk(index, chunk),
                            line_recv.at[side * line + away - 1, chunk],
                        ).wait()
                        cross(away, side, chunk).start()
                        put(away, side, chunk, False).start()

                    if away < line - 1:
                        pl.when(goes_on(away, side))(along(away, side, chunk).start)
        for other, target in zip(others, flip_refs):
            for step in range(fsdp):
                push(small_refs[-1], target.at[mine], (other, lax.rem(mine + step, fsdp)))
        dy_loaded.wait()
        for i in range(line):
            wide = 2 * cols
            to = flipped_by(me, 2 * i)
            source = dy_stage.at[:, pl.ds(pl.multiple_of(to // 2 * wide, wide), wide)]
            if i == 0:
                load(source, dy_line_ref.at[0])
            else:
                push(source, dy_line_ref.at[i], (to, mine))

        for copy in weight_chip:
            copy.wait_recv()
        far = by_part(weight_stage, flipped(mine, 2), part)
        weight_far = push(far, far, core)
        load(far, by_part(weight_ref, flipped(mine, 2), part))
        for copy in weight_core:
            copy.wait_recv()
        near = flipped(mine, 1)
        load(by_part(weight_stage, near, part), by_part(weight_ref, near, part))
        dy_chip.wait_recv()
        far = by_part(dy_all_ref, flipped(mine, 2), rows)
        push(far, far, core)
        every = [(side, chunk) for side in range(2) for chunk in range(chunks)]
        weight_far.wait_recv()
        far = flipped_by(mine, 3)
        load(by_part(weight_stage, far, part), by_part(weight_ref, far, part))
        for chunk in range(chunks):
            cross(0, 0, chunk).wait_recv()
            put(0, 0, chunk, True).start()
        for away in range(1, line):
            for side, chunk in every:

                @pl.when(has(away, side))
                def _():
                    cross(away, side, chunk).wait_recv()
                    put(away, side, chunk, True).start()

        for copy in started:
            if not any(copy is other for other in [dy_chip, weight_far] + weight_chip + weight_core):
                copy.wait_recv()
        for copy in kept:
            copy.wait()
        for copy in started:
            copy.wait_send()
        for chunk in range(chunks):
            cross(0, 0, chunk).wait_send()
        for chunk in range(chunks):
            put(0, 0, chunk, True).wait()
        for away in range(1, line):
            for side, chunk in every:

                @pl.when(has(away, side))
                def _():
                    put(away, side, chunk, False).wait()
                    put(away, side, chunk, True).wait()

        for away in range(line - 1):
            for side, chunk in every:
                pl.when(goes_on(away, side))(along(away, side, chunk).wait_send)
        for away in range(1, line):
            for side, chunk in every:
                pl.when(has(away, side))(cross(away, side, chunk).wait_send)

    return comm_call(
        kernel,
        "gather_inputs",
        collective_id,
        [
            jax.ShapeDtypeStruct((ctx * rows, width), tokens.dtype),
            jax.ShapeDtypeStruct((fsdp * part, kinds * cols), w_qkv.dtype),
            jax.ShapeDtypeStruct((fsdp * rows, width), dy.dtype),
        ]
        + [jax.ShapeDtypeStruct((row.shape[0], fsdp * part), row.dtype) for row in row_arrays]
        + [jax.ShapeDtypeStruct((fsdp,) + block.shape, block.dtype)] * (1 + flip_count)
        + [jax.ShapeDtypeStruct((line, rows, 2 * cols), dy.dtype)],
        [ANY] * (3 + small_count),
        [ANY] * (4 + small_count + flip_count),
        [
            pltpu.VMEM((ctx * rows, width), tokens.dtype),
            pltpu.VMEM((fsdp * part, kinds * cols), w_qkv.dtype),
            pltpu.VMEM((rows, width), dy.dtype),
            DMA((64,)),
            DMA((64,)),
            DMA((2 * line, chunks)),
            DMA((2 * line, chunks)),
            DMA((2 * line, chunks)),
            DMA((2 * line, chunks)),
            DMA((24,)),
            DMA((2 * line, chunks)),
            DMA((2 * line, chunks)),
        ],
        150 * 2**20,
        60,
    )(tokens, w_qkv, dy, *row_arrays, block)


def project(tokens, gain, weight):
    total, width = tokens.shape
    wide = weight.shape[1]
    cols = wide // 3
    size = math.gcd(total, 256)
    f32 = jnp.float32

    def kernel(tokens_ref, gain_ref, weight_ref, normed_ref, lin_ref, squares_ref):
        values = tokens_ref[...].astype(f32)
        normed = (values * rms_unit(values) * gain_ref[...]).astype(jnp.bfloat16)
        normed_ref[...] = normed
        lin = jnp.dot(normed, weight_ref[...], preferred_element_type=f32)
        lin_ref[...] = lin
        for kind in range(2):
            piece = lin[:, kind * cols : (kind + 1) * cols]
            squares_ref[:, kind : kind + 1] = jnp.sum(piece * piece, axis=1, keepdims=True)

    def by_rows(columns):
        return pl.BlockSpec((size, columns), lambda i: (i, 0))

    return pl.pallas_call(
        kernel,
        grid=(total // size,),
        out_shape=[
            jax.ShapeDtypeStruct((total, width), jnp.bfloat16),
            jax.ShapeDtypeStruct((total, wide), f32),
            jax.ShapeDtypeStruct((total, 2), f32),
        ],
        in_specs=[
            by_rows(width),
            pl.BlockSpec((1, width), lambda i: (0, 0)),
            pl.BlockSpec((width, wide), lambda i: (0, 0)),
        ],
        out_specs=[by_rows(width), by_rows(wide), by_rows(2)],
        compiler_params=pltpu.CompilerParams(vmem_limit_bytes=60 * 2**20),
        cost_estimate=pl.CostEstimate(
            flops=3 * 10**9, bytes_accessed=15 * 2**20, transcendentals=0
        ),
        name="project",
    )(tokens, gain, weight)


def project_back(back, projected, scales, inner_sums, value_grad, weight, normed, tokens):
    total, width = tokens.shape
    wide = weight.shape[1]
    cols = wide // 3
    size = math.gcd(total, 256)
    steps, runs = total // size, 4
    f32, bf16 = jnp.float32, jnp.bfloat16

    def kernel(
        back_ref,
        lin_ref,
        scales_ref,
        sums_ref,
        value_ref,
        weight_ref,
        normed_ref,
        tokens_ref,
        part_ref,
        g_qkv_ref,
        gain_ref,
        proj,
    ):
        i = pl.program_id(0)

        @pl.when(i == 0)
        def _():
            gain_ref[...] = jnp.zeros_like(gain_ref)

        @pl.when(i < steps)
        def _():
            pieces = []
            for kind in range(2):
                scale = scales_ref[:, kind : kind + 1]
                unit = lin_ref[:, kind * cols : (kind + 1) * cols] * scale
                grad = scale * (back_ref[kind] - unit * sums_ref[:, kind : kind + 1])
                pieces.append(grad.astype(bf16))
            grads = jnp.concatenate(pieces + [value_ref[...]], axis=1)
            proj[pl.ds(pl.multiple_of(i * size, size), size), :] = grads
            part = lax.dot_general(
                grads, weight_ref[...], (((1,), (1,)), ((), ())), preferred_element_type=f32
            )
            values = tokens_ref[...].astype(f32)
            gain_ref[...] += jnp.sum(part * (values * rms_unit(values)), axis=0, keepdims=True)
            part_ref[...] = part.astype(bf16)

        @pl.when(i >= steps)
        def _():
            g_qkv_ref[...] = lax.dot_general(
                normed_ref[...], proj[...], (((0,), (0,)), ((), ())), preferred_element_type=f32
            ).astype(bf16)

    def by_rows(columns):
        return pl.BlockSpec((size, columns), lambda i: (jnp.minimum(i, steps - 1), 0))

    def later(i):
        return jnp.maximum(i - steps, 0)

    return pl.pallas_call(
        kernel,
        grid=(steps + runs,),
        out_shape=[
            jax.ShapeDtypeStruct((total, width), bf16),
            jax.ShapeDtypeStruct((width, wide), bf16),
            jax.ShapeDtypeStruct((1, width), f32),
        ],
        in_specs=[
            pl.BlockSpec((2, size, cols), lambda i: (0, jnp.minimum(i, steps - 1), 0)),
            by_rows(wide),
            by_rows(2),
            by_rows(2),
            by_rows(cols),
            pl.BlockSpec((width, wide), lambda i: (0, 0)),
            pl.BlockSpec((total, width // runs), lambda i: (0, later(i))),
            by_rows(width),
        ],
        out_specs=[
            by_rows(width),
            pl.BlockSpec((width // runs, wide), lambda i: (later(i), 0)),
            pl.BlockSpec((1, width), lambda i: (0, 0)),
        ],
        scratch_shapes=[pltpu.VMEM((total, wide), bf16)],
        compiler_params=pltpu.CompilerParams(vmem_limit_bytes=60 * 2**20),
        cost_estimate=pl.CostEstimate(flops=0, bytes_accessed=2**20, transcendentals=0),
        name="project_back",
    )(back, projected, scales, inner_sums, value_grad, weight, normed, tokens)


def on_device_heads(
    tokens,
    doc_lengths,
    routes,
    slot_order,
    attn_gain,
    w_qkv,
    q_gain,
    k_gain,
    w_out,
    ffn_gain,
    w_router,
    w_gate,
    w_up,
    w_down,
    cotangent,
):
    rows, width = tokens.shape[1], tokens.shape[2]
    ctx, fsdp = lax.axis_size("ctx"), lax.axis_size("fsdp")
    me = lax.axis_index("ctx")
    head_dim = width // HEADS
    cols = HEADS // ctx * head_dim
    part = width // fsdp
    total = rows * ctx
    lengths = doc_lengths[0]
    bf16, f32 = jnp.bfloat16, jnp.float32

    experts, top = w_gate.shape[0], routes.shape[2]
    gains = jnp.concatenate([attn_gain, q_gain, k_gain, ffn_gain]).reshape(4, part)
    router_rows = jnp.pad(w_router.T, ((0, ROUTER_ROWS - experts), (0, 0)))
    pairs = jnp.concatenate([routes[0].T, slot_order[0].T], axis=0)
    pairs = jnp.pad(pairs, ((0, -pairs.shape[0] % 8), (0, 0)))
    tokens_all, qkv_weight, dy_all, gains, router_rows, *pairs, dy_parts = gather_inputs(
        tokens[0], w_qkv, cotangent[0], [gains, router_rows], pairs, [1, 2, 4, 6], 9
    )
    row_gain_one, gain_query, gain_key, row_gain_two = (
        gains[i : i + 1].astype(f32) for i in range(4)
    )
    flips = [0, 2, 4, 6]
    dy_parts = lax.all_gather(dy_parts, "fsdp", axis=0)

    stream_pos = dealt_position(jnp.arange(total, dtype=jnp.int32), rows, ctx)
    stream_doc, stream_inner = document_info(stream_pos, lengths)
    cosine, sine_part = rope_tables(stream_inner, head_dim)
    turn_tables = (
        jnp.concatenate([cosine, cosine], axis=1),
        jnp.concatenate([-sine_part, sine_part], axis=1),
    )
    sight = (
        (stream_pos - stream_inner).reshape(total, 1),
        stream_pos.reshape(total, 1),
        stream_pos.reshape(1, total),
    )
    normed_all, projected, squares = project(tokens_all, row_gain_one, qkv_weight)
    squares = squares.T
    squares = ctx_sum(squares.reshape(-1, 128), 1).reshape(2, total)
    scales = lax.rsqrt(squares / width + EPSILON).T
    own_gains = [
        lax.dynamic_slice_in_dim(gain, me * cols, cols, 1) for gain in (gain_query, gain_key)
    ]
    own_gains = jnp.concatenate(own_gains, axis=1)
    low, attended, attended_low, tops = attend(
        projected, scales, own_gains, *turn_tables, *sight, cols
    )

    attended_part = heads_to_rows(attended_low, 2)
    mixed_part = dot32("td,de->te", attended_part, w_out).astype(bf16)
    inputs = tokens[0].astype(f32)
    group, mixed, crossed = reduce_then_gather(
        mixed_part,
        [tokens[0], row_gain_two],
        [jax.ShapeDtypeStruct((rows, width), f32)],
        norm_chunk,
        "mix_and_norm",
        6,
        True,
        [],
    )

    capacity = rows * top // experts
    slot_by_expert, slots_other, *slots_line = slots_of(pairs, experts, top)
    moved_part, group_grad, g_router, scaled, gate_low, up_low = run_experts(
        group, dy_all, slot_by_expert, router_rows, w_gate, w_up, w_down, fsdp, capacity
    )
    scaled_line = [scaled] + [swap(scaled, flip) for flip in flips[1:]]
    mixed_all, mixed_grad, g_ffn_gain, gate_other, up_other = reduce_then_gather(
        group_grad,
        [mixed, row_gain_two, cotangent[0]],
        [jax.ShapeDtypeStruct((rows, width), f32), jax.ShapeDtypeStruct((1, width), f32)],
        norm_back_chunk,
        "norm_back",
        7,
        False,
        [gate_low, up_low],
    )
    g_ffn_gain = g_ffn_gain[0]
    crossed = lax.all_gather(crossed, "fsdp", axis=0, tiled=True)
    ups = expert_grads(
        [gate_low, up_low], [gate_other, up_other], group, crossed, slot_by_expert, slots_other, capacity
    )
    ups, mixed_all = lax.optimization_barrier((ups, mixed_all))
    output_part = dot32("te,de->td", mixed_all, w_out).astype(bf16)
    output_grad = rows_to_heads(output_part, 3)
    output_grad, moved_part, ups, mixed_all, scaled_line = lax.optimization_barrier(
        (output_grad, moved_part, ups, mixed_all, scaled_line)
    )
    moved = lax.psum_scatter(moved_part, "fsdp", scatter_dimension=0, tiled=True)
    gate_far, gate_own = swap(ups[3], 2), swap(ups[2], 2)
    downs = down_grads(scaled_line, dy_parts, [slot_by_expert] + slots_line, capacity)
    g_out = dot32("td,te->de", attended_part, mixed_all).astype(bf16)
    output_grad, ups, downs, g_out = lax.optimization_barrier((output_grad, ups, downs, g_out))

    back, value_grad, own_g_gains, inner_sums = attend_back(
        output_grad, low, attended, tops, projected, scales, own_gains, *turn_tables, *sight
    )
    inner_sums, gate_far, gate_own = lax.optimization_barrier((inner_sums, gate_far, gate_own))
    inner_sums = ctx_sum(inner_sums.T.reshape(-1, 128), 1)
    inner_sums, ups = lax.optimization_barrier((inner_sums, ups))
    up_far = swap(ups[7], 2)
    inner_sums = inner_sums.reshape(2, total).T / width

    normed_grad_part, g_qkv, g_attn_gain = project_back(
        back, projected, scales, inner_sums, value_grad, qkv_weight, normed_all, tokens_all
    )
    g_attn_gain = g_attn_gain[0]

    def placed_cols(values):
        return lax.dynamic_update_slice_in_dim(jnp.zeros((width,), f32), values, me * cols, 0)

    sums = jnp.concatenate(
        [
            jnp.stack([g_attn_gain, placed_cols(own_g_gains[0, 0]), placed_cols(own_g_gains[1, 0]), g_ffn_gain]),
            g_router[:experts],
        ],
        axis=0,
    )
    down_parts, gate_parts, up_parts, input_grad, out_part, qkv_part, sums, activations = finish_sums(
        downs,
        ups[0:2] + ups[4:7],
        gate_far,
        gate_own,
        up_far,
        normed_grad_part,
        g_out,
        g_qkv,
        jnp.pad(sums, ((0, -sums.shape[0] % 8), (0, 0))),
        tokens[0],
        mixed_grad,
        row_gain_one,
        mixed,
        moved,
        8,
    )
    return (
        activations[None],
        input_grad[None],
        sums[0],
        qkv_part,
        sums[1],
        sums[2],
        out_part,
        sums[3],
        sums[4 : 4 + experts].T,
        gate_parts,
        up_parts,
        down_parts,
    )


def solution(mesh):
    in_specs = (
        P("fsdp", "ctx", None),
        P("fsdp", None),
        P("fsdp", "ctx", None),
        P("fsdp", "ctx", None),
        P("fsdp"),
        P("fsdp", None),
        P("fsdp"),
        P("fsdp"),
        P("fsdp", None),
        P("fsdp"),
        P("fsdp", None),
        P(None, None, "fsdp"),
        P(None, None, "fsdp"),
        P(None, "fsdp", None),
        P("fsdp", "ctx", None),
    )
    out_specs = (
        P("fsdp", "ctx", None),
        P("fsdp", "ctx", None),
        P("fsdp"),
        P("fsdp", "ctx"),
        P("fsdp"),
        P("fsdp"),
        P("fsdp", "ctx"),
        P("fsdp"),
        P("fsdp", None),
        P(None, "ctx", "fsdp"),
        P(None, "ctx", "fsdp"),
        P(None, "fsdp", "ctx"),
    )
    ctx, fsdp = mesh.shape["ctx"], mesh.shape["fsdp"]
    by_heads = HEADS % ctx == 0 and ctx == 8 and fsdp == 4
    body = on_device_heads if by_heads else on_device
    return jax.shard_map(
        body, mesh=mesh, in_specs=in_specs, out_specs=out_specs, check_vma=False
    )
```

```python
import math

import jax
import jax.numpy as jnp
from jax import lax
from jax.experimental import pallas as pl
from jax.experimental.pallas import tpu as pltpu
from jax.sharding import PartitionSpec as P

HEADS = 16
MESH = pl.DeviceIdType.MESH
ANY = pl.BlockSpec(memory_space=pl.ANY)
VMEM = pl.BlockSpec(memory_space=pltpu.VMEM)
DMA = pltpu.SemaphoreType.DMA

EPSILON = 1e-05
ROPE_BASE = 10000.0
MASKED = -1e30


def rms_scale(values, gain_vector):
    return (
        values
        * lax.rsqrt(jnp.mean(values * values, axis=-1, keepdims=True) + EPSILON)
        * gain_vector
    )


def rotate(values, inner_pos):
    half_dim = values.shape[-1] // 2
    freq_table = ROPE_BASE ** (-2.0 * jnp.arange(half_dim, dtype=jnp.float32) / values.shape[-1])
    angles = inner_pos.astype(jnp.float32)[:, None] * freq_table[None, :]
    cosine = jnp.cos(angles)[:, None, :]
    sine_part = jnp.sin(angles)[:, None, :]
    first_half = values[..., :half_dim]
    second_half = values[..., half_dim:]
    return jnp.concatenate(
        [
            first_half * cosine - second_half * sine_part,
            second_half * cosine + first_half * sine_part,
        ],
        axis=-1,
    )


def dealt_position(flat_index, per_device, device_count):
    device_index = flat_index // per_device
    within = flat_index % per_device
    half_rows = per_device // 2
    return jnp.where(
        within < half_rows,
        device_index * half_rows + within,
        (2 * device_count - 1 - device_index) * half_rows + within - half_rows,
    )


def document_info(positions, lengths):
    doc_ends = jnp.sum(jnp.where(jnp.arange(lengths.shape[0])[:, None] >= jnp.arange(lengths.shape[0])[None, :], lengths[None, :], 0), axis=1)
    passed = doc_ends[None, :] <= positions[:, None]
    doc_ids = jnp.sum(passed.astype(jnp.int32), axis=1)
    inner_pos = positions - jnp.sum(jnp.where(passed, lengths[None, :], 0), axis=1)
    return (doc_ids, inner_pos)


def slot_table(route_ids, order_ids, capacity, expert_count):
    pair_count = route_ids.shape[0] * route_ids.shape[1]
    expert_flat = route_ids.reshape(pair_count)
    rank_flat = order_ids.reshape(pair_count)
    earlier = (expert_flat[None, :] == expert_flat[:, None]) & (
        rank_flat[None, :] < rank_flat[:, None]
    )
    slot_index = jnp.sum(earlier.astype(jnp.int32), axis=1)
    placed = jnp.where(
        slot_index < capacity, expert_flat * capacity + slot_index, expert_count * capacity
    )
    source = (
        jnp.full((expert_count * capacity + 1,), pair_count, jnp.int32)
        .at[placed]
        .set(jnp.arange(pair_count, dtype=jnp.int32))
    )
    return (placed, source[: expert_count * capacity])


def masked_scores(query_block, key_block, query_pos, query_doc, key_pos, key_doc, score_scale):
    scores = (
        jnp.einsum("qhd,khd->hqk", query_block, key_block, preferred_element_type=jnp.float32)
        * score_scale
    )
    allowed = (query_doc[:, None] == key_doc[None, :]) & (key_pos[None, :] <= query_pos[:, None])
    return jnp.where(allowed[None], scores, MASKED)


def silu_parts(hidden_grad, slot_gate, slot_up):
    sigma = jax.nn.sigmoid(slot_gate)
    gate_grad_low = (hidden_grad * slot_up * sigma * (1.0 + slot_gate * (1.0 - sigma))).astype(
        jnp.bfloat16
    )
    up_grad_low = (hidden_grad * slot_gate * sigma).astype(jnp.bfloat16)
    return (gate_grad_low, up_grad_low)


def on_device(
    tokens,
    doc_lengths,
    routes,
    slot_order,
    attn_gain,
    w_qkv,
    q_gain,
    k_gain,
    w_out,
    ffn_gain,
    w_router,
    w_gate,
    w_up,
    w_down,
    cotangent,
):
    row_count = tokens.shape[1]
    model_width = tokens.shape[2]
    head_count = HEADS
    head_dim = model_width // head_count
    score_scale = head_dim ** (-0.5)
    ctx_count = lax.axis_size("ctx")
    ctx_index = lax.axis_index("ctx")
    total_rows = row_count * ctx_count
    lengths = doc_lengths[0]
    local_pos = dealt_position(
        ctx_index * row_count + jnp.arange(row_count, dtype=jnp.int32), row_count, ctx_count
    )
    local_doc, local_inner = document_info(local_pos, lengths)
    stream_pos = dealt_position(jnp.arange(total_rows, dtype=jnp.int32), row_count, ctx_count)
    stream_doc, stream_inner = document_info(stream_pos, lengths)
    block_rows = math.gcd(total_rows, 512)
    block_count = total_rows // block_rows
    block_ids = jnp.arange(block_count, dtype=jnp.int32)
    gain_one, qkv_weight, gain_query, gain_key, out_weight = (
        lax.all_gather(attn_gain, "fsdp", axis=0, tiled=True),
        lax.all_gather(w_qkv, "fsdp", axis=0, tiled=True),
        lax.all_gather(q_gain, "fsdp", axis=0, tiled=True),
        lax.all_gather(k_gain, "fsdp", axis=0, tiled=True),
        lax.all_gather(w_out, "fsdp", axis=0, tiled=True),
    )
    gain_two, router_weight, gate_weight, up_weight, down_weight = (
        lax.all_gather(ffn_gain, "fsdp", axis=0, tiled=True),
        lax.all_gather(w_router, "fsdp", axis=0, tiled=True),
        lax.all_gather(w_gate, "fsdp", axis=2, tiled=True),
        lax.all_gather(w_up, "fsdp", axis=2, tiled=True),
        lax.all_gather(w_down, "fsdp", axis=1, tiled=True),
    )
    inputs = tokens[0].astype(jnp.float32)
    normed_f, norm_one_pull = jax.vjp(rms_scale, inputs, gain_one.astype(jnp.float32))
    normed_low = normed_f.astype(jnp.bfloat16)
    projected = jnp.dot(normed_low, qkv_weight, preferred_element_type=jnp.float32)
    query_lin = projected[:, :model_width]
    key_lin = projected[:, model_width : 2 * model_width]
    value_low = (
        projected[:, 2 * model_width :]
        .astype(jnp.bfloat16)
        .reshape(row_count, head_count, head_dim)
    )

    def head_shape(values, gain_vector):
        return rotate(
            rms_scale(values, gain_vector).reshape(row_count, head_count, head_dim), local_inner
        )

    query_f, query_pull = jax.vjp(head_shape, query_lin, gain_query.astype(jnp.float32))
    key_f, key_pull = jax.vjp(head_shape, key_lin, gain_key.astype(jnp.float32))
    query_low = query_f.astype(jnp.bfloat16)
    key_low = key_f.astype(jnp.bfloat16)
    keys_all, values_all = (
        lax.all_gather(key_low, "ctx", axis=0, tiled=True),
        lax.all_gather(value_low, "ctx", axis=0, tiled=True),
    )

    def key_slice(block_index):
        first_row = block_index * block_rows
        return (
            lax.dynamic_slice_in_dim(keys_all, first_row, block_rows, 0),
            lax.dynamic_slice_in_dim(values_all, first_row, block_rows, 0),
            lax.dynamic_slice_in_dim(stream_pos, first_row, block_rows, 0),
            lax.dynamic_slice_in_dim(stream_doc, first_row, block_rows, 0),
        )

    def stats_step(carry, block_index):
        running_top, running_total = carry
        key_block, value_block, key_pos, key_doc = key_slice(block_index)
        scores = masked_scores(
            query_low, key_block, local_pos, local_doc, key_pos, key_doc, score_scale
        )
        new_top = jnp.maximum(running_top, jnp.max(scores, axis=-1))
        running_total = running_total * jnp.exp(running_top - new_top) + jnp.sum(
            jnp.exp(scores - new_top[..., None]), axis=-1
        )
        return ((new_top, running_total), None)

    start_stats = (
        jnp.full((head_count, row_count), MASKED, jnp.float32),
        jnp.zeros((head_count, row_count), jnp.float32),
    )
    (score_top, score_total), _ = lax.scan(stats_step, start_stats, block_ids)
    log_total = score_top + jnp.log(score_total)

    def output_step(accum, block_index):
        key_block, value_block, key_pos, key_doc = key_slice(block_index)
        scores = masked_scores(
            query_low, key_block, local_pos, local_doc, key_pos, key_doc, score_scale
        )
        prob_block = jnp.exp(scores - log_total[..., None]).astype(jnp.bfloat16)
        return (
            accum
            + jnp.einsum(
                "hqk,khd->qhd", prob_block, value_block, preferred_element_type=jnp.float32
            ),
            None,
        )

    attended_f, _ = lax.scan(
        output_step, jnp.zeros((row_count, head_count, head_dim), jnp.float32), block_ids
    )
    attended_low = attended_f.reshape(row_count, model_width).astype(jnp.bfloat16)
    mixed = inputs + jnp.dot(attended_low, out_weight, preferred_element_type=jnp.float32)
    normed_two_f, norm_two_pull = jax.vjp(rms_scale, mixed, gain_two.astype(jnp.float32))
    normed_two = normed_two_f.astype(jnp.bfloat16)
    expert_count = gate_weight.shape[0]
    route_ids = routes[0]
    top_count = route_ids.shape[1]
    pair_count = row_count * top_count
    capacity = pair_count // expert_count
    logits = jnp.dot(normed_two, router_weight, preferred_element_type=jnp.float32)
    router_probs = jax.nn.softmax(logits, axis=-1)
    chosen = (
        route_ids[:, :, None] == jnp.arange(expert_count, dtype=jnp.int32)[None, None, :]
    ).astype(jnp.float32)
    gate_values = jnp.sum(chosen * router_probs[:, None, :], axis=-1)
    placed, source = slot_table(route_ids, slot_order[0], capacity, expert_count)
    padded_in = jnp.concatenate([normed_two, jnp.zeros((1, model_width), jnp.bfloat16)], axis=0)
    expert_in = padded_in[source // top_count].reshape(expert_count, capacity, model_width)
    gate_pre = jnp.einsum(
        "ecd,edh->ech", expert_in, gate_weight, preferred_element_type=jnp.float32
    )
    up_pre = jnp.einsum("ecd,edh->ech", expert_in, up_weight, preferred_element_type=jnp.float32)
    hidden_low = (jax.nn.silu(gate_pre) * up_pre).astype(jnp.bfloat16)
    expert_out = jnp.einsum(
        "ech,ehd->ecd", hidden_low, down_weight, preferred_element_type=jnp.float32
    )
    out_padded = jnp.concatenate(
        [
            expert_out.reshape(expert_count * capacity, model_width),
            jnp.zeros((1, model_width), jnp.float32),
        ],
        axis=0,
    )
    per_pair = out_padded[placed].reshape(row_count, top_count, model_width)
    layer_out = mixed + jnp.sum(gate_values[:, :, None] * per_pair, axis=1)
    out_grad = cotangent[0].astype(jnp.float32)
    gate_grad = jnp.sum(out_grad[:, None, :] * per_pair, axis=-1)
    pair_grad = (gate_values[:, :, None] * out_grad[:, None, :]).reshape(pair_count, model_width)
    pair_padded = jnp.concatenate([pair_grad, jnp.zeros((1, model_width), jnp.float32)], axis=0)
    slot_grad = (
        pair_padded[source].reshape(expert_count, capacity, model_width).astype(jnp.bfloat16)
    )

    def expert_step(carry, pieces):
        slot_in, slot_hidden, slot_dy, slot_gate, slot_up, gate_matrix, up_matrix, down_matrix = (
            pieces
        )
        hidden_grad = jnp.einsum(
            "cd,hd->ch", slot_dy, down_matrix, preferred_element_type=jnp.float32
        )
        gate_grad_low, up_grad_low = silu_parts(hidden_grad, slot_gate, slot_up)
        in_grad = jnp.einsum(
            "ch,dh->cd", gate_grad_low, gate_matrix, preferred_element_type=jnp.float32
        ) + jnp.einsum("ch,dh->cd", up_grad_low, up_matrix, preferred_element_type=jnp.float32)
        gate_term = jnp.einsum(
            "cd,ch->dh", slot_in, gate_grad_low, preferred_element_type=jnp.float32
        )
        up_term = jnp.einsum("cd,ch->dh", slot_in, up_grad_low, preferred_element_type=jnp.float32)
        down_term = jnp.einsum(
            "ch,cd->hd", slot_hidden, slot_dy, preferred_element_type=jnp.float32
        )
        gate_shard, up_shard, down_shard = (
            lax.psum_scatter(
                gate_term.astype(jnp.bfloat16), "fsdp", scatter_dimension=1, tiled=True
            ).astype(jnp.float32),
            lax.psum_scatter(
                up_term.astype(jnp.bfloat16), "fsdp", scatter_dimension=1, tiled=True
            ).astype(jnp.float32),
            lax.psum_scatter(
                down_term.astype(jnp.bfloat16), "fsdp", scatter_dimension=0, tiled=True
            ).astype(jnp.float32),
        )
        gate_part, up_part, down_part = (
            lax.psum_scatter(
                gate_shard.astype(jnp.bfloat16), "ctx", scatter_dimension=0, tiled=True
            ).astype(jnp.float32),
            lax.psum_scatter(
                up_shard.astype(jnp.bfloat16), "ctx", scatter_dimension=0, tiled=True
            ).astype(jnp.float32),
            lax.psum_scatter(
                down_shard.astype(jnp.bfloat16), "ctx", scatter_dimension=1, tiled=True
            ).astype(jnp.float32),
        )
        return (carry, (in_grad, gate_part, up_part, down_part))

    _, (expert_in_grad, gate_parts, up_parts, down_parts) = lax.scan(
        expert_step,
        None,
        (expert_in, hidden_low, slot_grad, gate_pre, up_pre, gate_weight, up_weight, down_weight),
    )
    in_padded = jnp.concatenate(
        [
            expert_in_grad.reshape(expert_count * capacity, model_width),
            jnp.zeros((1, model_width), jnp.float32),
        ],
        axis=0,
    )
    normed_two_grad = jnp.sum(in_padded[placed].reshape(row_count, top_count, model_width), axis=1)
    prob_grad_router = jnp.sum(chosen * gate_grad[:, :, None], axis=1)
    logit_grad = (
        router_probs
        * (prob_grad_router - jnp.sum(router_probs * prob_grad_router, axis=-1, keepdims=True))
    ).astype(jnp.bfloat16)
    normed_two_grad = normed_two_grad + jnp.einsum(
        "te,de->td", logit_grad, router_weight, preferred_element_type=jnp.float32
    )
    router_grad = jnp.einsum(
        "td,te->de", normed_two, logit_grad, preferred_element_type=jnp.float32
    )
    mixed_norm_grad, gain_two_grad = norm_two_pull(normed_two_grad)
    mixed_grad = out_grad + mixed_norm_grad
    mixed_low = mixed_grad.astype(jnp.bfloat16)
    out_weight_grad = jnp.einsum(
        "td,te->de", attended_low, mixed_low, preferred_element_type=jnp.float32
    )
    output_grad = (
        jnp.einsum("te,de->td", mixed_low, out_weight, preferred_element_type=jnp.float32)
        .astype(jnp.bfloat16)
        .reshape(row_count, head_count, head_dim)
    )
    row_delta = jnp.sum(output_grad.astype(jnp.float32) * attended_f, axis=-1).T

    def query_grad_step(accum, block_index):
        key_block, value_block, key_pos, key_doc = key_slice(block_index)
        scores = masked_scores(
            query_low, key_block, local_pos, local_doc, key_pos, key_doc, score_scale
        )
        prob_block = jnp.exp(scores - log_total[..., None])
        prob_grad = jnp.einsum(
            "qhd,khd->hqk", output_grad, value_block, preferred_element_type=jnp.float32
        )
        score_grad = (prob_block * (prob_grad - row_delta[..., None])).astype(jnp.bfloat16)
        return (
            accum
            + jnp.einsum("hqk,khd->qhd", score_grad, key_block, preferred_element_type=jnp.float32)
            * score_scale,
            None,
        )

    query_grad, _ = lax.scan(
        query_grad_step, jnp.zeros((row_count, head_count, head_dim), jnp.float32), block_ids
    )
    inner_rows = math.gcd(row_count * lax.axis_size("ctx"), 512)

    def piece_step(carry, piece_index):
        first_row = piece_index * inner_rows
        key_block = lax.dynamic_slice_in_dim(keys_all, first_row, inner_rows, 0)
        value_block = lax.dynamic_slice_in_dim(values_all, first_row, inner_rows, 0)
        key_pos = lax.dynamic_slice_in_dim(stream_pos, first_row, inner_rows, 0)
        key_doc = lax.dynamic_slice_in_dim(stream_doc, first_row, inner_rows, 0)
        scores = masked_scores(
            query_low, key_block, local_pos, local_doc, key_pos, key_doc, score_scale
        )
        prob_block = jnp.exp(scores - log_total[..., None])
        prob_grad = jnp.einsum(
            "qhd,khd->hqk", output_grad, value_block, preferred_element_type=jnp.float32
        )
        score_grad = (prob_block * (prob_grad - row_delta[..., None])).astype(jnp.bfloat16)
        value_part = jnp.einsum(
            "hqk,qhd->khd",
            prob_block.astype(jnp.bfloat16),
            output_grad,
            preferred_element_type=jnp.float32,
        )
        key_part = (
            jnp.einsum("hqk,qhd->khd", score_grad, query_low, preferred_element_type=jnp.float32)
            * score_scale
        )
        return (
            carry,
            jnp.concatenate(
                [
                    key_part.reshape(inner_rows, model_width),
                    value_part.reshape(inner_rows, model_width),
                ],
                axis=1,
            ),
        )

    _, stacked = lax.scan(
        piece_step,
        None,
        jnp.arange(row_count * lax.axis_size("ctx") // inner_rows, dtype=jnp.int32),
    )
    key_value_grad = lax.psum_scatter(
        stacked.reshape(row_count * lax.axis_size("ctx"), 2 * model_width).astype(jnp.bfloat16),
        "ctx",
        scatter_dimension=0,
        tiled=True,
    ).astype(jnp.float32)
    key_grad = key_value_grad[:, :model_width].reshape(row_count, head_count, head_dim)
    value_grad = key_value_grad[:, model_width:]
    query_lin_grad, gain_query_grad = query_pull(query_grad)
    key_lin_grad, gain_key_grad = key_pull(key_grad)
    proj_grad = jnp.concatenate(
        [
            query_lin_grad.astype(jnp.bfloat16),
            key_lin_grad.astype(jnp.bfloat16),
            value_grad.astype(jnp.bfloat16),
        ],
        axis=1,
    )
    qkv_weight_grad = jnp.einsum(
        "td,te->de", normed_low, proj_grad, preferred_element_type=jnp.float32
    )
    normed_grad = jnp.einsum("te,de->td", proj_grad, qkv_weight, preferred_element_type=jnp.float32)
    input_norm_grad, gain_one_grad = norm_one_pull(normed_grad)
    input_grad = mixed_grad + input_norm_grad
    qkv_shard, out_shard = (
        lax.psum_scatter(
            qkv_weight_grad.astype(jnp.bfloat16), "fsdp", scatter_dimension=0, tiled=True
        ).astype(jnp.float32),
        lax.psum_scatter(
            out_weight_grad.astype(jnp.bfloat16), "fsdp", scatter_dimension=0, tiled=True
        ).astype(jnp.float32),
    )
    qkv_part, out_part = (
        lax.psum_scatter(
            qkv_shard.astype(jnp.bfloat16), "ctx", scatter_dimension=1, tiled=True
        ).astype(jnp.float32),
        lax.psum_scatter(
            out_shard.astype(jnp.bfloat16), "ctx", scatter_dimension=1, tiled=True
        ).astype(jnp.float32),
    )
    gain_one_sum, gain_query_sum, gain_key_sum, gain_two_sum, router_sum = lax.psum(
        (gain_one_grad, gain_query_grad, gain_key_grad, gain_two_grad, router_grad), ("ctx", "fsdp")
    )
    shard_rows = model_width // lax.axis_size("fsdp")
    shard_start = lax.axis_index("fsdp") * shard_rows

    def own_rows(full_array):
        return lax.dynamic_slice_in_dim(full_array, shard_start, shard_rows, 0)

    return (
        layer_out.astype(jnp.bfloat16)[None],
        input_grad[None],
        own_rows(gain_one_sum),
        qkv_part,
        own_rows(gain_query_sum),
        own_rows(gain_key_sum),
        out_part,
        own_rows(gain_two_sum),
        own_rows(router_sum),
        gate_parts,
        up_parts,
        down_parts,
    )


def rms_unit(values):
    return lax.rsqrt(jnp.mean(values * values, axis=-1, keepdims=True) + EPSILON)


def rope_tables(inner_pos, head_dim):
    half_dim = head_dim // 2
    freq_table = ROPE_BASE ** (-2.0 * jnp.arange(half_dim, dtype=jnp.float32) / head_dim)
    angles = inner_pos.astype(jnp.float32)[:, None] * freq_table[None, :]
    return (jnp.cos(angles), jnp.sin(angles))


def dot32(spec, left, right):
    return jnp.einsum(spec, left, right, preferred_element_type=jnp.float32)


def greet(peers):
    barrier = pltpu.get_barrier_semaphore()
    for peer in peers:
        pl.semaphore_signal(barrier, inc=1, device_id=peer, device_id_type=MESH)
    pl.semaphore_wait(barrier, len(peers))


def send(source, target, send_sem, recv_sem, peer):
    copy = pltpu.make_async_remote_copy(
        source, target, send_sem, recv_sem, device_id=peer, device_id_type=MESH
    )
    copy.start()
    return copy


def comm_call(
    kernel, name, collective_id, out_shape, in_specs, out_specs, scratch_shapes, cost, vmem=16
):
    return pl.pallas_call(
        kernel,
        out_shape=out_shape,
        in_specs=in_specs,
        out_specs=out_specs,
        scratch_shapes=scratch_shapes,
        compiler_params=pltpu.CompilerParams(
            collective_id=collective_id, has_side_effects=True, vmem_limit_bytes=vmem * 2**20
        ),
        cost_estimate=pl.CostEstimate(flops=0, bytes_accessed=cost, transcendentals=0),
        name=name,
    )


def ctx_sum(values, collective_id):
    ctx = lax.axis_size("ctx")

    def kernel(own_ref, out_ref, held, send_sems, recv_sems):
        me, mine = lax.axis_index("ctx"), lax.axis_index("fsdp")
        peers = [(lax.rem(me + step, ctx), mine) for step in range(1, ctx)]
        greet(peers)
        copies = [
            send(own_ref, held.at[i], send_sems.at[i], recv_sems.at[i], peer)
            for i, peer in enumerate(peers)
        ]
        total = own_ref[...]
        for i, copy in enumerate(copies):
            copy.wait_recv()
            total = total + held[i]
        out_ref[...] = total
        for copy in copies:
            copy.wait_send()

    return comm_call(
        kernel,
        "ctx_sum",
        collective_id,
        jax.ShapeDtypeStruct(values.shape, values.dtype),
        [VMEM],
        VMEM,
        [
            pltpu.VMEM((ctx - 1,) + values.shape, values.dtype),
            DMA((ctx - 1,)),
            DMA((ctx - 1,)),
        ],
        20 * 2**20,
    )(values)


def heads_to_rows(values, collective_id):
    ctx, fsdp = lax.axis_size("ctx"), lax.axis_size("fsdp")
    rows, cols = values.shape[0] // ctx, values.shape[1]
    share = ctx // fsdp

    def kernel(own_ref, out_ref, send_sems, recv_sems):
        me, mine = lax.axis_index("ctx"), lax.axis_index("fsdp")
        keeper, place = me // share, lax.rem(me, share)
        own_keeper = (keeper == mine).astype(jnp.int32)
        barrier = pltpu.get_barrier_semaphore()
        for step in range(share * fsdp):
            source, stream = mine * share + step // fsdp, step % fsdp

            @pl.when(jnp.logical_or(source != me, stream != mine))
            def _():
                pl.semaphore_signal(
                    barrier, inc=1, device_id=(source, stream), device_id_type=MESH
                )

        pl.semaphore_wait(barrier, ctx - own_keeper)

        def block(index):
            return own_ref.at[pl.ds(pl.multiple_of(index * rows, rows), rows), :]

        def landing(stream, position):
            return out_ref.at[
                pl.ds(pl.multiple_of(stream * rows, rows), rows),
                pl.ds(pl.multiple_of(position * cols, cols), cols),
            ]

        slot = place * fsdp + mine

        def copy_to(step):
            other = lax.rem(me + step, ctx)
            return pltpu.make_async_remote_copy(
                block(other),
                landing(mine, place),
                send_sems.at[step],
                recv_sems.at[slot],
                device_id=(other, keeper),
                device_id_type=MESH,
            )

        kept = pltpu.make_async_copy(block(me), landing(mine, place), send_sems.at[0])
        for step in range(1, ctx):
            copy_to(step).start()

        @pl.when(own_keeper == 0)
        def _():
            copy_to(0).start()

        @pl.when(own_keeper == 1)
        def _():
            kept.start()
            kept.wait()

        for step in range(share * fsdp):

            @pl.when(
                jnp.logical_or(mine * share + step // fsdp != me, step % fsdp != mine)
            )
            def _():
                pltpu.make_async_copy(
                    block(0), landing(step % fsdp, step // fsdp), recv_sems.at[step]
                ).wait()

        for step in range(1, ctx):
            copy_to(step).wait_send()

        @pl.when(own_keeper == 0)
        def _():
            copy_to(0).wait_send()

    return comm_call(
        kernel,
        "heads_to_rows",
        collective_id,
        jax.ShapeDtypeStruct((fsdp * rows, share * cols), values.dtype),
        [ANY],
        ANY,
        [DMA((ctx,)), DMA((share * fsdp,))],
        40 * 2**20,
    )(values)


def rows_to_heads(values, collective_id):
    ctx, fsdp = lax.axis_size("ctx"), lax.axis_size("fsdp")
    share = ctx // fsdp
    rows, cols = values.shape[0] // fsdp, values.shape[1] // share

    def kernel(own_ref, out_ref, stage, stage_send, stage_recv, send_sems, recv_sems, done_sem):
        me, mine = lax.axis_index("ctx"), lax.axis_index("fsdp")
        ctx_peers = [(lax.rem(me + step, ctx), mine) for step in range(1, ctx)]
        greet(ctx_peers + [(me, lax.rem(mine + step, fsdp)) for step in range(1, fsdp)])

        def block(stream):
            return own_ref.at[pl.ds(pl.multiple_of(stream * rows, rows), rows), :]

        def landing(index):
            return out_ref.at[pl.ds(pl.multiple_of(index * rows, rows), rows), :]

        steps = [2, 3, 1]
        staged = {
            step: send(
                block(lax.rem(mine + step, fsdp)),
                stage.at[fsdp - step],
                stage_send.at[step],
                stage_recv.at[fsdp - step],
                (me, lax.rem(mine + step, fsdp)),
            )
            for step in steps
        }

        def piece(step, place):
            span = pl.ds(place * cols, cols)
            if step == 0:
                return own_ref.at[pl.ds(pl.multiple_of(mine * rows, rows), rows), span]
            return stage.at[step, :, span]

        def target(step, place):
            return lax.rem(mine + step, fsdp) * share + place

        def copy_to(step, place):
            return pltpu.make_async_remote_copy(
                piece(step, place),
                landing(me),
                send_sems.at[step * share + place],
                recv_sems.at[me],
                device_id=(target(step, place), mine),
                device_id_type=MESH,
            )

        def keep(step, place):
            return pltpu.make_async_copy(
                piece(step, place), landing(me), send_sems.at[step * share + place]
            )

        for step in [0, 1, 2, 3]:
            if step > 0:
                staged[fsdp - step].wait_recv()
            for place in range(share):
                far = target(step, place) != me
                pl.when(far)(copy_to(step, place).start)
                pl.when(jnp.logical_not(far))(keep(step, place).start)
        for step in range(1, ctx):
            source = lax.rem(me + step, ctx)
            pltpu.make_async_copy(
                piece(0, 0), landing(source), recv_sems.at[source]
            ).wait()
        for step in range(fsdp):
            for place in range(share):
                far = target(step, place) != me
                pl.when(far)(copy_to(step, place).wait_send)
                pl.when(jnp.logical_not(far))(keep(step, place).wait)
        for copy in staged.values():
            copy.wait_send()
        for peer in ctx_peers:
            pl.semaphore_signal(done_sem, inc=1, device_id=peer, device_id_type=MESH)
        pl.semaphore_wait(done_sem, ctx - 1)

    return comm_call(
        kernel,
        "rows_to_heads",
        collective_id,
        jax.ShapeDtypeStruct((ctx * rows, cols), values.dtype),
        [ANY],
        ANY,
        [
            pltpu.VMEM((fsdp, rows, share * cols), values.dtype),
            DMA((fsdp,)),
            DMA((fsdp,)),
            DMA((ctx,)),
            DMA((ctx,)),
            pltpu.SemaphoreType.REGULAR,
        ],
        2**20,
    )(values)


def swap(values, flip):
    return lax.ppermute(values, "ctx", [(i, i ^ flip) for i in range(lax.axis_size("ctx"))])


def reduce_then_gather(partial, extras, out_shapes, chunk_math, name, collective_id, crossed, bulk, vmem):
    ctx, fsdp = lax.axis_size("ctx"), lax.axis_size("fsdp")
    rows, width = partial.shape[0] // fsdp, partial.shape[1]
    chunks = 4
    size = rows // chunks
    count = len(extras)
    cols = width // ctx
    if crossed:
        out_shapes = out_shapes + [jax.ShapeDtypeStruct((rows, width // 2), jnp.bfloat16)]
    bulk_count, out_count = len(bulk), len(out_shapes)

    def kernel(*refs):
        part_ref, extra_refs = refs[0], refs[1 : 1 + count]
        bulk_refs, refs = refs[1 + count : 1 + count + bulk_count], refs[1 + count + bulk_count :]
        all_ref, out_refs = refs[0], refs[1 : 1 + out_count]
        bulk_out_refs, refs = refs[1 + out_count : 1 + out_count + bulk_count], refs[1 + out_count :]
        near_own, near_far, far_sum, far_own, sems, cross_sems, bulk_sems = refs[bulk_count:]
        me, mine = lax.axis_index("ctx"), lax.axis_index("fsdp")
        flip = 1 - 2 * lax.rem(mine, 2)
        core = mine + flip
        chip = lax.rem(mine + 2, fsdp)
        diagonal = lax.rem(core + 2, fsdp)
        to_x = (flipped(me, 1), mine)
        greet([(me, core), (me, chip)] + ([to_x] if crossed or bulk else []))

        def span(block, i):
            return pl.ds(pl.multiple_of(block * rows + i * size, size), size)

        def sem(kind, i):
            return sems.at[2 * kind, i], sems.at[2 * kind + 1, i]

        copies = []
        from_core_far, from_core_own, from_chip = [], [], []
        exchanged = [
            send(source, target, bulk_sems.at[0, i], bulk_sems.at[1, i], to_x)
            for i, (source, target) in enumerate(zip(bulk_refs, bulk_out_refs))
        ]
        for i in range(chunks):
            copy = send(
                part_ref.at[span(diagonal, i), :], near_far.at[i], *sem(0, i), (me, core)
            )
            from_core_far.append(copy)
        for i in range(chunks):
            copy = send(part_ref.at[span(core, i), :], near_own.at[i], *sem(1, i), (me, core))
            from_core_own.append(copy)
        for i in range(chunks):
            from_core_far[i].wait_recv()
            both = part_ref[span(chip, i), :].astype(jnp.float32) + near_far[i].astype(jnp.float32)
            far_sum[i] = both.astype(jnp.bfloat16)
            from_chip.append(send(far_sum.at[i], far_own.at[i], *sem(2, i), (me, chip)))
        to_chip = []
        for i in range(chunks):
            from_core_own[i].wait_recv()
            from_chip[i].wait_recv()
            total = (
                part_ref[span(mine, i), :].astype(jnp.float32)
                + near_own[i].astype(jnp.float32)
                + far_own[i].astype(jnp.float32)
            )
            all_ref[span(mine, i), :] = chunk_math(
                i, pl.ds(i * size, size), total, extra_refs, out_refs
            ).astype(jnp.bfloat16)
            own = all_ref.at[span(mine, i), :]
            to_chip.append(send(own, own, *sem(3, i), (me, chip)))
            copies.append(send(own, own, *sem(4, i), (me, core)))
            for run in range(ctx // 2 if crossed else 0):
                start = pl.multiple_of((2 * run + 1 - lax.rem(me, 2)) * cols, cols)
                copies.append(
                    send(
                        all_ref.at[span(mine, i), pl.ds(start, cols)],
                        out_refs[-1].at[pl.ds(i * size, size), pl.ds(run * cols, cols)],
                        cross_sems.at[0, i, run],
                        cross_sems.at[1, i, run],
                        to_x,
                    )
                )
        for i in range(chunks):
            to_chip[i].wait_recv()
            other = all_ref.at[span(chip, i), :]
            copies.append(send(other, other, *sem(5, i), (me, core)))
        for copy in copies + exchanged:
            copy.wait_recv()
        for copy in from_core_far + from_core_own + from_chip + to_chip + copies + exchanged:
            copy.wait_send()

    return comm_call(
        kernel,
        name,
        collective_id,
        [jax.ShapeDtypeStruct(partial.shape, jnp.bfloat16)]
        + out_shapes
        + [jax.ShapeDtypeStruct(values.shape, values.dtype) for values in bulk],
        [VMEM] * (1 + count) + [ANY] * bulk_count,
        [VMEM] * (1 + out_count) + [ANY] * bulk_count,
        [
            pltpu.VMEM((chunks, size, width), jnp.bfloat16),
            pltpu.VMEM((chunks, size, width), jnp.bfloat16),
            pltpu.VMEM((chunks, size, width), jnp.bfloat16),
            pltpu.VMEM((chunks, size, width), jnp.bfloat16),
            DMA((12, chunks)),
            DMA((2, chunks, ctx // 2)),
            DMA((2, max(1, bulk_count))),
        ],
        100 * 2**20,
        vmem,
    )(partial, *extras, *bulk)


def norm_chunk(index, span, total, extra_refs, out_refs):
    tokens_ref, gain_ref = extra_refs
    mixed = tokens_ref[span, :].astype(jnp.float32) + total
    out_refs[0][span, :] = mixed
    return mixed * rms_unit(mixed) * gain_ref[...]


def norm_back_chunk(index, span, total, extra_refs, out_refs):
    mixed_ref, gain_ref, dy_ref = extra_refs
    mixed = mixed_ref[span, :]
    scale = rms_unit(mixed)
    unit = mixed * scale
    pulled = total * gain_ref[...]
    grad = dy_ref[span, :].astype(jnp.float32) + scale * (
        pulled - unit * jnp.mean(unit * pulled, axis=-1, keepdims=True)
    )
    out_refs[0][span, :] = grad
    gain_grad = jnp.sum(total * unit, axis=0, keepdims=True)
    if index == 0:
        out_refs[1][...] = gain_grad
    else:
        out_refs[1][...] += gain_grad
    return grad


ROUTER_ROWS = 16


def one_hot(slots, capacity):
    return lax.broadcasted_iota(jnp.int32, (capacity, slots.shape[1]), 0) == slots


def slots_of(pairs, experts, top):
    lines, rows = pairs.shape
    absent = float(rows * top)

    def kernel(pairs_ref, out_ref):
        out_ref[...] = jnp.full(out_ref.shape, -1, jnp.int32)
        rank_rows = []
        for expert in range(experts):
            rank = jnp.full((1, rows), absent, jnp.float32)
            for k in range(top):
                rank = jnp.where(
                    pairs_ref[k : k + 1, :] == expert,
                    pairs_ref[top + k : top + k + 1, :].astype(jnp.float32),
                    rank,
                )
            rank_rows.append(rank)
        filler = jnp.full((rows - experts, rows), absent, jnp.float32)
        by_column = jnp.concatenate(rank_rows + [filler], axis=0).T
        for expert, rank in enumerate(rank_rows):
            earlier = jnp.where(by_column[:, expert : expert + 1] < rank, 1.0, 0.0)
            slot = jnp.where(rank < absent, jnp.sum(earlier, axis=0, keepdims=True), -1.0)
            out_ref[expert : expert + 1, :] = slot.astype(jnp.int32)

    return pl.pallas_call(
        kernel,
        out_shape=jax.ShapeDtypeStruct((lines, rows), jnp.int32),
        in_specs=[VMEM],
        out_specs=VMEM,
        cost_estimate=pl.CostEstimate(flops=10**7, bytes_accessed=2**20, transcendentals=0),
        name="slots_of",
    )(pairs)


def run_experts(group, dy_all, slots, router, w_gate, w_up, w_down, blocks, capacity):
    experts, width, units = w_gate.shape
    total = group.shape[0]
    rows = total // blocks
    held = blocks * capacity
    f32, bf16 = jnp.float32, jnp.bfloat16

    def kernel(
        group_ref,
        dy_ref,
        slots_ref,
        router_ref,
        gate_ref,
        up_ref,
        down_ref,
        moved_ref,
        grad_ref,
        g_router_ref,
        scaled_ref,
        gate_low_ref,
        up_low_ref,
        disp,
        ins,
        dys,
        probs,
        prob_grad,
    ):
        expert = pl.program_id(0)

        def block_rows(b):
            return pl.ds(b * rows, rows)

        @pl.when(expert == 0)
        def _():
            logits = lax.dot_general(
                router_ref[...],
                group_ref[...],
                (((1,), (1,)), ((), ())),
                preferred_element_type=f32,
            )
            real = lax.broadcasted_iota(jnp.int32, logits.shape, 0) < experts
            logits = jnp.where(real, logits, MASKED)
            weights = jnp.exp(logits - jnp.max(logits, axis=0, keepdims=True))
            probs[...] = weights / jnp.sum(weights, axis=0, keepdims=True)
            prob_grad[...] = jnp.zeros_like(prob_grad)
            for b in range(blocks):
                for e in range(experts):
                    disp[b, pl.ds(e * capacity, capacity), :] = (
                        one_hot(slots_ref[b, pl.ds(e, 1), :], capacity)
                        .astype(f32)
                        .astype(bf16)
                    )
                for source, target in ((group_ref, ins), (dy_ref, dys)):
                    picked = jnp.dot(
                        disp[b], source[block_rows(b), :], preferred_element_type=f32
                    ).astype(bf16)
                    for e in range(experts):
                        target[e, pl.ds(b * capacity, capacity), :] = picked[
                            e * capacity : (e + 1) * capacity
                        ]

        expert_in, slot_dy = ins[expert], dys[expert]
        gate_matrix, up_matrix, down_matrix = gate_ref[0], up_ref[0], down_ref[0]
        gate_pre = jnp.dot(expert_in, gate_matrix, preferred_element_type=f32)
        up_pre = jnp.dot(expert_in, up_matrix, preferred_element_type=f32)
        raw_grad = lax.dot_general(
            slot_dy, down_matrix, (((1,), (1,)), ((), ())), preferred_element_type=f32
        )
        own_probs = probs[pl.ds(expert, 1), :]
        hots = [one_hot(slots_ref[b, pl.ds(expert, 1), :], capacity) for b in range(blocks)]
        value = jnp.concatenate(
            [
                jnp.sum(
                    jnp.where(hots[b], own_probs[:, b * rows : (b + 1) * rows], 0.0),
                    axis=1,
                    keepdims=True,
                )
                for b in range(blocks)
            ],
            axis=0,
        )
        sigma = 1.0 / (1.0 + jnp.exp(-gate_pre))
        silu = gate_pre * sigma
        hidden = (silu * up_pre).astype(bf16)
        hidden_f = hidden.astype(f32)
        value_grad = jnp.sum(hidden_f * raw_grad, axis=1, keepdims=True)
        hidden_grad = raw_grad * value
        gate_low = (hidden_grad * up_pre * sigma * (1.0 + gate_pre * (1.0 - sigma))).astype(bf16)
        up_low = (hidden_grad * silu).astype(bf16)
        scaled = (hidden_f * value).astype(bf16)
        scaled_ref[0] = scaled
        gate_low_ref[0] = gate_low
        up_low_ref[0] = up_low
        for b in range(blocks):
            prob_grad[expert, :, block_rows(b)] = jnp.sum(
                jnp.where(hots[b], value_grad[b * capacity : (b + 1) * capacity], 0.0),
                axis=0,
                keepdims=True,
            )
        dys[expert] = jnp.dot(scaled, down_matrix, preferred_element_type=f32).astype(bf16)
        ins[expert] = (
            lax.dot_general(
                gate_low, gate_matrix, (((1,), (1,)), ((), ())), preferred_element_type=f32
            )
            + lax.dot_general(
                up_low, up_matrix, (((1,), (1,)), ((), ())), preferred_element_type=f32
            )
        ).astype(bf16)

        @pl.when(expert == experts - 1)
        def _():
            grads = jnp.concatenate([prob_grad[e] for e in range(ROUTER_ROWS)], axis=0)
            weights = probs[...]
            logit_grad = (
                weights * (grads - jnp.sum(weights * grads, axis=0, keepdims=True))
            ).astype(bf16)
            g_router_ref[...] = jnp.dot(logit_grad, group_ref[...], preferred_element_type=f32)
            for b in range(blocks):
                for source, target in ((dys, moved_ref), (ins, grad_ref)):
                    gathered = jnp.concatenate(
                        [source[e, pl.ds(b * capacity, capacity), :] for e in range(experts)],
                        axis=0,
                    )
                    back = lax.dot_general(
                        disp[b], gathered, (((0,), (0,)), ((), ())), preferred_element_type=f32
                    )
                    if target is grad_ref:
                        back = back + lax.dot_general(
                            logit_grad[:, b * rows : (b + 1) * rows],
                            router_ref[...],
                            (((0,), (0,)), ((), ())),
                            preferred_element_type=f32,
                        )
                    target[block_rows(b), :] = back.astype(bf16)

    def whole(shape):
        return pl.BlockSpec(shape, lambda e: (0,) * len(shape))

    def by_expert(shape):
        return pl.BlockSpec((1,) + shape, lambda e: (e, 0, 0))

    return pl.pallas_call(
        kernel,
        grid=(experts,),
        out_shape=[
            jax.ShapeDtypeStruct((total, width), bf16),
            jax.ShapeDtypeStruct((total, width), bf16),
            jax.ShapeDtypeStruct((ROUTER_ROWS, width), f32),
        ]
        + [jax.ShapeDtypeStruct((experts, held, units), bf16)] * 3,
        in_specs=[
            whole((total, width)),
            whole((total, width)),
            whole(slots.shape),
            whole((ROUTER_ROWS, width)),
            by_expert((width, units)),
            by_expert((width, units)),
            by_expert((units, width)),
        ],
        out_specs=[
            whole((total, width)),
            whole((total, width)),
            whole((ROUTER_ROWS, width)),
        ]
        + [by_expert((held, units))] * 3,
        scratch_shapes=[
            pltpu.VMEM((blocks, experts * capacity, rows), bf16),
            pltpu.VMEM((experts, held, width), bf16),
            pltpu.VMEM((experts, held, width), bf16),
            pltpu.VMEM((ROUTER_ROWS, total), f32),
            pltpu.VMEM((ROUTER_ROWS, 1, total), f32),
        ],
        compiler_params=pltpu.CompilerParams(vmem_limit_bytes=60 * 2**20),
        cost_estimate=pl.CostEstimate(
            flops=30 * 10**9, bytes_accessed=30 * 2**20, transcendentals=10**6
        ),
        name="run_experts",
    )(group, dy_all, slots, router, w_gate, w_up, w_down)


def expert_grads(slot_own, slot_other, rows_own, rows_other, slots_own, slots_other, capacity):
    kinds = len(slot_own)
    experts, held, units = slot_own[0].shape
    total, half = rows_other.shape
    blocks = held // capacity
    rows = total // blocks
    ctx = lax.axis_size("ctx")
    cols = 2 * half // ctx
    f32, bf16 = jnp.float32, jnp.bfloat16

    def kernel(*refs):
        own_refs, other_refs = refs[:kinds], refs[kinds : 2 * kinds]
        rows_own_ref, rows_other_ref, slots_own_ref, slots_other_ref = refs[2 * kinds : 2 * kinds + 4]
        out_refs, held_rows = refs[2 * kinds + 4 : -1], refs[-1]
        expert = pl.program_id(0)
        me = lax.axis_index("ctx")

        def columns(side, run):
            if side == 1:
                return pl.ds(run * cols, cols)
            return pl.ds(pl.multiple_of((2 * run + lax.rem(me, 2)) * cols, cols), cols)

        @pl.when(expert == 0)
        def _():
            for side, slots_ref, source in (
                (0, slots_own_ref, rows_own_ref),
                (1, slots_other_ref, rows_other_ref),
            ):
                for b in range(blocks):
                    span = pl.ds(b * rows, rows)
                    disp = jnp.concatenate(
                        [
                            one_hot(slots_ref[b, pl.ds(e, 1), :], capacity).astype(f32)
                            for e in range(experts)
                        ],
                        axis=0,
                    ).astype(bf16)
                    for run in range(ctx // 2):
                        picked = jnp.dot(
                            disp, source[span, columns(side, run)], preferred_element_type=f32
                        ).astype(bf16)
                        for e in range(experts):
                            held_rows[
                                e,
                                pl.ds(side * held + b * capacity, capacity),
                                pl.ds(run * cols, cols),
                            ] = picked[e * capacity : (e + 1) * capacity]

        low, high = lax.rem(me // 2, 2), me // 4
        stacked = [
            jnp.concatenate([own[0], other[0]], axis=0) for own, other in zip(own_refs, other_refs)
        ]
        contract = (((0,), (0,)), ((), ()))
        for run in range(ctx // 2):
            given = jnp.where(low == run % 2, 0, 2)
            place = given + jnp.where(high == run // 2, 0, 1)
            features = held_rows[expert, :, pl.ds(run * cols, cols)]
            for kind in range(kinds):
                total = lax.dot_general(
                    features, stacked[kind], contract, preferred_element_type=f32
                ).astype(bf16)
                for i in range(4):

                    @pl.when(place == i)
                    def _():
                        out_refs[4 * kind + i][0] = total

    def whole(shape):
        return pl.BlockSpec(shape, lambda e: (0,) * len(shape))

    slot_spec = pl.BlockSpec((1, held, units), lambda e: (e, 0, 0))
    return pl.pallas_call(
        kernel,
        grid=(experts,),
        out_shape=[jax.ShapeDtypeStruct((experts, units, cols), bf16)] * (4 * kinds),
        in_specs=[slot_spec] * (2 * kinds)
        + [whole((total, 2 * half)), whole((total, half))]
        + [whole(slots_own.shape)] * 2,
        out_specs=[pl.BlockSpec((1, units, cols), lambda e: (e, 0, 0))] * (4 * kinds),
        scratch_shapes=[pltpu.VMEM((experts, 2 * held, half), bf16)],
        compiler_params=pltpu.CompilerParams(vmem_limit_bytes=60 * 2**20),
        cost_estimate=pl.CostEstimate(flops=0, bytes_accessed=2**20, transcendentals=0),
        name="expert_grads",
    )(*slot_own, *slot_other, rows_own, rows_other, slots_own, slots_other)


def down_grads(scaled, dy_parts, slots, capacity):
    count = len(scaled)
    experts, held, units = scaled[0].shape
    blocks, _, rows, wide = dy_parts.shape
    cols = wide // 2
    f32, bf16 = jnp.float32, jnp.bfloat16

    def kernel(*refs):
        scaled_refs, dy_ref, slots_refs = refs[:count], refs[count], refs[count + 1 : 2 * count + 1]
        out_ref, held_rows = refs[2 * count + 1 :]
        expert = pl.program_id(0)

        @pl.when(expert == 0)
        def _():
            for i, slots_ref in enumerate(slots_refs):
                for b in range(blocks):
                    span = pl.ds(b * rows, rows)
                    disp = jnp.concatenate(
                        [
                            one_hot(slots_ref[b, pl.ds(e, 1), :], capacity).astype(f32)
                            for e in range(experts)
                        ],
                        axis=0,
                    ).astype(bf16)
                    picked = jnp.dot(disp, dy_ref[b, i], preferred_element_type=f32).astype(bf16)
                    for e in range(experts):
                        held_rows[e, pl.ds(i * held + b * capacity, capacity), :] = picked[
                            e * capacity : (e + 1) * capacity
                        ]

        stacked = jnp.concatenate([ref[0] for ref in scaled_refs], axis=0)
        total = lax.dot_general(
            stacked, held_rows[expert], (((0,), (0,)), ((), ())), preferred_element_type=f32
        ).astype(bf16)
        side = lax.rem(lax.axis_index("ctx"), 2)
        for x in range(2):
            kept = jnp.where(side == x, 1, 0)
            out_ref[pl.ds(kept, 1), 0] = total[:, x * cols : (x + 1) * cols][None]

    def whole(shape):
        return pl.BlockSpec(shape, lambda e: (0,) * len(shape))

    return pl.pallas_call(
        kernel,
        grid=(experts,),
        out_shape=jax.ShapeDtypeStruct((2, experts, units, cols), bf16),
        in_specs=[pl.BlockSpec((1, held, units), lambda e: (e, 0, 0))] * count
        + [whole(dy_parts.shape)]
        + [whole(slots[0].shape)] * count,
        out_specs=pl.BlockSpec((2, 1, units, cols), lambda e: (0, e, 0, 0)),
        scratch_shapes=[pltpu.VMEM((experts, count * held, wide), bf16)],
        compiler_params=pltpu.CompilerParams(vmem_limit_bytes=60 * 2**20),
        cost_estimate=pl.CostEstimate(flops=0, bytes_accessed=2**20, transcendentals=0),
        name="down_grads",
    )(*scaled, dy_parts, *slots)


def roll_half(values):
    return pltpu.roll(values, values.shape[1] // 2, 1)


def allowed_keys(first_ref, last_ref, span, places):
    return (places >= first_ref[span, :]) & (places <= last_ref[span, :])


def stored_runs(total):
    ctx = lax.axis_size("ctx")
    rows = total // ctx
    run = rows // 2
    starts = [i * rows for i in range(ctx)]
    return starts + [i * rows + run for i in reversed(range(ctx))], run


def attend(projected, scales, gains, cosine, sine_part, first, last, places, cols):
    total = projected.shape[0]
    head_dim = cosine.shape[1]
    heads = cols // head_dim
    size = math.gcd(total, 256)
    score_scale = head_dim ** (-0.5)
    starts, run = stored_runs(total)
    f32, bf16 = jnp.float32, jnp.bfloat16

    def kernel(
        lin_ref,
        scales_ref,
        gains_ref,
        cos_ref,
        sin_ref,
        first_ref,
        last_ref,
        places_ref,
        low_ref,
        attended_ref,
        attended_low_ref,
        top_ref,
    ):
        for kind in range(3):
            for h in range(heads):
                span = pl.ds(kind * cols + h * head_dim, head_dim)
                values = lin_ref[:, span]
                if kind < 2:
                    values = values * scales_ref[:, kind : kind + 1] * gains_ref[:, span]
                    values = values * cos_ref[...] + roll_half(values) * sin_ref[...]
                values = values.astype(bf16)
                for place, start in enumerate(starts):
                    low_ref[pl.ds(place * run, run), span] = values[start : start + run]
        for h in range(heads):
            head = pl.ds(h * head_dim, head_dim)
            for b in range(total // size):
                span, seen = pl.ds(b * size, size), pl.ds(0, (b + 1) * size)
                scores = lax.dot_general(
                    low_ref[span, head],
                    low_ref[seen, pl.ds(cols + h * head_dim, head_dim)],
                    (((1,), (1,)), ((), ())),
                    preferred_element_type=f32,
                )
                allowed = allowed_keys(first_ref, last_ref, span, places_ref[:, seen])
                scores = jnp.where(allowed, scores * score_scale, MASKED)
                top = jnp.max(scores, axis=1, keepdims=True)
                weights = jnp.exp(scores - top)
                sums = jnp.sum(weights, axis=1, keepdims=True)
                probs = (weights * (1.0 / sums)).astype(bf16)
                attended = jnp.dot(
                    probs,
                    low_ref[seen, pl.ds(2 * cols + h * head_dim, head_dim)],
                    preferred_element_type=f32,
                )
                attended_ref[span, head] = attended
                attended_low = attended.astype(bf16)
                for i in range(size // run):
                    start = starts[b * (size // run) + i]
                    attended_low_ref[pl.ds(start, run), head] = attended_low[i * run : (i + 1) * run]
                top_ref[span, head] = jnp.broadcast_to(top + jnp.log(sums), (size, head_dim))

    return pl.pallas_call(
        kernel,
        out_shape=[
            jax.ShapeDtypeStruct((total, 3 * cols), bf16),
            jax.ShapeDtypeStruct((total, cols), f32),
            jax.ShapeDtypeStruct((total, cols), bf16),
            jax.ShapeDtypeStruct((total, cols), f32),
        ],
        in_specs=[VMEM] * 8,
        out_specs=[VMEM] * 4,
        compiler_params=pltpu.CompilerParams(vmem_limit_bytes=24 * 2**20),
        cost_estimate=pl.CostEstimate(
            flops=2 * 10**9, bytes_accessed=20 * 2**20, transcendentals=2 * 10**6
        ),
        name="attend",
    )(projected, scales, gains, cosine, sine_part, first, last, places)


def attend_back(
    output_grad, low, attended, top, projected, scales, gains, cosine, sine_part, first, last, places
):
    total, cols = output_grad.shape
    head_dim = cosine.shape[1]
    heads = cols // head_dim
    size = math.gcd(total, 256)
    score_scale = head_dim ** (-0.5)
    f32, bf16 = jnp.float32, jnp.bfloat16
    contract_rows = (((0,), (0,)), ((), ()))
    starts, run = stored_runs(total)

    def kernel(
        grad_ref,
        low_ref,
        attended_ref,
        top_ref,
        lin_ref,
        scales_ref,
        gains_ref,
        cos_ref,
        sin_ref,
        first_ref,
        last_ref,
        places_ref,
        back_ref,
        value_ref,
        gain_ref,
        sums_ref,
        query_grad,
        key_grad,
        value_grad,
        grads_moved,
    ):
        for place, start in enumerate(starts):
            grads_moved[pl.ds(place * run, run), :] = grad_ref[pl.ds(start, run), :]

        def stored(values):
            pieces = sorted((start, place) for place, start in enumerate(starts))
            return jnp.concatenate([values[p * run : (p + 1) * run] for _, p in pieces], axis=0)

        totals = [jnp.zeros((total, 1), f32) for _ in range(2)]
        for h in range(heads):
            head = pl.ds(h * head_dim, head_dim)
            key_grad[...] = jnp.zeros_like(key_grad)
            value_grad[...] = jnp.zeros_like(value_grad)
            for b in range(total // size):
                span, seen = pl.ds(b * size, size), pl.ds(0, (b + 1) * size)
                queries, grads = low_ref[span, head], grads_moved[span, head]
                keys = low_ref[seen, pl.ds(cols + h * head_dim, head_dim)]
                scores = lax.dot_general(
                    queries, keys, (((1,), (1,)), ((), ())), preferred_element_type=f32
                )
                allowed = allowed_keys(first_ref, last_ref, span, places_ref[:, seen])
                scores = jnp.where(allowed, scores * score_scale, MASKED)
                probs = jnp.exp(scores - top_ref[span, head][:, :1])
                prob_grad = lax.dot_general(
                    grads,
                    low_ref[seen, pl.ds(2 * cols + h * head_dim, head_dim)],
                    (((1,), (1,)), ((), ())),
                    preferred_element_type=f32,
                )
                delta = jnp.sum(
                    grads.astype(f32) * attended_ref[span, head], axis=1, keepdims=True
                )
                score_grad = (probs * (prob_grad - delta)).astype(bf16)
                query_grad[span, :] = (
                    jnp.dot(score_grad, keys, preferred_element_type=f32) * score_scale
                )
                key_grad[seen, :] += lax.dot_general(
                    score_grad, queries, contract_rows, preferred_element_type=f32
                )
                value_grad[seen, :] += lax.dot_general(
                    probs.astype(bf16), grads, contract_rows, preferred_element_type=f32
                )
            value_ref[:, head] = stored(value_grad[...].astype(bf16))
            for kind, grad in ((0, query_grad[...]), (1, key_grad[...] * score_scale)):
                grad = stored(grad)
                span = pl.ds(kind * cols + h * head_dim, head_dim)
                unit = lin_ref[:, span] * scales_ref[:, kind : kind + 1]
                grad = grad * cos_ref[...] - roll_half(grad) * sin_ref[...]
                gain_ref[kind, :, head] = jnp.sum(grad * unit, axis=0, keepdims=True)
                grad = grad * gains_ref[:, span]
                back_ref[kind, :, head] = grad
                totals[kind] = totals[kind] + jnp.sum(grad * unit, axis=1, keepdims=True)
        for kind in range(2):
            sums_ref[:, kind : kind + 1] = totals[kind]

    return pl.pallas_call(
        kernel,
        out_shape=[
            jax.ShapeDtypeStruct((2, total, cols), f32),
            jax.ShapeDtypeStruct((total, cols), bf16),
            jax.ShapeDtypeStruct((2, 1, cols), f32),
            jax.ShapeDtypeStruct((total, 2), f32),
        ],
        in_specs=[VMEM] * 12,
        out_specs=[VMEM] * 4,
        scratch_shapes=[pltpu.VMEM((total, head_dim), f32)] * 3 + [pltpu.VMEM((total, cols), bf16)],
        compiler_params=pltpu.CompilerParams(vmem_limit_bytes=60 * 2**20),
        cost_estimate=pl.CostEstimate(flops=0, bytes_accessed=2**20, transcendentals=0),
        name="attend_back",
    )(
        output_grad,
        low,
        attended,
        top,
        projected,
        scales,
        gains,
        cosine,
        sine_part,
        first,
        last,
        places,
    )


def flipped(index, bit):
    return index + bit * (1 - 2 * lax.rem(index // bit, 2))


def flipped_by(index, flip):
    for bit in (1, 2, 4):
        index = flipped(index, bit) if flip & bit else index
    return index


def add_into(target, *sources):
    step = target.shape[0] if len(target.shape) == 3 else target.shape[0] // 64

    def body(i, carry):
        span = i if len(target.shape) == 3 else pl.ds(pl.multiple_of(i * 64, 64), 64)
        total = sources[0][span].astype(jnp.float32)
        for source in sources[1:]:
            total = total + source[span].astype(jnp.float32)
        target[span] = total.astype(target.dtype)
        return carry

    lax.fori_loop(0, step, body, 0)


def finish_sums(downs, ups, gate_far, gate_own, up_far, normed_part, out_part, qkv_part, small, tokens, mixed_grad, gain, mixed, moved, collective_id):
    ctx, fsdp = lax.axis_size("ctx"), lax.axis_size("fsdp")
    experts, units, cols = gate_far.shape
    kinds = 3
    rows, width = tokens.shape
    part = out_part.shape[0]
    f32, bf16 = jnp.float32, jnp.bfloat16
    small_rows, small_cols = small.shape[0], small.shape[1] // fsdp
    copies_most = 64

    def kernel(
        downs_ref,
        gate_near_ref,
        gate_high_ref,
        up_near_ref,
        up_high_ref,
        up_low_ref,
        gate_far_ref,
        gate_own_ref,
        up_far_ref,
        normed_ref,
        g_out_ref,
        g_qkv_ref,
        small_ref,
        tokens_ref,
        mixed_ref,
        gain_ref,
        forward_ref,
        moved_ref,
        down_ref,
        gate_ref,
        up_ref,
        input_ref,
        out_ref,
        qkv_ref,
        sums_ref,
        result_ref,
        kept,
        kept_low,
        kept_high,
        normed_own,
        normed_x,
        normed_low,
        normed_high,
        out_own,
        out_x,
        out_low,
        out_high,
        qkv_own,
        qkv_core,
        qkv_chip,
        qkv_sum,
        dealt,
        small_parts,
        small_sum,
        small_held,
        sends,
        recvs,
        locals_,
        deal_sems,
    ):
        me, mine = lax.axis_index("ctx"), lax.axis_index("fsdp")
        x, low, high = lax.rem(me, 2), lax.rem(me // 2, 2), me // 4
        to_x, to_low, to_high = ((flipped(me, bit), mine) for bit in (1, 2, 4))
        core, chip = flipped(mine, 1), flipped(mine, 2)
        diagonal = flipped(core, 2)
        ctx_peers = [(lax.rem(me + step, ctx), mine) for step in range(1, ctx)]
        near = [lax.rem(mine + step, fsdp) for step in range(1, fsdp)]
        greet(ctx_peers + [(me, other) for other in near])
        used, used_local, all_sends, loads = [0], [0], [], {}

        def push(source, target, peer):
            i = used[0]
            used[0] += 1
            copy = send(source, target, sends.at[i], recvs.at[i], peer)
            all_sends.append(copy)
            return copy

        def load(source, target):
            i = used_local[0]
            used_local[0] += 1
            copy = pltpu.make_async_copy(source, target, locals_.at[i])
            copy.start()
            return copy

        def normed_block(a, b, other):
            side = 1 - x if other else x
            block = (high + a - 2 * a * high) * 4 + (low + b - 2 * b * low) * 2 + side
            return normed_ref.at[pl.ds(pl.multiple_of(block * rows, rows), rows), :]

        def out_block(a, b, other):
            side = 1 - x if other else x
            block = (high + a - 2 * a * high) * 4 + (low + b - 2 * b * low) * 2 + side
            return g_out_ref.at[:, pl.ds(pl.multiple_of(block * cols, cols), cols)]

        def qkv_block(index):
            return g_qkv_ref.at[pl.ds(pl.multiple_of(index * part, part), part), :]

        def columns(index):
            return pl.ds(pl.multiple_of(index * small_cols, small_cols), small_cols)

        order = ((1, 1), (0, 1), (1, 0), (0, 0))
        small_copies = [
            push(small_ref.at[:, columns(other)], small_parts.at[i], (me, other))
            for i, other in enumerate(near)
        ]
        normed_copies = {
            ab: push(normed_block(*ab, True), normed_x.at[ab[0], ab[1]], to_x) for ab in order
        }

        low_copies = {
            (2, 0): push(up_low_ref, kept_low.at[2, 0], to_low),
            (0, 0): push(downs_ref.at[0], kept_low.at[0, 0], to_x),
        }
        early = {
            (1, 1): load(gate_far_ref, kept_low.at[1, 1]),
            (2, 1): load(up_far_ref, kept_low.at[2, 1]),
            (1, 0): load(gate_own_ref, kept_low.at[1, 0]),
        }
        kept_loads = {
            place: load(source, kept.at[place])
            for place, source in (
                ((1, 1), gate_high_ref),
                ((2, 1), up_high_ref),
                ((0, 0), downs_ref.at[1]),
                ((1, 0), gate_near_ref),
                ((2, 0), up_near_ref),
            )
        }
        qkv_copies = [
            push(qkv_block(diagonal), qkv_core.at[1], (me, core)),
            push(qkv_block(core), qkv_core.at[0], (me, core)),
        ]
        qkv_loads = [
            load(qkv_block(chip), qkv_own.at[1]),
            load(qkv_block(mine), qkv_own.at[0]),
        ]
        normed_loads = {
            ab: load(normed_block(*ab, False), normed_own.at[ab[0], ab[1]]) for ab in order
        }
        out_loads = {ab: load(out_block(*ab, False), out_own.at[ab[0], ab[1]]) for ab in order}

        total = small_ref[:, columns(mine)]
        for i, copy in enumerate(small_copies):
            copy.wait_recv()
            total = total + small_parts[i]
        small_sum[...] = total
        small_wide = [push(small_sum, small_held.at[i], peer) for i, peer in enumerate(ctx_peers)]

        qkv_copies[0].wait_recv()
        qkv_loads[0].wait()
        add_into(qkv_core.at[1], qkv_own.at[1], qkv_core.at[1])
        chip_copy = push(qkv_core.at[1], qkv_chip, (me, chip))

        def to_low_side(copies, loads, own, from_x, from_low, a):
            copies[a, 1].wait_recv()
            loads[a, 1].wait()
            add_into(from_x.at[a, 1], own.at[a, 1], from_x.at[a, 1])
            return push(from_x.at[a, 1], from_low.at[a], to_low)

        def to_high_side(copies, loads, lows, own, from_x, from_low, from_high):
            copies[1, 0].wait_recv()
            loads[1, 0].wait()
            lows[1].wait_recv()
            add_into(from_x.at[1, 0], own.at[1, 0], from_x.at[1, 0], from_low.at[1])
            return push(from_x.at[1, 0], from_high, to_high)

        def arrived(kind, a):
            if (kind, a) in early:
                early[kind, a].wait()
            else:
                low_copies[kind, a].wait_recv()

        def experts_high(kind):
            arrived(kind, 1)
            kept_loads[kind, 1].wait()
            add_into(kept_low.at[kind, 1], kept.at[kind, 1], kept_low.at[kind, 1])
            return push(kept_low.at[kind, 1], kept_high.at[kind], to_high)

        high_copies = {1: experts_high(1)}
        normed_args = (normed_copies, normed_loads)
        normed_lows = {1: to_low_side(*normed_args, normed_own, normed_x, normed_low, 1)}
        high_copies[2] = experts_high(2)
        normed_lows[0] = to_low_side(*normed_args, normed_own, normed_x, normed_low, 0)
        out_copies = {ab: push(out_block(*ab, True), out_x.at[ab[0], ab[1]], to_x) for ab in order}

        qkv_copies[1].wait_recv()
        qkv_loads[1].wait()
        chip_copy.wait_recv()
        add_into(qkv_sum, qkv_own.at[0], qkv_core.at[0], qkv_chip)

        def deal(kind):
            index = kind * ctx + me
            return pltpu.make_async_remote_copy(
                qkv_sum.at[:, pl.ds(kind * cols, cols)],
                dealt.at[lax.rem(index, kinds)],
                deal_sems.at[0, kind],
                deal_sems.at[1, lax.rem(index, kinds)],
                device_id=(index // kinds, mine),
                device_id_type=MESH,
            )

        def keep(kind):
            return pltpu.make_async_copy(
                qkv_sum.at[:, pl.ds(kind * cols, cols)],
                dealt.at[lax.rem(kind * ctx + me, kinds)],
                deal_sems.at[0, kind],
            )

        def is_far(kind):
            return (kind * ctx + me) // kinds != me

        for kind in range(kinds):
            pl.when(is_far(kind))(deal(kind).start)
            pl.when(jnp.logical_not(is_far(kind)))(keep(kind).start)

        normed_high_copy = to_high_side(
            *normed_args, normed_lows, normed_own, normed_x, normed_low, normed_high
        )
        out_args = (out_copies, out_loads)
        out_lows = {a: to_low_side(*out_args, out_own, out_x, out_low, a) for a in (1, 0)}

        def experts_end(kind):
            arrived(kind, 0)
            kept_loads[kind, 0].wait()
            sources = [kept.at[kind, 0], kept_low.at[kind, 0]]
            if kind > 0:
                high_copies[kind].wait_recv()
                sources.append(kept_high.at[kind])
            add_into((down_ref, gate_ref, up_ref)[kind], *sources)

        experts_end(0)

        normed_copies[0, 0].wait_recv()
        normed_loads[0, 0].wait()
        normed_lows[0].wait_recv()
        normed_high_copy.wait_recv()

        def norm_step(i, carry):
            span = pl.ds(pl.multiple_of(i * 16, 16), 16)
            grad = (
                normed_own[0, 0, span, :].astype(f32)
                + normed_x[0, 0, span, :].astype(f32)
                + normed_low[0, span, :].astype(f32)
                + normed_high[span, :].astype(f32)
            )
            values = tokens_ref[span, :].astype(f32)
            scale = rms_unit(values)
            unit = values * scale
            pulled = grad * gain_ref[...]
            input_ref[span, :] = mixed_ref[span, :] + scale * (
                pulled - unit * jnp.mean(unit * pulled, axis=-1, keepdims=True)
            )
            result_ref[span, :] = (forward_ref[span, :] + moved_ref[span, :].astype(f32)).astype(bf16)
            return carry

        lax.fori_loop(0, rows // 16, norm_step, 0)

        out_high_copy = to_high_side(*out_args, out_lows, out_own, out_x, out_low, out_high)
        experts_end(1)

        total = small_sum[...]
        for i, copy in enumerate(small_wide):
            copy.wait_recv()
            total = total + small_held[i]
        sums_ref[...] = total

        for kind in range(kinds):
            pl.when(is_far(kind))(deal(kind).wait_send)
            pl.when(jnp.logical_not(is_far(kind)))(keep(kind).wait)
        for slot in range(kinds):

            @pl.when(lax.rem(me * kinds + slot, ctx) != me)
            def _():
                pltpu.make_async_copy(
                    dealt.at[slot], dealt.at[slot], deal_sems.at[1, slot]
                ).wait()

            add_into(qkv_ref.at[:, pl.ds(slot * cols, cols)], dealt.at[slot])

        out_copies[0, 0].wait_recv()
        out_loads[0, 0].wait()
        out_lows[0].wait_recv()
        out_high_copy.wait_recv()
        add_into(out_ref, out_own.at[0, 0], out_x.at[0, 0], out_low.at[0], out_high)
        experts_end(2)
        for copy in all_sends:
            copy.wait_send()

    def block(*shape):
        return pltpu.VMEM(shape, bf16)

    gradient = (experts, units, cols)
    return comm_call(
        kernel,
        "finish_sums",
        collective_id,
        [
            jax.ShapeDtypeStruct(gradient, f32),
            jax.ShapeDtypeStruct(gradient, f32),
            jax.ShapeDtypeStruct(gradient, f32),
            jax.ShapeDtypeStruct((rows, width), f32),
            jax.ShapeDtypeStruct((part, cols), f32),
            jax.ShapeDtypeStruct((part, kinds * cols), f32),
            jax.ShapeDtypeStruct((small_rows, small_cols), f32),
            jax.ShapeDtypeStruct((rows, width), bf16),
        ],
        [ANY] * 12 + [VMEM] * 6,
        [VMEM] * 8,
        [
            block(kinds, 2, *gradient),
            block(kinds, 2, *gradient),
            block(kinds, *gradient),
            block(2, 2, rows, width),
            block(2, 2, rows, width),
            block(2, rows, width),
            block(rows, width),
            block(2, 2, part, cols),
            block(2, 2, part, cols),
            block(2, part, cols),
            block(part, cols),
            block(2, part, kinds * cols),
            block(2, part, kinds * cols),
            block(part, kinds * cols),
            block(part, kinds * cols),
            block(kinds, part, cols),
            pltpu.VMEM((fsdp - 1, small_rows, small_cols), f32),
            pltpu.VMEM((small_rows, small_cols), f32),
            pltpu.VMEM((ctx - 1, small_rows, small_cols), f32),
            DMA((copies_most,)),
            DMA((copies_most,)),
            DMA((32,)),
            DMA((2, kinds)),
        ],
        700 * 2**20,
        56,
    )(
        downs,
        *ups,
        gate_far,
        gate_own,
        up_far,
        normed_part,
        out_part,
        qkv_part,
        small,
        tokens,
        mixed_grad,
        gain,
        mixed,
        moved,
    )


def gather_inputs(tokens, w_qkv, dy, row_arrays, block, flips, collective_id):
    ctx, fsdp = lax.axis_size("ctx"), lax.axis_size("fsdp")
    rows, width = tokens.shape
    part = w_qkv.shape[0]
    kinds = 3
    cols = width // ctx
    line = ctx // 2
    chunks = 2
    size = rows // chunks
    row_count, flip_count = len(row_arrays), len(flips)
    small_count = row_count + 1

    def kernel(*refs):
        tokens_ref, w_qkv_ref, dy_ref = refs[:3]
        small_refs = refs[3 : 3 + small_count]
        all_ref, weight_ref, dy_all_ref = refs[3 + small_count : 6 + small_count]
        small_all_refs = refs[6 + small_count : 6 + 2 * small_count]
        refs = refs[6 + 2 * small_count :]
        run_kernel(
            tokens_ref,
            w_qkv_ref,
            dy_ref,
            small_refs,
            all_ref,
            weight_ref,
            dy_all_ref,
            small_all_refs,
            *refs,
        )

    def run_kernel(
        tokens_ref,
        w_qkv_ref,
        dy_ref,
        small_refs,
        all_ref,
        weight_ref,
        dy_all_ref,
        small_all_refs,
        *refs,
    ):
        flip_refs, dy_line_ref, refs = refs[:flip_count], refs[flip_count], refs[flip_count + 1 :]
        stage, weight_stage, dy_stage, sends, recvs, line_send, line_recv, cross_send, cross_recv, *refs = refs
        local_sems, line_out, cross_out = refs
        me, mine = lax.axis_index("ctx"), lax.axis_index("fsdp")
        z, x = me // 2, lax.rem(me, 2)
        to_x = (flipped(me, 1), mine)
        core, chip = (me, flipped(mine, 1)), (me, flipped(mine, 2))
        others = [flipped_by(me, flip) for flip in flips]
        greet(
            [(lax.rem(me + step, ctx), mine) for step in range(1, ctx)]
            + [(me, lax.rem(mine + step, fsdp)) for step in range(1, fsdp)]
            + [(other, lax.rem(mine + step, fsdp)) for other in others for step in range(1, fsdp)]
        )
        used, used_local, started, kept = [0], [0], [], []

        def push(source, target, peer):
            i = used[0]
            used[0] += 1
            copy = send(source, target, sends.at[i], recvs.at[i], peer)
            started.append(copy)
            return copy

        def load(source, target):
            i = used_local[0]
            used_local[0] += 1
            copy = pltpu.make_async_copy(source, target, local_sems.at[i])
            copy.start()
            kept.append(copy)

        def token_block(index):
            return all_ref.at[pl.ds(pl.multiple_of(index * rows, rows), rows), :]

        def token_chunk(index, chunk):
            start = pl.multiple_of(index * rows + chunk * size, size)
            return stage.at[pl.ds(start, size), :]

        def put(away, side, chunk, crossed):
            index = 2 * (z - away if side == 0 else z + away) + (1 - x if crossed else x)
            start = pl.multiple_of(index * rows + chunk * size, size)
            return pltpu.make_async_copy(
                stage.at[pl.ds(start, size), :],
                all_ref.at[pl.ds(start, size), :],
                (cross_out if crossed else line_out).at[side * line + away, chunk],
            )

        def taken(own, index, chunk):
            return tokens_ref.at[pl.ds(chunk * size, size), :] if own else token_chunk(index, chunk)

        def by_part(ref, index, count):
            return ref.at[pl.ds(pl.multiple_of(index * count, count), count), :]

        def cross(away, side, chunk):
            index = 2 * (z - away if side == 0 else z + away) + x
            i = side * line + away
            return pltpu.make_async_remote_copy(
                taken(away == 0, index, chunk),
                token_chunk(index, chunk),
                cross_send.at[i, chunk],
                cross_recv.at[i, chunk],
                device_id=to_x,
                device_id_type=MESH,
            )

        def along(away, side, chunk):
            index = 2 * (z - away if side == 0 else z + away) + x
            i = side * line + away
            return pltpu.make_async_remote_copy(
                taken(away == 0, index, chunk),
                token_chunk(index, chunk),
                line_send.at[i, chunk],
                line_recv.at[i, chunk],
                device_id=(me + 2 if side == 0 else me - 2, mine),
                device_id_type=MESH,
            )

        def has(away, side):
            return z >= away if side == 0 else z + away < line

        def goes_on(away, side):
            return jnp.logical_and(has(away, side), z < line - 1 if side == 0 else z > 0)

        for chunk in range(chunks):
            for side in range(2):
                pl.when(goes_on(0, side))(along(0, side, chunk).start)
            cross(0, 0, chunk).start()
        load(tokens_ref, token_block(me))

        own_weight = by_part(weight_stage, mine, part)
        pieces = []
        for kind in range(kinds):
            column = pl.ds(pl.multiple_of(kind * width + me * cols, cols), cols)
            target = own_weight.at[:, pl.ds(kind * cols, cols)]
            pieces.append(
                pltpu.make_async_copy(w_qkv_ref.at[:, column], target, local_sems.at[23 - kind])
            )
            pieces[-1].start()
        load(dy_ref, dy_stage)
        dy_loaded = kept.pop()
        for piece in pieces:
            piece.wait()
        weight_chip = [push(own_weight, own_weight, chip)]
        weight_core = [push(own_weight, own_weight, core)]
        load(own_weight, by_part(weight_ref, mine, part))
        columns = pl.ds(pl.multiple_of(mine * part, part), part)
        for i, (source, target) in enumerate(zip(small_refs, small_all_refs)):
            if i < row_count:
                target = target.at[:, columns]
            else:
                target = target.at[mine]
            for step in range(1, fsdp):
                push(source, target, (me, lax.rem(mine + step, fsdp)))
            load(source, target)
        dy_chip = push(dy_ref, by_part(dy_all_ref, mine, rows), chip)
        push(dy_ref, by_part(dy_all_ref, mine, rows), core)
        load(dy_ref, by_part(dy_all_ref, mine, rows))

        for away in range(1, line):
            for chunk in range(chunks):
                for side in range(2):

                    @pl.when(has(away, side))
                    def _():
                        index = 2 * (z - away if side == 0 else z + away) + x
                        pltpu.make_async_copy(
                            taken(True, index, chunk),
                            token_chunk(index, chunk),
                            line_recv.at[side * line + away - 1, chunk],
                        ).wait()
                        cross(away, side, chunk).start()
                        put(away, side, chunk, False).start()

                    if away < line - 1:
                        pl.when(goes_on(away, side))(along(away, side, chunk).start)
        for other, target in zip(others, flip_refs):
            for step in range(fsdp):
                push(small_refs[-1], target.at[mine], (other, lax.rem(mine + step, fsdp)))
        dy_loaded.wait()
        for i in range(line):
            wide = 2 * cols
            to = flipped_by(me, 2 * i)
            source = dy_stage.at[:, pl.ds(pl.multiple_of(to // 2 * wide, wide), wide)]
            if i == 0:
                load(source, dy_line_ref.at[0])
            else:
                push(source, dy_line_ref.at[i], (to, mine))

        for copy in weight_chip:
            copy.wait_recv()
        far = by_part(weight_stage, flipped(mine, 2), part)
        weight_far = push(far, far, core)
        load(far, by_part(weight_ref, flipped(mine, 2), part))
        for copy in weight_core:
            copy.wait_recv()
        near = flipped(mine, 1)
        load(by_part(weight_stage, near, part), by_part(weight_ref, near, part))
        dy_chip.wait_recv()
        far = by_part(dy_all_ref, flipped(mine, 2), rows)
        push(far, far, core)
        every = [(side, chunk) for side in range(2) for chunk in range(chunks)]
        weight_far.wait_recv()
        far = flipped_by(mine, 3)
        load(by_part(weight_stage, far, part), by_part(weight_ref, far, part))
        for chunk in range(chunks):
            cross(0, 0, chunk).wait_recv()
            put(0, 0, chunk, True).start()
        for away in range(1, line):
            for side, chunk in every:

                @pl.when(has(away, side))
                def _():
                    cross(away, side, chunk).wait_recv()
                    put(away, side, chunk, True).start()

        for copy in started:
            if not any(copy is other for other in [dy_chip, weight_far] + weight_chip + weight_core):
                copy.wait_recv()
        for copy in kept:
            copy.wait()
        for copy in started:
            copy.wait_send()
        for chunk in range(chunks):
            cross(0, 0, chunk).wait_send()
        for chunk in range(chunks):
            put(0, 0, chunk, True).wait()
        for away in range(1, line):
            for side, chunk in every:

                @pl.when(has(away, side))
                def _():
                    put(away, side, chunk, False).wait()
                    put(away, side, chunk, True).wait()

        for away in range(line - 1):
            for side, chunk in every:
                pl.when(goes_on(away, side))(along(away, side, chunk).wait_send)
        for away in range(1, line):
            for side, chunk in every:
                pl.when(has(away, side))(cross(away, side, chunk).wait_send)

    return comm_call(
        kernel,
        "gather_inputs",
        collective_id,
        [
            jax.ShapeDtypeStruct((ctx * rows, width), tokens.dtype),
            jax.ShapeDtypeStruct((fsdp * part, kinds * cols), w_qkv.dtype),
            jax.ShapeDtypeStruct((fsdp * rows, width), dy.dtype),
        ]
        + [jax.ShapeDtypeStruct((row.shape[0], fsdp * part), row.dtype) for row in row_arrays]
        + [jax.ShapeDtypeStruct((fsdp,) + block.shape, block.dtype)] * (1 + flip_count)
        + [jax.ShapeDtypeStruct((line, rows, 2 * cols), dy.dtype)],
        [ANY] * (3 + small_count),
        [ANY] * (4 + small_count + flip_count),
        [
            pltpu.VMEM((ctx * rows, width), tokens.dtype),
            pltpu.VMEM((fsdp * part, kinds * cols), w_qkv.dtype),
            pltpu.VMEM((rows, width), dy.dtype),
            DMA((64,)),
            DMA((64,)),
            DMA((2 * line, chunks)),
            DMA((2 * line, chunks)),
            DMA((2 * line, chunks)),
            DMA((2 * line, chunks)),
            DMA((24,)),
            DMA((2 * line, chunks)),
            DMA((2 * line, chunks)),
        ],
        150 * 2**20,
        60,
    )(tokens, w_qkv, dy, *row_arrays, block)


def project(tokens, gain, weight):
    total, width = tokens.shape
    wide = weight.shape[1]
    cols = wide // 3
    size = math.gcd(total, 256)
    f32 = jnp.float32

    def kernel(tokens_ref, gain_ref, weight_ref, normed_ref, lin_ref, squares_ref):
        values = tokens_ref[...].astype(f32)
        normed = (values * rms_unit(values) * gain_ref[...]).astype(jnp.bfloat16)
        normed_ref[...] = normed
        lin = jnp.dot(normed, weight_ref[...], preferred_element_type=f32)
        lin_ref[...] = lin
        for kind in range(2):
            piece = lin[:, kind * cols : (kind + 1) * cols]
            squares_ref[:, kind : kind + 1] = jnp.sum(piece * piece, axis=1, keepdims=True)

    def by_rows(columns):
        return pl.BlockSpec((size, columns), lambda i: (i, 0))

    return pl.pallas_call(
        kernel,
        grid=(total // size,),
        out_shape=[
            jax.ShapeDtypeStruct((total, width), jnp.bfloat16),
            jax.ShapeDtypeStruct((total, wide), f32),
            jax.ShapeDtypeStruct((total, 2), f32),
        ],
        in_specs=[
            by_rows(width),
            pl.BlockSpec((1, width), lambda i: (0, 0)),
            pl.BlockSpec((width, wide), lambda i: (0, 0)),
        ],
        out_specs=[by_rows(width), by_rows(wide), by_rows(2)],
        compiler_params=pltpu.CompilerParams(vmem_limit_bytes=60 * 2**20),
        cost_estimate=pl.CostEstimate(
            flops=3 * 10**9, bytes_accessed=15 * 2**20, transcendentals=0
        ),
        name="project",
    )(tokens, gain, weight)


def project_back(back, projected, scales, inner_sums, value_grad, weight, normed, tokens):
    total, width = tokens.shape
    wide = weight.shape[1]
    cols = wide // 3
    size = math.gcd(total, 256)
    steps, runs = total // size, 4
    f32, bf16 = jnp.float32, jnp.bfloat16

    def kernel(
        back_ref,
        lin_ref,
        scales_ref,
        sums_ref,
        value_ref,
        weight_ref,
        normed_ref,
        tokens_ref,
        part_ref,
        g_qkv_ref,
        gain_ref,
        proj,
    ):
        i = pl.program_id(0)

        @pl.when(i == 0)
        def _():
            gain_ref[...] = jnp.zeros_like(gain_ref)

        @pl.when(i < steps)
        def _():
            pieces = []
            for kind in range(2):
                scale = scales_ref[:, kind : kind + 1]
                unit = lin_ref[:, kind * cols : (kind + 1) * cols] * scale
                grad = scale * (back_ref[kind] - unit * sums_ref[:, kind : kind + 1])
                pieces.append(grad.astype(bf16))
            grads = jnp.concatenate(pieces + [value_ref[...]], axis=1)
            proj[pl.ds(pl.multiple_of(i * size, size), size), :] = grads
            part = lax.dot_general(
                grads, weight_ref[...], (((1,), (1,)), ((), ())), preferred_element_type=f32
            )
            values = tokens_ref[...].astype(f32)
            gain_ref[...] += jnp.sum(part * (values * rms_unit(values)), axis=0, keepdims=True)
            part_ref[...] = part.astype(bf16)

        @pl.when(i >= steps)
        def _():
            g_qkv_ref[...] = lax.dot_general(
                normed_ref[...], proj[...], (((0,), (0,)), ((), ())), preferred_element_type=f32
            ).astype(bf16)

    def by_rows(columns):
        return pl.BlockSpec((size, columns), lambda i: (jnp.minimum(i, steps - 1), 0))

    def later(i):
        return jnp.maximum(i - steps, 0)

    return pl.pallas_call(
        kernel,
        grid=(steps + runs,),
        out_shape=[
            jax.ShapeDtypeStruct((total, width), bf16),
            jax.ShapeDtypeStruct((width, wide), bf16),
            jax.ShapeDtypeStruct((1, width), f32),
        ],
        in_specs=[
            pl.BlockSpec((2, size, cols), lambda i: (0, jnp.minimum(i, steps - 1), 0)),
            by_rows(2 * cols),
            by_rows(2),
            by_rows(2),
            by_rows(cols),
            pl.BlockSpec((width, wide), lambda i: (0, 0)),
            pl.BlockSpec((total, width // runs), lambda i: (0, later(i))),
            by_rows(width),
        ],
        out_specs=[
            by_rows(width),
            pl.BlockSpec((width // runs, wide), lambda i: (later(i), 0)),
            pl.BlockSpec((1, width), lambda i: (0, 0)),
        ],
        scratch_shapes=[pltpu.VMEM((total, wide), bf16)],
        compiler_params=pltpu.CompilerParams(vmem_limit_bytes=60 * 2**20),
        cost_estimate=pl.CostEstimate(flops=0, bytes_accessed=2**20, transcendentals=0),
        name="project_back",
    )(back, projected, scales, inner_sums, value_grad, weight, normed, tokens)


def on_device_heads(
    tokens,
    doc_lengths,
    routes,
    slot_order,
    attn_gain,
    w_qkv,
    q_gain,
    k_gain,
    w_out,
    ffn_gain,
    w_router,
    w_gate,
    w_up,
    w_down,
    cotangent,
):
    rows, width = tokens.shape[1], tokens.shape[2]
    ctx, fsdp = lax.axis_size("ctx"), lax.axis_size("fsdp")
    me = lax.axis_index("ctx")
    head_dim = width // HEADS
    cols = HEADS // ctx * head_dim
    part = width // fsdp
    total = rows * ctx
    lengths = doc_lengths[0]
    bf16, f32 = jnp.bfloat16, jnp.float32

    experts, top = w_gate.shape[0], routes.shape[2]
    gains = jnp.concatenate([attn_gain, q_gain, k_gain, ffn_gain]).reshape(4, part)
    router_rows = jnp.pad(w_router.T, ((0, ROUTER_ROWS - experts), (0, 0)))
    pairs = jnp.concatenate([routes[0].T, slot_order[0].T], axis=0)
    pairs = jnp.pad(pairs, ((0, -pairs.shape[0] % 8), (0, 0)))
    tokens_all, qkv_weight, dy_all, gains, router_rows, *slots, dy_parts = gather_inputs(
        tokens[0],
        w_qkv,
        cotangent[0],
        [gains, router_rows],
        slots_of(pairs, experts, top),
        [1, 2, 4, 6],
        9,
    )
    row_gain_one, gain_query, gain_key, row_gain_two = (
        gains[i : i + 1].astype(f32) for i in range(4)
    )
    flips = [0, 2, 4, 6]
    dy_parts = lax.all_gather(dy_parts, "fsdp", axis=0)

    stream_pos = dealt_position(jnp.arange(total, dtype=jnp.int32), rows, ctx)
    stream_inner = document_info(stream_pos, lengths)[1]
    cosine, sine_part = rope_tables(stream_inner, head_dim)
    turn_tables = (
        jnp.concatenate([cosine, cosine], axis=1),
        jnp.concatenate([-sine_part, sine_part], axis=1),
    )
    places = jnp.arange(total, dtype=jnp.int32)
    sight = (
        (places - document_info(places, lengths)[1]).reshape(total, 1),
        places.reshape(total, 1),
        places.reshape(1, total),
    )
    normed_all, projected, squares = project(tokens_all, row_gain_one, qkv_weight)
    squares = squares.T
    squares = ctx_sum(squares.reshape(-1, 128), 1).reshape(2, total)
    scales = lax.rsqrt(squares / width + EPSILON).T
    own_gains = [
        lax.dynamic_slice_in_dim(gain, me * cols, cols, 1) for gain in (gain_query, gain_key)
    ]
    own_gains = jnp.concatenate(own_gains, axis=1)
    low, attended, attended_low, tops = attend(
        projected, scales, own_gains, *turn_tables, *sight, cols
    )

    attended_part = heads_to_rows(attended_low, 2)
    mixed_part = dot32("td,de->te", attended_part, w_out).astype(bf16)
    inputs = tokens[0].astype(f32)
    group, mixed, crossed = reduce_then_gather(
        mixed_part,
        [tokens[0], row_gain_two],
        [jax.ShapeDtypeStruct((rows, width), f32)],
        norm_chunk,
        "mix_and_norm",
        6,
        True,
        [],
        16,
    )

    capacity = rows * top // experts
    slot_by_expert, slots_other, *slots_line = slots
    moved_part, group_grad, g_router, scaled, gate_low, up_low = run_experts(
        group, dy_all, slot_by_expert, router_rows, w_gate, w_up, w_down, fsdp, capacity
    )
    scaled_line = [scaled] + [swap(scaled, flip) for flip in flips[1:]]
    mixed_all, mixed_grad, g_ffn_gain, gate_other, up_other = reduce_then_gather(
        group_grad,
        [mixed, row_gain_two, cotangent[0]],
        [jax.ShapeDtypeStruct((rows, width), f32), jax.ShapeDtypeStruct((1, width), f32)],
        norm_back_chunk,
        "norm_back",
        7,
        False,
        [gate_low, up_low],
        60,
    )
    g_ffn_gain = g_ffn_gain[0]
    crossed = lax.all_gather(crossed, "fsdp", axis=0, tiled=True)
    ups = expert_grads(
        [gate_low, up_low], [gate_other, up_other], group, crossed, slot_by_expert, slots_other, capacity
    )
    ups, mixed_all = lax.optimization_barrier((ups, mixed_all))
    output_part = dot32("te,de->td", mixed_all, w_out).astype(bf16)
    output_grad = rows_to_heads(output_part, 3)
    output_grad, moved_part, ups, mixed_all, scaled_line = lax.optimization_barrier(
        (output_grad, moved_part, ups, mixed_all, scaled_line)
    )
    moved = lax.psum_scatter(moved_part, "fsdp", scatter_dimension=0, tiled=True)
    gate_far, gate_own = swap(ups[3], 2), swap(ups[2], 2)
    downs = down_grads(scaled_line, dy_parts, [slot_by_expert] + slots_line, capacity)
    g_out = dot32("td,te->de", attended_part, mixed_all).astype(bf16)
    output_grad, ups, downs, g_out = lax.optimization_barrier((output_grad, ups, downs, g_out))

    back, value_grad, own_g_gains, inner_sums = attend_back(
        output_grad, low, attended, tops, projected, scales, own_gains, *turn_tables, *sight
    )
    inner_sums, gate_far, gate_own = lax.optimization_barrier((inner_sums, gate_far, gate_own))
    inner_sums = ctx_sum(inner_sums.T.reshape(-1, 128), 1)
    inner_sums, ups = lax.optimization_barrier((inner_sums, ups))
    up_far = swap(ups[7], 2)
    inner_sums = inner_sums.reshape(2, total).T / width

    normed_grad_part, g_qkv, g_attn_gain = project_back(
        back, projected, scales, inner_sums, value_grad, qkv_weight, normed_all, tokens_all
    )
    g_attn_gain = g_attn_gain[0]

    def placed_cols(values):
        return lax.dynamic_update_slice_in_dim(jnp.zeros((width,), f32), values, me * cols, 0)

    sums = jnp.concatenate(
        [
            jnp.stack([g_attn_gain, placed_cols(own_g_gains[0, 0]), placed_cols(own_g_gains[1, 0]), g_ffn_gain]),
            g_router[:experts],
        ],
        axis=0,
    )
    down_parts, gate_parts, up_parts, input_grad, out_part, qkv_part, sums, activations = finish_sums(
        downs,
        ups[0:2] + ups[4:7],
        gate_far,
        gate_own,
        up_far,
        normed_grad_part,
        g_out,
        g_qkv,
        jnp.pad(sums, ((0, -sums.shape[0] % 8), (0, 0))),
        tokens[0],
        mixed_grad,
        row_gain_one,
        mixed,
        moved,
        8,
    )
    return (
        activations[None],
        input_grad[None],
        sums[0],
        qkv_part,
        sums[1],
        sums[2],
        out_part,
        sums[3],
        sums[4 : 4 + experts].T,
        gate_parts,
        up_parts,
        down_parts,
    )


def solution(mesh):
    in_specs = (
        P("fsdp", "ctx", None),
        P("fsdp", None),
        P("fsdp", "ctx", None),
        P("fsdp", "ctx", None),
        P("fsdp"),
        P("fsdp", None),
        P("fsdp"),
        P("fsdp"),
        P("fsdp", None),
        P("fsdp"),
        P("fsdp", None),
        P(None, None, "fsdp"),
        P(None, None, "fsdp"),
        P(None, "fsdp", None),
        P("fsdp", "ctx", None),
    )
    out_specs = (
        P("fsdp", "ctx", None),
        P("fsdp", "ctx", None),
        P("fsdp"),
        P("fsdp", "ctx"),
        P("fsdp"),
        P("fsdp"),
        P("fsdp", "ctx"),
        P("fsdp"),
        P("fsdp", None),
        P(None, "ctx", "fsdp"),
        P(None, "ctx", "fsdp"),
        P(None, "fsdp", "ctx"),
    )
    ctx, fsdp = mesh.shape["ctx"], mesh.shape["fsdp"]
    by_heads = HEADS % ctx == 0 and ctx == 8 and fsdp == 4
    body = on_device_heads if by_heads else on_device
    return jax.shard_map(
        body, mesh=mesh, in_specs=in_specs, out_specs=out_specs, check_vma=False
    )
```

```python
import math

import jax
import jax.numpy as jnp
from jax import lax
from jax.experimental import pallas as pl
from jax.experimental.pallas import tpu as pltpu
from jax.sharding import PartitionSpec as P

HEADS = 16
MESH = pl.DeviceIdType.MESH
ANY = pl.BlockSpec(memory_space=pl.ANY)
VMEM = pl.BlockSpec(memory_space=pltpu.VMEM)
DMA = pltpu.SemaphoreType.DMA

EPSILON = 1e-05
ROPE_BASE = 10000.0
MASKED = -1e30


def rms_scale(values, gain_vector):
    return (
        values
        * lax.rsqrt(jnp.mean(values * values, axis=-1, keepdims=True) + EPSILON)
        * gain_vector
    )


def rotate(values, inner_pos):
    half_dim = values.shape[-1] // 2
    freq_table = ROPE_BASE ** (-2.0 * jnp.arange(half_dim, dtype=jnp.float32) / values.shape[-1])
    angles = inner_pos.astype(jnp.float32)[:, None] * freq_table[None, :]
    cosine = jnp.cos(angles)[:, None, :]
    sine_part = jnp.sin(angles)[:, None, :]
    first_half = values[..., :half_dim]
    second_half = values[..., half_dim:]
    return jnp.concatenate(
        [
            first_half * cosine - second_half * sine_part,
            second_half * cosine + first_half * sine_part,
        ],
        axis=-1,
    )


def dealt_position(flat_index, per_device, device_count):
    device_index = flat_index // per_device
    within = flat_index % per_device
    half_rows = per_device // 2
    return jnp.where(
        within < half_rows,
        device_index * half_rows + within,
        (2 * device_count - 1 - device_index) * half_rows + within - half_rows,
    )


def document_info(positions, lengths):
    doc_ends = jnp.sum(jnp.where(jnp.arange(lengths.shape[0])[:, None] >= jnp.arange(lengths.shape[0])[None, :], lengths[None, :], 0), axis=1)
    passed = doc_ends[None, :] <= positions[:, None]
    doc_ids = jnp.sum(passed.astype(jnp.int32), axis=1)
    inner_pos = positions - jnp.sum(jnp.where(passed, lengths[None, :], 0), axis=1)
    return (doc_ids, inner_pos)


def slot_table(route_ids, order_ids, capacity, expert_count):
    pair_count = route_ids.shape[0] * route_ids.shape[1]
    expert_flat = route_ids.reshape(pair_count)
    rank_flat = order_ids.reshape(pair_count)
    earlier = (expert_flat[None, :] == expert_flat[:, None]) & (
        rank_flat[None, :] < rank_flat[:, None]
    )
    slot_index = jnp.sum(earlier.astype(jnp.int32), axis=1)
    placed = jnp.where(
        slot_index < capacity, expert_flat * capacity + slot_index, expert_count * capacity
    )
    source = (
        jnp.full((expert_count * capacity + 1,), pair_count, jnp.int32)
        .at[placed]
        .set(jnp.arange(pair_count, dtype=jnp.int32))
    )
    return (placed, source[: expert_count * capacity])


def masked_scores(query_block, key_block, query_pos, query_doc, key_pos, key_doc, score_scale):
    scores = (
        jnp.einsum("qhd,khd->hqk", query_block, key_block, preferred_element_type=jnp.float32)
        * score_scale
    )
    allowed = (query_doc[:, None] == key_doc[None, :]) & (key_pos[None, :] <= query_pos[:, None])
    return jnp.where(allowed[None], scores, MASKED)


def silu_parts(hidden_grad, slot_gate, slot_up):
    sigma = jax.nn.sigmoid(slot_gate)
    gate_grad_low = (hidden_grad * slot_up * sigma * (1.0 + slot_gate * (1.0 - sigma))).astype(
        jnp.bfloat16
    )
    up_grad_low = (hidden_grad * slot_gate * sigma).astype(jnp.bfloat16)
    return (gate_grad_low, up_grad_low)


def on_device(
    tokens,
    doc_lengths,
    routes,
    slot_order,
    attn_gain,
    w_qkv,
    q_gain,
    k_gain,
    w_out,
    ffn_gain,
    w_router,
    w_gate,
    w_up,
    w_down,
    cotangent,
):
    row_count = tokens.shape[1]
    model_width = tokens.shape[2]
    head_count = HEADS
    head_dim = model_width // head_count
    score_scale = head_dim ** (-0.5)
    ctx_count = lax.axis_size("ctx")
    ctx_index = lax.axis_index("ctx")
    total_rows = row_count * ctx_count
    lengths = doc_lengths[0]
    local_pos = dealt_position(
        ctx_index * row_count + jnp.arange(row_count, dtype=jnp.int32), row_count, ctx_count
    )
    local_doc, local_inner = document_info(local_pos, lengths)
    stream_pos = dealt_position(jnp.arange(total_rows, dtype=jnp.int32), row_count, ctx_count)
    stream_doc, stream_inner = document_info(stream_pos, lengths)
    block_rows = math.gcd(total_rows, 512)
    block_count = total_rows // block_rows
    block_ids = jnp.arange(block_count, dtype=jnp.int32)
    gain_one, qkv_weight, gain_query, gain_key, out_weight = (
        lax.all_gather(attn_gain, "fsdp", axis=0, tiled=True),
        lax.all_gather(w_qkv, "fsdp", axis=0, tiled=True),
        lax.all_gather(q_gain, "fsdp", axis=0, tiled=True),
        lax.all_gather(k_gain, "fsdp", axis=0, tiled=True),
        lax.all_gather(w_out, "fsdp", axis=0, tiled=True),
    )
    gain_two, router_weight, gate_weight, up_weight, down_weight = (
        lax.all_gather(ffn_gain, "fsdp", axis=0, tiled=True),
        lax.all_gather(w_router, "fsdp", axis=0, tiled=True),
        lax.all_gather(w_gate, "fsdp", axis=2, tiled=True),
        lax.all_gather(w_up, "fsdp", axis=2, tiled=True),
        lax.all_gather(w_down, "fsdp", axis=1, tiled=True),
    )
    inputs = tokens[0].astype(jnp.float32)
    normed_f, norm_one_pull = jax.vjp(rms_scale, inputs, gain_one.astype(jnp.float32))
    normed_low = normed_f.astype(jnp.bfloat16)
    projected = jnp.dot(normed_low, qkv_weight, preferred_element_type=jnp.float32)
    query_lin = projected[:, :model_width]
    key_lin = projected[:, model_width : 2 * model_width]
    value_low = (
        projected[:, 2 * model_width :]
        .astype(jnp.bfloat16)
        .reshape(row_count, head_count, head_dim)
    )

    def head_shape(values, gain_vector):
        return rotate(
            rms_scale(values, gain_vector).reshape(row_count, head_count, head_dim), local_inner
        )

    query_f, query_pull = jax.vjp(head_shape, query_lin, gain_query.astype(jnp.float32))
    key_f, key_pull = jax.vjp(head_shape, key_lin, gain_key.astype(jnp.float32))
    query_low = query_f.astype(jnp.bfloat16)
    key_low = key_f.astype(jnp.bfloat16)
    keys_all, values_all = (
        lax.all_gather(key_low, "ctx", axis=0, tiled=True),
        lax.all_gather(value_low, "ctx", axis=0, tiled=True),
    )

    def key_slice(block_index):
        first_row = block_index * block_rows
        return (
            lax.dynamic_slice_in_dim(keys_all, first_row, block_rows, 0),
            lax.dynamic_slice_in_dim(values_all, first_row, block_rows, 0),
            lax.dynamic_slice_in_dim(stream_pos, first_row, block_rows, 0),
            lax.dynamic_slice_in_dim(stream_doc, first_row, block_rows, 0),
        )

    def stats_step(carry, block_index):
        running_top, running_total = carry
        key_block, value_block, key_pos, key_doc = key_slice(block_index)
        scores = masked_scores(
            query_low, key_block, local_pos, local_doc, key_pos, key_doc, score_scale
        )
        new_top = jnp.maximum(running_top, jnp.max(scores, axis=-1))
        running_total = running_total * jnp.exp(running_top - new_top) + jnp.sum(
            jnp.exp(scores - new_top[..., None]), axis=-1
        )
        return ((new_top, running_total), None)

    start_stats = (
        jnp.full((head_count, row_count), MASKED, jnp.float32),
        jnp.zeros((head_count, row_count), jnp.float32),
    )
    (score_top, score_total), _ = lax.scan(stats_step, start_stats, block_ids)
    log_total = score_top + jnp.log(score_total)

    def output_step(accum, block_index):
        key_block, value_block, key_pos, key_doc = key_slice(block_index)
        scores = masked_scores(
            query_low, key_block, local_pos, local_doc, key_pos, key_doc, score_scale
        )
        prob_block = jnp.exp(scores - log_total[..., None]).astype(jnp.bfloat16)
        return (
            accum
            + jnp.einsum(
                "hqk,khd->qhd", prob_block, value_block, preferred_element_type=jnp.float32
            ),
            None,
        )

    attended_f, _ = lax.scan(
        output_step, jnp.zeros((row_count, head_count, head_dim), jnp.float32), block_ids
    )
    attended_low = attended_f.reshape(row_count, model_width).astype(jnp.bfloat16)
    mixed = inputs + jnp.dot(attended_low, out_weight, preferred_element_type=jnp.float32)
    normed_two_f, norm_two_pull = jax.vjp(rms_scale, mixed, gain_two.astype(jnp.float32))
    normed_two = normed_two_f.astype(jnp.bfloat16)
    expert_count = gate_weight.shape[0]
    route_ids = routes[0]
    top_count = route_ids.shape[1]
    pair_count = row_count * top_count
    capacity = pair_count // expert_count
    logits = jnp.dot(normed_two, router_weight, preferred_element_type=jnp.float32)
    router_probs = jax.nn.softmax(logits, axis=-1)
    chosen = (
        route_ids[:, :, None] == jnp.arange(expert_count, dtype=jnp.int32)[None, None, :]
    ).astype(jnp.float32)
    gate_values = jnp.sum(chosen * router_probs[:, None, :], axis=-1)
    placed, source = slot_table(route_ids, slot_order[0], capacity, expert_count)
    padded_in = jnp.concatenate([normed_two, jnp.zeros((1, model_width), jnp.bfloat16)], axis=0)
    expert_in = padded_in[source // top_count].reshape(expert_count, capacity, model_width)
    gate_pre = jnp.einsum(
        "ecd,edh->ech", expert_in, gate_weight, preferred_element_type=jnp.float32
    )
    up_pre = jnp.einsum("ecd,edh->ech", expert_in, up_weight, preferred_element_type=jnp.float32)
    hidden_low = (jax.nn.silu(gate_pre) * up_pre).astype(jnp.bfloat16)
    expert_out = jnp.einsum(
        "ech,ehd->ecd", hidden_low, down_weight, preferred_element_type=jnp.float32
    )
    out_padded = jnp.concatenate(
        [
            expert_out.reshape(expert_count * capacity, model_width),
            jnp.zeros((1, model_width), jnp.float32),
        ],
        axis=0,
    )
    per_pair = out_padded[placed].reshape(row_count, top_count, model_width)
    layer_out = mixed + jnp.sum(gate_values[:, :, None] * per_pair, axis=1)
    out_grad = cotangent[0].astype(jnp.float32)
    gate_grad = jnp.sum(out_grad[:, None, :] * per_pair, axis=-1)
    pair_grad = (gate_values[:, :, None] * out_grad[:, None, :]).reshape(pair_count, model_width)
    pair_padded = jnp.concatenate([pair_grad, jnp.zeros((1, model_width), jnp.float32)], axis=0)
    slot_grad = (
        pair_padded[source].reshape(expert_count, capacity, model_width).astype(jnp.bfloat16)
    )

    def expert_step(carry, pieces):
        slot_in, slot_hidden, slot_dy, slot_gate, slot_up, gate_matrix, up_matrix, down_matrix = (
            pieces
        )
        hidden_grad = jnp.einsum(
            "cd,hd->ch", slot_dy, down_matrix, preferred_element_type=jnp.float32
        )
        gate_grad_low, up_grad_low = silu_parts(hidden_grad, slot_gate, slot_up)
        in_grad = jnp.einsum(
            "ch,dh->cd", gate_grad_low, gate_matrix, preferred_element_type=jnp.float32
        ) + jnp.einsum("ch,dh->cd", up_grad_low, up_matrix, preferred_element_type=jnp.float32)
        gate_term = jnp.einsum(
            "cd,ch->dh", slot_in, gate_grad_low, preferred_element_type=jnp.float32
        )
        up_term = jnp.einsum("cd,ch->dh", slot_in, up_grad_low, preferred_element_type=jnp.float32)
        down_term = jnp.einsum(
            "ch,cd->hd", slot_hidden, slot_dy, preferred_element_type=jnp.float32
        )
        gate_shard, up_shard, down_shard = (
            lax.psum_scatter(
                gate_term.astype(jnp.bfloat16), "fsdp", scatter_dimension=1, tiled=True
            ).astype(jnp.float32),
            lax.psum_scatter(
                up_term.astype(jnp.bfloat16), "fsdp", scatter_dimension=1, tiled=True
            ).astype(jnp.float32),
            lax.psum_scatter(
                down_term.astype(jnp.bfloat16), "fsdp", scatter_dimension=0, tiled=True
            ).astype(jnp.float32),
        )
        gate_part, up_part, down_part = (
            lax.psum_scatter(
                gate_shard.astype(jnp.bfloat16), "ctx", scatter_dimension=0, tiled=True
            ).astype(jnp.float32),
            lax.psum_scatter(
                up_shard.astype(jnp.bfloat16), "ctx", scatter_dimension=0, tiled=True
            ).astype(jnp.float32),
            lax.psum_scatter(
                down_shard.astype(jnp.bfloat16), "ctx", scatter_dimension=1, tiled=True
            ).astype(jnp.float32),
        )
        return (carry, (in_grad, gate_part, up_part, down_part))

    _, (expert_in_grad, gate_parts, up_parts, down_parts) = lax.scan(
        expert_step,
        None,
        (expert_in, hidden_low, slot_grad, gate_pre, up_pre, gate_weight, up_weight, down_weight),
    )
    in_padded = jnp.concatenate(
        [
            expert_in_grad.reshape(expert_count * capacity, model_width),
            jnp.zeros((1, model_width), jnp.float32),
        ],
        axis=0,
    )
    normed_two_grad = jnp.sum(in_padded[placed].reshape(row_count, top_count, model_width), axis=1)
    prob_grad_router = jnp.sum(chosen * gate_grad[:, :, None], axis=1)
    logit_grad = (
        router_probs
        * (prob_grad_router - jnp.sum(router_probs * prob_grad_router, axis=-1, keepdims=True))
    ).astype(jnp.bfloat16)
    normed_two_grad = normed_two_grad + jnp.einsum(
        "te,de->td", logit_grad, router_weight, preferred_element_type=jnp.float32
    )
    router_grad = jnp.einsum(
        "td,te->de", normed_two, logit_grad, preferred_element_type=jnp.float32
    )
    mixed_norm_grad, gain_two_grad = norm_two_pull(normed_two_grad)
    mixed_grad = out_grad + mixed_norm_grad
    mixed_low = mixed_grad.astype(jnp.bfloat16)
    out_weight_grad = jnp.einsum(
        "td,te->de", attended_low, mixed_low, preferred_element_type=jnp.float32
    )
    output_grad = (
        jnp.einsum("te,de->td", mixed_low, out_weight, preferred_element_type=jnp.float32)
        .astype(jnp.bfloat16)
        .reshape(row_count, head_count, head_dim)
    )
    row_delta = jnp.sum(output_grad.astype(jnp.float32) * attended_f, axis=-1).T

    def query_grad_step(accum, block_index):
        key_block, value_block, key_pos, key_doc = key_slice(block_index)
        scores = masked_scores(
            query_low, key_block, local_pos, local_doc, key_pos, key_doc, score_scale
        )
        prob_block = jnp.exp(scores - log_total[..., None])
        prob_grad = jnp.einsum(
            "qhd,khd->hqk", output_grad, value_block, preferred_element_type=jnp.float32
        )
        score_grad = (prob_block * (prob_grad - row_delta[..., None])).astype(jnp.bfloat16)
        return (
            accum
            + jnp.einsum("hqk,khd->qhd", score_grad, key_block, preferred_element_type=jnp.float32)
            * score_scale,
            None,
        )

    query_grad, _ = lax.scan(
        query_grad_step, jnp.zeros((row_count, head_count, head_dim), jnp.float32), block_ids
    )
    inner_rows = math.gcd(row_count * lax.axis_size("ctx"), 512)

    def piece_step(carry, piece_index):
        first_row = piece_index * inner_rows
        key_block = lax.dynamic_slice_in_dim(keys_all, first_row, inner_rows, 0)
        value_block = lax.dynamic_slice_in_dim(values_all, first_row, inner_rows, 0)
        key_pos = lax.dynamic_slice_in_dim(stream_pos, first_row, inner_rows, 0)
        key_doc = lax.dynamic_slice_in_dim(stream_doc, first_row, inner_rows, 0)
        scores = masked_scores(
            query_low, key_block, local_pos, local_doc, key_pos, key_doc, score_scale
        )
        prob_block = jnp.exp(scores - log_total[..., None])
        prob_grad = jnp.einsum(
            "qhd,khd->hqk", output_grad, value_block, preferred_element_type=jnp.float32
        )
        score_grad = (prob_block * (prob_grad - row_delta[..., None])).astype(jnp.bfloat16)
        value_part = jnp.einsum(
            "hqk,qhd->khd",
            prob_block.astype(jnp.bfloat16),
            output_grad,
            preferred_element_type=jnp.float32,
        )
        key_part = (
            jnp.einsum("hqk,qhd->khd", score_grad, query_low, preferred_element_type=jnp.float32)
            * score_scale
        )
        return (
            carry,
            jnp.concatenate(
                [
                    key_part.reshape(inner_rows, model_width),
                    value_part.reshape(inner_rows, model_width),
                ],
                axis=1,
            ),
        )

    _, stacked = lax.scan(
        piece_step,
        None,
        jnp.arange(row_count * lax.axis_size("ctx") // inner_rows, dtype=jnp.int32),
    )
    key_value_grad = lax.psum_scatter(
        stacked.reshape(row_count * lax.axis_size("ctx"), 2 * model_width).astype(jnp.bfloat16),
        "ctx",
        scatter_dimension=0,
        tiled=True,
    ).astype(jnp.float32)
    key_grad = key_value_grad[:, :model_width].reshape(row_count, head_count, head_dim)
    value_grad = key_value_grad[:, model_width:]
    query_lin_grad, gain_query_grad = query_pull(query_grad)
    key_lin_grad, gain_key_grad = key_pull(key_grad)
    proj_grad = jnp.concatenate(
        [
            query_lin_grad.astype(jnp.bfloat16),
            key_lin_grad.astype(jnp.bfloat16),
            value_grad.astype(jnp.bfloat16),
        ],
        axis=1,
    )
    qkv_weight_grad = jnp.einsum(
        "td,te->de", normed_low, proj_grad, preferred_element_type=jnp.float32
    )
    normed_grad = jnp.einsum("te,de->td", proj_grad, qkv_weight, preferred_element_type=jnp.float32)
    input_norm_grad, gain_one_grad = norm_one_pull(normed_grad)
    input_grad = mixed_grad + input_norm_grad
    qkv_shard, out_shard = (
        lax.psum_scatter(
            qkv_weight_grad.astype(jnp.bfloat16), "fsdp", scatter_dimension=0, tiled=True
        ).astype(jnp.float32),
        lax.psum_scatter(
            out_weight_grad.astype(jnp.bfloat16), "fsdp", scatter_dimension=0, tiled=True
        ).astype(jnp.float32),
    )
    qkv_part, out_part = (
        lax.psum_scatter(
            qkv_shard.astype(jnp.bfloat16), "ctx", scatter_dimension=1, tiled=True
        ).astype(jnp.float32),
        lax.psum_scatter(
            out_shard.astype(jnp.bfloat16), "ctx", scatter_dimension=1, tiled=True
        ).astype(jnp.float32),
    )
    gain_one_sum, gain_query_sum, gain_key_sum, gain_two_sum, router_sum = lax.psum(
        (gain_one_grad, gain_query_grad, gain_key_grad, gain_two_grad, router_grad), ("ctx", "fsdp")
    )
    shard_rows = model_width // lax.axis_size("fsdp")
    shard_start = lax.axis_index("fsdp") * shard_rows

    def own_rows(full_array):
        return lax.dynamic_slice_in_dim(full_array, shard_start, shard_rows, 0)

    return (
        layer_out.astype(jnp.bfloat16)[None],
        input_grad[None],
        own_rows(gain_one_sum),
        qkv_part,
        own_rows(gain_query_sum),
        own_rows(gain_key_sum),
        out_part,
        own_rows(gain_two_sum),
        own_rows(router_sum),
        gate_parts,
        up_parts,
        down_parts,
    )


def rms_unit(values):
    return lax.rsqrt(jnp.mean(values * values, axis=-1, keepdims=True) + EPSILON)


def rope_tables(inner_pos, head_dim):
    half_dim = head_dim // 2
    freq_table = ROPE_BASE ** (-2.0 * jnp.arange(half_dim, dtype=jnp.float32) / head_dim)
    angles = inner_pos.astype(jnp.float32)[:, None] * freq_table[None, :]
    return (jnp.cos(angles), jnp.sin(angles))


def dot32(spec, left, right):
    return jnp.einsum(spec, left, right, preferred_element_type=jnp.float32)


def greet(peers):
    barrier = pltpu.get_barrier_semaphore()
    for peer in peers:
        pl.semaphore_signal(barrier, inc=1, device_id=peer, device_id_type=MESH)
    pl.semaphore_wait(barrier, len(peers))


def send(source, target, send_sem, recv_sem, peer):
    copy = pltpu.make_async_remote_copy(
        source, target, send_sem, recv_sem, device_id=peer, device_id_type=MESH
    )
    copy.start()
    return copy


def comm_call(
    kernel, name, collective_id, out_shape, in_specs, out_specs, scratch_shapes, cost, vmem=16
):
    return pl.pallas_call(
        kernel,
        out_shape=out_shape,
        in_specs=in_specs,
        out_specs=out_specs,
        scratch_shapes=scratch_shapes,
        compiler_params=pltpu.CompilerParams(
            collective_id=collective_id, has_side_effects=True, vmem_limit_bytes=vmem * 2**20
        ),
        cost_estimate=pl.CostEstimate(flops=0, bytes_accessed=cost, transcendentals=0),
        name=name,
    )


def ctx_sum(values, collective_id):
    ctx = lax.axis_size("ctx")

    def kernel(own_ref, out_ref, held, send_sems, recv_sems):
        me, mine = lax.axis_index("ctx"), lax.axis_index("fsdp")
        peers = [(lax.rem(me + step, ctx), mine) for step in range(1, ctx)]
        greet(peers)
        copies = [
            send(own_ref, held.at[i], send_sems.at[i], recv_sems.at[i], peer)
            for i, peer in enumerate(peers)
        ]
        total = own_ref[...]
        for i, copy in enumerate(copies):
            copy.wait_recv()
            total = total + held[i]
        out_ref[...] = total
        for copy in copies:
            copy.wait_send()

    return comm_call(
        kernel,
        "ctx_sum",
        collective_id,
        jax.ShapeDtypeStruct(values.shape, values.dtype),
        [VMEM],
        VMEM,
        [
            pltpu.VMEM((ctx - 1,) + values.shape, values.dtype),
            DMA((ctx - 1,)),
            DMA((ctx - 1,)),
        ],
        20 * 2**20,
    )(values)


def heads_to_rows(values, collective_id):
    ctx, fsdp = lax.axis_size("ctx"), lax.axis_size("fsdp")
    rows, cols = values.shape[0] // ctx, values.shape[1]
    share = ctx // fsdp

    def kernel(own_ref, out_ref, send_sems, recv_sems):
        me, mine = lax.axis_index("ctx"), lax.axis_index("fsdp")
        keeper, place = me // share, lax.rem(me, share)
        own_keeper = (keeper == mine).astype(jnp.int32)
        barrier = pltpu.get_barrier_semaphore()
        for step in range(share * fsdp):
            source, stream = mine * share + step // fsdp, step % fsdp

            @pl.when(jnp.logical_or(source != me, stream != mine))
            def _():
                pl.semaphore_signal(
                    barrier, inc=1, device_id=(source, stream), device_id_type=MESH
                )

        pl.semaphore_wait(barrier, ctx - own_keeper)

        def block(index):
            return own_ref.at[pl.ds(pl.multiple_of(index * rows, rows), rows), :]

        def landing(stream, position):
            return out_ref.at[
                pl.ds(pl.multiple_of(stream * rows, rows), rows),
                pl.ds(pl.multiple_of(position * cols, cols), cols),
            ]

        slot = place * fsdp + mine

        def copy_to(step):
            other = lax.rem(me + step, ctx)
            return pltpu.make_async_remote_copy(
                block(other),
                landing(mine, place),
                send_sems.at[step],
                recv_sems.at[slot],
                device_id=(other, keeper),
                device_id_type=MESH,
            )

        kept = pltpu.make_async_copy(block(me), landing(mine, place), send_sems.at[0])
        for step in range(1, ctx):
            copy_to(step).start()

        @pl.when(own_keeper == 0)
        def _():
            copy_to(0).start()

        @pl.when(own_keeper == 1)
        def _():
            kept.start()
            kept.wait()

        for step in range(share * fsdp):

            @pl.when(
                jnp.logical_or(mine * share + step // fsdp != me, step % fsdp != mine)
            )
            def _():
                pltpu.make_async_copy(
                    block(0), landing(step % fsdp, step // fsdp), recv_sems.at[step]
                ).wait()

        for step in range(1, ctx):
            copy_to(step).wait_send()

        @pl.when(own_keeper == 0)
        def _():
            copy_to(0).wait_send()

    return comm_call(
        kernel,
        "heads_to_rows",
        collective_id,
        jax.ShapeDtypeStruct((fsdp * rows, share * cols), values.dtype),
        [ANY],
        ANY,
        [DMA((ctx,)), DMA((share * fsdp,))],
        40 * 2**20,
    )(values)


def rows_to_heads(values, collective_id):
    ctx, fsdp = lax.axis_size("ctx"), lax.axis_size("fsdp")
    share = ctx // fsdp
    rows, cols = values.shape[0] // fsdp, values.shape[1] // share

    def kernel(own_ref, out_ref, stage, stage_send, stage_recv, send_sems, recv_sems, done_sem):
        me, mine = lax.axis_index("ctx"), lax.axis_index("fsdp")
        ctx_peers = [(lax.rem(me + step, ctx), mine) for step in range(1, ctx)]
        greet(ctx_peers + [(me, lax.rem(mine + step, fsdp)) for step in range(1, fsdp)])

        def block(stream):
            return own_ref.at[pl.ds(pl.multiple_of(stream * rows, rows), rows), :]

        def landing(index):
            return out_ref.at[pl.ds(pl.multiple_of(index * rows, rows), rows), :]

        steps = [2, 3, 1]
        staged = {
            step: send(
                block(lax.rem(mine + step, fsdp)),
                stage.at[fsdp - step],
                stage_send.at[step],
                stage_recv.at[fsdp - step],
                (me, lax.rem(mine + step, fsdp)),
            )
            for step in steps
        }

        def piece(step, place):
            span = pl.ds(place * cols, cols)
            if step == 0:
                return own_ref.at[pl.ds(pl.multiple_of(mine * rows, rows), rows), span]
            return stage.at[step, :, span]

        def target(step, place):
            return lax.rem(mine + step, fsdp) * share + place

        def copy_to(step, place):
            return pltpu.make_async_remote_copy(
                piece(step, place),
                landing(me),
                send_sems.at[step * share + place],
                recv_sems.at[me],
                device_id=(target(step, place), mine),
                device_id_type=MESH,
            )

        def keep(step, place):
            return pltpu.make_async_copy(
                piece(step, place), landing(me), send_sems.at[step * share + place]
            )

        for step in [0, 1, 2, 3]:
            if step > 0:
                staged[fsdp - step].wait_recv()
            for place in range(share):
                far = target(step, place) != me
                pl.when(far)(copy_to(step, place).start)
                pl.when(jnp.logical_not(far))(keep(step, place).start)
        for step in range(1, ctx):
            source = lax.rem(me + step, ctx)
            pltpu.make_async_copy(
                piece(0, 0), landing(source), recv_sems.at[source]
            ).wait()
        for step in range(fsdp):
            for place in range(share):
                far = target(step, place) != me
                pl.when(far)(copy_to(step, place).wait_send)
                pl.when(jnp.logical_not(far))(keep(step, place).wait)
        for copy in staged.values():
            copy.wait_send()
        for peer in ctx_peers:
            pl.semaphore_signal(done_sem, inc=1, device_id=peer, device_id_type=MESH)
        pl.semaphore_wait(done_sem, ctx - 1)

    return comm_call(
        kernel,
        "rows_to_heads",
        collective_id,
        jax.ShapeDtypeStruct((ctx * rows, cols), values.dtype),
        [ANY],
        ANY,
        [
            pltpu.VMEM((fsdp, rows, share * cols), values.dtype),
            DMA((fsdp,)),
            DMA((fsdp,)),
            DMA((ctx,)),
            DMA((ctx,)),
            pltpu.SemaphoreType.REGULAR,
        ],
        2**20,
    )(values)


def swap(values, flip):
    return lax.ppermute(values, "ctx", [(i, i ^ flip) for i in range(lax.axis_size("ctx"))])


def reduce_then_gather(partial, extras, out_shapes, chunk_math, name, collective_id, crossed, bulk, vmem):
    ctx, fsdp = lax.axis_size("ctx"), lax.axis_size("fsdp")
    rows, width = partial.shape[0] // fsdp, partial.shape[1]
    chunks = 4
    size = rows // chunks
    count = len(extras)
    cols = width // ctx
    if crossed:
        out_shapes = out_shapes + [jax.ShapeDtypeStruct((rows, width // 2), jnp.bfloat16)]
    bulk_count, out_count = len(bulk), len(out_shapes)

    def kernel(*refs):
        part_ref, extra_refs = refs[0], refs[1 : 1 + count]
        bulk_refs, refs = refs[1 + count : 1 + count + bulk_count], refs[1 + count + bulk_count :]
        all_ref, out_refs = refs[0], refs[1 : 1 + out_count]
        bulk_out_refs, refs = refs[1 + out_count : 1 + out_count + bulk_count], refs[1 + out_count :]
        near_own, near_far, far_sum, far_own, sems, cross_sems, bulk_sems = refs[bulk_count:]
        me, mine = lax.axis_index("ctx"), lax.axis_index("fsdp")
        flip = 1 - 2 * lax.rem(mine, 2)
        core = mine + flip
        chip = lax.rem(mine + 2, fsdp)
        diagonal = lax.rem(core + 2, fsdp)
        to_x = (flipped(me, 1), mine)
        greet([(me, core), (me, chip)] + ([to_x] if crossed or bulk else []))

        def span(block, i):
            return pl.ds(pl.multiple_of(block * rows + i * size, size), size)

        def sem(kind, i):
            return sems.at[2 * kind, i], sems.at[2 * kind + 1, i]

        copies = []
        from_core_far, from_core_own, from_chip = [], [], []
        exchanged = [
            send(source, target, bulk_sems.at[0, i], bulk_sems.at[1, i], to_x)
            for i, (source, target) in enumerate(zip(bulk_refs, bulk_out_refs))
        ]
        for i in range(chunks):
            copy = send(
                part_ref.at[span(diagonal, i), :], near_far.at[i], *sem(0, i), (me, core)
            )
            from_core_far.append(copy)
        for i in range(chunks):
            copy = send(part_ref.at[span(core, i), :], near_own.at[i], *sem(1, i), (me, core))
            from_core_own.append(copy)
        for i in range(chunks):
            from_core_far[i].wait_recv()
            both = part_ref[span(chip, i), :].astype(jnp.float32) + near_far[i].astype(jnp.float32)
            far_sum[i] = both.astype(jnp.bfloat16)
            from_chip.append(send(far_sum.at[i], far_own.at[i], *sem(2, i), (me, chip)))
        to_chip = []
        for i in range(chunks):
            from_core_own[i].wait_recv()
            from_chip[i].wait_recv()
            total = (
                part_ref[span(mine, i), :].astype(jnp.float32)
                + near_own[i].astype(jnp.float32)
                + far_own[i].astype(jnp.float32)
            )
            all_ref[span(mine, i), :] = chunk_math(
                i, pl.ds(i * size, size), total, extra_refs, out_refs
            ).astype(jnp.bfloat16)
            own = all_ref.at[span(mine, i), :]
            to_chip.append(send(own, own, *sem(3, i), (me, chip)))
            copies.append(send(own, own, *sem(4, i), (me, core)))
            for run in range(ctx // 2 if crossed else 0):
                start = pl.multiple_of((2 * run + 1 - lax.rem(me, 2)) * cols, cols)
                copies.append(
                    send(
                        all_ref.at[span(mine, i), pl.ds(start, cols)],
                        out_refs[-1].at[pl.ds(i * size, size), pl.ds(run * cols, cols)],
                        cross_sems.at[0, i, run],
                        cross_sems.at[1, i, run],
                        to_x,
                    )
                )
        for i in range(chunks):
            to_chip[i].wait_recv()
            other = all_ref.at[span(chip, i), :]
            copies.append(send(other, other, *sem(5, i), (me, core)))
        for copy in copies + exchanged:
            copy.wait_recv()
        for copy in from_core_far + from_core_own + from_chip + to_chip + copies + exchanged:
            copy.wait_send()

    return comm_call(
        kernel,
        name,
        collective_id,
        [jax.ShapeDtypeStruct(partial.shape, jnp.bfloat16)]
        + out_shapes
        + [jax.ShapeDtypeStruct(values.shape, values.dtype) for values in bulk],
        [VMEM] * (1 + count) + [ANY] * bulk_count,
        [VMEM] * (1 + out_count) + [ANY] * bulk_count,
        [
            pltpu.VMEM((chunks, size, width), jnp.bfloat16),
            pltpu.VMEM((chunks, size, width), jnp.bfloat16),
            pltpu.VMEM((chunks, size, width), jnp.bfloat16),
            pltpu.VMEM((chunks, size, width), jnp.bfloat16),
            DMA((12, chunks)),
            DMA((2, chunks, ctx // 2)),
            DMA((2, max(1, bulk_count))),
        ],
        100 * 2**20,
        vmem,
    )(partial, *extras, *bulk)


def norm_chunk(index, span, total, extra_refs, out_refs):
    tokens_ref, gain_ref = extra_refs
    mixed = tokens_ref[span, :].astype(jnp.float32) + total
    out_refs[0][span, :] = mixed
    return mixed * rms_unit(mixed) * gain_ref[...]


def norm_back_chunk(index, span, total, extra_refs, out_refs):
    mixed_ref, gain_ref, dy_ref = extra_refs
    mixed = mixed_ref[span, :]
    scale = rms_unit(mixed)
    unit = mixed * scale
    pulled = total * gain_ref[...]
    grad = dy_ref[span, :].astype(jnp.float32) + scale * (
        pulled - unit * jnp.mean(unit * pulled, axis=-1, keepdims=True)
    )
    out_refs[0][span, :] = grad
    gain_grad = jnp.sum(total * unit, axis=0, keepdims=True)
    if index == 0:
        out_refs[1][...] = gain_grad
    else:
        out_refs[1][...] += gain_grad
    return grad


ROUTER_ROWS = 16


def one_hot(slots, capacity):
    return lax.broadcasted_iota(jnp.int32, (capacity, slots.shape[1]), 0) == slots


def slots_of(pairs, experts, top):
    lines, rows = pairs.shape
    absent = float(rows * top)

    def kernel(pairs_ref, out_ref):
        out_ref[...] = jnp.full(out_ref.shape, -1, jnp.int32)
        rank_rows = []
        for expert in range(experts):
            rank = jnp.full((1, rows), absent, jnp.float32)
            for k in range(top):
                rank = jnp.where(
                    pairs_ref[k : k + 1, :] == expert,
                    pairs_ref[top + k : top + k + 1, :].astype(jnp.float32),
                    rank,
                )
            rank_rows.append(rank)
        filler = jnp.full((rows - experts, rows), absent, jnp.float32)
        by_column = jnp.concatenate(rank_rows + [filler], axis=0).T
        for expert, rank in enumerate(rank_rows):
            earlier = jnp.where(by_column[:, expert : expert + 1] < rank, 1.0, 0.0)
            slot = jnp.where(rank < absent, jnp.sum(earlier, axis=0, keepdims=True), -1.0)
            out_ref[expert : expert + 1, :] = slot.astype(jnp.int32)

    return pl.pallas_call(
        kernel,
        out_shape=jax.ShapeDtypeStruct((lines, rows), jnp.int32),
        in_specs=[VMEM],
        out_specs=VMEM,
        cost_estimate=pl.CostEstimate(flops=10**7, bytes_accessed=2**20, transcendentals=0),
        name="slots_of",
    )(pairs)


def run_experts(group, dy_all, slots, router, w_gate, w_up, w_down, blocks, capacity):
    experts, width, units = w_gate.shape
    total = group.shape[0]
    rows = total // blocks
    held = blocks * capacity
    f32, bf16 = jnp.float32, jnp.bfloat16

    def kernel(
        group_ref,
        dy_ref,
        slots_ref,
        router_ref,
        gate_ref,
        up_ref,
        down_ref,
        moved_ref,
        grad_ref,
        g_router_ref,
        scaled_ref,
        gate_low_ref,
        up_low_ref,
        disp,
        ins,
        dys,
        probs,
        prob_grad,
    ):
        expert = pl.program_id(0)

        def block_rows(b):
            return pl.ds(b * rows, rows)

        @pl.when(expert == 0)
        def _():
            logits = lax.dot_general(
                router_ref[...],
                group_ref[...],
                (((1,), (1,)), ((), ())),
                preferred_element_type=f32,
            )
            real = lax.broadcasted_iota(jnp.int32, logits.shape, 0) < experts
            logits = jnp.where(real, logits, MASKED)
            weights = jnp.exp(logits - jnp.max(logits, axis=0, keepdims=True))
            probs[...] = weights / jnp.sum(weights, axis=0, keepdims=True)
            prob_grad[...] = jnp.zeros_like(prob_grad)
            for b in range(blocks):
                for e in range(experts):
                    disp[b, pl.ds(e * capacity, capacity), :] = (
                        one_hot(slots_ref[b, pl.ds(e, 1), :], capacity)
                        .astype(f32)
                        .astype(bf16)
                    )
                for source, target in ((group_ref, ins), (dy_ref, dys)):
                    picked = jnp.dot(
                        disp[b], source[block_rows(b), :], preferred_element_type=f32
                    ).astype(bf16)
                    for e in range(experts):
                        target[e, pl.ds(b * capacity, capacity), :] = picked[
                            e * capacity : (e + 1) * capacity
                        ]

        expert_in, slot_dy = ins[expert], dys[expert]
        gate_matrix, up_matrix, down_matrix = gate_ref[0], up_ref[0], down_ref[0]
        gate_pre = jnp.dot(expert_in, gate_matrix, preferred_element_type=f32)
        up_pre = jnp.dot(expert_in, up_matrix, preferred_element_type=f32)
        raw_grad = lax.dot_general(
            slot_dy, down_matrix, (((1,), (1,)), ((), ())), preferred_element_type=f32
        )
        own_probs = probs[pl.ds(expert, 1), :]
        hots = [one_hot(slots_ref[b, pl.ds(expert, 1), :], capacity) for b in range(blocks)]
        value = jnp.concatenate(
            [
                jnp.sum(
                    jnp.where(hots[b], own_probs[:, b * rows : (b + 1) * rows], 0.0),
                    axis=1,
                    keepdims=True,
                )
                for b in range(blocks)
            ],
            axis=0,
        )
        sigma = 1.0 / (1.0 + jnp.exp(-gate_pre))
        silu = gate_pre * sigma
        hidden = (silu * up_pre).astype(bf16)
        hidden_f = hidden.astype(f32)
        value_grad = jnp.sum(hidden_f * raw_grad, axis=1, keepdims=True)
        hidden_grad = raw_grad * value
        gate_low = (hidden_grad * up_pre * sigma * (1.0 + gate_pre * (1.0 - sigma))).astype(bf16)
        up_low = (hidden_grad * silu).astype(bf16)
        scaled = (hidden_f * value).astype(bf16)
        scaled_ref[0] = scaled
        gate_low_ref[0] = gate_low
        up_low_ref[0] = up_low
        for b in range(blocks):
            prob_grad[expert, :, block_rows(b)] = jnp.sum(
                jnp.where(hots[b], value_grad[b * capacity : (b + 1) * capacity], 0.0),
                axis=0,
                keepdims=True,
            )
        dys[expert] = jnp.dot(scaled, down_matrix, preferred_element_type=f32).astype(bf16)
        ins[expert] = (
            lax.dot_general(
                gate_low, gate_matrix, (((1,), (1,)), ((), ())), preferred_element_type=f32
            )
            + lax.dot_general(
                up_low, up_matrix, (((1,), (1,)), ((), ())), preferred_element_type=f32
            )
        ).astype(bf16)

        @pl.when(expert == experts - 1)
        def _():
            grads = jnp.concatenate([prob_grad[e] for e in range(ROUTER_ROWS)], axis=0)
            weights = probs[...]
            logit_grad = (
                weights * (grads - jnp.sum(weights * grads, axis=0, keepdims=True))
            ).astype(bf16)
            g_router_ref[...] = jnp.dot(logit_grad, group_ref[...], preferred_element_type=f32)
            for b in range(blocks):
                for source, target in ((dys, moved_ref), (ins, grad_ref)):
                    gathered = jnp.concatenate(
                        [source[e, pl.ds(b * capacity, capacity), :] for e in range(experts)],
                        axis=0,
                    )
                    back = lax.dot_general(
                        disp[b], gathered, (((0,), (0,)), ((), ())), preferred_element_type=f32
                    )
                    if target is grad_ref:
                        back = back + lax.dot_general(
                            logit_grad[:, b * rows : (b + 1) * rows],
                            router_ref[...],
                            (((0,), (0,)), ((), ())),
                            preferred_element_type=f32,
                        )
                    target[block_rows(b), :] = back.astype(bf16)

    def whole(shape):
        return pl.BlockSpec(shape, lambda e: (0,) * len(shape))

    def by_expert(shape):
        return pl.BlockSpec((1,) + shape, lambda e: (e, 0, 0))

    return pl.pallas_call(
        kernel,
        grid=(experts,),
        out_shape=[
            jax.ShapeDtypeStruct((total, width), bf16),
            jax.ShapeDtypeStruct((total, width), bf16),
            jax.ShapeDtypeStruct((ROUTER_ROWS, width), f32),
        ]
        + [jax.ShapeDtypeStruct((experts, held, units), bf16)] * 3,
        in_specs=[
            whole((total, width)),
            whole((total, width)),
            whole(slots.shape),
            whole((ROUTER_ROWS, width)),
            by_expert((width, units)),
            by_expert((width, units)),
            by_expert((units, width)),
        ],
        out_specs=[
            whole((total, width)),
            whole((total, width)),
            whole((ROUTER_ROWS, width)),
        ]
        + [by_expert((held, units))] * 3,
        scratch_shapes=[
            pltpu.VMEM((blocks, experts * capacity, rows), bf16),
            pltpu.VMEM((experts, held, width), bf16),
            pltpu.VMEM((experts, held, width), bf16),
            pltpu.VMEM((ROUTER_ROWS, total), f32),
            pltpu.VMEM((ROUTER_ROWS, 1, total), f32),
        ],
        compiler_params=pltpu.CompilerParams(vmem_limit_bytes=60 * 2**20),
        cost_estimate=pl.CostEstimate(
            flops=30 * 10**9, bytes_accessed=30 * 2**20, transcendentals=10**6
        ),
        name="run_experts",
    )(group, dy_all, slots, router, w_gate, w_up, w_down)


def expert_grads(slot_own, slot_other, rows_own, rows_other, slots_own, slots_other, capacity):
    kinds = len(slot_own)
    experts, held, units = slot_own[0].shape
    total, half = rows_other.shape
    blocks = held // capacity
    rows = total // blocks
    ctx = lax.axis_size("ctx")
    cols = 2 * half // ctx
    f32, bf16 = jnp.float32, jnp.bfloat16

    def kernel(*refs):
        own_refs, other_refs = refs[:kinds], refs[kinds : 2 * kinds]
        rows_own_ref, rows_other_ref, slots_own_ref, slots_other_ref = refs[2 * kinds : 2 * kinds + 4]
        out_refs, held_rows = refs[2 * kinds + 4 : -1], refs[-1]
        expert = pl.program_id(0)
        me = lax.axis_index("ctx")

        def columns(side, run):
            if side == 1:
                return pl.ds(run * cols, cols)
            return pl.ds(pl.multiple_of((2 * run + lax.rem(me, 2)) * cols, cols), cols)

        @pl.when(expert == 0)
        def _():
            for side, slots_ref, source in (
                (0, slots_own_ref, rows_own_ref),
                (1, slots_other_ref, rows_other_ref),
            ):
                for b in range(blocks):
                    span = pl.ds(b * rows, rows)
                    disp = jnp.concatenate(
                        [
                            one_hot(slots_ref[b, pl.ds(e, 1), :], capacity).astype(f32)
                            for e in range(experts)
                        ],
                        axis=0,
                    ).astype(bf16)
                    for run in range(ctx // 2):
                        picked = jnp.dot(
                            disp, source[span, columns(side, run)], preferred_element_type=f32
                        ).astype(bf16)
                        for e in range(experts):
                            held_rows[
                                e,
                                pl.ds(side * held + b * capacity, capacity),
                                pl.ds(run * cols, cols),
                            ] = picked[e * capacity : (e + 1) * capacity]

        low, high = lax.rem(me // 2, 2), me // 4
        stacked = [
            jnp.concatenate([own[0], other[0]], axis=0) for own, other in zip(own_refs, other_refs)
        ]
        contract = (((0,), (0,)), ((), ()))
        for run in range(ctx // 2):
            given = jnp.where(low == run % 2, 0, 2)
            place = given + jnp.where(high == run // 2, 0, 1)
            features = held_rows[expert, :, pl.ds(run * cols, cols)]
            for kind in range(kinds):
                total = lax.dot_general(
                    features, stacked[kind], contract, preferred_element_type=f32
                ).astype(bf16)
                for i in range(4):

                    @pl.when(place == i)
                    def _():
                        out_refs[4 * kind + i][0] = total

    def whole(shape):
        return pl.BlockSpec(shape, lambda e: (0,) * len(shape))

    slot_spec = pl.BlockSpec((1, held, units), lambda e: (e, 0, 0))
    return pl.pallas_call(
        kernel,
        grid=(experts,),
        out_shape=[jax.ShapeDtypeStruct((experts, units, cols), bf16)] * (4 * kinds),
        in_specs=[slot_spec] * (2 * kinds)
        + [whole((total, 2 * half)), whole((total, half))]
        + [whole(slots_own.shape)] * 2,
        out_specs=[pl.BlockSpec((1, units, cols), lambda e: (e, 0, 0))] * (4 * kinds),
        scratch_shapes=[pltpu.VMEM((experts, 2 * held, half), bf16)],
        compiler_params=pltpu.CompilerParams(vmem_limit_bytes=60 * 2**20),
        cost_estimate=pl.CostEstimate(flops=0, bytes_accessed=2**20, transcendentals=0),
        name="expert_grads",
    )(*slot_own, *slot_other, rows_own, rows_other, slots_own, slots_other)


def down_grads(scaled, dy_parts, slots, capacity):
    count = len(scaled)
    experts, held, units = scaled[0].shape
    blocks, _, rows, wide = dy_parts.shape
    cols = wide // 2
    f32, bf16 = jnp.float32, jnp.bfloat16

    def kernel(*refs):
        scaled_refs, dy_ref, slots_refs = refs[:count], refs[count], refs[count + 1 : 2 * count + 1]
        out_ref, held_rows = refs[2 * count + 1 :]
        expert = pl.program_id(0)

        @pl.when(expert == 0)
        def _():
            for i, slots_ref in enumerate(slots_refs):
                for b in range(blocks):
                    span = pl.ds(b * rows, rows)
                    disp = jnp.concatenate(
                        [
                            one_hot(slots_ref[b, pl.ds(e, 1), :], capacity).astype(f32)
                            for e in range(experts)
                        ],
                        axis=0,
                    ).astype(bf16)
                    picked = jnp.dot(disp, dy_ref[b, i], preferred_element_type=f32).astype(bf16)
                    for e in range(experts):
                        held_rows[e, pl.ds(i * held + b * capacity, capacity), :] = picked[
                            e * capacity : (e + 1) * capacity
                        ]

        stacked = jnp.concatenate([ref[0] for ref in scaled_refs], axis=0)
        total = lax.dot_general(
            stacked, held_rows[expert], (((0,), (0,)), ((), ())), preferred_element_type=f32
        ).astype(bf16)
        side = lax.rem(lax.axis_index("ctx"), 2)
        for x in range(2):
            kept = jnp.where(side == x, 1, 0)
            out_ref[pl.ds(kept, 1), 0] = total[:, x * cols : (x + 1) * cols][None]

    def whole(shape):
        return pl.BlockSpec(shape, lambda e: (0,) * len(shape))

    return pl.pallas_call(
        kernel,
        grid=(experts,),
        out_shape=jax.ShapeDtypeStruct((2, experts, units, cols), bf16),
        in_specs=[pl.BlockSpec((1, held, units), lambda e: (e, 0, 0))] * count
        + [whole(dy_parts.shape)]
        + [whole(slots[0].shape)] * count,
        out_specs=pl.BlockSpec((2, 1, units, cols), lambda e: (0, e, 0, 0)),
        scratch_shapes=[pltpu.VMEM((experts, count * held, wide), bf16)],
        compiler_params=pltpu.CompilerParams(vmem_limit_bytes=60 * 2**20),
        cost_estimate=pl.CostEstimate(flops=0, bytes_accessed=2**20, transcendentals=0),
        name="down_grads",
    )(*scaled, dy_parts, *slots)


def roll_half(values):
    return pltpu.roll(values, values.shape[1] // 2, 1)


def allowed_keys(first_ref, last_ref, span, places):
    return (places >= first_ref[span, :]) & (places <= last_ref[span, :])


def stored_runs(total):
    ctx = lax.axis_size("ctx")
    rows = total // ctx
    run = rows // 2
    starts = [i * rows for i in range(ctx)]
    return starts + [i * rows + run for i in reversed(range(ctx))], run


def attend(projected, scales, gains, cosine, sine_part, first, last, places, cols):
    total = projected.shape[0]
    head_dim = cosine.shape[1]
    heads = cols // head_dim
    size = math.gcd(total, 256)
    score_scale = head_dim ** (-0.5)
    starts, run = stored_runs(total)
    f32, bf16 = jnp.float32, jnp.bfloat16

    def kernel(
        lin_ref,
        scales_ref,
        gains_ref,
        cos_ref,
        sin_ref,
        first_ref,
        last_ref,
        places_ref,
        low_ref,
        attended_ref,
        attended_low_ref,
        top_ref,
    ):
        for kind in range(3):
            for h in range(heads):
                span = pl.ds(kind * cols + h * head_dim, head_dim)
                values = lin_ref[:, span]
                if kind < 2:
                    values = values * scales_ref[:, kind : kind + 1] * gains_ref[:, span]
                    values = values * cos_ref[...] + roll_half(values) * sin_ref[...]
                values = values.astype(bf16)
                for place, start in enumerate(starts):
                    low_ref[pl.ds(place * run, run), span] = values[start : start + run]
        for h in range(heads):
            head = pl.ds(h * head_dim, head_dim)
            for b in range(total // size):
                span, seen = pl.ds(b * size, size), pl.ds(0, (b + 1) * size)
                scores = lax.dot_general(
                    low_ref[span, head],
                    low_ref[seen, pl.ds(cols + h * head_dim, head_dim)],
                    (((1,), (1,)), ((), ())),
                    preferred_element_type=f32,
                )
                allowed = allowed_keys(first_ref, last_ref, span, places_ref[:, seen])
                scores = jnp.where(allowed, scores * score_scale, MASKED)
                top = jnp.max(scores, axis=1, keepdims=True)
                weights = jnp.exp(scores - top)
                sums = jnp.sum(weights, axis=1, keepdims=True)
                probs = (weights * (1.0 / sums)).astype(bf16)
                attended = jnp.dot(
                    probs,
                    low_ref[seen, pl.ds(2 * cols + h * head_dim, head_dim)],
                    preferred_element_type=f32,
                )
                attended_ref[span, head] = attended
                attended_low = attended.astype(bf16)
                for i in range(size // run):
                    start = starts[b * (size // run) + i]
                    attended_low_ref[pl.ds(start, run), head] = attended_low[i * run : (i + 1) * run]
                top_ref[span, head] = jnp.broadcast_to(top + jnp.log(sums), (size, head_dim))

    return pl.pallas_call(
        kernel,
        out_shape=[
            jax.ShapeDtypeStruct((total, 3 * cols), bf16),
            jax.ShapeDtypeStruct((total, cols), f32),
            jax.ShapeDtypeStruct((total, cols), bf16),
            jax.ShapeDtypeStruct((total, cols), f32),
        ],
        in_specs=[VMEM] * 8,
        out_specs=[VMEM] * 4,
        compiler_params=pltpu.CompilerParams(vmem_limit_bytes=24 * 2**20),
        cost_estimate=pl.CostEstimate(
            flops=2 * 10**9, bytes_accessed=20 * 2**20, transcendentals=2 * 10**6
        ),
        name="attend",
    )(projected, scales, gains, cosine, sine_part, first, last, places)


def attend_back(
    output_grad, low, attended, top, projected, scales, gains, cosine, sine_part, first, last, places
):
    total, cols = output_grad.shape
    head_dim = cosine.shape[1]
    heads = cols // head_dim
    size = math.gcd(total, 256)
    score_scale = head_dim ** (-0.5)
    f32, bf16 = jnp.float32, jnp.bfloat16
    contract_rows = (((0,), (0,)), ((), ()))
    starts, run = stored_runs(total)

    def kernel(
        grad_ref,
        low_ref,
        attended_ref,
        top_ref,
        lin_ref,
        scales_ref,
        gains_ref,
        cos_ref,
        sin_ref,
        first_ref,
        last_ref,
        places_ref,
        back_ref,
        value_ref,
        gain_ref,
        sums_ref,
        query_grad,
        key_grad,
        value_grad,
        grads_moved,
    ):
        for place, start in enumerate(starts):
            grads_moved[pl.ds(place * run, run), :] = grad_ref[pl.ds(start, run), :]

        def stored(values):
            pieces = sorted((start, place) for place, start in enumerate(starts))
            return jnp.concatenate([values[p * run : (p + 1) * run] for _, p in pieces], axis=0)

        totals = [jnp.zeros((total, 1), f32) for _ in range(2)]
        for h in range(heads):
            head = pl.ds(h * head_dim, head_dim)
            key_grad[...] = jnp.zeros_like(key_grad)
            value_grad[...] = jnp.zeros_like(value_grad)
            for b in range(total // size):
                span, seen = pl.ds(b * size, size), pl.ds(0, (b + 1) * size)
                queries, grads = low_ref[span, head], grads_moved[span, head]
                keys = low_ref[seen, pl.ds(cols + h * head_dim, head_dim)]
                scores = lax.dot_general(
                    queries, keys, (((1,), (1,)), ((), ())), preferred_element_type=f32
                )
                allowed = allowed_keys(first_ref, last_ref, span, places_ref[:, seen])
                scores = jnp.where(allowed, scores * score_scale, MASKED)
                probs = jnp.exp(scores - top_ref[span, head][:, :1])
                prob_grad = lax.dot_general(
                    grads,
                    low_ref[seen, pl.ds(2 * cols + h * head_dim, head_dim)],
                    (((1,), (1,)), ((), ())),
                    preferred_element_type=f32,
                )
                delta = jnp.sum(
                    grads.astype(f32) * attended_ref[span, head], axis=1, keepdims=True
                )
                score_grad = (probs * (prob_grad - delta)).astype(bf16)
                query_grad[span, :] = (
                    jnp.dot(score_grad, keys, preferred_element_type=f32) * score_scale
                )
                key_grad[seen, :] += lax.dot_general(
                    score_grad, queries, contract_rows, preferred_element_type=f32
                )
                value_grad[seen, :] += lax.dot_general(
                    probs.astype(bf16), grads, contract_rows, preferred_element_type=f32
                )
            value_ref[:, head] = stored(value_grad[...].astype(bf16))
            for kind, grad in ((0, query_grad[...]), (1, key_grad[...] * score_scale)):
                grad = stored(grad)
                span = pl.ds(kind * cols + h * head_dim, head_dim)
                unit = lin_ref[:, span] * scales_ref[:, kind : kind + 1]
                grad = grad * cos_ref[...] - roll_half(grad) * sin_ref[...]
                gain_ref[kind, :, head] = jnp.sum(grad * unit, axis=0, keepdims=True)
                grad = grad * gains_ref[:, span]
                back_ref[kind, :, head] = grad
                totals[kind] = totals[kind] + jnp.sum(grad * unit, axis=1, keepdims=True)
        for kind in range(2):
            sums_ref[:, kind : kind + 1] = totals[kind]

    return pl.pallas_call(
        kernel,
        out_shape=[
            jax.ShapeDtypeStruct((2, total, cols), f32),
            jax.ShapeDtypeStruct((total, cols), bf16),
            jax.ShapeDtypeStruct((2, 1, cols), f32),
            jax.ShapeDtypeStruct((total, 2), f32),
        ],
        in_specs=[VMEM] * 12,
        out_specs=[VMEM] * 4,
        scratch_shapes=[pltpu.VMEM((total, head_dim), f32)] * 3 + [pltpu.VMEM((total, cols), bf16)],
        compiler_params=pltpu.CompilerParams(vmem_limit_bytes=60 * 2**20),
        cost_estimate=pl.CostEstimate(flops=0, bytes_accessed=2**20, transcendentals=0),
        name="attend_back",
    )(
        output_grad,
        low,
        attended,
        top,
        projected,
        scales,
        gains,
        cosine,
        sine_part,
        first,
        last,
        places,
    )


def flipped(index, bit):
    return index + bit * (1 - 2 * lax.rem(index // bit, 2))


def flipped_by(index, flip):
    for bit in (1, 2, 4):
        index = flipped(index, bit) if flip & bit else index
    return index


def add_into(target, *sources):
    step = target.shape[0] if len(target.shape) == 3 else target.shape[0] // 64

    def body(i, carry):
        span = i if len(target.shape) == 3 else pl.ds(pl.multiple_of(i * 64, 64), 64)
        total = sources[0][span].astype(jnp.float32)
        for source in sources[1:]:
            total = total + source[span].astype(jnp.float32)
        target[span] = total.astype(target.dtype)
        return carry

    lax.fori_loop(0, step, body, 0)


def finish_sums(downs, ups, gate_far, gate_own, up_far, normed_part, out_part, qkv_part, small, tokens, mixed_grad, gain, mixed, moved, collective_id):
    ctx, fsdp = lax.axis_size("ctx"), lax.axis_size("fsdp")
    experts, units, cols = gate_far.shape
    kinds = 3
    rows, width = tokens.shape
    part = out_part.shape[0]
    f32, bf16 = jnp.float32, jnp.bfloat16
    small_rows, small_cols = small.shape[0], small.shape[1] // fsdp
    copies_most = 64

    def kernel(
        downs_ref,
        gate_near_ref,
        gate_high_ref,
        up_near_ref,
        up_high_ref,
        up_low_ref,
        gate_far_ref,
        gate_own_ref,
        up_far_ref,
        normed_ref,
        g_out_ref,
        g_qkv_ref,
        small_ref,
        tokens_ref,
        mixed_ref,
        gain_ref,
        forward_ref,
        moved_ref,
        down_ref,
        gate_ref,
        up_ref,
        input_ref,
        out_ref,
        qkv_ref,
        sums_ref,
        result_ref,
        kept,
        kept_low,
        kept_high,
        normed_own,
        normed_x,
        normed_low,
        normed_high,
        out_own,
        out_x,
        out_low,
        out_high,
        qkv_own,
        qkv_core,
        qkv_chip,
        qkv_sum,
        dealt,
        small_parts,
        small_sum,
        small_held,
        sends,
        recvs,
        locals_,
        deal_sems,
    ):
        me, mine = lax.axis_index("ctx"), lax.axis_index("fsdp")
        x, low, high = lax.rem(me, 2), lax.rem(me // 2, 2), me // 4
        to_x, to_low, to_high = ((flipped(me, bit), mine) for bit in (1, 2, 4))
        core, chip = flipped(mine, 1), flipped(mine, 2)
        diagonal = flipped(core, 2)
        ctx_peers = [(lax.rem(me + step, ctx), mine) for step in range(1, ctx)]
        near = [lax.rem(mine + step, fsdp) for step in range(1, fsdp)]
        greet(ctx_peers + [(me, other) for other in near])
        used, used_local, all_sends, loads = [0], [0], [], {}

        def push(source, target, peer):
            i = used[0]
            used[0] += 1
            copy = send(source, target, sends.at[i], recvs.at[i], peer)
            all_sends.append(copy)
            return copy

        def load(source, target):
            i = used_local[0]
            used_local[0] += 1
            copy = pltpu.make_async_copy(source, target, locals_.at[i])
            copy.start()
            return copy

        def normed_block(a, b, other):
            side = 1 - x if other else x
            block = (high + a - 2 * a * high) * 4 + (low + b - 2 * b * low) * 2 + side
            return normed_ref.at[pl.ds(pl.multiple_of(block * rows, rows), rows), :]

        def out_block(a, b, other):
            side = 1 - x if other else x
            block = (high + a - 2 * a * high) * 4 + (low + b - 2 * b * low) * 2 + side
            return g_out_ref.at[:, pl.ds(pl.multiple_of(block * cols, cols), cols)]

        def qkv_block(index):
            return g_qkv_ref.at[pl.ds(pl.multiple_of(index * part, part), part), :]

        def columns(index):
            return pl.ds(pl.multiple_of(index * small_cols, small_cols), small_cols)

        order = ((1, 1), (0, 1), (1, 0), (0, 0))
        small_copies = [
            push(small_ref.at[:, columns(other)], small_parts.at[i], (me, other))
            for i, other in enumerate(near)
        ]
        normed_copies = {
            ab: push(normed_block(*ab, True), normed_x.at[ab[0], ab[1]], to_x) for ab in order
        }

        low_copies = {
            (2, 0): push(up_low_ref, kept_low.at[2, 0], to_low),
            (0, 0): push(downs_ref.at[0], kept_low.at[0, 0], to_x),
        }
        early = {
            (1, 1): load(gate_far_ref, kept_low.at[1, 1]),
            (2, 1): load(up_far_ref, kept_low.at[2, 1]),
            (1, 0): load(gate_own_ref, kept_low.at[1, 0]),
        }
        kept_loads = {
            place: load(source, kept.at[place])
            for place, source in (
                ((1, 1), gate_high_ref),
                ((2, 1), up_high_ref),
                ((0, 0), downs_ref.at[1]),
                ((1, 0), gate_near_ref),
                ((2, 0), up_near_ref),
            )
        }
        qkv_copies = [
            push(qkv_block(diagonal), qkv_core.at[1], (me, core)),
            push(qkv_block(core), qkv_core.at[0], (me, core)),
        ]
        qkv_loads = [
            load(qkv_block(chip), qkv_own.at[1]),
            load(qkv_block(mine), qkv_own.at[0]),
        ]
        normed_loads = {
            ab: load(normed_block(*ab, False), normed_own.at[ab[0], ab[1]]) for ab in order
        }
        out_loads = {ab: load(out_block(*ab, False), out_own.at[ab[0], ab[1]]) for ab in order}

        total = small_ref[:, columns(mine)]
        for i, copy in enumerate(small_copies):
            copy.wait_recv()
            total = total + small_parts[i]
        small_sum[...] = total
        small_wide = [push(small_sum, small_held.at[i], peer) for i, peer in enumerate(ctx_peers)]

        qkv_copies[0].wait_recv()
        qkv_loads[0].wait()
        add_into(qkv_core.at[1], qkv_own.at[1], qkv_core.at[1])
        chip_copy = push(qkv_core.at[1], qkv_chip, (me, chip))

        def to_low_side(copies, loads, own, from_x, from_low, a):
            copies[a, 1].wait_recv()
            loads[a, 1].wait()
            add_into(from_x.at[a, 1], own.at[a, 1], from_x.at[a, 1])
            return push(from_x.at[a, 1], from_low.at[a], to_low)

        def to_high_side(copies, loads, lows, own, from_x, from_low, from_high):
            copies[1, 0].wait_recv()
            loads[1, 0].wait()
            lows[1].wait_recv()
            add_into(from_x.at[1, 0], own.at[1, 0], from_x.at[1, 0], from_low.at[1])
            return push(from_x.at[1, 0], from_high, to_high)

        def arrived(kind, a):
            if (kind, a) in early:
                early[kind, a].wait()
            else:
                low_copies[kind, a].wait_recv()

        def experts_high(kind):
            arrived(kind, 1)
            kept_loads[kind, 1].wait()
            add_into(kept_low.at[kind, 1], kept.at[kind, 1], kept_low.at[kind, 1])
            return push(kept_low.at[kind, 1], kept_high.at[kind], to_high)

        high_copies = {1: experts_high(1)}
        normed_args = (normed_copies, normed_loads)
        normed_lows = {1: to_low_side(*normed_args, normed_own, normed_x, normed_low, 1)}
        high_copies[2] = experts_high(2)
        normed_lows[0] = to_low_side(*normed_args, normed_own, normed_x, normed_low, 0)
        out_copies = {ab: push(out_block(*ab, True), out_x.at[ab[0], ab[1]], to_x) for ab in order}

        qkv_copies[1].wait_recv()
        qkv_loads[1].wait()
        chip_copy.wait_recv()
        add_into(qkv_sum, qkv_own.at[0], qkv_core.at[0], qkv_chip)

        def deal(kind):
            index = kind * ctx + me
            return pltpu.make_async_remote_copy(
                qkv_sum.at[:, pl.ds(kind * cols, cols)],
                dealt.at[lax.rem(index, kinds)],
                deal_sems.at[0, kind],
                deal_sems.at[1, lax.rem(index, kinds)],
                device_id=(index // kinds, mine),
                device_id_type=MESH,
            )

        def keep(kind):
            return pltpu.make_async_copy(
                qkv_sum.at[:, pl.ds(kind * cols, cols)],
                dealt.at[lax.rem(kind * ctx + me, kinds)],
                deal_sems.at[0, kind],
            )

        def is_far(kind):
            return (kind * ctx + me) // kinds != me

        for kind in range(kinds):
            pl.when(is_far(kind))(deal(kind).start)
            pl.when(jnp.logical_not(is_far(kind)))(keep(kind).start)

        normed_high_copy = to_high_side(
            *normed_args, normed_lows, normed_own, normed_x, normed_low, normed_high
        )
        out_args = (out_copies, out_loads)
        out_lows = {a: to_low_side(*out_args, out_own, out_x, out_low, a) for a in (1, 0)}

        def experts_end(kind):
            arrived(kind, 0)
            kept_loads[kind, 0].wait()
            sources = [kept.at[kind, 0], kept_low.at[kind, 0]]
            if kind > 0:
                high_copies[kind].wait_recv()
                sources.append(kept_high.at[kind])
            add_into((down_ref, gate_ref, up_ref)[kind], *sources)

        experts_end(0)

        normed_copies[0, 0].wait_recv()
        normed_loads[0, 0].wait()
        normed_lows[0].wait_recv()
        normed_high_copy.wait_recv()

        def norm_step(i, carry):
            span = pl.ds(pl.multiple_of(i * 16, 16), 16)
            grad = (
                normed_own[0, 0, span, :].astype(f32)
                + normed_x[0, 0, span, :].astype(f32)
                + normed_low[0, span, :].astype(f32)
                + normed_high[span, :].astype(f32)
            )
            values = tokens_ref[span, :].astype(f32)
            scale = rms_unit(values)
            unit = values * scale
            pulled = grad * gain_ref[...]
            input_ref[span, :] = mixed_ref[span, :] + scale * (
                pulled - unit * jnp.mean(unit * pulled, axis=-1, keepdims=True)
            )
            result_ref[span, :] = (forward_ref[span, :] + moved_ref[span, :].astype(f32)).astype(bf16)
            return carry

        lax.fori_loop(0, rows // 16, norm_step, 0)

        out_high_copy = to_high_side(*out_args, out_lows, out_own, out_x, out_low, out_high)
        experts_end(1)

        total = small_sum[...]
        for i, copy in enumerate(small_wide):
            copy.wait_recv()
            total = total + small_held[i]
        sums_ref[...] = total

        for kind in range(kinds):
            pl.when(is_far(kind))(deal(kind).wait_send)
            pl.when(jnp.logical_not(is_far(kind)))(keep(kind).wait)
        for slot in range(kinds):

            @pl.when(lax.rem(me * kinds + slot, ctx) != me)
            def _():
                pltpu.make_async_copy(
                    dealt.at[slot], dealt.at[slot], deal_sems.at[1, slot]
                ).wait()

            add_into(qkv_ref.at[:, pl.ds(slot * cols, cols)], dealt.at[slot])

        out_copies[0, 0].wait_recv()
        out_loads[0, 0].wait()
        out_lows[0].wait_recv()
        out_high_copy.wait_recv()
        add_into(out_ref, out_own.at[0, 0], out_x.at[0, 0], out_low.at[0], out_high)
        experts_end(2)
        for copy in all_sends:
            copy.wait_send()

    def block(*shape):
        return pltpu.VMEM(shape, bf16)

    gradient = (experts, units, cols)
    return comm_call(
        kernel,
        "finish_sums",
        collective_id,
        [
            jax.ShapeDtypeStruct(gradient, f32),
            jax.ShapeDtypeStruct(gradient, f32),
            jax.ShapeDtypeStruct(gradient, f32),
            jax.ShapeDtypeStruct((rows, width), f32),
            jax.ShapeDtypeStruct((part, cols), f32),
            jax.ShapeDtypeStruct((part, kinds * cols), f32),
            jax.ShapeDtypeStruct((small_rows, small_cols), f32),
            jax.ShapeDtypeStruct((rows, width), bf16),
        ],
        [ANY] * 12 + [VMEM] * 6,
        [VMEM] * 8,
        [
            block(kinds, 2, *gradient),
            block(kinds, 2, *gradient),
            block(kinds, *gradient),
            block(2, 2, rows, width),
            block(2, 2, rows, width),
            block(2, rows, width),
            block(rows, width),
            block(2, 2, part, cols),
            block(2, 2, part, cols),
            block(2, part, cols),
            block(part, cols),
            block(2, part, kinds * cols),
            block(2, part, kinds * cols),
            block(part, kinds * cols),
            block(part, kinds * cols),
            block(kinds, part, cols),
            pltpu.VMEM((fsdp - 1, small_rows, small_cols), f32),
            pltpu.VMEM((small_rows, small_cols), f32),
            pltpu.VMEM((ctx - 1, small_rows, small_cols), f32),
            DMA((copies_most,)),
            DMA((copies_most,)),
            DMA((32,)),
            DMA((2, kinds)),
        ],
        700 * 2**20,
        56,
    )(
        downs,
        *ups,
        gate_far,
        gate_own,
        up_far,
        normed_part,
        out_part,
        qkv_part,
        small,
        tokens,
        mixed_grad,
        gain,
        mixed,
        moved,
    )


def gather_inputs(tokens, w_qkv, dy, row_arrays, block, flips, collective_id):
    ctx, fsdp = lax.axis_size("ctx"), lax.axis_size("fsdp")
    rows, width = tokens.shape
    part = w_qkv.shape[0]
    kinds = 3
    cols = width // ctx
    line = ctx // 2
    chunks = 2
    size = rows // chunks
    row_count, flip_count = len(row_arrays), len(flips)
    small_count = row_count + 1

    def kernel(*refs):
        tokens_ref, w_qkv_ref, dy_ref = refs[:3]
        small_refs = refs[3 : 3 + small_count]
        all_ref, weight_ref, dy_all_ref = refs[3 + small_count : 6 + small_count]
        small_all_refs = refs[6 + small_count : 6 + 2 * small_count]
        refs = refs[6 + 2 * small_count :]
        run_kernel(
            tokens_ref,
            w_qkv_ref,
            dy_ref,
            small_refs,
            all_ref,
            weight_ref,
            dy_all_ref,
            small_all_refs,
            *refs,
        )

    def run_kernel(
        tokens_ref,
        w_qkv_ref,
        dy_ref,
        small_refs,
        all_ref,
        weight_ref,
        dy_all_ref,
        small_all_refs,
        *refs,
    ):
        flip_refs, dy_line_ref, refs = refs[:flip_count], refs[flip_count], refs[flip_count + 1 :]
        stage, weight_stage, dy_stage, sends, recvs, line_send, line_recv, cross_send, cross_recv, *refs = refs
        local_sems, line_out, cross_out = refs
        me, mine = lax.axis_index("ctx"), lax.axis_index("fsdp")
        z, x = me // 2, lax.rem(me, 2)
        to_x = (flipped(me, 1), mine)
        core, chip = (me, flipped(mine, 1)), (me, flipped(mine, 2))
        others = [flipped_by(me, flip) for flip in flips]
        greet(
            [(lax.rem(me + step, ctx), mine) for step in range(1, ctx)]
            + [(me, lax.rem(mine + step, fsdp)) for step in range(1, fsdp)]
            + [(other, lax.rem(mine + step, fsdp)) for other in others for step in range(1, fsdp)]
        )
        used, used_local, started, kept = [0], [0], [], []

        def push(source, target, peer):
            i = used[0]
            used[0] += 1
            copy = send(source, target, sends.at[i], recvs.at[i], peer)
            started.append(copy)
            return copy

        def load(source, target):
            i = used_local[0]
            used_local[0] += 1
            copy = pltpu.make_async_copy(source, target, local_sems.at[i])
            copy.start()
            kept.append(copy)

        def token_block(index):
            return all_ref.at[pl.ds(pl.multiple_of(index * rows, rows), rows), :]

        def token_chunk(index, chunk):
            start = pl.multiple_of(index * rows + chunk * size, size)
            return stage.at[pl.ds(start, size), :]

        def put(away, side, chunk, crossed):
            index = 2 * (z - away if side == 0 else z + away) + (1 - x if crossed else x)
            start = pl.multiple_of(index * rows + chunk * size, size)
            return pltpu.make_async_copy(
                stage.at[pl.ds(start, size), :],
                all_ref.at[pl.ds(start, size), :],
                (cross_out if crossed else line_out).at[side * line + away, chunk],
            )

        def taken(own, index, chunk):
            return tokens_ref.at[pl.ds(chunk * size, size), :] if own else token_chunk(index, chunk)

        def by_part(ref, index, count):
            return ref.at[pl.ds(pl.multiple_of(index * count, count), count), :]

        def cross(away, side, chunk):
            index = 2 * (z - away if side == 0 else z + away) + x
            i = side * line + away
            return pltpu.make_async_remote_copy(
                taken(away == 0, index, chunk),
                token_chunk(index, chunk),
                cross_send.at[i, chunk],
                cross_recv.at[i, chunk],
                device_id=to_x,
                device_id_type=MESH,
            )

        def along(away, side, chunk):
            index = 2 * (z - away if side == 0 else z + away) + x
            i = side * line + away
            return pltpu.make_async_remote_copy(
                taken(away == 0, index, chunk),
                token_chunk(index, chunk),
                line_send.at[i, chunk],
                line_recv.at[i, chunk],
                device_id=(me + 2 if side == 0 else me - 2, mine),
                device_id_type=MESH,
            )

        def has(away, side):
            return z >= away if side == 0 else z + away < line

        def goes_on(away, side):
            return jnp.logical_and(has(away, side), z < line - 1 if side == 0 else z > 0)

        for chunk in range(chunks):
            for side in range(2):
                pl.when(goes_on(0, side))(along(0, side, chunk).start)
            cross(0, 0, chunk).start()
        load(tokens_ref, token_block(me))

        own_weight = by_part(weight_stage, mine, part)
        pieces = []
        for kind in range(kinds):
            column = pl.ds(pl.multiple_of(kind * width + me * cols, cols), cols)
            target = own_weight.at[:, pl.ds(kind * cols, cols)]
            pieces.append(
                pltpu.make_async_copy(w_qkv_ref.at[:, column], target, local_sems.at[23 - kind])
            )
            pieces[-1].start()
        load(dy_ref, dy_stage)
        dy_loaded = kept.pop()
        for piece in pieces:
            piece.wait()
        weight_chip = [push(own_weight, own_weight, chip)]
        weight_core = [push(own_weight, own_weight, core)]
        load(own_weight, by_part(weight_ref, mine, part))
        columns = pl.ds(pl.multiple_of(mine * part, part), part)
        for i, (source, target) in enumerate(zip(small_refs, small_all_refs)):
            if i < row_count:
                target = target.at[:, columns]
            else:
                target = target.at[mine]
            for step in range(1, fsdp):
                push(source, target, (me, lax.rem(mine + step, fsdp)))
            load(source, target)
        dy_chip = push(dy_ref, by_part(dy_all_ref, mine, rows), chip)
        push(dy_ref, by_part(dy_all_ref, mine, rows), core)
        load(dy_ref, by_part(dy_all_ref, mine, rows))

        for away in range(1, line):
            for chunk in range(chunks):
                for side in range(2):

                    @pl.when(has(away, side))
                    def _():
                        index = 2 * (z - away if side == 0 else z + away) + x
                        pltpu.make_async_copy(
                            taken(True, index, chunk),
                            token_chunk(index, chunk),
                            line_recv.at[side * line + away - 1, chunk],
                        ).wait()
                        cross(away, side, chunk).start()
                        put(away, side, chunk, False).start()

                    if away < line - 1:
                        pl.when(goes_on(away, side))(along(away, side, chunk).start)
        for other, target in zip(others, flip_refs):
            for step in range(fsdp):
                push(small_refs[-1], target.at[mine], (other, lax.rem(mine + step, fsdp)))
        dy_loaded.wait()
        for i in range(line):
            wide = 2 * cols
            to = flipped_by(me, 2 * i)
            source = dy_stage.at[:, pl.ds(pl.multiple_of(to // 2 * wide, wide), wide)]
            if i == 0:
                load(source, dy_line_ref.at[0])
            else:
                push(source, dy_line_ref.at[i], (to, mine))

        for copy in weight_chip:
            copy.wait_recv()
        far = by_part(weight_stage, flipped(mine, 2), part)
        weight_far = push(far, far, core)
        load(far, by_part(weight_ref, flipped(mine, 2), part))
        for copy in weight_core:
            copy.wait_recv()
        near = flipped(mine, 1)
        load(by_part(weight_stage, near, part), by_part(weight_ref, near, part))
        dy_chip.wait_recv()
        far = by_part(dy_all_ref, flipped(mine, 2), rows)
        push(far, far, core)
        every = [(side, chunk) for side in range(2) for chunk in range(chunks)]
        weight_far.wait_recv()
        far = flipped_by(mine, 3)
        load(by_part(weight_stage, far, part), by_part(weight_ref, far, part))
        for chunk in range(chunks):
            cross(0, 0, chunk).wait_recv()
            put(0, 0, chunk, True).start()
        for away in range(1, line):
            for side, chunk in every:

                @pl.when(has(away, side))
                def _():
                    cross(away, side, chunk).wait_recv()
                    put(away, side, chunk, True).start()

        for copy in started:
            if not any(copy is other for other in [dy_chip, weight_far] + weight_chip + weight_core):
                copy.wait_recv()
        for copy in kept:
            copy.wait()
        for copy in started:
            copy.wait_send()
        for chunk in range(chunks):
            cross(0, 0, chunk).wait_send()
        for chunk in range(chunks):
            put(0, 0, chunk, True).wait()
        for away in range(1, line):
            for side, chunk in every:

                @pl.when(has(away, side))
                def _():
                    put(away, side, chunk, False).wait()
                    put(away, side, chunk, True).wait()

        for away in range(line - 1):
            for side, chunk in every:
                pl.when(goes_on(away, side))(along(away, side, chunk).wait_send)
        for away in range(1, line):
            for side, chunk in every:
                pl.when(has(away, side))(cross(away, side, chunk).wait_send)

    return comm_call(
        kernel,
        "gather_inputs",
        collective_id,
        [
            jax.ShapeDtypeStruct((ctx * rows, width), tokens.dtype),
            jax.ShapeDtypeStruct((fsdp * part, kinds * cols), w_qkv.dtype),
            jax.ShapeDtypeStruct((fsdp * rows, width), dy.dtype),
        ]
        + [jax.ShapeDtypeStruct((row.shape[0], fsdp * part), row.dtype) for row in row_arrays]
        + [jax.ShapeDtypeStruct((fsdp,) + block.shape, block.dtype)] * (1 + flip_count)
        + [jax.ShapeDtypeStruct((line, rows, 2 * cols), dy.dtype)],
        [ANY] * (3 + small_count),
        [ANY] * (4 + small_count + flip_count),
        [
            pltpu.VMEM((ctx * rows, width), tokens.dtype),
            pltpu.VMEM((fsdp * part, kinds * cols), w_qkv.dtype),
            pltpu.VMEM((rows, width), dy.dtype),
            DMA((64,)),
            DMA((64,)),
            DMA((2 * line, chunks)),
            DMA((2 * line, chunks)),
            DMA((2 * line, chunks)),
            DMA((2 * line, chunks)),
            DMA((24,)),
            DMA((2 * line, chunks)),
            DMA((2 * line, chunks)),
        ],
        150 * 2**20,
        60,
    )(tokens, w_qkv, dy, *row_arrays, block)


def project(tokens, gain, weight):
    total, width = tokens.shape
    wide = weight.shape[1]
    cols = wide // 3
    size = math.gcd(total, 256)
    f32 = jnp.float32

    def kernel(tokens_ref, gain_ref, weight_ref, normed_ref, lin_ref, squares_ref):
        values = tokens_ref[...].astype(f32)
        normed = (values * rms_unit(values) * gain_ref[...]).astype(jnp.bfloat16)
        normed_ref[...] = normed
        lin = jnp.dot(normed, weight_ref[...], preferred_element_type=f32)
        lin_ref[...] = lin
        for kind in range(2):
            piece = lin[:, kind * cols : (kind + 1) * cols]
            squares_ref[:, kind : kind + 1] = jnp.sum(piece * piece, axis=1, keepdims=True)

    def by_rows(columns):
        return pl.BlockSpec((size, columns), lambda i: (i, 0))

    return pl.pallas_call(
        kernel,
        grid=(total // size,),
        out_shape=[
            jax.ShapeDtypeStruct((total, width), jnp.bfloat16),
            jax.ShapeDtypeStruct((total, wide), f32),
            jax.ShapeDtypeStruct((total, 2), f32),
        ],
        in_specs=[
            by_rows(width),
            pl.BlockSpec((1, width), lambda i: (0, 0)),
            pl.BlockSpec((width, wide), lambda i: (0, 0)),
        ],
        out_specs=[by_rows(width), by_rows(wide), by_rows(2)],
        compiler_params=pltpu.CompilerParams(vmem_limit_bytes=60 * 2**20),
        cost_estimate=pl.CostEstimate(
            flops=3 * 10**9, bytes_accessed=15 * 2**20, transcendentals=0
        ),
        name="project",
    )(tokens, gain, weight)


def project_back(back, projected, scales, inner_sums, value_grad, weight, normed, tokens):
    total, width = tokens.shape
    wide = weight.shape[1]
    cols = wide // 3
    size = math.gcd(total, 256)
    steps, runs = total // size, 4
    f32, bf16 = jnp.float32, jnp.bfloat16

    def kernel(
        back_ref,
        lin_ref,
        scales_ref,
        sums_ref,
        value_ref,
        weight_ref,
        normed_ref,
        tokens_ref,
        part_ref,
        g_qkv_ref,
        gain_ref,
        proj,
    ):
        i = pl.program_id(0)

        @pl.when(i == 0)
        def _():
            gain_ref[...] = jnp.zeros_like(gain_ref)

        @pl.when(i < steps)
        def _():
            pieces = []
            for kind in range(2):
                scale = scales_ref[:, kind : kind + 1]
                unit = lin_ref[:, kind * cols : (kind + 1) * cols] * scale
                grad = scale * (back_ref[kind] - unit * sums_ref[:, kind : kind + 1])
                pieces.append(grad.astype(bf16))
            grads = jnp.concatenate(pieces + [value_ref[...]], axis=1)
            proj[pl.ds(pl.multiple_of(i * size, size), size), :] = grads
            part = lax.dot_general(
                grads, weight_ref[...], (((1,), (1,)), ((), ())), preferred_element_type=f32
            )
            values = tokens_ref[...].astype(f32)
            gain_ref[...] += jnp.sum(part * (values * rms_unit(values)), axis=0, keepdims=True)
            part_ref[...] = part.astype(bf16)

        @pl.when(i >= steps)
        def _():
            g_qkv_ref[...] = lax.dot_general(
                normed_ref[...], proj[...], (((0,), (0,)), ((), ())), preferred_element_type=f32
            ).astype(bf16)

    def by_rows(columns):
        return pl.BlockSpec((size, columns), lambda i: (jnp.minimum(i, steps - 1), 0))

    def later(i):
        return jnp.maximum(i - steps, 0)

    return pl.pallas_call(
        kernel,
        grid=(steps + runs,),
        out_shape=[
            jax.ShapeDtypeStruct((total, width), bf16),
            jax.ShapeDtypeStruct((width, wide), bf16),
            jax.ShapeDtypeStruct((1, width), f32),
        ],
        in_specs=[
            pl.BlockSpec((2, size, cols), lambda i: (0, jnp.minimum(i, steps - 1), 0)),
            by_rows(2 * cols),
            by_rows(2),
            by_rows(2),
            by_rows(cols),
            pl.BlockSpec((width, wide), lambda i: (0, 0)),
            pl.BlockSpec((total, width // runs), lambda i: (0, later(i))),
            by_rows(width),
        ],
        out_specs=[
            by_rows(width),
            pl.BlockSpec((width // runs, wide), lambda i: (later(i), 0)),
            pl.BlockSpec((1, width), lambda i: (0, 0)),
        ],
        scratch_shapes=[pltpu.VMEM((total, wide), bf16)],
        compiler_params=pltpu.CompilerParams(vmem_limit_bytes=60 * 2**20),
        cost_estimate=pl.CostEstimate(flops=0, bytes_accessed=2**20, transcendentals=0),
        name="project_back",
    )(back, projected, scales, inner_sums, value_grad, weight, normed, tokens)


def on_device_heads(
    tokens,
    doc_lengths,
    routes,
    slot_order,
    attn_gain,
    w_qkv,
    q_gain,
    k_gain,
    w_out,
    ffn_gain,
    w_router,
    w_gate,
    w_up,
    w_down,
    cotangent,
):
    rows, width = tokens.shape[1], tokens.shape[2]
    ctx, fsdp = lax.axis_size("ctx"), lax.axis_size("fsdp")
    me = lax.axis_index("ctx")
    head_dim = width // HEADS
    cols = HEADS // ctx * head_dim
    part = width // fsdp
    total = rows * ctx
    lengths = doc_lengths[0]
    bf16, f32 = jnp.bfloat16, jnp.float32

    experts, top = w_gate.shape[0], routes.shape[2]
    gains = jnp.concatenate([attn_gain, q_gain, k_gain, ffn_gain]).reshape(4, part)
    router_rows = jnp.pad(w_router.T, ((0, ROUTER_ROWS - experts), (0, 0)))
    pairs = jnp.concatenate([routes[0].T, slot_order[0].T], axis=0)
    pairs = jnp.pad(pairs, ((0, -pairs.shape[0] % 8), (0, 0)))
    tokens_all, qkv_weight, dy_all, gains, router_rows, *slots, dy_parts = gather_inputs(
        tokens[0],
        w_qkv,
        cotangent[0],
        [gains, router_rows],
        slots_of(pairs, experts, top),
        [1, 2, 4, 6],
        9,
    )
    row_gain_one, gain_query, gain_key, row_gain_two = (
        gains[i : i + 1].astype(f32) for i in range(4)
    )
    flips = [0, 2, 4, 6]
    dy_parts = lax.all_gather(dy_parts, "fsdp", axis=0)

    stream_pos = dealt_position(jnp.arange(total, dtype=jnp.int32), rows, ctx)
    stream_inner = document_info(stream_pos, lengths)[1]
    cosine, sine_part = rope_tables(stream_inner, head_dim)
    turn_tables = (
        jnp.concatenate([cosine, cosine], axis=1),
        jnp.concatenate([-sine_part, sine_part], axis=1),
    )
    places = jnp.arange(total, dtype=jnp.int32)
    sight = (
        (places - document_info(places, lengths)[1]).reshape(total, 1),
        places.reshape(total, 1),
        places.reshape(1, total),
    )
    normed_all, projected, squares = project(tokens_all, row_gain_one, qkv_weight)
    squares = squares.T
    squares = ctx_sum(squares.reshape(-1, 128), 1).reshape(2, total)
    scales = lax.rsqrt(squares / width + EPSILON).T
    own_gains = [
        lax.dynamic_slice_in_dim(gain, me * cols, cols, 1) for gain in (gain_query, gain_key)
    ]
    own_gains = jnp.concatenate(own_gains, axis=1)
    low, attended, attended_low, tops = attend(
        projected, scales, own_gains, *turn_tables, *sight, cols
    )

    attended_part = heads_to_rows(attended_low, 2)
    mixed_part = dot32("td,de->te", attended_part, w_out).astype(bf16)
    inputs = tokens[0].astype(f32)
    group, mixed, crossed = reduce_then_gather(
        mixed_part,
        [tokens[0], row_gain_two],
        [jax.ShapeDtypeStruct((rows, width), f32)],
        norm_chunk,
        "mix_and_norm",
        6,
        True,
        [],
        16,
    )

    capacity = rows * top // experts
    slot_by_expert, slots_other, *slots_line = slots
    moved_part, group_grad, g_router, scaled, gate_low, up_low = run_experts(
        group, dy_all, slot_by_expert, router_rows, w_gate, w_up, w_down, fsdp, capacity
    )
    scaled_line = [scaled] + [swap(scaled, flip) for flip in flips[1:]]
    mixed_all, mixed_grad, g_ffn_gain, gate_other, up_other = reduce_then_gather(
        group_grad,
        [mixed, row_gain_two, cotangent[0]],
        [jax.ShapeDtypeStruct((rows, width), f32), jax.ShapeDtypeStruct((1, width), f32)],
        norm_back_chunk,
        "norm_back",
        7,
        False,
        [gate_low, up_low],
        60,
    )
    g_ffn_gain = g_ffn_gain[0]
    crossed = lax.all_gather(crossed, "fsdp", axis=0, tiled=True)
    ups = expert_grads(
        [gate_low, up_low], [gate_other, up_other], group, crossed, slot_by_expert, slots_other, capacity
    )
    ups, mixed_all = lax.optimization_barrier((ups, mixed_all))
    output_part = dot32("te,de->td", mixed_all, w_out).astype(bf16)
    output_grad = rows_to_heads(output_part, 3)
    output_grad, moved_part, ups, mixed_all, scaled_line = lax.optimization_barrier(
        (output_grad, moved_part, ups, mixed_all, scaled_line)
    )
    moved = lax.psum_scatter(moved_part, "fsdp", scatter_dimension=0, tiled=True)
    gate_far, gate_own = swap(ups[3], 2), swap(ups[2], 2)
    downs = down_grads(scaled_line, dy_parts, [slot_by_expert] + slots_line, capacity)
    g_out = dot32("td,te->de", attended_part, mixed_all).astype(bf16)
    output_grad, ups, downs, g_out = lax.optimization_barrier((output_grad, ups, downs, g_out))

    back, value_grad, own_g_gains, inner_sums = attend_back(
        output_grad, low, attended, tops, projected, scales, own_gains, *turn_tables, *sight
    )
    inner_sums, gate_far = lax.optimization_barrier((inner_sums, gate_far))
    inner_sums = ctx_sum(inner_sums.T.reshape(-1, 128), 1)
    inner_sums, ups, gate_own = lax.optimization_barrier((inner_sums, ups, gate_own))
    up_far = swap(ups[7], 2)
    inner_sums = inner_sums.reshape(2, total).T / width

    normed_grad_part, g_qkv, g_attn_gain = project_back(
        back, projected, scales, inner_sums, value_grad, qkv_weight, normed_all, tokens_all
    )
    g_attn_gain = g_attn_gain[0]

    def placed_cols(values):
        return lax.dynamic_update_slice_in_dim(jnp.zeros((width,), f32), values, me * cols, 0)

    sums = jnp.concatenate(
        [
            jnp.stack([g_attn_gain, placed_cols(own_g_gains[0, 0]), placed_cols(own_g_gains[1, 0]), g_ffn_gain]),
            g_router[:experts],
        ],
        axis=0,
    )
    down_parts, gate_parts, up_parts, input_grad, out_part, qkv_part, sums, activations = finish_sums(
        downs,
        ups[0:2] + ups[4:7],
        gate_far,
        gate_own,
        up_far,
        normed_grad_part,
        g_out,
        g_qkv,
        jnp.pad(sums, ((0, -sums.shape[0] % 8), (0, 0))),
        tokens[0],
        mixed_grad,
        row_gain_one,
        mixed,
        moved,
        8,
    )
    return (
        activations[None],
        input_grad[None],
        sums[0],
        qkv_part,
        sums[1],
        sums[2],
        out_part,
        sums[3],
        sums[4 : 4 + experts].T,
        gate_parts,
        up_parts,
        down_parts,
    )


def solution(mesh):
    in_specs = (
        P("fsdp", "ctx", None),
        P("fsdp", None),
        P("fsdp", "ctx", None),
        P("fsdp", "ctx", None),
        P("fsdp"),
        P("fsdp", None),
        P("fsdp"),
        P("fsdp"),
        P("fsdp", None),
        P("fsdp"),
        P("fsdp", None),
        P(None, None, "fsdp"),
        P(None, None, "fsdp"),
        P(None, "fsdp", None),
        P("fsdp", "ctx", None),
    )
    out_specs = (
        P("fsdp", "ctx", None),
        P("fsdp", "ctx", None),
        P("fsdp"),
        P("fsdp", "ctx"),
        P("fsdp"),
        P("fsdp"),
        P("fsdp", "ctx"),
        P("fsdp"),
        P("fsdp", None),
        P(None, "ctx", "fsdp"),
        P(None, "ctx", "fsdp"),
        P(None, "fsdp", "ctx"),
    )
    ctx, fsdp = mesh.shape["ctx"], mesh.shape["fsdp"]
    by_heads = HEADS % ctx == 0 and ctx == 8 and fsdp == 4
    body = on_device_heads if by_heads else on_device
    return jax.shard_map(
        body, mesh=mesh, in_specs=in_specs, out_specs=out_specs, check_vma=False
    )
```

```python
import math

import jax
import jax.numpy as jnp
from jax import lax
from jax.experimental import pallas as pl
from jax.experimental.pallas import tpu as pltpu
from jax.sharding import PartitionSpec as P

HEADS = 16
MESH = pl.DeviceIdType.MESH
ANY = pl.BlockSpec(memory_space=pl.ANY)
VMEM = pl.BlockSpec(memory_space=pltpu.VMEM)
DMA = pltpu.SemaphoreType.DMA

EPSILON = 1e-05
ROPE_BASE = 10000.0
MASKED = -1e30


def rms_scale(values, gain_vector):
    return (
        values
        * lax.rsqrt(jnp.mean(values * values, axis=-1, keepdims=True) + EPSILON)
        * gain_vector
    )


def rotate(values, inner_pos):
    half_dim = values.shape[-1] // 2
    freq_table = ROPE_BASE ** (-2.0 * jnp.arange(half_dim, dtype=jnp.float32) / values.shape[-1])
    angles = inner_pos.astype(jnp.float32)[:, None] * freq_table[None, :]
    cosine = jnp.cos(angles)[:, None, :]
    sine_part = jnp.sin(angles)[:, None, :]
    first_half = values[..., :half_dim]
    second_half = values[..., half_dim:]
    return jnp.concatenate(
        [
            first_half * cosine - second_half * sine_part,
            second_half * cosine + first_half * sine_part,
        ],
        axis=-1,
    )


def dealt_position(flat_index, per_device, device_count):
    device_index = flat_index // per_device
    within = flat_index % per_device
    half_rows = per_device // 2
    return jnp.where(
        within < half_rows,
        device_index * half_rows + within,
        (2 * device_count - 1 - device_index) * half_rows + within - half_rows,
    )


def document_info(positions, lengths):
    doc_ends = jnp.sum(jnp.where(jnp.arange(lengths.shape[0])[:, None] >= jnp.arange(lengths.shape[0])[None, :], lengths[None, :], 0), axis=1)
    passed = doc_ends[None, :] <= positions[:, None]
    doc_ids = jnp.sum(passed.astype(jnp.int32), axis=1)
    inner_pos = positions - jnp.sum(jnp.where(passed, lengths[None, :], 0), axis=1)
    return (doc_ids, inner_pos)


def slot_table(route_ids, order_ids, capacity, expert_count):
    pair_count = route_ids.shape[0] * route_ids.shape[1]
    expert_flat = route_ids.reshape(pair_count)
    rank_flat = order_ids.reshape(pair_count)
    earlier = (expert_flat[None, :] == expert_flat[:, None]) & (
        rank_flat[None, :] < rank_flat[:, None]
    )
    slot_index = jnp.sum(earlier.astype(jnp.int32), axis=1)
    placed = jnp.where(
        slot_index < capacity, expert_flat * capacity + slot_index, expert_count * capacity
    )
    source = (
        jnp.full((expert_count * capacity + 1,), pair_count, jnp.int32)
        .at[placed]
        .set(jnp.arange(pair_count, dtype=jnp.int32))
    )
    return (placed, source[: expert_count * capacity])


def masked_scores(query_block, key_block, query_pos, query_doc, key_pos, key_doc, score_scale):
    scores = (
        jnp.einsum("qhd,khd->hqk", query_block, key_block, preferred_element_type=jnp.float32)
        * score_scale
    )
    allowed = (query_doc[:, None] == key_doc[None, :]) & (key_pos[None, :] <= query_pos[:, None])
    return jnp.where(allowed[None], scores, MASKED)


def silu_parts(hidden_grad, slot_gate, slot_up):
    sigma = jax.nn.sigmoid(slot_gate)
    gate_grad_low = (hidden_grad * slot_up * sigma * (1.0 + slot_gate * (1.0 - sigma))).astype(
        jnp.bfloat16
    )
    up_grad_low = (hidden_grad * slot_gate * sigma).astype(jnp.bfloat16)
    return (gate_grad_low, up_grad_low)


def on_device(
    tokens,
    doc_lengths,
    routes,
    slot_order,
    attn_gain,
    w_qkv,
    q_gain,
    k_gain,
    w_out,
    ffn_gain,
    w_router,
    w_gate,
    w_up,
    w_down,
    cotangent,
):
    row_count = tokens.shape[1]
    model_width = tokens.shape[2]
    head_count = HEADS
    head_dim = model_width // head_count
    score_scale = head_dim ** (-0.5)
    ctx_count = lax.axis_size("ctx")
    ctx_index = lax.axis_index("ctx")
    total_rows = row_count * ctx_count
    lengths = doc_lengths[0]
    local_pos = dealt_position(
        ctx_index * row_count + jnp.arange(row_count, dtype=jnp.int32), row_count, ctx_count
    )
    local_doc, local_inner = document_info(local_pos, lengths)
    stream_pos = dealt_position(jnp.arange(total_rows, dtype=jnp.int32), row_count, ctx_count)
    stream_doc, stream_inner = document_info(stream_pos, lengths)
    block_rows = math.gcd(total_rows, 512)
    block_count = total_rows // block_rows
    block_ids = jnp.arange(block_count, dtype=jnp.int32)
    gain_one, qkv_weight, gain_query, gain_key, out_weight = (
        lax.all_gather(attn_gain, "fsdp", axis=0, tiled=True),
        lax.all_gather(w_qkv, "fsdp", axis=0, tiled=True),
        lax.all_gather(q_gain, "fsdp", axis=0, tiled=True),
        lax.all_gather(k_gain, "fsdp", axis=0, tiled=True),
        lax.all_gather(w_out, "fsdp", axis=0, tiled=True),
    )
    gain_two, router_weight, gate_weight, up_weight, down_weight = (
        lax.all_gather(ffn_gain, "fsdp", axis=0, tiled=True),
        lax.all_gather(w_router, "fsdp", axis=0, tiled=True),
        lax.all_gather(w_gate, "fsdp", axis=2, tiled=True),
        lax.all_gather(w_up, "fsdp", axis=2, tiled=True),
        lax.all_gather(w_down, "fsdp", axis=1, tiled=True),
    )
    inputs = tokens[0].astype(jnp.float32)
    normed_f, norm_one_pull = jax.vjp(rms_scale, inputs, gain_one.astype(jnp.float32))
    normed_low = normed_f.astype(jnp.bfloat16)
    projected = jnp.dot(normed_low, qkv_weight, preferred_element_type=jnp.float32)
    query_lin = projected[:, :model_width]
    key_lin = projected[:, model_width : 2 * model_width]
    value_low = (
        projected[:, 2 * model_width :]
        .astype(jnp.bfloat16)
        .reshape(row_count, head_count, head_dim)
    )

    def head_shape(values, gain_vector):
        return rotate(
            rms_scale(values, gain_vector).reshape(row_count, head_count, head_dim), local_inner
        )

    query_f, query_pull = jax.vjp(head_shape, query_lin, gain_query.astype(jnp.float32))
    key_f, key_pull = jax.vjp(head_shape, key_lin, gain_key.astype(jnp.float32))
    query_low = query_f.astype(jnp.bfloat16)
    key_low = key_f.astype(jnp.bfloat16)
    keys_all, values_all = (
        lax.all_gather(key_low, "ctx", axis=0, tiled=True),
        lax.all_gather(value_low, "ctx", axis=0, tiled=True),
    )

    def key_slice(block_index):
        first_row = block_index * block_rows
        return (
            lax.dynamic_slice_in_dim(keys_all, first_row, block_rows, 0),
            lax.dynamic_slice_in_dim(values_all, first_row, block_rows, 0),
            lax.dynamic_slice_in_dim(stream_pos, first_row, block_rows, 0),
            lax.dynamic_slice_in_dim(stream_doc, first_row, block_rows, 0),
        )

    def stats_step(carry, block_index):
        running_top, running_total = carry
        key_block, value_block, key_pos, key_doc = key_slice(block_index)
        scores = masked_scores(
            query_low, key_block, local_pos, local_doc, key_pos, key_doc, score_scale
        )
        new_top = jnp.maximum(running_top, jnp.max(scores, axis=-1))
        running_total = running_total * jnp.exp(running_top - new_top) + jnp.sum(
            jnp.exp(scores - new_top[..., None]), axis=-1
        )
        return ((new_top, running_total), None)

    start_stats = (
        jnp.full((head_count, row_count), MASKED, jnp.float32),
        jnp.zeros((head_count, row_count), jnp.float32),
    )
    (score_top, score_total), _ = lax.scan(stats_step, start_stats, block_ids)
    log_total = score_top + jnp.log(score_total)

    def output_step(accum, block_index):
        key_block, value_block, key_pos, key_doc = key_slice(block_index)
        scores = masked_scores(
            query_low, key_block, local_pos, local_doc, key_pos, key_doc, score_scale
        )
        prob_block = jnp.exp(scores - log_total[..., None]).astype(jnp.bfloat16)
        return (
            accum
            + jnp.einsum(
                "hqk,khd->qhd", prob_block, value_block, preferred_element_type=jnp.float32
            ),
            None,
        )

    attended_f, _ = lax.scan(
        output_step, jnp.zeros((row_count, head_count, head_dim), jnp.float32), block_ids
    )
    attended_low = attended_f.reshape(row_count, model_width).astype(jnp.bfloat16)
    mixed = inputs + jnp.dot(attended_low, out_weight, preferred_element_type=jnp.float32)
    normed_two_f, norm_two_pull = jax.vjp(rms_scale, mixed, gain_two.astype(jnp.float32))
    normed_two = normed_two_f.astype(jnp.bfloat16)
    expert_count = gate_weight.shape[0]
    route_ids = routes[0]
    top_count = route_ids.shape[1]
    pair_count = row_count * top_count
    capacity = pair_count // expert_count
    logits = jnp.dot(normed_two, router_weight, preferred_element_type=jnp.float32)
    router_probs = jax.nn.softmax(logits, axis=-1)
    chosen = (
        route_ids[:, :, None] == jnp.arange(expert_count, dtype=jnp.int32)[None, None, :]
    ).astype(jnp.float32)
    gate_values = jnp.sum(chosen * router_probs[:, None, :], axis=-1)
    placed, source = slot_table(route_ids, slot_order[0], capacity, expert_count)
    padded_in = jnp.concatenate([normed_two, jnp.zeros((1, model_width), jnp.bfloat16)], axis=0)
    expert_in = padded_in[source // top_count].reshape(expert_count, capacity, model_width)
    gate_pre = jnp.einsum(
        "ecd,edh->ech", expert_in, gate_weight, preferred_element_type=jnp.float32
    )
    up_pre = jnp.einsum("ecd,edh->ech", expert_in, up_weight, preferred_element_type=jnp.float32)
    hidden_low = (jax.nn.silu(gate_pre) * up_pre).astype(jnp.bfloat16)
    expert_out = jnp.einsum(
        "ech,ehd->ecd", hidden_low, down_weight, preferred_element_type=jnp.float32
    )
    out_padded = jnp.concatenate(
        [
            expert_out.reshape(expert_count * capacity, model_width),
            jnp.zeros((1, model_width), jnp.float32),
        ],
        axis=0,
    )
    per_pair = out_padded[placed].reshape(row_count, top_count, model_width)
    layer_out = mixed + jnp.sum(gate_values[:, :, None] * per_pair, axis=1)
    out_grad = cotangent[0].astype(jnp.float32)
    gate_grad = jnp.sum(out_grad[:, None, :] * per_pair, axis=-1)
    pair_grad = (gate_values[:, :, None] * out_grad[:, None, :]).reshape(pair_count, model_width)
    pair_padded = jnp.concatenate([pair_grad, jnp.zeros((1, model_width), jnp.float32)], axis=0)
    slot_grad = (
        pair_padded[source].reshape(expert_count, capacity, model_width).astype(jnp.bfloat16)
    )

    def expert_step(carry, pieces):
        slot_in, slot_hidden, slot_dy, slot_gate, slot_up, gate_matrix, up_matrix, down_matrix = (
            pieces
        )
        hidden_grad = jnp.einsum(
            "cd,hd->ch", slot_dy, down_matrix, preferred_element_type=jnp.float32
        )
        gate_grad_low, up_grad_low = silu_parts(hidden_grad, slot_gate, slot_up)
        in_grad = jnp.einsum(
            "ch,dh->cd", gate_grad_low, gate_matrix, preferred_element_type=jnp.float32
        ) + jnp.einsum("ch,dh->cd", up_grad_low, up_matrix, preferred_element_type=jnp.float32)
        gate_term = jnp.einsum(
            "cd,ch->dh", slot_in, gate_grad_low, preferred_element_type=jnp.float32
        )
        up_term = jnp.einsum("cd,ch->dh", slot_in, up_grad_low, preferred_element_type=jnp.float32)
        down_term = jnp.einsum(
            "ch,cd->hd", slot_hidden, slot_dy, preferred_element_type=jnp.float32
        )
        gate_shard, up_shard, down_shard = (
            lax.psum_scatter(
                gate_term.astype(jnp.bfloat16), "fsdp", scatter_dimension=1, tiled=True
            ).astype(jnp.float32),
            lax.psum_scatter(
                up_term.astype(jnp.bfloat16), "fsdp", scatter_dimension=1, tiled=True
            ).astype(jnp.float32),
            lax.psum_scatter(
                down_term.astype(jnp.bfloat16), "fsdp", scatter_dimension=0, tiled=True
            ).astype(jnp.float32),
        )
        gate_part, up_part, down_part = (
            lax.psum_scatter(
                gate_shard.astype(jnp.bfloat16), "ctx", scatter_dimension=0, tiled=True
            ).astype(jnp.float32),
            lax.psum_scatter(
                up_shard.astype(jnp.bfloat16), "ctx", scatter_dimension=0, tiled=True
            ).astype(jnp.float32),
            lax.psum_scatter(
                down_shard.astype(jnp.bfloat16), "ctx", scatter_dimension=1, tiled=True
            ).astype(jnp.float32),
        )
        return (carry, (in_grad, gate_part, up_part, down_part))

    _, (expert_in_grad, gate_parts, up_parts, down_parts) = lax.scan(
        expert_step,
        None,
        (expert_in, hidden_low, slot_grad, gate_pre, up_pre, gate_weight, up_weight, down_weight),
    )
    in_padded = jnp.concatenate(
        [
            expert_in_grad.reshape(expert_count * capacity, model_width),
            jnp.zeros((1, model_width), jnp.float32),
        ],
        axis=0,
    )
    normed_two_grad = jnp.sum(in_padded[placed].reshape(row_count, top_count, model_width), axis=1)
    prob_grad_router = jnp.sum(chosen * gate_grad[:, :, None], axis=1)
    logit_grad = (
        router_probs
        * (prob_grad_router - jnp.sum(router_probs * prob_grad_router, axis=-1, keepdims=True))
    ).astype(jnp.bfloat16)
    normed_two_grad = normed_two_grad + jnp.einsum(
        "te,de->td", logit_grad, router_weight, preferred_element_type=jnp.float32
    )
    router_grad = jnp.einsum(
        "td,te->de", normed_two, logit_grad, preferred_element_type=jnp.float32
    )
    mixed_norm_grad, gain_two_grad = norm_two_pull(normed_two_grad)
    mixed_grad = out_grad + mixed_norm_grad
    mixed_low = mixed_grad.astype(jnp.bfloat16)
    out_weight_grad = jnp.einsum(
        "td,te->de", attended_low, mixed_low, preferred_element_type=jnp.float32
    )
    output_grad = (
        jnp.einsum("te,de->td", mixed_low, out_weight, preferred_element_type=jnp.float32)
        .astype(jnp.bfloat16)
        .reshape(row_count, head_count, head_dim)
    )
    row_delta = jnp.sum(output_grad.astype(jnp.float32) * attended_f, axis=-1).T

    def query_grad_step(accum, block_index):
        key_block, value_block, key_pos, key_doc = key_slice(block_index)
        scores = masked_scores(
            query_low, key_block, local_pos, local_doc, key_pos, key_doc, score_scale
        )
        prob_block = jnp.exp(scores - log_total[..., None])
        prob_grad = jnp.einsum(
            "qhd,khd->hqk", output_grad, value_block, preferred_element_type=jnp.float32
        )
        score_grad = (prob_block * (prob_grad - row_delta[..., None])).astype(jnp.bfloat16)
        return (
            accum
            + jnp.einsum("hqk,khd->qhd", score_grad, key_block, preferred_element_type=jnp.float32)
            * score_scale,
            None,
        )

    query_grad, _ = lax.scan(
        query_grad_step, jnp.zeros((row_count, head_count, head_dim), jnp.float32), block_ids
    )
    inner_rows = math.gcd(row_count * lax.axis_size("ctx"), 512)

    def piece_step(carry, piece_index):
        first_row = piece_index * inner_rows
        key_block = lax.dynamic_slice_in_dim(keys_all, first_row, inner_rows, 0)
        value_block = lax.dynamic_slice_in_dim(values_all, first_row, inner_rows, 0)
        key_pos = lax.dynamic_slice_in_dim(stream_pos, first_row, inner_rows, 0)
        key_doc = lax.dynamic_slice_in_dim(stream_doc, first_row, inner_rows, 0)
        scores = masked_scores(
            query_low, key_block, local_pos, local_doc, key_pos, key_doc, score_scale
        )
        prob_block = jnp.exp(scores - log_total[..., None])
        prob_grad = jnp.einsum(
            "qhd,khd->hqk", output_grad, value_block, preferred_element_type=jnp.float32
        )
        score_grad = (prob_block * (prob_grad - row_delta[..., None])).astype(jnp.bfloat16)
        value_part = jnp.einsum(
            "hqk,qhd->khd",
            prob_block.astype(jnp.bfloat16),
            output_grad,
            preferred_element_type=jnp.float32,
        )
        key_part = (
            jnp.einsum("hqk,qhd->khd", score_grad, query_low, preferred_element_type=jnp.float32)
            * score_scale
        )
        return (
            carry,
            jnp.concatenate(
                [
                    key_part.reshape(inner_rows, model_width),
                    value_part.reshape(inner_rows, model_width),
                ],
                axis=1,
            ),
        )

    _, stacked = lax.scan(
        piece_step,
        None,
        jnp.arange(row_count * lax.axis_size("ctx") // inner_rows, dtype=jnp.int32),
    )
    key_value_grad = lax.psum_scatter(
        stacked.reshape(row_count * lax.axis_size("ctx"), 2 * model_width).astype(jnp.bfloat16),
        "ctx",
        scatter_dimension=0,
        tiled=True,
    ).astype(jnp.float32)
    key_grad = key_value_grad[:, :model_width].reshape(row_count, head_count, head_dim)
    value_grad = key_value_grad[:, model_width:]
    query_lin_grad, gain_query_grad = query_pull(query_grad)
    key_lin_grad, gain_key_grad = key_pull(key_grad)
    proj_grad = jnp.concatenate(
        [
            query_lin_grad.astype(jnp.bfloat16),
            key_lin_grad.astype(jnp.bfloat16),
            value_grad.astype(jnp.bfloat16),
        ],
        axis=1,
    )
    qkv_weight_grad = jnp.einsum(
        "td,te->de", normed_low, proj_grad, preferred_element_type=jnp.float32
    )
    normed_grad = jnp.einsum("te,de->td", proj_grad, qkv_weight, preferred_element_type=jnp.float32)
    input_norm_grad, gain_one_grad = norm_one_pull(normed_grad)
    input_grad = mixed_grad + input_norm_grad
    qkv_shard, out_shard = (
        lax.psum_scatter(
            qkv_weight_grad.astype(jnp.bfloat16), "fsdp", scatter_dimension=0, tiled=True
        ).astype(jnp.float32),
        lax.psum_scatter(
            out_weight_grad.astype(jnp.bfloat16), "fsdp", scatter_dimension=0, tiled=True
        ).astype(jnp.float32),
    )
    qkv_part, out_part = (
        lax.psum_scatter(
            qkv_shard.astype(jnp.bfloat16), "ctx", scatter_dimension=1, tiled=True
        ).astype(jnp.float32),
        lax.psum_scatter(
            out_shard.astype(jnp.bfloat16), "ctx", scatter_dimension=1, tiled=True
        ).astype(jnp.float32),
    )
    gain_one_sum, gain_query_sum, gain_key_sum, gain_two_sum, router_sum = lax.psum(
        (gain_one_grad, gain_query_grad, gain_key_grad, gain_two_grad, router_grad), ("ctx", "fsdp")
    )
    shard_rows = model_width // lax.axis_size("fsdp")
    shard_start = lax.axis_index("fsdp") * shard_rows

    def own_rows(full_array):
        return lax.dynamic_slice_in_dim(full_array, shard_start, shard_rows, 0)

    return (
        layer_out.astype(jnp.bfloat16)[None],
        input_grad[None],
        own_rows(gain_one_sum),
        qkv_part,
        own_rows(gain_query_sum),
        own_rows(gain_key_sum),
        out_part,
        own_rows(gain_two_sum),
        own_rows(router_sum),
        gate_parts,
        up_parts,
        down_parts,
    )


def rms_unit(values):
    return lax.rsqrt(jnp.mean(values * values, axis=-1, keepdims=True) + EPSILON)


def rope_tables(inner_pos, head_dim):
    half_dim = head_dim // 2
    freq_table = ROPE_BASE ** (-2.0 * jnp.arange(half_dim, dtype=jnp.float32) / head_dim)
    angles = inner_pos.astype(jnp.float32)[:, None] * freq_table[None, :]
    return (jnp.cos(angles), jnp.sin(angles))


def dot32(spec, left, right):
    return jnp.einsum(spec, left, right, preferred_element_type=jnp.float32)


def greet(peers):
    barrier = pltpu.get_barrier_semaphore()
    for peer in peers:
        pl.semaphore_signal(barrier, inc=1, device_id=peer, device_id_type=MESH)
    pl.semaphore_wait(barrier, len(peers))


def send(source, target, send_sem, recv_sem, peer):
    copy = pltpu.make_async_remote_copy(
        source, target, send_sem, recv_sem, device_id=peer, device_id_type=MESH
    )
    copy.start()
    return copy


def comm_call(
    kernel, name, collective_id, out_shape, in_specs, out_specs, scratch_shapes, cost, vmem=16
):
    return pl.pallas_call(
        kernel,
        out_shape=out_shape,
        in_specs=in_specs,
        out_specs=out_specs,
        scratch_shapes=scratch_shapes,
        compiler_params=pltpu.CompilerParams(
            collective_id=collective_id, has_side_effects=True, vmem_limit_bytes=vmem * 2**20
        ),
        cost_estimate=pl.CostEstimate(flops=0, bytes_accessed=cost, transcendentals=0),
        name=name,
    )


def ctx_sum(values, collective_id):
    ctx = lax.axis_size("ctx")

    def kernel(own_ref, out_ref, held, send_sems, recv_sems):
        me, mine = lax.axis_index("ctx"), lax.axis_index("fsdp")
        peers = [(lax.rem(me + step, ctx), mine) for step in range(1, ctx)]
        greet(peers)
        copies = [
            send(own_ref, held.at[i], send_sems.at[i], recv_sems.at[i], peer)
            for i, peer in enumerate(peers)
        ]
        total = own_ref[...]
        for i, copy in enumerate(copies):
            copy.wait_recv()
            total = total + held[i]
        out_ref[...] = total
        for copy in copies:
            copy.wait_send()

    return comm_call(
        kernel,
        "ctx_sum",
        collective_id,
        jax.ShapeDtypeStruct(values.shape, values.dtype),
        [VMEM],
        VMEM,
        [
            pltpu.VMEM((ctx - 1,) + values.shape, values.dtype),
            DMA((ctx - 1,)),
            DMA((ctx - 1,)),
        ],
        20 * 2**20,
    )(values)


def heads_to_rows(values, collective_id):
    ctx, fsdp = lax.axis_size("ctx"), lax.axis_size("fsdp")
    rows, cols = values.shape[0] // ctx, values.shape[1]
    share = ctx // fsdp

    def kernel(own_ref, out_ref, send_sems, recv_sems):
        me, mine = lax.axis_index("ctx"), lax.axis_index("fsdp")
        keeper, place = me // share, lax.rem(me, share)
        own_keeper = (keeper == mine).astype(jnp.int32)
        barrier = pltpu.get_barrier_semaphore()
        for step in range(share * fsdp):
            source, stream = mine * share + step // fsdp, step % fsdp

            @pl.when(jnp.logical_or(source != me, stream != mine))
            def _():
                pl.semaphore_signal(
                    barrier, inc=1, device_id=(source, stream), device_id_type=MESH
                )

        pl.semaphore_wait(barrier, ctx - own_keeper)

        def block(index):
            return own_ref.at[pl.ds(pl.multiple_of(index * rows, rows), rows), :]

        def landing(stream, position):
            return out_ref.at[
                pl.ds(pl.multiple_of(stream * rows, rows), rows),
                pl.ds(pl.multiple_of(position * cols, cols), cols),
            ]

        slot = place * fsdp + mine

        def copy_to(step):
            other = lax.rem(me + step, ctx)
            return pltpu.make_async_remote_copy(
                block(other),
                landing(mine, place),
                send_sems.at[step],
                recv_sems.at[slot],
                device_id=(other, keeper),
                device_id_type=MESH,
            )

        kept = pltpu.make_async_copy(block(me), landing(mine, place), send_sems.at[0])
        for step in range(1, ctx):
            copy_to(step).start()

        @pl.when(own_keeper == 0)
        def _():
            copy_to(0).start()

        @pl.when(own_keeper == 1)
        def _():
            kept.start()
            kept.wait()

        for step in range(share * fsdp):

            @pl.when(
                jnp.logical_or(mine * share + step // fsdp != me, step % fsdp != mine)
            )
            def _():
                pltpu.make_async_copy(
                    block(0), landing(step % fsdp, step // fsdp), recv_sems.at[step]
                ).wait()

        for step in range(1, ctx):
            copy_to(step).wait_send()

        @pl.when(own_keeper == 0)
        def _():
            copy_to(0).wait_send()

    return comm_call(
        kernel,
        "heads_to_rows",
        collective_id,
        jax.ShapeDtypeStruct((fsdp * rows, share * cols), values.dtype),
        [ANY],
        ANY,
        [DMA((ctx,)), DMA((share * fsdp,))],
        40 * 2**20,
    )(values)


def rows_to_heads(values, collective_id):
    ctx, fsdp = lax.axis_size("ctx"), lax.axis_size("fsdp")
    share = ctx // fsdp
    rows, cols = values.shape[0] // fsdp, values.shape[1] // share

    def kernel(own_ref, out_ref, stage, stage_send, stage_recv, send_sems, recv_sems):
        me, mine = lax.axis_index("ctx"), lax.axis_index("fsdp")
        ctx_peers = [(lax.rem(me + step, ctx), mine) for step in range(1, ctx)]
        greet(ctx_peers + [(me, lax.rem(mine + step, fsdp)) for step in range(1, fsdp)])

        def block(stream):
            return own_ref.at[pl.ds(pl.multiple_of(stream * rows, rows), rows), :]

        def landing(index):
            return out_ref.at[pl.ds(pl.multiple_of(index * rows, rows), rows), :]

        steps = [2, 3, 1]
        staged = {
            step: send(
                block(lax.rem(mine + step, fsdp)),
                stage.at[fsdp - step],
                stage_send.at[step],
                stage_recv.at[fsdp - step],
                (me, lax.rem(mine + step, fsdp)),
            )
            for step in steps
        }

        def piece(step, place):
            span = pl.ds(place * cols, cols)
            if step == 0:
                return own_ref.at[pl.ds(pl.multiple_of(mine * rows, rows), rows), span]
            return stage.at[step, :, span]

        def target(step, place):
            return lax.rem(mine + step, fsdp) * share + place

        def copy_to(step, place):
            return pltpu.make_async_remote_copy(
                piece(step, place),
                landing(me),
                send_sems.at[step * share + place],
                recv_sems.at[me],
                device_id=(target(step, place), mine),
                device_id_type=MESH,
            )

        def keep(step, place):
            return pltpu.make_async_copy(
                piece(step, place), landing(me), send_sems.at[step * share + place]
            )

        for step in [0, 1, 2, 3]:
            if step > 0:
                staged[fsdp - step].wait_recv()
            for place in range(share):
                far = target(step, place) != me
                pl.when(far)(copy_to(step, place).start)
                pl.when(jnp.logical_not(far))(keep(step, place).start)
        for step in range(1, ctx):
            source = lax.rem(me + step, ctx)
            pltpu.make_async_copy(
                piece(0, 0), landing(source), recv_sems.at[source]
            ).wait()
        for step in range(fsdp):
            for place in range(share):
                far = target(step, place) != me
                pl.when(far)(copy_to(step, place).wait_send)
                pl.when(jnp.logical_not(far))(keep(step, place).wait)
        for copy in staged.values():
            copy.wait_send()

    return comm_call(
        kernel,
        "rows_to_heads",
        collective_id,
        jax.ShapeDtypeStruct((ctx * rows, cols), values.dtype),
        [ANY],
        ANY,
        [
            pltpu.VMEM((fsdp, rows, share * cols), values.dtype),
            DMA((fsdp,)),
            DMA((fsdp,)),
            DMA((ctx,)),
            DMA((ctx,)),
        ],
        2**20,
    )(values)


def swap(values, flip):
    return lax.ppermute(values, "ctx", [(i, i ^ flip) for i in range(lax.axis_size("ctx"))])


def reduce_then_gather(partial, extras, out_shapes, chunk_math, name, collective_id, crossed, bulk, vmem):
    ctx, fsdp = lax.axis_size("ctx"), lax.axis_size("fsdp")
    rows, width = partial.shape[0] // fsdp, partial.shape[1]
    chunks = 4
    size = rows // chunks
    count = len(extras)
    cols = width // ctx
    if crossed:
        out_shapes = out_shapes + [jax.ShapeDtypeStruct((rows, width // 2), jnp.bfloat16)]
    bulk_count, out_count = len(bulk), len(out_shapes)

    def kernel(*refs):
        part_ref, extra_refs = refs[0], refs[1 : 1 + count]
        bulk_refs, refs = refs[1 + count : 1 + count + bulk_count], refs[1 + count + bulk_count :]
        all_ref, out_refs = refs[0], refs[1 : 1 + out_count]
        bulk_out_refs, refs = refs[1 + out_count : 1 + out_count + bulk_count], refs[1 + out_count :]
        near_own, near_far, far_sum, far_own, sems, cross_sems, bulk_sems = refs[bulk_count:]
        me, mine = lax.axis_index("ctx"), lax.axis_index("fsdp")
        flip = 1 - 2 * lax.rem(mine, 2)
        core = mine + flip
        chip = lax.rem(mine + 2, fsdp)
        diagonal = lax.rem(core + 2, fsdp)
        to_x = (flipped(me, 1), mine)
        greet([(me, core), (me, chip)] + ([to_x] if crossed or bulk else []))

        def span(block, i):
            return pl.ds(pl.multiple_of(block * rows + i * size, size), size)

        def sem(kind, i):
            return sems.at[2 * kind, i], sems.at[2 * kind + 1, i]

        copies = []
        from_core_far, from_core_own, from_chip = [], [], []
        exchanged = [
            send(source, target, bulk_sems.at[0, i], bulk_sems.at[1, i], to_x)
            for i, (source, target) in enumerate(zip(bulk_refs, bulk_out_refs))
        ]
        for i in range(chunks):
            copy = send(
                part_ref.at[span(diagonal, i), :], near_far.at[i], *sem(0, i), (me, core)
            )
            from_core_far.append(copy)
        for i in range(chunks):
            copy = send(part_ref.at[span(core, i), :], near_own.at[i], *sem(1, i), (me, core))
            from_core_own.append(copy)
        for i in range(chunks):
            from_core_far[i].wait_recv()
            both = part_ref[span(chip, i), :].astype(jnp.float32) + near_far[i].astype(jnp.float32)
            far_sum[i] = both.astype(jnp.bfloat16)
            from_chip.append(send(far_sum.at[i], far_own.at[i], *sem(2, i), (me, chip)))
        to_chip = []
        for i in range(chunks):
            from_core_own[i].wait_recv()
            from_chip[i].wait_recv()
            total = (
                part_ref[span(mine, i), :].astype(jnp.float32)
                + near_own[i].astype(jnp.float32)
                + far_own[i].astype(jnp.float32)
            )
            all_ref[span(mine, i), :] = chunk_math(
                i, pl.ds(i * size, size), total, extra_refs, out_refs
            ).astype(jnp.bfloat16)
            own = all_ref.at[span(mine, i), :]
            to_chip.append(send(own, own, *sem(3, i), (me, chip)))
            copies.append(send(own, own, *sem(4, i), (me, core)))
            for run in range(ctx // 2 if crossed else 0):
                start = pl.multiple_of((2 * run + 1 - lax.rem(me, 2)) * cols, cols)
                copies.append(
                    send(
                        all_ref.at[span(mine, i), pl.ds(start, cols)],
                        out_refs[-1].at[pl.ds(i * size, size), pl.ds(run * cols, cols)],
                        cross_sems.at[0, i, run],
                        cross_sems.at[1, i, run],
                        to_x,
                    )
                )
        for i in range(chunks):
            to_chip[i].wait_recv()
            other = all_ref.at[span(chip, i), :]
            copies.append(send(other, other, *sem(5, i), (me, core)))
        for copy in copies + exchanged:
            copy.wait_recv()
        for copy in from_core_far + from_core_own + from_chip + to_chip + copies + exchanged:
            copy.wait_send()

    return comm_call(
        kernel,
        name,
        collective_id,
        [jax.ShapeDtypeStruct(partial.shape, jnp.bfloat16)]
        + out_shapes
        + [jax.ShapeDtypeStruct(values.shape, values.dtype) for values in bulk],
        [VMEM] * (1 + count) + [ANY] * bulk_count,
        [VMEM] * (1 + out_count) + [ANY] * bulk_count,
        [
            pltpu.VMEM((chunks, size, width), jnp.bfloat16),
            pltpu.VMEM((chunks, size, width), jnp.bfloat16),
            pltpu.VMEM((chunks, size, width), jnp.bfloat16),
            pltpu.VMEM((chunks, size, width), jnp.bfloat16),
            DMA((12, chunks)),
            DMA((2, chunks, ctx // 2)),
            DMA((2, max(1, bulk_count))),
        ],
        100 * 2**20,
        vmem,
    )(partial, *extras, *bulk)


def norm_chunk(index, span, total, extra_refs, out_refs):
    tokens_ref, gain_ref = extra_refs
    mixed = tokens_ref[span, :].astype(jnp.float32) + total
    out_refs[0][span, :] = mixed
    return mixed * rms_unit(mixed) * gain_ref[...]


def norm_back_chunk(index, span, total, extra_refs, out_refs):
    mixed_ref, gain_ref, dy_ref = extra_refs
    mixed = mixed_ref[span, :]
    scale = rms_unit(mixed)
    unit = mixed * scale
    pulled = total * gain_ref[...]
    grad = dy_ref[span, :].astype(jnp.float32) + scale * (
        pulled - unit * jnp.mean(unit * pulled, axis=-1, keepdims=True)
    )
    out_refs[0][span, :] = grad
    gain_grad = jnp.sum(total * unit, axis=0, keepdims=True)
    if index == 0:
        out_refs[1][...] = gain_grad
    else:
        out_refs[1][...] += gain_grad
    return grad


ROUTER_ROWS = 16


def one_hot(slots, capacity):
    return lax.broadcasted_iota(jnp.int32, (capacity, slots.shape[1]), 0) == slots


def slots_of(pairs, experts, top):
    lines, rows = pairs.shape
    absent = float(rows * top)

    def kernel(pairs_ref, out_ref):
        out_ref[...] = jnp.full(out_ref.shape, -1, jnp.int32)
        rank_rows = []
        for expert in range(experts):
            rank = jnp.full((1, rows), absent, jnp.float32)
            for k in range(top):
                rank = jnp.where(
                    pairs_ref[k : k + 1, :] == expert,
                    pairs_ref[top + k : top + k + 1, :].astype(jnp.float32),
                    rank,
                )
            rank_rows.append(rank)
        filler = jnp.full((rows - experts, rows), absent, jnp.float32)
        by_column = jnp.concatenate(rank_rows + [filler], axis=0).T
        for expert, rank in enumerate(rank_rows):
            earlier = jnp.where(by_column[:, expert : expert + 1] < rank, 1.0, 0.0)
            slot = jnp.where(rank < absent, jnp.sum(earlier, axis=0, keepdims=True), -1.0)
            out_ref[expert : expert + 1, :] = slot.astype(jnp.int32)

    return pl.pallas_call(
        kernel,
        out_shape=jax.ShapeDtypeStruct((lines, rows), jnp.int32),
        in_specs=[VMEM],
        out_specs=VMEM,
        cost_estimate=pl.CostEstimate(flops=10**7, bytes_accessed=2**20, transcendentals=0),
        name="slots_of",
    )(pairs)


def run_experts(group, dy_all, slots, router, w_gate, w_up, w_down, blocks, capacity):
    experts, width, units = w_gate.shape
    total = group.shape[0]
    rows = total // blocks
    held = blocks * capacity
    f32, bf16 = jnp.float32, jnp.bfloat16

    def kernel(
        group_ref,
        dy_ref,
        slots_ref,
        router_ref,
        gate_ref,
        up_ref,
        down_ref,
        moved_ref,
        grad_ref,
        g_router_ref,
        scaled_ref,
        gate_low_ref,
        up_low_ref,
        disp,
        ins,
        dys,
        probs,
        prob_grad,
    ):
        expert = pl.program_id(0)

        def block_rows(b):
            return pl.ds(b * rows, rows)

        @pl.when(expert == 0)
        def _():
            logits = lax.dot_general(
                router_ref[...],
                group_ref[...],
                (((1,), (1,)), ((), ())),
                preferred_element_type=f32,
            )
            real = lax.broadcasted_iota(jnp.int32, logits.shape, 0) < experts
            logits = jnp.where(real, logits, MASKED)
            weights = jnp.exp(logits - jnp.max(logits, axis=0, keepdims=True))
            probs[...] = weights / jnp.sum(weights, axis=0, keepdims=True)
            prob_grad[...] = jnp.zeros_like(prob_grad)
            for b in range(blocks):
                for e in range(experts):
                    disp[b, pl.ds(e * capacity, capacity), :] = (
                        one_hot(slots_ref[b, pl.ds(e, 1), :], capacity)
                        .astype(f32)
                        .astype(bf16)
                    )
                for source, target in ((group_ref, ins), (dy_ref, dys)):
                    picked = jnp.dot(
                        disp[b], source[block_rows(b), :], preferred_element_type=f32
                    ).astype(bf16)
                    for e in range(experts):
                        target[e, pl.ds(b * capacity, capacity), :] = picked[
                            e * capacity : (e + 1) * capacity
                        ]

        expert_in, slot_dy = ins[expert], dys[expert]
        gate_matrix, up_matrix, down_matrix = gate_ref[0], up_ref[0], down_ref[0]
        gate_pre = jnp.dot(expert_in, gate_matrix, preferred_element_type=f32)
        up_pre = jnp.dot(expert_in, up_matrix, preferred_element_type=f32)
        raw_grad = lax.dot_general(
            slot_dy, down_matrix, (((1,), (1,)), ((), ())), preferred_element_type=f32
        )
        own_probs = probs[pl.ds(expert, 1), :]
        hots = [one_hot(slots_ref[b, pl.ds(expert, 1), :], capacity) for b in range(blocks)]
        value = jnp.concatenate(
            [
                jnp.sum(
                    jnp.where(hots[b], own_probs[:, b * rows : (b + 1) * rows], 0.0),
                    axis=1,
                    keepdims=True,
                )
                for b in range(blocks)
            ],
            axis=0,
        )
        sigma = 1.0 / (1.0 + jnp.exp(-gate_pre))
        silu = gate_pre * sigma
        hidden = (silu * up_pre).astype(bf16)
        hidden_f = hidden.astype(f32)
        value_grad = jnp.sum(hidden_f * raw_grad, axis=1, keepdims=True)
        hidden_grad = raw_grad * value
        gate_low = (hidden_grad * up_pre * sigma * (1.0 + gate_pre * (1.0 - sigma))).astype(bf16)
        up_low = (hidden_grad * silu).astype(bf16)
        scaled = (hidden_f * value).astype(bf16)
        scaled_ref[0] = scaled
        gate_low_ref[0] = gate_low
        up_low_ref[0] = up_low
        for b in range(blocks):
            prob_grad[expert, :, block_rows(b)] = jnp.sum(
                jnp.where(hots[b], value_grad[b * capacity : (b + 1) * capacity], 0.0),
                axis=0,
                keepdims=True,
            )
        dys[expert] = jnp.dot(scaled, down_matrix, preferred_element_type=f32).astype(bf16)
        ins[expert] = (
            lax.dot_general(
                gate_low, gate_matrix, (((1,), (1,)), ((), ())), preferred_element_type=f32
            )
            + lax.dot_general(
                up_low, up_matrix, (((1,), (1,)), ((), ())), preferred_element_type=f32
            )
        ).astype(bf16)

        @pl.when(expert == experts - 1)
        def _():
            grads = jnp.concatenate([prob_grad[e] for e in range(ROUTER_ROWS)], axis=0)
            weights = probs[...]
            logit_grad = (
                weights * (grads - jnp.sum(weights * grads, axis=0, keepdims=True))
            ).astype(bf16)
            g_router_ref[...] = jnp.dot(logit_grad, group_ref[...], preferred_element_type=f32)
            for b in range(blocks):
                for source, target in ((dys, moved_ref), (ins, grad_ref)):
                    gathered = jnp.concatenate(
                        [source[e, pl.ds(b * capacity, capacity), :] for e in range(experts)],
                        axis=0,
                    )
                    back = lax.dot_general(
                        disp[b], gathered, (((0,), (0,)), ((), ())), preferred_element_type=f32
                    )
                    if target is grad_ref:
                        back = back + lax.dot_general(
                            logit_grad[:, b * rows : (b + 1) * rows],
                            router_ref[...],
                            (((0,), (0,)), ((), ())),
                            preferred_element_type=f32,
                        )
                    target[block_rows(b), :] = back.astype(bf16)

    def whole(shape):
        return pl.BlockSpec(shape, lambda e: (0,) * len(shape))

    def by_expert(shape):
        return pl.BlockSpec((1,) + shape, lambda e: (e, 0, 0))

    return pl.pallas_call(
        kernel,
        grid=(experts,),
        out_shape=[
            jax.ShapeDtypeStruct((total, width), bf16),
            jax.ShapeDtypeStruct((total, width), bf16),
            jax.ShapeDtypeStruct((ROUTER_ROWS, width), f32),
        ]
        + [jax.ShapeDtypeStruct((experts, held, units), bf16)] * 3,
        in_specs=[
            whole((total, width)),
            whole((total, width)),
            whole(slots.shape),
            whole((ROUTER_ROWS, width)),
            by_expert((width, units)),
            by_expert((width, units)),
            by_expert((units, width)),
        ],
        out_specs=[
            whole((total, width)),
            whole((total, width)),
            whole((ROUTER_ROWS, width)),
        ]
        + [by_expert((held, units))] * 3,
        scratch_shapes=[
            pltpu.VMEM((blocks, experts * capacity, rows), bf16),
            pltpu.VMEM((experts, held, width), bf16),
            pltpu.VMEM((experts, held, width), bf16),
            pltpu.VMEM((ROUTER_ROWS, total), f32),
            pltpu.VMEM((ROUTER_ROWS, 1, total), f32),
        ],
        compiler_params=pltpu.CompilerParams(vmem_limit_bytes=60 * 2**20),
        cost_estimate=pl.CostEstimate(
            flops=30 * 10**9, bytes_accessed=30 * 2**20, transcendentals=10**6
        ),
        name="run_experts",
    )(group, dy_all, slots, router, w_gate, w_up, w_down)


def expert_grads(slot_own, slot_other, rows_own, rows_other, slots_own, slots_other, capacity):
    kinds = len(slot_own)
    experts, held, units = slot_own[0].shape
    total, half = rows_other.shape
    blocks = held // capacity
    rows = total // blocks
    ctx = lax.axis_size("ctx")
    cols = 2 * half // ctx
    f32, bf16 = jnp.float32, jnp.bfloat16

    def kernel(*refs):
        own_refs, other_refs = refs[:kinds], refs[kinds : 2 * kinds]
        rows_own_ref, rows_other_ref, slots_own_ref, slots_other_ref = refs[2 * kinds : 2 * kinds + 4]
        out_refs, held_rows = refs[2 * kinds + 4 : -1], refs[-1]
        expert = pl.program_id(0)
        me = lax.axis_index("ctx")

        def columns(side, run):
            if side == 1:
                return pl.ds(run * cols, cols)
            return pl.ds(pl.multiple_of((2 * run + lax.rem(me, 2)) * cols, cols), cols)

        @pl.when(expert == 0)
        def _():
            for side, slots_ref, source in (
                (0, slots_own_ref, rows_own_ref),
                (1, slots_other_ref, rows_other_ref),
            ):
                for b in range(blocks):
                    span = pl.ds(b * rows, rows)
                    disp = jnp.concatenate(
                        [
                            one_hot(slots_ref[b, pl.ds(e, 1), :], capacity).astype(f32)
                            for e in range(experts)
                        ],
                        axis=0,
                    ).astype(bf16)
                    for run in range(ctx // 2):
                        picked = jnp.dot(
                            disp, source[span, columns(side, run)], preferred_element_type=f32
                        ).astype(bf16)
                        for e in range(experts):
                            held_rows[
                                e,
                                pl.ds(side * held + b * capacity, capacity),
                                pl.ds(run * cols, cols),
                            ] = picked[e * capacity : (e + 1) * capacity]

        low, high = lax.rem(me // 2, 2), me // 4
        stacked = [
            jnp.concatenate([own[0], other[0]], axis=0) for own, other in zip(own_refs, other_refs)
        ]
        contract = (((0,), (0,)), ((), ()))
        for run in range(ctx // 2):
            given = jnp.where(low == run % 2, 0, 2)
            place = given + jnp.where(high == run // 2, 0, 1)
            features = held_rows[expert, :, pl.ds(run * cols, cols)]
            for kind in range(kinds):
                total = lax.dot_general(
                    features, stacked[kind], contract, preferred_element_type=f32
                ).astype(bf16)
                for i in range(4):

                    @pl.when(place == i)
                    def _():
                        out_refs[4 * kind + i][0] = total

    def whole(shape):
        return pl.BlockSpec(shape, lambda e: (0,) * len(shape))

    slot_spec = pl.BlockSpec((1, held, units), lambda e: (e, 0, 0))
    return pl.pallas_call(
        kernel,
        grid=(experts,),
        out_shape=[jax.ShapeDtypeStruct((experts, units, cols), bf16)] * (4 * kinds),
        in_specs=[slot_spec] * (2 * kinds)
        + [whole((total, 2 * half)), whole((total, half))]
        + [whole(slots_own.shape)] * 2,
        out_specs=[pl.BlockSpec((1, units, cols), lambda e: (e, 0, 0))] * (4 * kinds),
        scratch_shapes=[pltpu.VMEM((experts, 2 * held, half), bf16)],
        compiler_params=pltpu.CompilerParams(vmem_limit_bytes=60 * 2**20),
        cost_estimate=pl.CostEstimate(flops=0, bytes_accessed=2**20, transcendentals=0),
        name="expert_grads",
    )(*slot_own, *slot_other, rows_own, rows_other, slots_own, slots_other)


def down_grads(scaled, dy_parts, slots, capacity):
    count = len(scaled)
    experts, held, units = scaled[0].shape
    blocks, _, rows, wide = dy_parts.shape
    cols = wide // 2
    f32, bf16 = jnp.float32, jnp.bfloat16

    def kernel(*refs):
        scaled_refs, dy_ref, slots_refs = refs[:count], refs[count], refs[count + 1 : 2 * count + 1]
        out_ref, held_rows = refs[2 * count + 1 :]
        expert = pl.program_id(0)

        @pl.when(expert == 0)
        def _():
            for i, slots_ref in enumerate(slots_refs):
                for b in range(blocks):
                    span = pl.ds(b * rows, rows)
                    disp = jnp.concatenate(
                        [
                            one_hot(slots_ref[b, pl.ds(e, 1), :], capacity).astype(f32)
                            for e in range(experts)
                        ],
                        axis=0,
                    ).astype(bf16)
                    picked = jnp.dot(disp, dy_ref[b, i], preferred_element_type=f32).astype(bf16)
                    for e in range(experts):
                        held_rows[e, pl.ds(i * held + b * capacity, capacity), :] = picked[
                            e * capacity : (e + 1) * capacity
                        ]

        stacked = jnp.concatenate([ref[0] for ref in scaled_refs], axis=0)
        total = lax.dot_general(
            stacked, held_rows[expert], (((0,), (0,)), ((), ())), preferred_element_type=f32
        ).astype(bf16)
        side = lax.rem(lax.axis_index("ctx"), 2)
        for x in range(2):
            kept = jnp.where(side == x, 1, 0)
            out_ref[pl.ds(kept, 1), 0] = total[:, x * cols : (x + 1) * cols][None]

    def whole(shape):
        return pl.BlockSpec(shape, lambda e: (0,) * len(shape))

    return pl.pallas_call(
        kernel,
        grid=(experts,),
        out_shape=jax.ShapeDtypeStruct((2, experts, units, cols), bf16),
        in_specs=[pl.BlockSpec((1, held, units), lambda e: (e, 0, 0))] * count
        + [whole(dy_parts.shape)]
        + [whole(slots[0].shape)] * count,
        out_specs=pl.BlockSpec((2, 1, units, cols), lambda e: (0, e, 0, 0)),
        scratch_shapes=[pltpu.VMEM((experts, count * held, wide), bf16)],
        compiler_params=pltpu.CompilerParams(vmem_limit_bytes=60 * 2**20),
        cost_estimate=pl.CostEstimate(flops=0, bytes_accessed=2**20, transcendentals=0),
        name="down_grads",
    )(*scaled, dy_parts, *slots)


def roll_half(values):
    return pltpu.roll(values, values.shape[1] // 2, 1)


def allowed_keys(first_ref, last_ref, span, places):
    return (places >= first_ref[span, :]) & (places <= last_ref[span, :])


def stored_runs(total):
    ctx = lax.axis_size("ctx")
    rows = total // ctx
    run = rows // 2
    starts = [i * rows for i in range(ctx)]
    return starts + [i * rows + run for i in reversed(range(ctx))], run


def attend(projected, scales, gains, cosine, sine_part, first, last, places, cols):
    total = projected.shape[0]
    head_dim = cosine.shape[1]
    heads = cols // head_dim
    size = math.gcd(total, 256)
    score_scale = head_dim ** (-0.5)
    starts, run = stored_runs(total)
    f32, bf16 = jnp.float32, jnp.bfloat16

    def kernel(
        lin_ref,
        scales_ref,
        gains_ref,
        cos_ref,
        sin_ref,
        first_ref,
        last_ref,
        places_ref,
        low_ref,
        attended_ref,
        attended_low_ref,
        top_ref,
    ):
        for kind in range(3):
            for h in range(heads):
                span = pl.ds(kind * cols + h * head_dim, head_dim)
                values = lin_ref[:, span]
                if kind < 2:
                    values = values * scales_ref[:, kind : kind + 1] * gains_ref[:, span]
                    values = values * cos_ref[...] + roll_half(values) * sin_ref[...]
                values = values.astype(bf16)
                for place, start in enumerate(starts):
                    low_ref[pl.ds(place * run, run), span] = values[start : start + run]
        for h in range(heads):
            head = pl.ds(h * head_dim, head_dim)
            for b in range(total // size):
                span, seen = pl.ds(b * size, size), pl.ds(0, (b + 1) * size)
                scores = lax.dot_general(
                    low_ref[span, head],
                    low_ref[seen, pl.ds(cols + h * head_dim, head_dim)],
                    (((1,), (1,)), ((), ())),
                    preferred_element_type=f32,
                )
                allowed = allowed_keys(first_ref, last_ref, span, places_ref[:, seen])
                scores = jnp.where(allowed, scores * score_scale, MASKED)
                top = jnp.max(scores, axis=1, keepdims=True)
                weights = jnp.exp(scores - top)
                sums = jnp.sum(weights, axis=1, keepdims=True)
                probs = (weights * (1.0 / sums)).astype(bf16)
                attended = jnp.dot(
                    probs,
                    low_ref[seen, pl.ds(2 * cols + h * head_dim, head_dim)],
                    preferred_element_type=f32,
                )
                attended_ref[span, head] = attended
                attended_low = attended.astype(bf16)
                for i in range(size // run):
                    start = starts[b * (size // run) + i]
                    attended_low_ref[pl.ds(start, run), head] = attended_low[i * run : (i + 1) * run]
                top_ref[span, head] = jnp.broadcast_to(top + jnp.log(sums), (size, head_dim))

    return pl.pallas_call(
        kernel,
        out_shape=[
            jax.ShapeDtypeStruct((total, 3 * cols), bf16),
            jax.ShapeDtypeStruct((total, cols), f32),
            jax.ShapeDtypeStruct((total, cols), bf16),
            jax.ShapeDtypeStruct((total, cols), f32),
        ],
        in_specs=[VMEM] * 8,
        out_specs=[VMEM] * 4,
        compiler_params=pltpu.CompilerParams(vmem_limit_bytes=24 * 2**20),
        cost_estimate=pl.CostEstimate(
            flops=2 * 10**9, bytes_accessed=20 * 2**20, transcendentals=2 * 10**6
        ),
        name="attend",
    )(projected, scales, gains, cosine, sine_part, first, last, places)


def attend_back(
    output_grad, low, attended, top, projected, scales, gains, cosine, sine_part, first, last, places
):
    total, cols = output_grad.shape
    head_dim = cosine.shape[1]
    heads = cols // head_dim
    size = math.gcd(total, 256)
    score_scale = head_dim ** (-0.5)
    f32, bf16 = jnp.float32, jnp.bfloat16
    contract_rows = (((0,), (0,)), ((), ()))
    starts, run = stored_runs(total)

    def kernel(
        grad_ref,
        low_ref,
        attended_ref,
        top_ref,
        lin_ref,
        scales_ref,
        gains_ref,
        cos_ref,
        sin_ref,
        first_ref,
        last_ref,
        places_ref,
        back_ref,
        value_ref,
        gain_ref,
        sums_ref,
        query_grad,
        key_grad,
        value_grad,
        grads_moved,
    ):
        for place, start in enumerate(starts):
            grads_moved[pl.ds(place * run, run), :] = grad_ref[pl.ds(start, run), :]

        def stored(values):
            pieces = sorted((start, place) for place, start in enumerate(starts))
            return jnp.concatenate([values[p * run : (p + 1) * run] for _, p in pieces], axis=0)

        totals = [jnp.zeros((total, 1), f32) for _ in range(2)]
        for h in range(heads):
            head = pl.ds(h * head_dim, head_dim)
            key_grad[...] = jnp.zeros_like(key_grad)
            value_grad[...] = jnp.zeros_like(value_grad)
            for b in range(total // size):
                span, seen = pl.ds(b * size, size), pl.ds(0, (b + 1) * size)
                queries, grads = low_ref[span, head], grads_moved[span, head]
                keys = low_ref[seen, pl.ds(cols + h * head_dim, head_dim)]
                scores = lax.dot_general(
                    queries, keys, (((1,), (1,)), ((), ())), preferred_element_type=f32
                )
                allowed = allowed_keys(first_ref, last_ref, span, places_ref[:, seen])
                scores = jnp.where(allowed, scores * score_scale, MASKED)
                probs = jnp.exp(scores - top_ref[span, head][:, :1])
                prob_grad = lax.dot_general(
                    grads,
                    low_ref[seen, pl.ds(2 * cols + h * head_dim, head_dim)],
                    (((1,), (1,)), ((), ())),
                    preferred_element_type=f32,
                )
                delta = jnp.sum(
                    grads.astype(f32) * attended_ref[span, head], axis=1, keepdims=True
                )
                score_grad = (probs * (prob_grad - delta)).astype(bf16)
                query_grad[span, :] = (
                    jnp.dot(score_grad, keys, preferred_element_type=f32) * score_scale
                )
                key_grad[seen, :] += lax.dot_general(
                    score_grad, queries, contract_rows, preferred_element_type=f32
                )
                value_grad[seen, :] += lax.dot_general(
                    probs.astype(bf16), grads, contract_rows, preferred_element_type=f32
                )
            value_ref[:, head] = stored(value_grad[...].astype(bf16))
            for kind, grad in ((0, query_grad[...]), (1, key_grad[...] * score_scale)):
                grad = stored(grad)
                span = pl.ds(kind * cols + h * head_dim, head_dim)
                unit = lin_ref[:, span] * scales_ref[:, kind : kind + 1]
                grad = grad * cos_ref[...] - roll_half(grad) * sin_ref[...]
                gain_ref[kind, :, head] = jnp.sum(grad * unit, axis=0, keepdims=True)
                grad = grad * gains_ref[:, span]
                back_ref[kind, :, head] = grad
                totals[kind] = totals[kind] + jnp.sum(grad * unit, axis=1, keepdims=True)
        for kind in range(2):
            sums_ref[:, kind : kind + 1] = totals[kind]

    return pl.pallas_call(
        kernel,
        out_shape=[
            jax.ShapeDtypeStruct((2, total, cols), f32),
            jax.ShapeDtypeStruct((total, cols), bf16),
            jax.ShapeDtypeStruct((2, 1, cols), f32),
            jax.ShapeDtypeStruct((total, 2), f32),
        ],
        in_specs=[VMEM] * 12,
        out_specs=[VMEM] * 4,
        scratch_shapes=[pltpu.VMEM((total, head_dim), f32)] * 3 + [pltpu.VMEM((total, cols), bf16)],
        compiler_params=pltpu.CompilerParams(vmem_limit_bytes=60 * 2**20),
        cost_estimate=pl.CostEstimate(flops=0, bytes_accessed=2**20, transcendentals=0),
        name="attend_back",
    )(
        output_grad,
        low,
        attended,
        top,
        projected,
        scales,
        gains,
        cosine,
        sine_part,
        first,
        last,
        places,
    )


def flipped(index, bit):
    return index + bit * (1 - 2 * lax.rem(index // bit, 2))


def flipped_by(index, flip):
    for bit in (1, 2, 4):
        index = flipped(index, bit) if flip & bit else index
    return index


def add_into(target, *sources):
    step = target.shape[0] if len(target.shape) == 3 else target.shape[0] // 64

    def body(i, carry):
        span = i if len(target.shape) == 3 else pl.ds(pl.multiple_of(i * 64, 64), 64)
        total = sources[0][span].astype(jnp.float32)
        for source in sources[1:]:
            total = total + source[span].astype(jnp.float32)
        target[span] = total.astype(target.dtype)
        return carry

    lax.fori_loop(0, step, body, 0)


def finish_sums(downs, ups, gate_far, gate_own, up_far, normed_part, out_part, qkv_part, small, tokens, mixed_grad, gain, mixed, moved, collective_id):
    ctx, fsdp = lax.axis_size("ctx"), lax.axis_size("fsdp")
    experts, units, cols = gate_far.shape
    kinds = 3
    rows, width = tokens.shape
    part = out_part.shape[0]
    f32, bf16 = jnp.float32, jnp.bfloat16
    small_rows, small_cols = small.shape[0], small.shape[1] // fsdp
    copies_most = 64

    def kernel(
        downs_ref,
        gate_near_ref,
        gate_high_ref,
        up_near_ref,
        up_high_ref,
        up_low_ref,
        gate_far_ref,
        gate_own_ref,
        up_far_ref,
        normed_ref,
        g_out_ref,
        g_qkv_ref,
        small_ref,
        tokens_ref,
        mixed_ref,
        gain_ref,
        forward_ref,
        moved_ref,
        down_ref,
        gate_ref,
        up_ref,
        input_ref,
        out_ref,
        qkv_ref,
        sums_ref,
        result_ref,
        kept,
        kept_low,
        kept_high,
        normed_own,
        normed_x,
        normed_low,
        normed_high,
        out_own,
        out_x,
        out_low,
        out_high,
        qkv_own,
        qkv_core,
        qkv_chip,
        qkv_sum,
        dealt,
        small_parts,
        small_sum,
        small_held,
        sends,
        recvs,
        locals_,
        deal_sems,
    ):
        me, mine = lax.axis_index("ctx"), lax.axis_index("fsdp")
        x, low, high = lax.rem(me, 2), lax.rem(me // 2, 2), me // 4
        to_x, to_low, to_high = ((flipped(me, bit), mine) for bit in (1, 2, 4))
        core, chip = flipped(mine, 1), flipped(mine, 2)
        diagonal = flipped(core, 2)
        ctx_peers = [(lax.rem(me + step, ctx), mine) for step in range(1, ctx)]
        near = [lax.rem(mine + step, fsdp) for step in range(1, fsdp)]
        greet(ctx_peers + [(me, other) for other in near])
        used, used_local, all_sends, loads = [0], [0], [], {}

        def push(source, target, peer):
            i = used[0]
            used[0] += 1
            copy = send(source, target, sends.at[i], recvs.at[i], peer)
            all_sends.append(copy)
            return copy

        def load(source, target):
            i = used_local[0]
            used_local[0] += 1
            copy = pltpu.make_async_copy(source, target, locals_.at[i])
            copy.start()
            return copy

        def normed_block(a, b, other):
            side = 1 - x if other else x
            block = (high + a - 2 * a * high) * 4 + (low + b - 2 * b * low) * 2 + side
            return normed_ref.at[pl.ds(pl.multiple_of(block * rows, rows), rows), :]

        def out_block(a, b, other):
            side = 1 - x if other else x
            block = (high + a - 2 * a * high) * 4 + (low + b - 2 * b * low) * 2 + side
            return g_out_ref.at[:, pl.ds(pl.multiple_of(block * cols, cols), cols)]

        def qkv_block(index):
            return g_qkv_ref.at[pl.ds(pl.multiple_of(index * part, part), part), :]

        def columns(index):
            return pl.ds(pl.multiple_of(index * small_cols, small_cols), small_cols)

        order = ((1, 1), (0, 1), (1, 0), (0, 0))
        small_copies = [
            push(small_ref.at[:, columns(other)], small_parts.at[i], (me, other))
            for i, other in enumerate(near)
        ]
        normed_copies = {
            ab: push(normed_block(*ab, True), normed_x.at[ab[0], ab[1]], to_x) for ab in order
        }

        low_copies = {
            (2, 0): push(up_low_ref, kept_low.at[2, 0], to_low),
            (0, 0): push(downs_ref.at[0], kept_low.at[0, 0], to_x),
        }
        early = {
            (1, 1): load(gate_far_ref, kept_low.at[1, 1]),
            (2, 1): load(up_far_ref, kept_low.at[2, 1]),
            (1, 0): load(gate_own_ref, kept_low.at[1, 0]),
        }
        kept_loads = {
            place: load(source, kept.at[place])
            for place, source in (
                ((1, 1), gate_high_ref),
                ((2, 1), up_high_ref),
                ((0, 0), downs_ref.at[1]),
                ((1, 0), gate_near_ref),
                ((2, 0), up_near_ref),
            )
        }
        qkv_copies = [
            push(qkv_block(diagonal), qkv_core.at[1], (me, core)),
            push(qkv_block(core), qkv_core.at[0], (me, core)),
        ]
        qkv_loads = [
            load(qkv_block(chip), qkv_own.at[1]),
            load(qkv_block(mine), qkv_own.at[0]),
        ]
        normed_loads = {
            ab: load(normed_block(*ab, False), normed_own.at[ab[0], ab[1]]) for ab in order
        }
        out_loads = {ab: load(out_block(*ab, False), out_own.at[ab[0], ab[1]]) for ab in order}

        total = small_ref[:, columns(mine)]
        for i, copy in enumerate(small_copies):
            copy.wait_recv()
            total = total + small_parts[i]
        small_sum[...] = total
        small_wide = [push(small_sum, small_held.at[i], peer) for i, peer in enumerate(ctx_peers)]

        qkv_copies[0].wait_recv()
        qkv_loads[0].wait()
        add_into(qkv_core.at[1], qkv_own.at[1], qkv_core.at[1])
        chip_copy = push(qkv_core.at[1], qkv_chip, (me, chip))

        def to_low_side(copies, loads, own, from_x, from_low, a):
            copies[a, 1].wait_recv()
            loads[a, 1].wait()
            add_into(from_x.at[a, 1], own.at[a, 1], from_x.at[a, 1])
            return push(from_x.at[a, 1], from_low.at[a], to_low)

        def to_high_side(copies, loads, lows, own, from_x, from_low, from_high):
            copies[1, 0].wait_recv()
            loads[1, 0].wait()
            lows[1].wait_recv()
            add_into(from_x.at[1, 0], own.at[1, 0], from_x.at[1, 0], from_low.at[1])
            return push(from_x.at[1, 0], from_high, to_high)

        def arrived(kind, a):
            if (kind, a) in early:
                early[kind, a].wait()
            else:
                low_copies[kind, a].wait_recv()

        def experts_high(kind):
            arrived(kind, 1)
            kept_loads[kind, 1].wait()
            add_into(kept_low.at[kind, 1], kept.at[kind, 1], kept_low.at[kind, 1])
            return push(kept_low.at[kind, 1], kept_high.at[kind], to_high)

        high_copies = {1: experts_high(1)}
        normed_args = (normed_copies, normed_loads)
        normed_lows = {1: to_low_side(*normed_args, normed_own, normed_x, normed_low, 1)}
        high_copies[2] = experts_high(2)
        normed_lows[0] = to_low_side(*normed_args, normed_own, normed_x, normed_low, 0)
        out_copies = {ab: push(out_block(*ab, True), out_x.at[ab[0], ab[1]], to_x) for ab in order}

        qkv_copies[1].wait_recv()
        qkv_loads[1].wait()
        chip_copy.wait_recv()
        add_into(qkv_sum, qkv_own.at[0], qkv_core.at[0], qkv_chip)

        def deal(kind):
            index = kind * ctx + me
            return pltpu.make_async_remote_copy(
                qkv_sum.at[:, pl.ds(kind * cols, cols)],
                dealt.at[lax.rem(index, kinds)],
                deal_sems.at[0, kind],
                deal_sems.at[1, lax.rem(index, kinds)],
                device_id=(index // kinds, mine),
                device_id_type=MESH,
            )

        def keep(kind):
            return pltpu.make_async_copy(
                qkv_sum.at[:, pl.ds(kind * cols, cols)],
                dealt.at[lax.rem(kind * ctx + me, kinds)],
                deal_sems.at[0, kind],
            )

        def is_far(kind):
            return (kind * ctx + me) // kinds != me

        for kind in range(kinds):
            pl.when(is_far(kind))(deal(kind).start)
            pl.when(jnp.logical_not(is_far(kind)))(keep(kind).start)

        normed_high_copy = to_high_side(
            *normed_args, normed_lows, normed_own, normed_x, normed_low, normed_high
        )
        out_args = (out_copies, out_loads)
        out_lows = {a: to_low_side(*out_args, out_own, out_x, out_low, a) for a in (1, 0)}

        def experts_end(kind):
            arrived(kind, 0)
            kept_loads[kind, 0].wait()
            sources = [kept.at[kind, 0], kept_low.at[kind, 0]]
            if kind > 0:
                high_copies[kind].wait_recv()
                sources.append(kept_high.at[kind])
            add_into((down_ref, gate_ref, up_ref)[kind], *sources)

        experts_end(0)

        normed_copies[0, 0].wait_recv()
        normed_loads[0, 0].wait()
        normed_lows[0].wait_recv()
        normed_high_copy.wait_recv()

        def norm_step(i, carry):
            span = pl.ds(pl.multiple_of(i * 16, 16), 16)
            grad = (
                normed_own[0, 0, span, :].astype(f32)
                + normed_x[0, 0, span, :].astype(f32)
                + normed_low[0, span, :].astype(f32)
                + normed_high[span, :].astype(f32)
            )
            values = tokens_ref[span, :].astype(f32)
            scale = rms_unit(values)
            unit = values * scale
            pulled = grad * gain_ref[...]
            input_ref[span, :] = mixed_ref[span, :] + scale * (
                pulled - unit * jnp.mean(unit * pulled, axis=-1, keepdims=True)
            )
            result_ref[span, :] = (forward_ref[span, :] + moved_ref[span, :].astype(f32)).astype(bf16)
            return carry

        lax.fori_loop(0, rows // 16, norm_step, 0)

        out_high_copy = to_high_side(*out_args, out_lows, out_own, out_x, out_low, out_high)
        experts_end(1)

        total = small_sum[...]
        for i, copy in enumerate(small_wide):
            copy.wait_recv()
            total = total + small_held[i]
        sums_ref[...] = total

        for kind in range(kinds):
            pl.when(is_far(kind))(deal(kind).wait_send)
            pl.when(jnp.logical_not(is_far(kind)))(keep(kind).wait)
        for slot in range(kinds):

            @pl.when(lax.rem(me * kinds + slot, ctx) != me)
            def _():
                pltpu.make_async_copy(
                    dealt.at[slot], dealt.at[slot], deal_sems.at[1, slot]
                ).wait()

            add_into(qkv_ref.at[:, pl.ds(slot * cols, cols)], dealt.at[slot])

        out_copies[0, 0].wait_recv()
        out_loads[0, 0].wait()
        out_lows[0].wait_recv()
        out_high_copy.wait_recv()
        add_into(out_ref, out_own.at[0, 0], out_x.at[0, 0], out_low.at[0], out_high)
        experts_end(2)
        for copy in all_sends:
            copy.wait_send()

    def block(*shape):
        return pltpu.VMEM(shape, bf16)

    gradient = (experts, units, cols)
    return comm_call(
        kernel,
        "finish_sums",
        collective_id,
        [
            jax.ShapeDtypeStruct(gradient, f32),
            jax.ShapeDtypeStruct(gradient, f32),
            jax.ShapeDtypeStruct(gradient, f32),
            jax.ShapeDtypeStruct((rows, width), f32),
            jax.ShapeDtypeStruct((part, cols), f32),
            jax.ShapeDtypeStruct((part, kinds * cols), f32),
            jax.ShapeDtypeStruct((small_rows, small_cols), f32),
            jax.ShapeDtypeStruct((rows, width), bf16),
        ],
        [ANY] * 12 + [VMEM] * 6,
        [VMEM] * 8,
        [
            block(kinds, 2, *gradient),
            block(kinds, 2, *gradient),
            block(kinds, *gradient),
            block(2, 2, rows, width),
            block(2, 2, rows, width),
            block(2, rows, width),
            block(rows, width),
            block(2, 2, part, cols),
            block(2, 2, part, cols),
            block(2, part, cols),
            block(part, cols),
            block(2, part, kinds * cols),
            block(2, part, kinds * cols),
            block(part, kinds * cols),
            block(part, kinds * cols),
            block(kinds, part, cols),
            pltpu.VMEM((fsdp - 1, small_rows, small_cols), f32),
            pltpu.VMEM((small_rows, small_cols), f32),
            pltpu.VMEM((ctx - 1, small_rows, small_cols), f32),
            DMA((copies_most,)),
            DMA((copies_most,)),
            DMA((32,)),
            DMA((2, kinds)),
        ],
        700 * 2**20,
        56,
    )(
        downs,
        *ups,
        gate_far,
        gate_own,
        up_far,
        normed_part,
        out_part,
        qkv_part,
        small,
        tokens,
        mixed_grad,
        gain,
        mixed,
        moved,
    )


def gather_inputs(tokens, w_qkv, dy, row_arrays, block, flips, collective_id):
    ctx, fsdp = lax.axis_size("ctx"), lax.axis_size("fsdp")
    rows, width = tokens.shape
    part = w_qkv.shape[0]
    kinds = 3
    cols = width // ctx
    line = ctx // 2
    chunks = 2
    size = rows // chunks
    row_count, flip_count = len(row_arrays), len(flips)
    small_count = row_count + 1

    def kernel(*refs):
        tokens_ref, w_qkv_ref, dy_ref = refs[:3]
        small_refs = refs[3 : 3 + small_count]
        all_ref, weight_ref, dy_all_ref = refs[3 + small_count : 6 + small_count]
        small_all_refs = refs[6 + small_count : 6 + 2 * small_count]
        refs = refs[6 + 2 * small_count :]
        run_kernel(
            tokens_ref,
            w_qkv_ref,
            dy_ref,
            small_refs,
            all_ref,
            weight_ref,
            dy_all_ref,
            small_all_refs,
            *refs,
        )

    def run_kernel(
        tokens_ref,
        w_qkv_ref,
        dy_ref,
        small_refs,
        all_ref,
        weight_ref,
        dy_all_ref,
        small_all_refs,
        *refs,
    ):
        flip_refs, dy_line_ref, refs = refs[:flip_count], refs[flip_count], refs[flip_count + 1 :]
        stage, weight_stage, dy_stage, sends, recvs, line_send, line_recv, cross_send, cross_recv, *refs = refs
        local_sems, line_out, cross_out = refs
        me, mine = lax.axis_index("ctx"), lax.axis_index("fsdp")
        z, x = me // 2, lax.rem(me, 2)
        to_x = (flipped(me, 1), mine)
        core, chip = (me, flipped(mine, 1)), (me, flipped(mine, 2))
        others = [flipped_by(me, flip) for flip in flips]
        greet(
            [(lax.rem(me + step, ctx), mine) for step in range(1, ctx)]
            + [(me, lax.rem(mine + step, fsdp)) for step in range(1, fsdp)]
            + [(other, lax.rem(mine + step, fsdp)) for other in others for step in range(1, fsdp)]
        )
        used, used_local, started, kept = [0], [0], [], []

        def push(source, target, peer):
            i = used[0]
            used[0] += 1
            copy = send(source, target, sends.at[i], recvs.at[i], peer)
            started.append(copy)
            return copy

        def load(source, target):
            i = used_local[0]
            used_local[0] += 1
            copy = pltpu.make_async_copy(source, target, local_sems.at[i])
            copy.start()
            kept.append(copy)

        def token_block(index):
            return all_ref.at[pl.ds(pl.multiple_of(index * rows, rows), rows), :]

        def token_chunk(index, chunk):
            start = pl.multiple_of(index * rows + chunk * size, size)
            return stage.at[pl.ds(start, size), :]

        def put(away, side, chunk, crossed):
            index = 2 * (z - away if side == 0 else z + away) + (1 - x if crossed else x)
            start = pl.multiple_of(index * rows + chunk * size, size)
            return pltpu.make_async_copy(
                stage.at[pl.ds(start, size), :],
                all_ref.at[pl.ds(start, size), :],
                (cross_out if crossed else line_out).at[side * line + away, chunk],
            )

        def taken(own, index, chunk):
            return tokens_ref.at[pl.ds(chunk * size, size), :] if own else token_chunk(index, chunk)

        def by_part(ref, index, count):
            return ref.at[pl.ds(pl.multiple_of(index * count, count), count), :]

        def cross(away, side, chunk):
            index = 2 * (z - away if side == 0 else z + away) + x
            i = side * line + away
            return pltpu.make_async_remote_copy(
                taken(away == 0, index, chunk),
                token_chunk(index, chunk),
                cross_send.at[i, chunk],
                cross_recv.at[i, chunk],
                device_id=to_x,
                device_id_type=MESH,
            )

        def along(away, side, chunk):
            index = 2 * (z - away if side == 0 else z + away) + x
            i = side * line + away
            return pltpu.make_async_remote_copy(
                taken(away == 0, index, chunk),
                token_chunk(index, chunk),
                line_send.at[i, chunk],
                line_recv.at[i, chunk],
                device_id=(me + 2 if side == 0 else me - 2, mine),
                device_id_type=MESH,
            )

        def has(away, side):
            return z >= away if side == 0 else z + away < line

        def goes_on(away, side):
            return jnp.logical_and(has(away, side), z < line - 1 if side == 0 else z > 0)

        for chunk in range(chunks):
            for side in range(2):
                pl.when(goes_on(0, side))(along(0, side, chunk).start)
            cross(0, 0, chunk).start()
        load(tokens_ref, token_block(me))

        own_weight = by_part(weight_stage, mine, part)
        pieces = []
        for kind in range(kinds):
            column = pl.ds(pl.multiple_of(kind * width + me * cols, cols), cols)
            target = own_weight.at[:, pl.ds(kind * cols, cols)]
            pieces.append(
                pltpu.make_async_copy(w_qkv_ref.at[:, column], target, local_sems.at[23 - kind])
            )
            pieces[-1].start()
        load(dy_ref, dy_stage)
        dy_loaded = kept.pop()
        for piece in pieces:
            piece.wait()
        weight_chip = [push(own_weight, own_weight, chip)]
        weight_core = [push(own_weight, own_weight, core)]
        load(own_weight, by_part(weight_ref, mine, part))
        columns = pl.ds(pl.multiple_of(mine * part, part), part)
        for i, (source, target) in enumerate(zip(small_refs, small_all_refs)):
            if i < row_count:
                target = target.at[:, columns]
            else:
                target = target.at[mine]
            for step in range(1, fsdp):
                push(source, target, (me, lax.rem(mine + step, fsdp)))
            load(source, target)
        dy_chip = push(dy_ref, by_part(dy_all_ref, mine, rows), chip)
        push(dy_ref, by_part(dy_all_ref, mine, rows), core)
        load(dy_ref, by_part(dy_all_ref, mine, rows))

        for away in range(1, line):
            for chunk in range(chunks):
                for side in range(2):

                    @pl.when(has(away, side))
                    def _():
                        index = 2 * (z - away if side == 0 else z + away) + x
                        pltpu.make_async_copy(
                            taken(True, index, chunk),
                            token_chunk(index, chunk),
                            line_recv.at[side * line + away - 1, chunk],
                        ).wait()
                        cross(away, side, chunk).start()
                        put(away, side, chunk, False).start()

                    if away < line - 1:
                        pl.when(goes_on(away, side))(along(away, side, chunk).start)
        for other, target in zip(others, flip_refs):
            for step in range(fsdp):
                push(small_refs[-1], target.at[mine], (other, lax.rem(mine + step, fsdp)))
        dy_loaded.wait()
        for i in range(line):
            wide = 2 * cols
            to = flipped_by(me, 2 * i)
            source = dy_stage.at[:, pl.ds(pl.multiple_of(to // 2 * wide, wide), wide)]
            if i == 0:
                load(source, dy_line_ref.at[0])
            else:
                push(source, dy_line_ref.at[i], (to, mine))

        for copy in weight_chip:
            copy.wait_recv()
        far = by_part(weight_stage, flipped(mine, 2), part)
        weight_far = push(far, far, core)
        load(far, by_part(weight_ref, flipped(mine, 2), part))
        for copy in weight_core:
            copy.wait_recv()
        near = flipped(mine, 1)
        load(by_part(weight_stage, near, part), by_part(weight_ref, near, part))
        dy_chip.wait_recv()
        far = by_part(dy_all_ref, flipped(mine, 2), rows)
        push(far, far, core)
        every = [(side, chunk) for side in range(2) for chunk in range(chunks)]
        weight_far.wait_recv()
        far = flipped_by(mine, 3)
        load(by_part(weight_stage, far, part), by_part(weight_ref, far, part))
        for chunk in range(chunks):
            cross(0, 0, chunk).wait_recv()
            put(0, 0, chunk, True).start()
        for away in range(1, line):
            for side, chunk in every:

                @pl.when(has(away, side))
                def _():
                    cross(away, side, chunk).wait_recv()
                    put(away, side, chunk, True).start()

        for copy in started:
            if not any(copy is other for other in [dy_chip, weight_far] + weight_chip + weight_core):
                copy.wait_recv()
        for copy in kept:
            copy.wait()
        for copy in started:
            copy.wait_send()
        for chunk in range(chunks):
            cross(0, 0, chunk).wait_send()
        for chunk in range(chunks):
            put(0, 0, chunk, True).wait()
        for away in range(1, line):
            for side, chunk in every:

                @pl.when(has(away, side))
                def _():
                    put(away, side, chunk, False).wait()
                    put(away, side, chunk, True).wait()

        for away in range(line - 1):
            for side, chunk in every:
                pl.when(goes_on(away, side))(along(away, side, chunk).wait_send)
        for away in range(1, line):
            for side, chunk in every:
                pl.when(has(away, side))(cross(away, side, chunk).wait_send)

    return comm_call(
        kernel,
        "gather_inputs",
        collective_id,
        [
            jax.ShapeDtypeStruct((ctx * rows, width), tokens.dtype),
            jax.ShapeDtypeStruct((fsdp * part, kinds * cols), w_qkv.dtype),
            jax.ShapeDtypeStruct((fsdp * rows, width), dy.dtype),
        ]
        + [jax.ShapeDtypeStruct((row.shape[0], fsdp * part), row.dtype) for row in row_arrays]
        + [jax.ShapeDtypeStruct((fsdp,) + block.shape, block.dtype)] * (1 + flip_count)
        + [jax.ShapeDtypeStruct((line, rows, 2 * cols), dy.dtype)],
        [ANY] * (3 + small_count),
        [ANY] * (4 + small_count + flip_count),
        [
            pltpu.VMEM((ctx * rows, width), tokens.dtype),
            pltpu.VMEM((fsdp * part, kinds * cols), w_qkv.dtype),
            pltpu.VMEM((rows, width), dy.dtype),
            DMA((64,)),
            DMA((64,)),
            DMA((2 * line, chunks)),
            DMA((2 * line, chunks)),
            DMA((2 * line, chunks)),
            DMA((2 * line, chunks)),
            DMA((24,)),
            DMA((2 * line, chunks)),
            DMA((2 * line, chunks)),
        ],
        150 * 2**20,
        60,
    )(tokens, w_qkv, dy, *row_arrays, block)


def project(tokens, gain, weight):
    total, width = tokens.shape
    wide = weight.shape[1]
    cols = wide // 3
    size = math.gcd(total, 256)
    f32 = jnp.float32

    def kernel(tokens_ref, gain_ref, weight_ref, normed_ref, lin_ref, squares_ref):
        values = tokens_ref[...].astype(f32)
        normed = (values * rms_unit(values) * gain_ref[...]).astype(jnp.bfloat16)
        normed_ref[...] = normed
        lin = jnp.dot(normed, weight_ref[...], preferred_element_type=f32)
        lin_ref[...] = lin
        for kind in range(2):
            piece = lin[:, kind * cols : (kind + 1) * cols]
            squares_ref[:, kind : kind + 1] = jnp.sum(piece * piece, axis=1, keepdims=True)

    def by_rows(columns):
        return pl.BlockSpec((size, columns), lambda i: (i, 0))

    return pl.pallas_call(
        kernel,
        grid=(total // size,),
        out_shape=[
            jax.ShapeDtypeStruct((total, width), jnp.bfloat16),
            jax.ShapeDtypeStruct((total, wide), f32),
            jax.ShapeDtypeStruct((total, 2), f32),
        ],
        in_specs=[
            by_rows(width),
            pl.BlockSpec((1, width), lambda i: (0, 0)),
            pl.BlockSpec((width, wide), lambda i: (0, 0)),
        ],
        out_specs=[by_rows(width), by_rows(wide), by_rows(2)],
        compiler_params=pltpu.CompilerParams(vmem_limit_bytes=60 * 2**20),
        cost_estimate=pl.CostEstimate(
            flops=3 * 10**9, bytes_accessed=15 * 2**20, transcendentals=0
        ),
        name="project",
    )(tokens, gain, weight)


def project_back(back, projected, scales, inner_sums, value_grad, weight, normed, tokens):
    total, width = tokens.shape
    wide = weight.shape[1]
    cols = wide // 3
    size = math.gcd(total, 256)
    steps, runs = total // size, 4
    f32, bf16 = jnp.float32, jnp.bfloat16

    def kernel(
        back_ref,
        lin_ref,
        scales_ref,
        sums_ref,
        value_ref,
        weight_ref,
        normed_ref,
        tokens_ref,
        part_ref,
        g_qkv_ref,
        gain_ref,
        proj,
    ):
        i = pl.program_id(0)

        @pl.when(i == 0)
        def _():
            gain_ref[...] = jnp.zeros_like(gain_ref)

        @pl.when(i < steps)
        def _():
            pieces = []
            for kind in range(2):
                scale = scales_ref[:, kind : kind + 1]
                unit = lin_ref[:, kind * cols : (kind + 1) * cols] * scale
                grad = scale * (back_ref[kind] - unit * sums_ref[:, kind : kind + 1])
                pieces.append(grad.astype(bf16))
            grads = jnp.concatenate(pieces + [value_ref[...]], axis=1)
            proj[pl.ds(pl.multiple_of(i * size, size), size), :] = grads
            part = lax.dot_general(
                grads, weight_ref[...], (((1,), (1,)), ((), ())), preferred_element_type=f32
            )
            values = tokens_ref[...].astype(f32)
            gain_ref[...] += jnp.sum(part * (values * rms_unit(values)), axis=0, keepdims=True)
            part_ref[...] = part.astype(bf16)

        @pl.when(i >= steps)
        def _():
            g_qkv_ref[...] = lax.dot_general(
                normed_ref[...], proj[...], (((0,), (0,)), ((), ())), preferred_element_type=f32
            ).astype(bf16)

    def by_rows(columns):
        return pl.BlockSpec((size, columns), lambda i: (jnp.minimum(i, steps - 1), 0))

    def later(i):
        return jnp.maximum(i - steps, 0)

    return pl.pallas_call(
        kernel,
        grid=(steps + runs,),
        out_shape=[
            jax.ShapeDtypeStruct((total, width), bf16),
            jax.ShapeDtypeStruct((width, wide), bf16),
            jax.ShapeDtypeStruct((1, width), f32),
        ],
        in_specs=[
            pl.BlockSpec((2, size, cols), lambda i: (0, jnp.minimum(i, steps - 1), 0)),
            by_rows(2 * cols),
            by_rows(2),
            by_rows(2),
            by_rows(cols),
            pl.BlockSpec((width, wide), lambda i: (0, 0)),
            pl.BlockSpec((total, width // runs), lambda i: (0, later(i))),
            by_rows(width),
        ],
        out_specs=[
            by_rows(width),
            pl.BlockSpec((width // runs, wide), lambda i: (later(i), 0)),
            pl.BlockSpec((1, width), lambda i: (0, 0)),
        ],
        scratch_shapes=[pltpu.VMEM((total, wide), bf16)],
        compiler_params=pltpu.CompilerParams(vmem_limit_bytes=60 * 2**20),
        cost_estimate=pl.CostEstimate(flops=0, bytes_accessed=2**20, transcendentals=0),
        name="project_back",
    )(back, projected, scales, inner_sums, value_grad, weight, normed, tokens)


def on_device_heads(
    tokens,
    doc_lengths,
    routes,
    slot_order,
    attn_gain,
    w_qkv,
    q_gain,
    k_gain,
    w_out,
    ffn_gain,
    w_router,
    w_gate,
    w_up,
    w_down,
    cotangent,
):
    rows, width = tokens.shape[1], tokens.shape[2]
    ctx, fsdp = lax.axis_size("ctx"), lax.axis_size("fsdp")
    me = lax.axis_index("ctx")
    head_dim = width // HEADS
    cols = HEADS // ctx * head_dim
    part = width // fsdp
    total = rows * ctx
    lengths = doc_lengths[0]
    bf16, f32 = jnp.bfloat16, jnp.float32

    experts, top = w_gate.shape[0], routes.shape[2]
    gains = jnp.concatenate([attn_gain, q_gain, k_gain, ffn_gain]).reshape(4, part)
    router_rows = jnp.pad(w_router.T, ((0, ROUTER_ROWS - experts), (0, 0)))
    pairs = jnp.concatenate([routes[0].T, slot_order[0].T], axis=0)
    pairs = jnp.pad(pairs, ((0, -pairs.shape[0] % 8), (0, 0)))
    tokens_all, qkv_weight, dy_all, gains, router_rows, *slots, dy_parts = gather_inputs(
        tokens[0],
        w_qkv,
        cotangent[0],
        [gains, router_rows],
        slots_of(pairs, experts, top),
        [1, 2, 4, 6],
        9,
    )
    row_gain_one, gain_query, gain_key, row_gain_two = (
        gains[i : i + 1].astype(f32) for i in range(4)
    )
    flips = [0, 2, 4, 6]
    dy_parts = lax.all_gather(dy_parts, "fsdp", axis=0)

    stream_pos = dealt_position(jnp.arange(total, dtype=jnp.int32), rows, ctx)
    stream_inner = document_info(stream_pos, lengths)[1]
    cosine, sine_part = rope_tables(stream_inner, head_dim)
    turn_tables = (
        jnp.concatenate([cosine, cosine], axis=1),
        jnp.concatenate([-sine_part, sine_part], axis=1),
    )
    places = jnp.arange(total, dtype=jnp.int32)
    sight = (
        (places - document_info(places, lengths)[1]).reshape(total, 1),
        places.reshape(total, 1),
        places.reshape(1, total),
    )
    normed_all, projected, squares = project(tokens_all, row_gain_one, qkv_weight)
    squares = squares.T
    squares = ctx_sum(squares.reshape(-1, 128), 1).reshape(2, total)
    scales = lax.rsqrt(squares / width + EPSILON).T
    own_gains = [
        lax.dynamic_slice_in_dim(gain, me * cols, cols, 1) for gain in (gain_query, gain_key)
    ]
    own_gains = jnp.concatenate(own_gains, axis=1)
    low, attended, attended_low, tops = attend(
        projected, scales, own_gains, *turn_tables, *sight, cols
    )

    attended_part = heads_to_rows(attended_low, 2)
    mixed_part = dot32("td,de->te", attended_part, w_out).astype(bf16)
    inputs = tokens[0].astype(f32)
    group, mixed, crossed = reduce_then_gather(
        mixed_part,
        [tokens[0], row_gain_two],
        [jax.ShapeDtypeStruct((rows, width), f32)],
        norm_chunk,
        "mix_and_norm",
        6,
        True,
        [],
        16,
    )

    capacity = rows * top // experts
    slot_by_expert, slots_other, *slots_line = slots
    moved_part, group_grad, g_router, scaled, gate_low, up_low = run_experts(
        group, dy_all, slot_by_expert, router_rows, w_gate, w_up, w_down, fsdp, capacity
    )
    scaled_line = [scaled] + [swap(scaled, flip) for flip in flips[1:]]
    mixed_all, mixed_grad, g_ffn_gain, gate_other, up_other = reduce_then_gather(
        group_grad,
        [mixed, row_gain_two, cotangent[0]],
        [jax.ShapeDtypeStruct((rows, width), f32), jax.ShapeDtypeStruct((1, width), f32)],
        norm_back_chunk,
        "norm_back",
        7,
        False,
        [gate_low, up_low],
        60,
    )
    g_ffn_gain = g_ffn_gain[0]
    crossed = lax.all_gather(crossed, "fsdp", axis=0, tiled=True)
    ups = expert_grads(
        [gate_low, up_low], [gate_other, up_other], group, crossed, slot_by_expert, slots_other, capacity
    )
    ups, mixed_all = lax.optimization_barrier((ups, mixed_all))
    output_part = dot32("te,de->td", mixed_all, w_out).astype(bf16)
    output_grad = rows_to_heads(output_part, 3)
    output_grad, moved_part, ups, mixed_all, scaled_line = lax.optimization_barrier(
        (output_grad, moved_part, ups, mixed_all, scaled_line)
    )
    moved = lax.psum_scatter(moved_part, "fsdp", scatter_dimension=0, tiled=True)
    gate_far, gate_own = swap(ups[3], 2), swap(ups[2], 2)
    downs = down_grads(scaled_line, dy_parts, [slot_by_expert] + slots_line, capacity)
    g_out = dot32("td,te->de", attended_part, mixed_all).astype(bf16)
    output_grad, ups, downs, g_out = lax.optimization_barrier((output_grad, ups, downs, g_out))

    back, value_grad, own_g_gains, inner_sums = attend_back(
        output_grad, low, attended, tops, projected, scales, own_gains, *turn_tables, *sight
    )
    inner_sums, gate_far = lax.optimization_barrier((inner_sums, gate_far))
    inner_sums = ctx_sum(inner_sums.T.reshape(-1, 128), 1)
    inner_sums, ups, gate_own = lax.optimization_barrier((inner_sums, ups, gate_own))
    up_far = swap(ups[7], 2)
    inner_sums = inner_sums.reshape(2, total).T / width

    normed_grad_part, g_qkv, g_attn_gain = project_back(
        back, projected, scales, inner_sums, value_grad, qkv_weight, normed_all, tokens_all
    )
    g_attn_gain = g_attn_gain[0]

    def placed_cols(values):
        return lax.dynamic_update_slice_in_dim(jnp.zeros((width,), f32), values, me * cols, 0)

    sums = jnp.concatenate(
        [
            jnp.stack([g_attn_gain, placed_cols(own_g_gains[0, 0]), placed_cols(own_g_gains[1, 0]), g_ffn_gain]),
            g_router[:experts],
        ],
        axis=0,
    )
    down_parts, gate_parts, up_parts, input_grad, out_part, qkv_part, sums, activations = finish_sums(
        downs,
        ups[0:2] + ups[4:7],
        gate_far,
        gate_own,
        up_far,
        normed_grad_part,
        g_out,
        g_qkv,
        jnp.pad(sums, ((0, -sums.shape[0] % 8), (0, 0))),
        tokens[0],
        mixed_grad,
        row_gain_one,
        mixed,
        moved,
        8,
    )
    return (
        activations[None],
        input_grad[None],
        sums[0],
        qkv_part,
        sums[1],
        sums[2],
        out_part,
        sums[3],
        sums[4 : 4 + experts].T,
        gate_parts,
        up_parts,
        down_parts,
    )


def solution(mesh):
    in_specs = (
        P("fsdp", "ctx", None),
        P("fsdp", None),
        P("fsdp", "ctx", None),
        P("fsdp", "ctx", None),
        P("fsdp"),
        P("fsdp", None),
        P("fsdp"),
        P("fsdp"),
        P("fsdp", None),
        P("fsdp"),
        P("fsdp", None),
        P(None, None, "fsdp"),
        P(None, None, "fsdp"),
        P(None, "fsdp", None),
        P("fsdp", "ctx", None),
    )
    out_specs = (
        P("fsdp", "ctx", None),
        P("fsdp", "ctx", None),
        P("fsdp"),
        P("fsdp", "ctx"),
        P("fsdp"),
        P("fsdp"),
        P("fsdp", "ctx"),
        P("fsdp"),
        P("fsdp", None),
        P(None, "ctx", "fsdp"),
        P(None, "ctx", "fsdp"),
        P(None, "fsdp", "ctx"),
    )
    ctx, fsdp = mesh.shape["ctx"], mesh.shape["fsdp"]
    by_heads = HEADS % ctx == 0 and ctx == 8 and fsdp == 4
    body = on_device_heads if by_heads else on_device
    return jax.shard_map(
        body, mesh=mesh, in_specs=in_specs, out_specs=out_specs, check_vma=False
    )
```
